32 devices in a mesh: dp: 4 (over y, x), fsdp: 8 (over z, core).
Axes of the slice: x: 2, y: 2, z: 4, core: 2. Of those that a mesh axis runs over, the one named last changes fastest.
Arguments:
- states: bfloat16 [16384, 1024], P(('dp', 'fsdp')), may hold values from -6 to 6
- pad_mask: int32 [128, 128], P(('dp', 'fsdp')), may hold values from 0 to 1, as said below
- query_proj: bfloat16 [1024, 1024], P(('dp', 'fsdp')), may hold values from -0.1875 to 0.1875
- key_proj: bfloat16 [1024, 1024], P(('dp', 'fsdp')), may hold values from -0.1875 to 0.1875
- value_proj: bfloat16 [1024, 1024], P(('dp', 'fsdp')), may hold values from -0.1875 to 0.1875
- attn_proj: bfloat16 [1024, 1024], P(('dp', 'fsdp')), may hold values from -2 to 2
- query_bias: bfloat16 [1024], P(('dp', 'fsdp')), may hold values from -3 to 3
- value_bias: bfloat16 [1024], P(('dp', 'fsdp')), may hold values from -3 to 3
- attn_bias: bfloat16 [1024], P(('dp', 'fsdp')), may hold values from -3 to 3
- first_gain: bfloat16 [1024], P(('dp', 'fsdp')), may hold values from 0.5 to 1.5
- first_shift: bfloat16 [1024], P(('dp', 'fsdp')), may hold values from -3 to 3
- inner_proj: bfloat16 [1024, 4096], P(('dp', 'fsdp')), may hold values from -0.1875 to 0.1875
- inner_bias: bfloat16 [4096], P(('dp', 'fsdp')), may hold values from -3 to 3
- outer_proj: bfloat16 [4096, 1024], P(('dp', 'fsdp')), may hold values from -0.09375 to 0.09375
- outer_bias: bfloat16 [1024], P(('dp', 'fsdp')), may hold values from -3 to 3
- second_gain: bfloat16 [1024], P(('dp', 'fsdp')), may hold values from 0.5 to 1.5
- second_shift: bfloat16 [1024], P(('dp', 'fsdp')), may hold values from -3 to 3
- out_grad: bfloat16 [16384, 1024], P(('dp', 'fsdp')), may hold values from -6 to 6
Outputs:
- encoded: bfloat16 [16384, 1024], P(('dp', 'fsdp'))
- states_grad: float32 [16384, 1024], P(('dp', 'fsdp'))
- query_grad: float32 [1024, 1024], P(('dp', 'fsdp'))
- keys_grad: float32 [1024, 1024], P(('dp', 'fsdp'))
- values_grad: float32 [1024, 1024], P(('dp', 'fsdp'))
- attn_grad: float32 [1024, 1024], P(('dp', 'fsdp'))
- qbias_grad: float32 [1024], P(('dp', 'fsdp'))
- vbias_grad: float32 [1024], P(('dp', 'fsdp'))
- abias_grad: float32 [1024], P(('dp', 'fsdp'))
- fgain_grad: float32 [1024], P(('dp', 'fsdp'))
- fshift_grad: float32 [1024], P(('dp', 'fsdp'))
- inner_grad: float32 [1024, 4096], P(('dp', 'fsdp'))
- ibias_grad: float32 [4096], P(('dp', 'fsdp'))
- outer_grad: float32 [4096, 1024], P(('dp', 'fsdp'))
- obias_grad: float32 [1024], P(('dp', 'fsdp'))
- sgain_grad: float32 [1024], P(('dp', 'fsdp'))
- sshift_grad: float32 [1024], P(('dp', 'fsdp'))
The draws below stay inside these ranges and needn't reach their ends.
Inputs may be any that keep to these rules, and one draw needn't show every extreme that they name: `pad_mask`: in each segment the ones form a prefix of 32 to 128 tokens.
All inputs are finite; a program needn't handle non-finite values.
Results may differ from the reference program's by a relative error of at most 0.014.
Values may be sent and summed in bfloat16 or wider, within the bound.
A program may use at most 256 MiB of HBM per device.

```python
import math
import jax
import jax.numpy as jnp
from jax import lax

D = 1024
HEADS = 16
FF = 4096
HDIM = 64
SEG_LEN = 128
SEGS = 128
TOKENS = 16384


def draw_pad_mask(key, part):
    key = jax.random.fold_in(key, 11)
    lengths = jax.random.randint(key, (SEGS,), SEG_LEN // 4, SEG_LEN + 1)
    lengths = lengths.at[0].set(SEG_LEN // 4).at[1].set(SEG_LEN)
    places = jnp.arange(SEG_LEN, dtype=jnp.int32)
    return (places[None, :] < lengths[:, None]).astype(jnp.int32)


def spiked(array, rng, source, target, parts, factor):
    def block_of(axis_at):
        return (jnp.arange(array.shape[axis_at]) // (array.shape[axis_at] // parts)).reshape((-1,) + (1,) * (array.ndim - 1 - axis_at))

    first = jax.random.permutation(rng, parts)[block_of(target)]
    far = (block_of(target) + parts // 2) % parts
    return jnp.where((block_of(source) == first) | (block_of(source) == far), factor * array, array)


def block_scale(key, extent, cuts, smallest, high):
    def one(axis_at, shards_of):
        draws = jax.random.uniform(jax.random.fold_in(jax.random.fold_in(key, 6), axis_at), (shards_of,), jnp.float32, smallest / len(cuts), high / len(cuts))
        return jnp.repeat(jnp.exp(draws), extent[axis_at] // shards_of).reshape((-1,) + (1,) * (len(extent) - axis_at - 1))

    level = one(*cuts[0])
    for cut in cuts[1:]:
        level = level * one(*cut)
    return level


def noise(own_key, dims, deviation, bound, shards=(), held_as=jnp.bfloat16):
    values = deviation * jax.random.normal(own_key, dims, jnp.float32)
    if shards:
        values = values * block_scale(own_key, dims, shards, -0.22, 0.18)
    return jnp.clip(values, -bound, bound).astype(held_as)


def bell_draw_with(own_key, extent, scale, reach, pieces, heavy, kind=jnp.bfloat16):
    values = scale * jax.random.normal(own_key, extent, jnp.float32)
    if pieces:
        values = values * block_scale(own_key, extent, pieces, -0.22, 0.18)
    return jnp.clip(spiked(values, jax.random.fold_in(own_key, 3), *heavy), -reach, reach).astype(kind)


def setup_inputs(seed: int = 0) -> dict:
    key_of = jax.random.split(jax.random.key(seed), 19)
    states = bell_draw_with(key_of[0], (TOKENS, D), 1.0, 6.0, ((0, 32),), (0, 1, 32, 2.75))
    pad_mask = draw_pad_mask(jax.random.fold_in(key_of[18], 71), 0)
    query_proj = noise(key_of[2], (D, D), D ** -0.5, 0.1875, ((0, 32),))
    key_proj = noise(key_of[3], (D, D), D ** -0.5, 0.1875, ((0, 32),))
    value_proj = noise(key_of[4], (D, D), D ** -0.5, 0.1875, ((0, 32),))
    attn_proj = noise(key_of[5], (D, D), (D // SEG_LEN) ** -0.5, 2.0, ((0, 32),))
    query_bias = noise(key_of[6], (D,), 0.5, 3.0, ((0, 32),))
    value_bias = noise(key_of[7], (D,), 0.5, 3.0, ((0, 32),))
    attn_bias = noise(key_of[8], (D,), 0.5, 3.0, ((0, 32),))
    first_gain = jnp.clip(1.0 + 0.1 * jax.random.normal(key_of[9], (D,), jnp.float32), 0.5, 1.5).astype(jnp.bfloat16)
    first_shift = noise(key_of[10], (D,), 0.5, 3.0, ((0, 32),))
    inner_proj = noise(key_of[11], (D, FF), D ** -0.5, 0.1875, ((0, 32),))
    inner_bias = noise(key_of[12], (FF,), 0.5, 3.0, ((0, 32),))
    outer_proj = noise(key_of[13], (FF, D), FF ** -0.5, 0.09375, ((0, 32),))
    outer_bias = noise(key_of[14], (D,), 0.5, 3.0, ((0, 32),))
    second_gain = jnp.clip(1.0 + 0.1 * jax.random.normal(key_of[15], (D,), jnp.float32), 0.5, 1.5).astype(jnp.bfloat16)
    second_shift = noise(key_of[16], (D,), 0.5, 3.0, ((0, 32),))
    out_grad = bell_draw_with(key_of[17], (TOKENS, D), 1.0, 6.0, ((0, 32),), (0, 1, 32, 2.75))
    return {"states": states, "pad_mask": pad_mask, "query_proj": query_proj, "key_proj": key_proj, "value_proj": value_proj, "attn_proj": attn_proj, "query_bias": query_bias, "value_bias": value_bias, "attn_bias": attn_bias, "first_gain": first_gain, "first_shift": first_shift, "inner_proj": inner_proj, "inner_bias": inner_bias, "outer_proj": outer_proj, "outer_bias": outer_bias, "second_gain": second_gain, "second_shift": second_shift, "out_grad": out_grad}


@jax.custom_vjp
def low(v):
    return lax.optimization_barrier(v.astype(jnp.bfloat16)).astype(jnp.float32)

@jax.custom_vjp
def low_back(v):
    return v

def low_keep(v):
    return (low(v), None)

def low_pass(kept, grad):
    return (grad,)

def back_keep(v):
    return (v, None)

def back_low(kept, grad):
    return (low(grad),)
low.defvjp(low_keep, low_pass)
low_back.defvjp(back_keep, back_low)
epsilon = 1e-05
neg_fill = -1e+30

def rounded_both(value):
    return low(low_back(value))

def matmul(left, right):
    return jnp.dot(left, right, precision=lax.Precision.HIGHEST)

def normalize(hidden, gain, shift):
    center = hidden - lax.optimization_barrier(jnp.mean(hidden, axis=-1, keepdims=True))
    spread = lax.optimization_barrier(jnp.mean(center * center, axis=-1, keepdims=True))
    return center * lax.rsqrt(spread + epsilon) * gain + shift

def forward(rows, keep, query_proj, key_proj, value_proj, attn_proj, query_bias, value_bias, attn_bias, first_gain, first_shift, inner_proj, inner_bias, outer_proj, outer_bias, second_gain, second_shift):
    segments = keep.shape[0]
    shape_heads = (segments, SEG_LEN, HEADS, HDIM)
    queries = rounded_both(matmul(rows, query_proj) + query_bias).reshape(shape_heads)
    keysets = rounded_both(matmul(rows, key_proj)).reshape(shape_heads)
    valuesets = rounded_both(matmul(rows, value_proj) + value_bias).reshape(shape_heads)
    scores = jnp.einsum('sqhd,skhd->shqk', queries, keysets, precision=lax.Precision.HIGHEST) * HDIM ** (-0.5)
    scores = low_back(scores)
    scores = jnp.where(keep[:, None, None, :] > 0, scores, neg_fill)
    peaks = lax.optimization_barrier(jnp.max(scores, axis=-1, keepdims=True))
    raised = jnp.exp(scores - peaks)
    probs = low(raised / lax.optimization_barrier(jnp.sum(raised, axis=-1, keepdims=True)))
    context = jnp.einsum('shqk,skhd->sqhd', probs, valuesets, precision=lax.Precision.HIGHEST)
    context = rounded_both(context.reshape(rows.shape[0], D))
    attended = low_back(matmul(context, attn_proj) + attn_bias)
    first_norm = normalize(rows + attended, first_gain, first_shift)
    inner_act = low_back(matmul(low(first_norm), inner_proj) + inner_bias)
    activated = low(jax.nn.gelu(inner_act, approximate=False))
    outer_act = low_back(matmul(activated, outer_proj) + outer_bias)
    return normalize(first_norm + outer_act, second_gain, second_shift)

def reference(states, pad_mask, query_proj, key_proj, value_proj, attn_proj, query_bias, value_bias, attn_bias, first_gain, first_shift, inner_proj, inner_bias, outer_proj, outer_bias, second_gain, second_shift, out_grad):
    params = tuple((weight.astype(jnp.float32) for weight in (query_proj, key_proj, value_proj, attn_proj, query_bias, value_bias, attn_bias, first_gain, first_shift, inner_proj, inner_bias, outer_proj, outer_bias, second_gain, second_shift)))
    group = math.gcd(SEGS, max(1, 4096 // SEG_LEN))
    blocks = SEGS // group
    rows_all = states.reshape(blocks, group * SEG_LEN, D)
    keep_all = pad_mask.reshape(blocks, group, SEG_LEN)
    cot_all = out_grad.reshape(blocks, group * SEG_LEN, D)

    def one_block(totals, inputs):
        rows, keep, cotangent = inputs

        def apply(block_rows, *weights):
            return forward(block_rows, keep, *weights)
        result, pull = jax.vjp(apply, rows.astype(jnp.float32), *params)
        pulled = pull(cotangent.astype(jnp.float32))
        totals = tuple((left + right for left, right in zip(totals, pulled[1:])))
        return (totals, (result.astype(jnp.bfloat16), pulled[0]))
    start = tuple((jnp.zeros(weight.shape, jnp.float32) for weight in params))
    totals, (encoded, states_grad) = lax.scan(one_block, start, (rows_all, keep_all, cot_all))
    return (encoded.reshape(TOKENS, D), states_grad.reshape(TOKENS, D), totals[0], totals[1], totals[2], totals[3], totals[4], totals[5], totals[6], totals[7], totals[8], totals[9], totals[10], totals[11], totals[12], totals[13], totals[14])
```

```python
import functools

import jax
import jax.numpy as jnp
from jax import lax
from jax.experimental import pallas as pl
from jax.experimental.pallas import tpu as pltpu
from jax.sharding import PartitionSpec as P

HEADS = 16
MESH = pl.DeviceIdType.MESH

epsilon = 1e-05
neg_fill = -1e30


class Place:
    def __init__(self, depth):
        dp = lax.axis_index("dp")
        fsdp = lax.axis_index("fsdp")
        self.depth = depth
        self.dp = dp
        self.z = fsdp // 2
        self.core = lax.rem(fsdp, 2)
        flip_x = dp + 1 - 2 * lax.rem(dp, 2)
        flip_y = lax.rem(dp + 2, 4)
        self.near = flip_x + self.core * (flip_y - flip_x)
        self.far = flip_y + self.core * (flip_x - flip_y)
        self.both = lax.rem(flip_x + 2, 4)
        self.fsdp = fsdp
        self.sibling = fsdp + 1 - 2 * self.core

    def up(self, step):
        return lax.rem(self.z + step, self.depth)

    def down(self, step):
        return lax.rem(self.z + self.depth - step, self.depth)

    def along(self, z):
        return (self.dp, z * 2 + self.core)

    def greet(self):
        barrier = pltpu.get_barrier_semaphore()
        others = [self.along(self.up(step)) for step in range(1, self.depth)]
        others += [(self.near, self.fsdp), (self.far, self.fsdp), (self.dp, self.sibling)]
        for other in others:
            pl.semaphore_signal(barrier, inc=1, device_id=other, device_id_type=MESH)
        pl.semaphore_wait(barrier, len(others))


def remote(source, target, send, recv, device):
    return pltpu.make_async_remote_copy(
        src_ref=source, dst_ref=target, send_sem=send, recv_sem=recv, device_id=device, device_id_type=MESH
    )


class Gather:
    def __init__(self, place, full, sems, piece):
        self.place, self.full, self.piece = place, full, piece
        self.sz, self.rz, self.sb, self.rb, self.sa, self.ra, self.sc, self.rc = sems

    def copy_z(self, step, arriving=False):
        p = self.place
        z = p.down(step) if arriving else p.z
        block = self.full.at[p.dp, z, p.core]
        return remote(block, block, self.sz.at[self.piece, step - 1], self.rz.at[self.piece, step - 1], p.along(p.up(step)))

    def copy_near(self, step, arriving=False):
        p = self.place
        block = self.full.at[p.near if arriving else p.dp, p.down(step), p.core]
        return remote(block, block, self.sb.at[self.piece, step], self.rb.at[self.piece, step], (p.near, p.fsdp))

    def copy_far(self, half, step, arriving=False):
        p = self.place
        row = (p.both if half else p.far) if arriving else (p.near if half else p.dp)
        block = self.full.at[row, p.down(step), p.core]
        at = half * p.depth + step
        return remote(block, block, self.sa.at[self.piece, at], self.ra.at[self.piece, at], (p.far, p.fsdp))

    def copy_core(self, part, arriving=False):
        p = self.place
        if arriving:
            row = (p.dp, p.far, p.near, p.both)[part]
            block = self.full.at[row, :, 1 - p.core]
        else:
            row = (p.dp, p.near, p.far, p.both)[part]
            block = self.full.at[row, :, p.core]
        return remote(block, block, self.sc.at[self.piece, part], self.rc.at[self.piece, part], (p.dp, p.sibling))

    def start_z(self):
        for step in range(1, self.place.depth):
            self.copy_z(step).start()
        self.copy_near(0).start()
        self.copy_far(0, 0).start()

    def spread(self):
        for step in range(1, self.place.depth):
            self.copy_z(step, True).wait_recv()
            self.copy_near(step).start()
            self.copy_far(0, step).start()
        self.copy_core(0).start()

    def spread_far(self):
        for step in range(self.place.depth):
            self.copy_near(step, True).wait_recv()
            self.copy_far(1, step).start()
        self.copy_core(1).start()

    def finish(self):
        p = self.place
        for half in range(2):
            for step in range(p.depth):
                self.copy_far(half, step, True).wait_recv()
            self.copy_core(2 + half).start()
        for part in range(4):
            self.copy_core(part, True).wait_recv()

    def drain(self):
        p = self.place
        for step in range(1, p.depth):
            self.copy_z(step).wait_send()
        for step in range(p.depth):
            self.copy_near(step).wait_send()
            self.copy_far(0, step).wait_send()
            self.copy_far(1, step).wait_send()
        for part in range(4):
            self.copy_core(part).wait_send()


def gather_sems(pieces, depth):
    counts = (depth - 1, depth - 1, depth, depth, 2 * depth, 2 * depth, 4, 4)
    return [pltpu.SemaphoreType.DMA((pieces, count)) for count in counts]


def gather_kernel(depth, groups, *refs):
    count = sum(groups)
    sources = refs[:count]
    fulls = refs[count : count + len(groups)]
    own_sem = refs[count + len(groups)]
    sems = refs[count + len(groups) + 1 :]
    place = Place(depth)
    local = []
    at = 0
    for full, parts in zip(fulls, groups):
        width = full.shape[4] // parts
        for part in range(parts):
            target = full.at[place.dp, place.z, place.core, :, pl.ds(part * width, width)]
            local.append(pltpu.make_async_copy(sources[at], target, own_sem.at[at]))
            at += 1
    for copy in local:
        copy.start()
    place.greet()
    for copy in local:
        copy.wait()
    nets = [Gather(place, full, sems, piece) for piece, full in enumerate(fulls)]
    for net in nets:
        net.start_z()
    for net in nets:
        net.spread()
        net.spread_far()
    for net in nets:
        net.finish()
    for net in nets:
        net.drain()


def gather_all(depth, groups):
    flat = [block for group in groups for block in group]
    shapes = []
    for group in groups:
        rows = group[0].shape[0]
        columns = sum(block.shape[1] for block in group)
        shapes.append(jax.ShapeDtypeStruct((4, depth, 2, rows, columns), group[0].dtype))
    return pl.pallas_call(
        functools.partial(gather_kernel, depth, tuple(len(group) for group in groups)),
        out_shape=shapes,
        in_specs=[pl.BlockSpec(memory_space=pl.ANY)] * len(flat),
        out_specs=[pl.BlockSpec(memory_space=pl.ANY)] * len(shapes),
        scratch_shapes=[pltpu.SemaphoreType.DMA((len(flat),))] + gather_sems(len(groups), depth),
        compiler_params=pltpu.CompilerParams(collective_id=0, has_side_effects=True),
        name="gather_weights",
    )(*flat)


def add_into(target, other):
    count, rows, _ = target.shape
    tile = 8 if target.dtype == jnp.float32 else 16
    steps = rows // tile

    def one(index, _):
        part = index // steps
        at = pl.ds(pl.multiple_of(lax.rem(index, steps) * tile, tile), tile)
        target[part, at, :] = target[part, at, :] + other[part, at, :]
        return 0

    lax.fori_loop(0, count * steps, one, 0)


class Scatter:
    def __init__(self, place, sums, slots, sems, piece):
        self.place, self.sums, self.piece = place, sums, piece
        self.from_core, self.from_far, self.from_near, self.from_z = slots
        self.sc, self.rc, self.sa, self.ra, self.sb, self.rb, self.sz, self.rz = sems

    def copy_core(self, whole, part):
        p = self.place
        return remote(
            whole.at[part, :, 1 - p.core], self.from_core.at[part], self.sc.at[self.piece, part],
            self.rc.at[self.piece, part], (p.dp, p.sibling),
        )

    def rows_of(self, half, away):
        p = self.place
        if away:
            return p.both if half else p.far
        return p.near if half else p.dp

    def copy_far(self, half):
        p = self.place
        return remote(
            self.sums.at[self.rows_of(half, True)], self.from_far.at[half], self.sa.at[self.piece, half],
            self.ra.at[self.piece, half], (p.far, p.fsdp),
        )

    def copy_near(self):
        p = self.place
        return remote(
            self.sums.at[p.near], self.from_near, self.sb.at[self.piece], self.rb.at[self.piece], (p.near, p.fsdp)
        )

    def copy_z(self, step):
        p = self.place
        return remote(
            self.sums.at[p.dp, p.up(step)], self.from_z.at[step - 1], self.sz.at[self.piece, step - 1],
            self.rz.at[self.piece, step - 1], p.along(p.up(step)),
        )

    def add_core(self, whole):
        p = self.place
        for half in (1, 0):
            for away in (True, False):
                row = self.rows_of(half, away)
                self.copy_core(whole, row).wait_recv()
                add_into(self.sums.at[row], self.from_core.at[row])
                if away:
                    self.copy_far(half).start()

    def add_far(self, half):
        self.copy_far(half).wait_recv()
        add_into(self.sums.at[self.rows_of(half, False)], self.from_far.at[half])
        if half:
            self.copy_near().start()

    def add_near(self):
        p = self.place
        self.copy_near().wait_recv()
        add_into(self.sums.at[p.dp], self.from_near)
        for step in range(1, p.depth):
            self.copy_z(step).start()

    def finish(self, out):
        p = self.place
        for step in range(1, p.depth):
            self.copy_z(step).wait_recv()
        rows = out.shape[0]
        tile = 8 if self.sums.dtype == jnp.float32 else 16

        def one(index, _):
            at = pl.ds(pl.multiple_of(index * tile, tile), tile)
            total = self.sums[p.dp, p.z, at, :].astype(jnp.float32)
            for step in range(p.depth - 1):
                total = total + self.from_z[step, at, :].astype(jnp.float32)
            out[at, :] = total
            return 0

        lax.fori_loop(0, rows // tile, one, 0)

    def drain(self, whole):
        for part in range(4):
            self.copy_core(whole, part).wait_send()
        self.copy_far(1).wait_send()
        self.copy_far(0).wait_send()
        self.copy_near().wait_send()
        for step in range(1, self.place.depth):
            self.copy_z(step).wait_send()


def scatter_sems(pieces, depth):
    dma = pltpu.SemaphoreType.DMA
    return [
        dma((pieces, 4)), dma((pieces, 4)), dma((pieces, 2)), dma((pieces, 2)), dma((pieces,)), dma((pieces,)),
        dma((pieces, depth - 1)), dma((pieces, depth - 1)),
    ]


def scatter_slots(shape, dtype):
    dps, depth, _, rows, columns = shape
    return [
        pltpu.VMEM((dps, depth, rows, columns), dtype),
        pltpu.VMEM((dps, depth, rows, columns), dtype),
        pltpu.VMEM((2, depth, rows, columns), dtype),
        pltpu.VMEM((depth, rows, columns), dtype),
        pltpu.VMEM((depth - 1, rows, columns), dtype),
    ]


def scatter_kernel(depth, count, *refs):
    wholes = refs[:count]
    outs = refs[count : 2 * count]
    scratch = refs[2 * count : 7 * count]
    own_sem = refs[7 * count]
    sems = refs[7 * count + 1 :]
    place = Place(depth)
    nets = []
    local = []
    for piece in range(count):
        sums, *slots = scratch[5 * piece : 5 * piece + 5]
        nets.append(Scatter(place, sums, slots, sems, piece))
        local.append(pltpu.make_async_copy(wholes[piece].at[:, :, place.core], sums, own_sem.at[piece]))
    for copy in local:
        copy.start()
    place.greet()
    for net, whole in zip(nets, wholes):
        for half in (1, 0):
            for away in (False, True):
                net.copy_core(whole, net.rows_of(half, away)).start()
    for piece in range(count):
        local[piece].wait()
        nets[piece].add_core(wholes[piece])
    for net in nets:
        net.add_far(1)
        net.add_far(0)
        net.add_near()
    for net, out in zip(nets, outs):
        net.finish(out)
    for net, whole in zip(nets, wholes):
        net.drain(whole)


def scatter_all(depth, wholes):
    shapes = [jax.ShapeDtypeStruct(whole.shape[3:], jnp.float32) for whole in wholes]
    scratch = []
    for whole in wholes:
        scratch += scatter_slots(whole.shape, whole.dtype)
    return pl.pallas_call(
        functools.partial(scatter_kernel, depth, len(wholes)),
        out_shape=shapes,
        in_specs=[pl.BlockSpec(memory_space=pl.ANY)] * len(wholes),
        out_specs=[pl.BlockSpec(memory_space=pltpu.VMEM)] * len(wholes),
        scratch_shapes=scratch + [pltpu.SemaphoreType.DMA((len(wholes),))] + scatter_sems(len(wholes), depth),
        compiler_params=pltpu.CompilerParams(
            collective_id=1, has_side_effects=True, vmem_limit_bytes=60 * 1024 * 1024
        ),
        name="scatter_gradients",
    )(*wholes)


def normalize(hidden, gain, shift):
    center = hidden - jnp.mean(hidden, axis=-1, keepdims=True)
    spread = jnp.mean(center * center, axis=-1, keepdims=True)
    return center * lax.rsqrt(spread + epsilon) * gain + shift


def exact_gelu(value):
    return jax.nn.gelu(value, approximate=False)


def contract_rows(left, right):
    return lax.dot_general(
        left, right, (((0,), (0,)), ((), ())), preferred_element_type=jnp.float32
    )


def times_transposed(left, right):
    return lax.dot_general(
        left, right, (((1,), (1,)), ((), ())), preferred_element_type=jnp.float32
    )


def collect(merged, attn, inner, outer, vectors, widened):
    return (
        lax.all_gather(merged, ("dp", "fsdp"), axis=0, tiled=True),
        lax.all_gather(attn, ("dp", "fsdp"), axis=0, tiled=True),
        lax.all_gather(inner, ("dp", "fsdp"), axis=0, tiled=True),
        lax.all_gather(outer, ("dp", "fsdp"), axis=0, tiled=True),
        lax.all_gather(vectors, ("dp", "fsdp"), axis=0, tiled=True),
        lax.all_gather(widened, ("dp", "fsdp"), axis=0, tiled=True),
    )


def reduce_grads(merged, attn, inner, outer, vectors, widened):
    return (
        lax.psum_scatter(merged, ("dp", "fsdp"), scatter_dimension=0, tiled=True),
        lax.psum_scatter(attn, ("dp", "fsdp"), scatter_dimension=0, tiled=True),
        lax.psum_scatter(inner, ("dp", "fsdp"), scatter_dimension=0, tiled=True),
        lax.psum_scatter(outer, ("dp", "fsdp"), scatter_dimension=0, tiled=True),
        lax.psum_scatter(vectors, ("dp", "fsdp"), scatter_dimension=0, tiled=True),
        lax.psum_scatter(widened, ("dp", "fsdp"), scatter_dimension=0, tiled=True),
    )


def split_heads(projected, segments):
    total_rows, triple = projected.shape
    width = triple // 3
    return projected.reshape(segments, total_rows // segments, 3, HEADS, width // HEADS)


def attention_probs(queries, keysets, keep, scale):
    scores = (
        jnp.einsum("sqhd,skhd->shqk", queries, keysets, preferred_element_type=jnp.float32) * scale
    )
    scores = jnp.where(keep[:, None, None, :] > 0, scores, neg_fill)
    peaks = jnp.max(scores, axis=-1, keepdims=True)
    raised = jnp.exp(scores - peaks)
    return raised / jnp.sum(raised, axis=-1, keepdims=True)


def forward_pass(rows, keep, weights):
    merged, attn, inner, outer, vectors, widened = weights
    vector_full = vectors.astype(jnp.float32)
    width = rows.shape[1]
    scale = (width // HEADS) ** (-0.5)
    merged_bias = jnp.concatenate(
        (vector_full[:, 0], jnp.zeros((width,), jnp.float32), vector_full[:, 1])
    )
    projected = (jnp.dot(rows, merged, preferred_element_type=jnp.float32) + merged_bias).astype(
        jnp.bfloat16
    )
    split = split_heads(projected, keep.shape[0])
    probs = attention_probs(split[:, :, 0], split[:, :, 1], keep, scale).astype(jnp.bfloat16)
    context = jnp.einsum(
        "shqk,skhd->sqhd", probs, split[:, :, 2], preferred_element_type=jnp.float32
    )
    context = context.reshape(rows.shape[0], width).astype(jnp.bfloat16)
    attended = jnp.dot(context, attn, preferred_element_type=jnp.float32) + vector_full[:, 2]
    first_sum = rows.astype(jnp.float32) + attended
    first_norm = normalize(first_sum, vector_full[:, 3], vector_full[:, 4])
    first_low = first_norm.astype(jnp.bfloat16)
    inner_act = jnp.dot(first_low, inner, preferred_element_type=jnp.float32) + widened.astype(
        jnp.float32
    )
    activated = exact_gelu(inner_act).astype(jnp.bfloat16)
    outer_act = jnp.dot(activated, outer, preferred_element_type=jnp.float32) + vector_full[:, 5]
    second_sum = first_norm + outer_act
    encoded = normalize(second_sum, vector_full[:, 6], vector_full[:, 7]).astype(jnp.bfloat16)
    return (encoded, (projected, context, first_sum, first_low, inner_act, activated, second_sum))


def backward_pass(rows, keep, cotangent, weights, kept):
    merged, attn, inner, outer, vectors, widened = weights
    projected, context, first_sum, first_low, inner_act, activated, second_sum = kept
    vector_full = vectors.astype(jnp.float32)
    width = rows.shape[1]
    scale = (width // HEADS) ** (-0.5)
    second_out, second_pull = jax.vjp(normalize, second_sum, vector_full[:, 6], vector_full[:, 7])
    second_grad, second_gain_g, second_shift_g = second_pull(cotangent.astype(jnp.float32))
    outer_low = second_grad.astype(jnp.bfloat16)
    outer_bias_g = jnp.sum(outer_low.astype(jnp.float32), axis=0)
    outer_weight_g = contract_rows(activated, outer_low)
    act_grad = times_transposed(outer_low, outer)
    gelu_out, gelu_pull = jax.vjp(exact_gelu, inner_act)
    inner_low = gelu_pull(act_grad)[0].astype(jnp.bfloat16)
    inner_bias_g = jnp.sum(inner_low.astype(jnp.float32), axis=0)
    inner_weight_g = contract_rows(first_low, inner_low)
    first_total = second_grad + times_transposed(inner_low, inner)
    first_out, first_pull = jax.vjp(normalize, first_sum, vector_full[:, 3], vector_full[:, 4])
    first_grad, first_gain_g, first_shift_g = first_pull(first_total)
    attended_low = first_grad.astype(jnp.bfloat16)
    attn_bias_g = jnp.sum(attended_low.astype(jnp.float32), axis=0)
    attn_weight_g = contract_rows(context, attended_low)
    context_low = times_transposed(attended_low, attn).astype(jnp.bfloat16)
    split = split_heads(projected, keep.shape[0])
    queries = split[:, :, 0]
    keysets = split[:, :, 1]
    valuesets = split[:, :, 2]
    probs = attention_probs(queries, keysets, keep, scale)
    probs_low = probs.astype(jnp.bfloat16)
    context_heads = context_low.reshape(queries.shape)
    prob_grad = jnp.einsum(
        "sqhd,skhd->shqk", context_heads, valuesets, preferred_element_type=jnp.float32
    )
    value_grad = jnp.einsum(
        "shqk,sqhd->skhd", probs_low, context_heads, preferred_element_type=jnp.float32
    )
    score_low = (probs * (prob_grad - jnp.sum(probs * prob_grad, axis=-1, keepdims=True))).astype(
        jnp.bfloat16
    )
    query_grad = (
        jnp.einsum("shqk,skhd->sqhd", score_low, keysets, preferred_element_type=jnp.float32)
        * scale
    )
    key_grad = (
        jnp.einsum("shqk,sqhd->skhd", score_low, queries, preferred_element_type=jnp.float32)
        * scale
    )
    merged_low = jnp.stack((query_grad, key_grad, value_grad), axis=2).astype(jnp.bfloat16)
    merged_low = merged_low.reshape(rows.shape[0], 3 * width)
    merged_weight_g = contract_rows(rows, merged_low)
    merged_bias_g = jnp.sum(merged_low.astype(jnp.float32), axis=0)
    states_part = first_grad + times_transposed(merged_low, merged)
    vector_grads = jnp.stack(
        (
            merged_bias_g[:width],
            merged_bias_g[2 * width :],
            attn_bias_g,
            first_gain_g,
            first_shift_g,
            outer_bias_g,
            second_gain_g,
            second_shift_g,
        ),
        axis=1,
    )
    return (
        states_part,
        (
            merged_weight_g,
            attn_weight_g,
            inner_weight_g,
            outer_weight_g,
            vector_grads,
            inner_bias_g,
        ),
    )


def pack_vectors(vectors, widened):
    flat = jnp.concatenate(list(vectors) + [widened])
    rows = flat.shape[0] // 128
    return jnp.pad(flat.reshape(rows, 128), ((0, 16 - rows), (0, 0)))


def shards(depth, *arrays):
    (states, pad_mask, query_proj, key_proj, value_proj, attn_proj, query_bias, value_bias, attn_bias, first_gain,
     first_shift, inner_proj, inner_bias, outer_proj, outer_bias, second_gain, second_shift, out_grad) = arrays
    width = states.shape[1]
    short = (query_bias, value_bias, attn_bias, first_gain, first_shift, outer_bias, second_gain, second_shift)
    if depth:
        return kernel_shards(depth, short, states, pad_mask, query_proj, key_proj, value_proj, attn_proj, inner_proj,
                             inner_bias, outer_proj, out_grad)
    merged_shard = jnp.concatenate((query_proj, key_proj, value_proj), axis=1)
    fetched = collect(merged_shard, attn_proj, inner_proj, outer_proj, jnp.stack(short, axis=1), inner_bias)
    encoded, kept = forward_pass(states, pad_mask, fetched)
    states_part, totals = backward_pass(states, pad_mask, out_grad, fetched, kept)
    merged_sum, attn_sum, inner_sum, outer_sum, vector_sum, widened_sum = reduce_grads(*totals)
    return ordered(encoded, states_part, merged_sum, attn_sum, inner_sum, outer_sum, vector_sum.T, widened_sum)


def ordered(encoded, states_part, merged_sum, attn_sum, inner_sum, outer_sum, vectors, widened_sum):
    width = attn_sum.shape[1]
    return (encoded, states_part, merged_sum[:, :width], merged_sum[:, width : 2 * width], merged_sum[:, 2 * width :],
            attn_sum, vectors[0], vectors[1], vectors[2], vectors[3], vectors[4], inner_sum, widened_sum, outer_sum,
            vectors[5], vectors[6], vectors[7])


def kernel_shards(depth, short, states, pad_mask, query_proj, key_proj, value_proj, attn_proj, inner_proj, inner_bias,
                  outer_proj, out_grad):
    width = states.shape[1]
    block = short[0].shape[0]
    long_block = inner_bias.shape[0]
    places = 8 * depth
    packed = pack_vectors(short, inner_bias)
    merged, attn, inner, outer, table = gather_all(
        depth, [[query_proj, key_proj, value_proj], [attn_proj], [inner_proj], [outer_proj], [packed]]
    )
    table = table.reshape(places, -1)
    vectors = table[:, : 8 * block].reshape(places, 8, block).transpose(0, 2, 1).reshape(width, 8)
    widened = table[:, 8 * block : 8 * block + long_block].reshape(-1)
    weights = (merged.reshape(width, -1), attn.reshape(width, -1), inner.reshape(width, -1), outer.reshape(-1, width),
               vectors, widened)
    encoded, kept = forward_pass(states, pad_mask, weights)
    states_part, totals = backward_pass(states, pad_mask, out_grad, weights, kept)
    merged_g, attn_g, inner_g, outer_g, vector_g, widened_g = totals
    low = [
        part.astype(jnp.bfloat16).reshape(4, depth, 2, part.shape[0] // places, part.shape[1])
        for part in (outer_g, inner_g, merged_g, attn_g)
    ]
    table_g = jnp.concatenate(
        (vector_g.reshape(places, block, 8).transpose(0, 2, 1).reshape(places, -1), widened_g.reshape(places, -1)), axis=1
    )
    table_g = jnp.pad(table_g, ((0, 0), (0, 1024 - table_g.shape[1]))).reshape(4, depth, 2, 8, 128)
    outer_sum, inner_sum, merged_sum, attn_sum, table_sum = scatter_all(depth, low + [table_g])
    flat = table_sum.reshape(-1)
    vector_sum = flat[: 8 * block].reshape(8, block)
    widened_sum = flat[8 * block : 8 * block + long_block]
    return ordered(encoded, states_part, merged_sum, attn_sum, inner_sum, outer_sum, vector_sum, widened_sum)


def solution(mesh):
    dps, others = mesh.shape["dp"], mesh.shape["fsdp"]
    matrix = P(("dp", "fsdp"), None)
    vector = P(("dp", "fsdp"))

    def whole(*arrays):
        rows = arrays[2].shape[0] // (dps * others)
        depth = others // 2 if rows % 16 == 0 and dps == 4 and others % 2 == 0 else 0
        return jax.shard_map(
            functools.partial(shards, depth),
            mesh=mesh,
            in_specs=(matrix,) * 6 + (vector,) * 5 + (matrix, vector, matrix) + (vector,) * 3 + (matrix,),
            out_specs=(matrix,) * 6 + (vector,) * 5 + (matrix, vector, matrix) + (vector,) * 3,
            check_vma=False,
        )(*arrays)

    return whole
```

```python
import functools

import jax
import jax.numpy as jnp
from jax import lax
from jax.experimental import pallas as pl
from jax.experimental.pallas import tpu as pltpu
from jax.sharding import PartitionSpec as P

HEADS = 16
MESH = pl.DeviceIdType.MESH

epsilon = 1e-05
neg_fill = -1e30


class Place:
    def __init__(self, depth):
        dp = lax.axis_index("dp")
        fsdp = lax.axis_index("fsdp")
        self.depth = depth
        self.dp = dp
        self.z = fsdp // 2
        self.core = lax.rem(fsdp, 2)
        flip_x = dp + 1 - 2 * lax.rem(dp, 2)
        flip_y = lax.rem(dp + 2, 4)
        self.near = flip_x + self.core * (flip_y - flip_x)
        self.far = flip_y + self.core * (flip_x - flip_y)
        self.both = lax.rem(flip_x + 2, 4)
        self.fsdp = fsdp
        self.sibling = fsdp + 1 - 2 * self.core

    def up(self, step):
        return lax.rem(self.z + step, self.depth)

    def down(self, step):
        return lax.rem(self.z + self.depth - step, self.depth)

    def along(self, z):
        return (self.dp, z * 2 + self.core)

    def greet(self):
        barrier = pltpu.get_barrier_semaphore()
        others = [self.along(self.up(step)) for step in range(1, self.depth)]
        others += [(self.near, self.fsdp), (self.far, self.fsdp), (self.dp, self.sibling)]
        for other in others:
            pl.semaphore_signal(barrier, inc=1, device_id=other, device_id_type=MESH)
        pl.semaphore_wait(barrier, len(others))


def remote(source, target, send, recv, device):
    return pltpu.make_async_remote_copy(
        src_ref=source, dst_ref=target, send_sem=send, recv_sem=recv, device_id=device, device_id_type=MESH
    )


class Gather:
    def __init__(self, place, full, own, sems, piece):
        self.place, self.full, self.own, self.piece = place, full, own, piece
        self.su, self.ru, self.sd, self.rd, self.sb, self.rb, self.sa, self.ra, self.sc, self.rc, self.so = sems

    def copy_own(self):
        p = self.place
        return pltpu.make_async_copy(self.own, self.full.at[p.dp, p.z, p.core], self.so.at[self.piece])

    def copy_up(self, z, first=False):
        p = self.place
        block = self.full.at[p.dp, z, p.core]
        source = self.own if first else block
        return remote(source, block, self.su.at[self.piece, z], self.ru.at[self.piece, z], p.along(p.z + 1))

    def copy_down(self, z, first=False):
        p = self.place
        block = self.full.at[p.dp, z, p.core]
        source = self.own if first else block
        return remote(source, block, self.sd.at[self.piece, z], self.rd.at[self.piece, z], p.along(p.z - 1))

    def copy_near(self, z, first=False, arriving=False):
        p = self.place
        block = self.full.at[p.near if arriving else p.dp, z, p.core]
        source = self.own if first else block
        return remote(source, block, self.sb.at[self.piece, z], self.rb.at[self.piece, z], (p.near, p.fsdp))

    def copy_far(self, half, z, first=False, arriving=False):
        p = self.place
        row = (p.both if half else p.far) if arriving else (p.near if half else p.dp)
        block = self.full.at[row, z, p.core]
        source = self.own if first else block
        at = half * p.depth + z
        return remote(source, block, self.sa.at[self.piece, at], self.ra.at[self.piece, at], (p.far, p.fsdp))

    def copy_core(self, part, arriving=False):
        p = self.place
        if arriving:
            row = (p.dp, p.far, p.near, p.both)[part]
            block = self.full.at[row, :, 1 - p.core]
        else:
            row = (p.dp, p.near, p.far, p.both)[part]
            block = self.full.at[row, :, p.core]
        return remote(block, block, self.sc.at[self.piece, part], self.rc.at[self.piece, part], (p.dp, p.sibling))

    def start(self):
        p = self.place
        pl.when(p.z < p.depth - 1)(lambda: self.copy_up(p.z, True).start())
        pl.when(p.z > 0)(lambda: self.copy_down(p.z, True).start())
        self.copy_near(p.z, True).start()
        self.copy_far(0, p.z, True).start()
        self.copy_own().start()

    def hop(self, step):
        p = self.place

        @pl.when(p.z >= step)
        def _():
            z = p.z - step
            self.copy_up(z).wait_recv()
            pl.when(p.z < p.depth - 1)(lambda: self.copy_up(z).start())
            self.copy_near(z).start()
            self.copy_far(0, z).start()

        @pl.when(p.z + step < p.depth)
        def _():
            z = p.z + step
            self.copy_down(z).wait_recv()
            pl.when(p.z > 0)(lambda: self.copy_down(z).start())
            self.copy_near(z).start()
            self.copy_far(0, z).start()

    def last_hop(self):
        self.hop(self.place.depth - 1)
        self.copy_own().wait()
        self.copy_core(0).start()

    def spread(self, step):
        p = self.place

        def act(z):
            self.copy_near(z, arriving=True).wait_recv()
            self.copy_far(1, z).start()

        if step == 0:
            act(p.z)
        else:
            pl.when(p.z >= step)(lambda: act(p.z - step))
            pl.when(p.z + step < p.depth)(lambda: act(p.z + step))
        if step == p.depth - 1:
            self.copy_core(1).start()

    def arrive_far(self, half):
        p = self.place
        for z in range(p.depth):
            self.copy_far(half, z, arriving=True).wait_recv()
        self.copy_core(2 + half).start()

    def arrive_core(self, *parts):
        for part in parts:
            self.copy_core(part, arriving=True).wait_recv()

    def drain(self):
        p = self.place
        for z in range(p.depth):
            pl.when((p.z < p.depth - 1) & (z <= p.z))(lambda: self.copy_up(z).wait_send())
            pl.when((p.z > 0) & (z >= p.z))(lambda: self.copy_down(z).wait_send())
            self.copy_near(z).wait_send()
            self.copy_far(0, z).wait_send()
            self.copy_far(1, z).wait_send()
        for part in range(4):
            self.copy_core(part).wait_send()


def gather_sems(pieces, depth):
    dma = pltpu.SemaphoreType.DMA
    counts = (depth, depth, depth, depth, depth, depth, 2 * depth, 2 * depth, 4, 4)
    return [dma((pieces, count)) for count in counts] + [dma((pieces,))]


def matmul(left, right):
    return lax.dot_general(left, right, (((1,), (0,)), ((), ())), preferred_element_type=jnp.float32)


def matmul_nt(left, right):
    return lax.dot_general(left, right, (((1,), (1,)), ((), ())), preferred_element_type=jnp.float32)


def matmul_tn(left, right):
    return lax.dot_general(left, right, (((0,), (0,)), ((), ())), preferred_element_type=jnp.float32)


def flat(value):
    return value.reshape(-1, value.shape[-1])


def span(index, size):
    return pl.ds(pl.multiple_of(index * size, size), size)


def unpack_table(table, block, vectors):
    places = table.shape[0] * table.shape[1] * table.shape[2]
    width = vectors.shape[1]
    per_row = 128 // block
    lane = lax.broadcasted_iota(jnp.int32, (128, width), 1)
    source = lax.broadcasted_iota(jnp.int32, (128, width), 0)
    owner = lax.broadcasted_iota(jnp.int32, (places, width), 1) // block
    mine = owner == lax.broadcasted_iota(jnp.int32, (places, width), 0)
    for vector in range(8):
        row = table[:, :, :, vector // per_row, :].reshape(places, 128).astype(jnp.bfloat16)
        pick = jnp.where(source == lax.rem(lane, block) + block * (vector % per_row), 1.0, 0.0).astype(jnp.bfloat16)
        spread = jnp.where(mine, matmul(row, pick), 0.0)
        vectors[vector : vector + 1, :] = jnp.sum(spread, axis=0, keepdims=True)


def project(rows, weights, vectors, projected):
    width = rows.shape[1]
    for part, bias in ((0, 0), (1, None), (2, 1)):
        weight = flat(weights[:, :, :, :, part * width : (part + 1) * width])

        def one(index, _):
            at = span(index, 256)
            total = matmul(rows[at, :], weight)
            if bias is not None:
                total = total + vectors[bias : bias + 1, :]
            projected[at, part * width : (part + 1) * width] = total.astype(jnp.bfloat16)
            return 0

        lax.fori_loop(0, rows.shape[0] // 256, one, 0)


def head_lanes(heads, rows, size):
    lane = lax.broadcasted_iota(jnp.int32, (rows, heads * size), 1) // size
    return [lane == head for head in range(heads)]


def stack_heads(value, lanes):
    return jnp.concatenate([jnp.where(lane, value, jnp.zeros_like(value)) for lane in lanes], axis=0)


def merge_heads(value, lanes):
    rows = value.shape[0] // len(lanes)
    result = value[:rows]
    for head in range(1, len(lanes)):
        result = jnp.where(lanes[head], value[head * rows : (head + 1) * rows], result)
    return result


QUAD = 4


def attend(projected, keep, probs, context):
    width = context.shape[1]
    size = width // HEADS
    segments, length = keep.shape
    scale = size ** (-0.5)
    lanes = head_lanes(QUAD, length, size)
    quads = HEADS // QUAD

    def one(index, _):
        segment = index // quads
        quad = lax.rem(index, quads)
        at = span(segment, length)
        queries = projected[at, span(quad, QUAD * size)]
        keysets = projected[at, span(quad + quads, QUAD * size)]
        valuesets = projected[at, span(quad + 2 * quads, QUAD * size)]
        scores = matmul_nt(stack_heads(queries, lanes), keysets) * scale
        mask = keep[pl.ds(segment, 1), :] > 0
        scores = jnp.where(mask, scores, neg_fill)
        raised = jnp.exp(scores - jnp.max(scores, axis=1, keepdims=True))
        low = (raised / jnp.sum(raised, axis=1, keepdims=True)).astype(jnp.bfloat16)
        probs[index] = low
        context[at, span(quad, QUAD * size)] = merge_heads(matmul(low, valuesets), lanes).astype(jnp.bfloat16)
        return 0

    lax.fori_loop(0, segments * quads, one, 0)


def center_scale(hidden):
    center = hidden - jnp.mean(hidden, axis=1, keepdims=True)
    spread = jnp.mean(center * center, axis=1, keepdims=True)
    rate = lax.rsqrt(spread + epsilon)
    return center * rate, rate


def first_block(rows, context, weights, vectors, first_sum, first_norm, first_low):
    weight = flat(weights[...])

    def one(index, _):
        at = span(index, 128)
        total = rows[at, :].astype(jnp.float32) + (matmul(context[at, :], weight) + vectors[2:3, :])
        first_sum[at, :] = total
        normed, _ = center_scale(total)
        result = normed * vectors[3:4, :] + vectors[4:5, :]
        first_norm[at, :] = result
        first_low[at, :] = result.astype(jnp.bfloat16)
        return 0

    lax.fori_loop(0, rows.shape[0] // 128, one, 0)


def inner_block(first_low, weights, table, row_at, activated, slope):
    count = first_low.shape[0]
    biases = table.shape[0] * table.shape[1] * table.shape[2]
    chunks = weights.shape[4] // 512
    per_chunk = biases // chunks
    rows_of = table[:, :, :, row_at, :].reshape(biases, 128)
    for chunk in range(chunks):
        columns = slice(chunk * 512, (chunk + 1) * 512)
        weight = flat(weights[:, :, :, :, columns])
        first = chunk * per_chunk
        bias = jnp.concatenate([rows_of[first + part : first + part + 1] for part in range(per_chunk)], axis=1)

        def one(index, _):
            at = span(index, 128)
            value = matmul(first_low[at, :], weight) + bias
            share = 0.5 * (1.0 + lax.erf(value * (0.5**0.5)))
            bell = jnp.exp(-0.5 * value * value) * ((0.5 / jnp.pi) ** 0.5)
            activated[at, columns] = (value * share).astype(jnp.bfloat16)
            slope[at, columns] = (share + value * bell).astype(jnp.bfloat16)
            return 0

        lax.fori_loop(0, count // 128, one, 0)


def outer_part(activated, weights, row, total, fresh):
    weight = flat(weights[row])
    size = weight.shape[0]

    def one(index, _):
        at = span(index, 256)
        value = matmul(activated[at, span(row, size)], weight)
        total[at, :] = value if fresh else total[at, :] + value
        return 0

    lax.fori_loop(0, activated.shape[0] // 256, one, 0)


def norm_back(grad, normed, rate, gain):
    scaled = grad * gain
    mean = jnp.mean(scaled, axis=1, keepdims=True)
    along = jnp.mean(scaled * normed, axis=1, keepdims=True)
    return rate * (scaled - mean - normed * along)


def second_block(first_norm, total, cotangent, vectors, encoded, second_grad, outer_low, sums):
    sums[...] = jnp.zeros_like(sums)

    def one(index, _):
        at = span(index, 128)
        normed, rate = center_scale(first_norm[at, :] + (total[at, :] + vectors[5:6, :]))
        gain = vectors[6:7, :]
        encoded[at, :] = (normed * gain + vectors[7:8, :]).astype(jnp.bfloat16)
        grad = cotangent[at, :].astype(jnp.float32)
        back = norm_back(grad, normed, rate, gain)
        low = back.astype(jnp.bfloat16)
        second_grad[at, :] = back
        outer_low[at, :] = low
        sums[5:6, :] += jnp.sum(low.astype(jnp.float32), axis=0, keepdims=True)
        sums[6:7, :] += jnp.sum(grad * normed, axis=0, keepdims=True)
        sums[7:8, :] += jnp.sum(grad, axis=0, keepdims=True)
        return 0

    lax.fori_loop(0, first_norm.shape[0] // 128, one, 0)


def forward_kernel(depth, block, *refs):
    (rows, keep, cotangent, query_own, key_own, value_own, attn_own, inner_own, outer_own, table_own) = refs[:10]
    merged_out, attn_out, inner_out, outer_out = refs[10:14]
    (encoded_out, projected_out, probs_out, context_out, first_sum_out, first_low_out, activated_out, slope_out,
     second_grad_out, outer_low_out, vectors, sums) = refs[14:26]
    (merged_own, table, merged, attn, inner, outer, projected, probs, context, first_sum, first_norm, first_low, activated,
     slope, total, encoded, second_grad, outer_low, save_sem) = refs[26:45]
    sems = refs[45:]
    place = Place(depth)
    width = rows.shape[1]
    for part, own in enumerate((query_own, key_own, value_own)):
        merged_own[:, part * width : (part + 1) * width] = own[...]
    net_table = Gather(place, table, table_own, sems, 0)
    net_merged = Gather(place, merged, merged_own, sems, 1)
    net_attn = Gather(place, attn, attn_own, sems, 2)
    net_inner = Gather(place, inner, inner_own, sems, 3)
    net_outer = Gather(place, outer, outer_own, sems, 4)
    nets = (net_table, net_merged, net_attn, net_inner, net_outer)
    front = nets[:3]
    place.greet()
    saves = []

    def save(source, target):
        copy = pltpu.make_async_copy(source, target, save_sem.at[len(saves)])
        copy.start()
        saves.append(copy)

    def hop(net, step):
        if step == depth - 1:
            net.last_hop()
        else:
            net.hop(step)

    for net in front:
        net.start()
    for step in range(1, depth):
        for net in front:
            hop(net, step)
        if step == 1:
            net_inner.start()
        for net in front:
            net.spread(step - 1)
    for net in front:
        net.spread(depth - 1)
    hop(net_inner, 1)
    net_inner.spread(0)
    net_outer.start()
    for net in front:
        net.arrive_far(0)
        net.arrive_far(1)
        net.arrive_core(0, 1, 2, 3)
    save(merged, merged_out)
    save(attn, attn_out)
    unpack_table(table, block, vectors)
    project(rows, merged, vectors, projected)
    save(projected, projected_out)
    for step in range(2, depth):
        hop(net_inner, step)
        net_inner.spread(step - 1)
    net_inner.spread(depth - 1)
    attend(projected, keep, probs, context)
    save(probs, probs_out)
    save(context, context_out)
    hop(net_outer, 1)
    net_outer.spread(0)
    first_block(rows, context, attn, vectors, first_sum, first_norm, first_low)
    save(first_sum, first_sum_out)
    save(first_low, first_low_out)
    for step in range(2, depth):
        hop(net_outer, step)
        net_outer.spread(step - 1)
    net_outer.spread(depth - 1)
    net_inner.arrive_far(0)
    net_inner.arrive_far(1)
    net_inner.arrive_core(0, 1, 2, 3)
    save(inner, inner_out)
    inner_block(first_low, inner, table, 8 * block // 128, activated, slope)
    save(activated, activated_out)
    save(slope, slope_out)
    net_outer.arrive_core(0)
    outer_part(activated, outer, place.dp, total, True)
    net_outer.arrive_far(0)
    net_outer.arrive_core(1, 2)
    outer_part(activated, outer, place.near, total, False)
    outer_part(activated, outer, place.far, total, False)
    net_outer.arrive_far(1)
    net_outer.arrive_core(3)
    save(outer, outer_out)
    outer_part(activated, outer, place.both, total, False)
    second_block(first_norm, total, cotangent, vectors, encoded, second_grad, outer_low, sums)
    save(encoded, encoded_out)
    save(second_grad, second_grad_out)
    save(outer_low, outer_low_out)
    for net in nets:
        net.drain()
    for copy in saves:
        copy.wait()


def forward_all(depth, block, rows, keep, cotangent, owns):
    query_own, _, _, attn_own, inner_own, outer_own, table_own = owns
    tokens, width = rows.shape
    hidden = inner_own.shape[1]
    segments, length = keep.shape
    low, high = jnp.bfloat16, jnp.float32

    def fulls(own, columns):
        return (4, depth, 2, own.shape[0], columns)

    full_shapes = [fulls(query_own, 3 * width), fulls(attn_own, width), fulls(inner_own, hidden), fulls(outer_own, width)]
    kept = [
        ((tokens, width), low),
        ((tokens, 3 * width), low),
        ((segments * HEADS // QUAD, QUAD * length, length), low),
        ((tokens, width), low),
        ((tokens, width), high),
        ((tokens, width), low),
        ((tokens, hidden), low),
        ((tokens, hidden), low),
        ((tokens, width), high),
        ((tokens, width), low),
    ]
    small = [((8, width), high), ((8, width), high)]
    shapes = [jax.ShapeDtypeStruct(shape, low) for shape in full_shapes]
    shapes += [jax.ShapeDtypeStruct(*one) for one in kept + small]
    held = {name: pltpu.VMEM(*one) for name, one in zip(
        ("encoded", "projected", "probs", "context", "first_sum", "first_low", "activated", "slope", "second_grad", "outer_low"),
        kept)}
    scratch = [pltpu.VMEM((query_own.shape[0], 3 * width), low), pltpu.VMEM(fulls(table_own, 128), high)]
    scratch += [pltpu.VMEM(shape, low) for shape in full_shapes]
    scratch += [held[name] for name in ("projected", "probs", "context", "first_sum")]
    scratch += [pltpu.VMEM((tokens, width), high)]
    scratch += [held[name] for name in ("first_low", "activated", "slope")]
    scratch += [pltpu.VMEM((tokens, width), high)]
    scratch += [held[name] for name in ("encoded", "second_grad", "outer_low")]
    scratch += [pltpu.SemaphoreType.DMA((len(full_shapes) + len(kept),))]
    here = pl.BlockSpec(memory_space=pltpu.VMEM)
    away = pl.BlockSpec(memory_space=pl.ANY)
    return pl.pallas_call(
        functools.partial(forward_kernel, depth, block),
        out_shape=shapes,
        in_specs=[here] * 10,
        out_specs=[away] * (len(full_shapes) + len(kept)) + [here] * 2,
        scratch_shapes=scratch + gather_sems(5, depth),
        compiler_params=pltpu.CompilerParams(
            collective_id=0, has_side_effects=True, vmem_limit_bytes=60 * 1024 * 1024
        ),
        name="forward",
    )(rows, keep, cotangent, *owns)


def add_into(target, other):
    count, rows, _ = target.shape
    tile = 8 if target.dtype == jnp.float32 else 16
    steps = rows // tile

    def one(index, _):
        part = index // steps
        at = pl.ds(pl.multiple_of(lax.rem(index, steps) * tile, tile), tile)
        target[part, at, :] = target[part, at, :] + other[part, at, :]
        return 0

    lax.fori_loop(0, count * steps, one, 0)


class Scatter:
    def __init__(self, place, sums, slots, sems, piece):
        self.place, self.sums, self.piece = place, sums, piece
        self.from_core, self.from_far, self.from_near, self.from_z = slots
        self.sc, self.rc, self.sa, self.ra, self.sb, self.rb, self.sz, self.rz = sems

    def copy_core(self, whole, part):
        p = self.place
        return remote(
            whole.at[part, :, 1 - p.core], self.from_core.at[part], self.sc.at[self.piece, part],
            self.rc.at[self.piece, part], (p.dp, p.sibling),
        )

    def rows_of(self, half, away):
        p = self.place
        if away:
            return p.both if half else p.far
        return p.near if half else p.dp

    def copy_far(self, half):
        p = self.place
        return remote(
            self.sums.at[self.rows_of(half, True)], self.from_far.at[half], self.sa.at[self.piece, half],
            self.ra.at[self.piece, half], (p.far, p.fsdp),
        )

    def copy_near(self):
        p = self.place
        return remote(
            self.sums.at[p.near], self.from_near, self.sb.at[self.piece], self.rb.at[self.piece], (p.near, p.fsdp)
        )

    def copy_z(self, step):
        p = self.place
        return remote(
            self.sums.at[p.dp, p.up(step)], self.from_z.at[step - 1], self.sz.at[self.piece, step - 1],
            self.rz.at[self.piece, step - 1], p.along(p.up(step)),
        )

    def add_core(self, whole):
        p = self.place
        for half in (1, 0):
            for away in (True, False):
                row = self.rows_of(half, away)
                self.copy_core(whole, row).wait_recv()
                add_into(self.sums.at[row], self.from_core.at[row])
                if away:
                    self.copy_far(half).start()

    def add_far(self, half):
        self.copy_far(half).wait_recv()
        add_into(self.sums.at[self.rows_of(half, False)], self.from_far.at[half])
        if half:
            self.copy_near().start()

    def add_near(self):
        p = self.place
        self.copy_near().wait_recv()
        add_into(self.sums.at[p.dp], self.from_near)
        for step in range(1, p.depth):
            self.copy_z(step).start()

    def finish(self, out):
        p = self.place
        for step in range(1, p.depth):
            self.copy_z(step).wait_recv()
        rows = out.shape[0]
        tile = 8 if self.sums.dtype == jnp.float32 else 16

        def one(index, _):
            at = pl.ds(pl.multiple_of(index * tile, tile), tile)
            total = self.sums[p.dp, p.z, at, :].astype(jnp.float32)
            for step in range(p.depth - 1):
                total = total + self.from_z[step, at, :].astype(jnp.float32)
            out[at, :] = total
            return 0

        lax.fori_loop(0, rows // tile, one, 0)

    def drain(self, whole):
        for part in range(4):
            self.copy_core(whole, part).wait_send()
        self.copy_far(1).wait_send()
        self.copy_far(0).wait_send()
        self.copy_near().wait_send()
        for step in range(1, self.place.depth):
            self.copy_z(step).wait_send()


def scatter_sems(pieces, depth):
    dma = pltpu.SemaphoreType.DMA
    return [
        dma((pieces, 4)), dma((pieces, 4)), dma((pieces, 2)), dma((pieces, 2)), dma((pieces,)), dma((pieces,)),
        dma((pieces, depth - 1)), dma((pieces, depth - 1)),
    ]


def scatter_slots(shape, dtype):
    dps, depth, _, rows, columns = shape
    return [
        pltpu.VMEM((dps, depth, rows, columns), dtype),
        pltpu.VMEM((dps, depth, rows, columns), dtype),
        pltpu.VMEM((2, depth, rows, columns), dtype),
        pltpu.VMEM((depth, rows, columns), dtype),
        pltpu.VMEM((depth - 1, rows, columns), dtype),
    ]


def scatter_kernel(depth, count, *refs):
    wholes = refs[:count]
    outs = refs[count : 2 * count]
    scratch = refs[2 * count : 7 * count]
    own_sem = refs[7 * count]
    sems = refs[7 * count + 1 :]
    place = Place(depth)
    nets = []
    local = []
    for piece in range(count):
        sums, *slots = scratch[5 * piece : 5 * piece + 5]
        nets.append(Scatter(place, sums, slots, sems, piece))
        local.append(pltpu.make_async_copy(wholes[piece].at[:, :, place.core], sums, own_sem.at[piece]))
    for copy in local:
        copy.start()
    place.greet()
    for net, whole in zip(nets, wholes):
        for half in (1, 0):
            for away in (False, True):
                net.copy_core(whole, net.rows_of(half, away)).start()
    for piece in range(count):
        local[piece].wait()
        nets[piece].add_core(wholes[piece])
    for net in nets:
        net.add_far(1)
        net.add_far(0)
        net.add_near()
    for net, out in zip(nets, outs):
        net.finish(out)
    for net, whole in zip(nets, wholes):
        net.drain(whole)


def scatter_all(depth, wholes):
    shapes = [jax.ShapeDtypeStruct(whole.shape[3:], jnp.float32) for whole in wholes]
    scratch = []
    for whole in wholes:
        scratch += scatter_slots(whole.shape, whole.dtype)
    return pl.pallas_call(
        functools.partial(scatter_kernel, depth, len(wholes)),
        out_shape=shapes,
        in_specs=[pl.BlockSpec(memory_space=pl.ANY)] * len(wholes),
        out_specs=[pl.BlockSpec(memory_space=pltpu.VMEM)] * len(wholes),
        scratch_shapes=scratch + [pltpu.SemaphoreType.DMA((len(wholes),))] + scatter_sems(len(wholes), depth),
        compiler_params=pltpu.CompilerParams(
            collective_id=1, has_side_effects=True, vmem_limit_bytes=60 * 1024 * 1024
        ),
        name="scatter_gradients",
    )(*wholes)


def normalize(hidden, gain, shift):
    center = hidden - jnp.mean(hidden, axis=-1, keepdims=True)
    spread = jnp.mean(center * center, axis=-1, keepdims=True)
    return center * lax.rsqrt(spread + epsilon) * gain + shift


def exact_gelu(value):
    return jax.nn.gelu(value, approximate=False)


def contract_rows(left, right):
    return lax.dot_general(
        left, right, (((0,), (0,)), ((), ())), preferred_element_type=jnp.float32
    )


def times_transposed(left, right):
    return lax.dot_general(
        left, right, (((1,), (1,)), ((), ())), preferred_element_type=jnp.float32
    )


def collect(merged, attn, inner, outer, vectors, widened):
    return (
        lax.all_gather(merged, ("dp", "fsdp"), axis=0, tiled=True),
        lax.all_gather(attn, ("dp", "fsdp"), axis=0, tiled=True),
        lax.all_gather(inner, ("dp", "fsdp"), axis=0, tiled=True),
        lax.all_gather(outer, ("dp", "fsdp"), axis=0, tiled=True),
        lax.all_gather(vectors, ("dp", "fsdp"), axis=0, tiled=True),
        lax.all_gather(widened, ("dp", "fsdp"), axis=0, tiled=True),
    )


def reduce_grads(merged, attn, inner, outer, vectors, widened):
    return (
        lax.psum_scatter(merged, ("dp", "fsdp"), scatter_dimension=0, tiled=True),
        lax.psum_scatter(attn, ("dp", "fsdp"), scatter_dimension=0, tiled=True),
        lax.psum_scatter(inner, ("dp", "fsdp"), scatter_dimension=0, tiled=True),
        lax.psum_scatter(outer, ("dp", "fsdp"), scatter_dimension=0, tiled=True),
        lax.psum_scatter(vectors, ("dp", "fsdp"), scatter_dimension=0, tiled=True),
        lax.psum_scatter(widened, ("dp", "fsdp"), scatter_dimension=0, tiled=True),
    )


def split_heads(projected, segments):
    total_rows, triple = projected.shape
    width = triple // 3
    return projected.reshape(segments, total_rows // segments, 3, HEADS, width // HEADS)


def attention_probs(queries, keysets, keep, scale):
    scores = (
        jnp.einsum("sqhd,skhd->shqk", queries, keysets, preferred_element_type=jnp.float32) * scale
    )
    scores = jnp.where(keep[:, None, None, :] > 0, scores, neg_fill)
    peaks = jnp.max(scores, axis=-1, keepdims=True)
    raised = jnp.exp(scores - peaks)
    return raised / jnp.sum(raised, axis=-1, keepdims=True)


def forward_pass(rows, keep, weights):
    merged, attn, inner, outer, vectors, widened = weights
    vector_full = vectors.astype(jnp.float32)
    width = rows.shape[1]
    scale = (width // HEADS) ** (-0.5)
    merged_bias = jnp.concatenate(
        (vector_full[:, 0], jnp.zeros((width,), jnp.float32), vector_full[:, 1])
    )
    projected = (jnp.dot(rows, merged, preferred_element_type=jnp.float32) + merged_bias).astype(
        jnp.bfloat16
    )
    split = split_heads(projected, keep.shape[0])
    probs = attention_probs(split[:, :, 0], split[:, :, 1], keep, scale).astype(jnp.bfloat16)
    context = jnp.einsum(
        "shqk,skhd->sqhd", probs, split[:, :, 2], preferred_element_type=jnp.float32
    )
    context = context.reshape(rows.shape[0], width).astype(jnp.bfloat16)
    attended = jnp.dot(context, attn, preferred_element_type=jnp.float32) + vector_full[:, 2]
    first_sum = rows.astype(jnp.float32) + attended
    first_norm = normalize(first_sum, vector_full[:, 3], vector_full[:, 4])
    first_low = first_norm.astype(jnp.bfloat16)
    inner_act = jnp.dot(first_low, inner, preferred_element_type=jnp.float32) + widened.astype(
        jnp.float32
    )
    activated = exact_gelu(inner_act).astype(jnp.bfloat16)
    outer_act = jnp.dot(activated, outer, preferred_element_type=jnp.float32) + vector_full[:, 5]
    second_sum = first_norm + outer_act
    encoded = normalize(second_sum, vector_full[:, 6], vector_full[:, 7]).astype(jnp.bfloat16)
    return (encoded, (projected, context, first_sum, first_low, inner_act, activated, second_sum))


def backward_pass(rows, keep, cotangent, weights, kept):
    merged, attn, inner, outer, vectors, widened = weights
    projected, context, first_sum, first_low, inner_act, activated, second_sum = kept
    vector_full = vectors.astype(jnp.float32)
    width = rows.shape[1]
    scale = (width // HEADS) ** (-0.5)
    second_out, second_pull = jax.vjp(normalize, second_sum, vector_full[:, 6], vector_full[:, 7])
    second_grad, second_gain_g, second_shift_g = second_pull(cotangent.astype(jnp.float32))
    outer_low = second_grad.astype(jnp.bfloat16)
    outer_bias_g = jnp.sum(outer_low.astype(jnp.float32), axis=0)
    outer_weight_g = contract_rows(activated, outer_low)
    act_grad = times_transposed(outer_low, outer)
    gelu_out, gelu_pull = jax.vjp(exact_gelu, inner_act)
    inner_low = gelu_pull(act_grad)[0].astype(jnp.bfloat16)
    inner_bias_g = jnp.sum(inner_low.astype(jnp.float32), axis=0)
    inner_weight_g = contract_rows(first_low, inner_low)
    first_total = second_grad + times_transposed(inner_low, inner)
    first_out, first_pull = jax.vjp(normalize, first_sum, vector_full[:, 3], vector_full[:, 4])
    first_grad, first_gain_g, first_shift_g = first_pull(first_total)
    attended_low = first_grad.astype(jnp.bfloat16)
    attn_bias_g = jnp.sum(attended_low.astype(jnp.float32), axis=0)
    attn_weight_g = contract_rows(context, attended_low)
    context_low = times_transposed(attended_low, attn).astype(jnp.bfloat16)
    split = split_heads(projected, keep.shape[0])
    queries = split[:, :, 0]
    keysets = split[:, :, 1]
    valuesets = split[:, :, 2]
    probs = attention_probs(queries, keysets, keep, scale)
    probs_low = probs.astype(jnp.bfloat16)
    context_heads = context_low.reshape(queries.shape)
    prob_grad = jnp.einsum(
        "sqhd,skhd->shqk", context_heads, valuesets, preferred_element_type=jnp.float32
    )
    value_grad = jnp.einsum(
        "shqk,sqhd->skhd", probs_low, context_heads, preferred_element_type=jnp.float32
    )
    score_low = (probs * (prob_grad - jnp.sum(probs * prob_grad, axis=-1, keepdims=True))).astype(
        jnp.bfloat16
    )
    query_grad = (
        jnp.einsum("shqk,skhd->sqhd", score_low, keysets, preferred_element_type=jnp.float32)
        * scale
    )
    key_grad = (
        jnp.einsum("shqk,sqhd->skhd", score_low, queries, preferred_element_type=jnp.float32)
        * scale
    )
    merged_low = jnp.stack((query_grad, key_grad, value_grad), axis=2).astype(jnp.bfloat16)
    merged_low = merged_low.reshape(rows.shape[0], 3 * width)
    merged_weight_g = contract_rows(rows, merged_low)
    merged_bias_g = jnp.sum(merged_low.astype(jnp.float32), axis=0)
    states_part = first_grad + times_transposed(merged_low, merged)
    vector_grads = jnp.stack(
        (
            merged_bias_g[:width],
            merged_bias_g[2 * width :],
            attn_bias_g,
            first_gain_g,
            first_shift_g,
            outer_bias_g,
            second_gain_g,
            second_shift_g,
        ),
        axis=1,
    )
    return (
        states_part,
        (
            merged_weight_g,
            attn_weight_g,
            inner_weight_g,
            outer_weight_g,
            vector_grads,
            inner_bias_g,
        ),
    )


def pack_vectors(vectors, widened):
    joined = jnp.concatenate(list(vectors) + [widened]).astype(jnp.float32)
    rows = joined.shape[0] // 128
    return jnp.pad(joined.reshape(rows, 128), ((0, 8 - rows), (0, 0)))


def shards(depth, *arrays):
    (states, pad_mask, query_proj, key_proj, value_proj, attn_proj, query_bias, value_bias, attn_bias, first_gain,
     first_shift, inner_proj, inner_bias, outer_proj, outer_bias, second_gain, second_shift, out_grad) = arrays
    width = states.shape[1]
    short = (query_bias, value_bias, attn_bias, first_gain, first_shift, outer_bias, second_gain, second_shift)
    if depth:
        return kernel_shards(depth, short, states, pad_mask, query_proj, key_proj, value_proj, attn_proj, inner_proj,
                             inner_bias, outer_proj, out_grad)
    merged_shard = jnp.concatenate((query_proj, key_proj, value_proj), axis=1)
    fetched = collect(merged_shard, attn_proj, inner_proj, outer_proj, jnp.stack(short, axis=1), inner_bias)
    encoded, kept = forward_pass(states, pad_mask, fetched)
    states_part, totals = backward_pass(states, pad_mask, out_grad, fetched, kept)
    merged_sum, attn_sum, inner_sum, outer_sum, vector_sum, widened_sum = reduce_grads(*totals)
    return ordered(encoded, states_part, merged_sum, attn_sum, inner_sum, outer_sum, vector_sum.T, widened_sum)


def ordered(encoded, states_part, merged_sum, attn_sum, inner_sum, outer_sum, vectors, widened_sum):
    width = attn_sum.shape[1]
    return (encoded, states_part, merged_sum[:, :width], merged_sum[:, width : 2 * width], merged_sum[:, 2 * width :],
            attn_sum, vectors[0], vectors[1], vectors[2], vectors[3], vectors[4], inner_sum, widened_sum, outer_sum,
            vectors[5], vectors[6], vectors[7])


def attention_back(projected, probs, context_low, scale):
    tokens = projected.shape[0]
    width = projected.shape[1] // 3
    quads = HEADS // QUAD
    segments = probs.shape[0] // quads
    length = probs.shape[2]
    split = projected.reshape(segments, length, 3, HEADS, width // HEADS)
    queries, keysets, valuesets = split[:, :, 0], split[:, :, 1], split[:, :, 2]
    probs_low = probs.reshape(segments, HEADS, length, length)
    heads = context_low.reshape(queries.shape)
    prob_grad = jnp.einsum("sqhd,skhd->shqk", heads, valuesets, preferred_element_type=jnp.float32)
    value_low = jnp.einsum("shqk,sqhd->skhd", probs_low, heads, preferred_element_type=jnp.float32)
    wide = probs_low.astype(jnp.float32)
    score_low = (wide * (prob_grad - jnp.sum(wide * prob_grad, axis=-1, keepdims=True))).astype(jnp.bfloat16)
    query_low = jnp.einsum("shqk,skhd->sqhd", score_low, keysets, preferred_element_type=jnp.float32) * scale
    key_low = jnp.einsum("shqk,sqhd->skhd", score_low, queries, preferred_element_type=jnp.float32) * scale
    return jnp.stack((query_low, key_low, value_low), axis=2).astype(jnp.bfloat16).reshape(tokens, 3 * width)


def kernel_shards(depth, short, states, pad_mask, query_proj, key_proj, value_proj, attn_proj, inner_proj, inner_bias,
                  outer_proj, out_grad):
    width = states.shape[1]
    block = short[0].shape[0]
    long_block = inner_bias.shape[0]
    places = 8 * depth
    packed = pack_vectors(short, inner_bias)
    (merged, attn, inner, outer, encoded, projected, probs, context, first_sum, first_low, activated, slope, second_grad,
     outer_low, vectors, sums) = forward_all(
        depth, block, states, pad_mask, out_grad,
        (query_proj, key_proj, value_proj, attn_proj, inner_proj, outer_proj, packed))
    merged = merged.reshape(width, -1)
    attn = attn.reshape(width, -1)
    inner = inner.reshape(width, -1)
    outer = outer.reshape(-1, width)
    outer_g = contract_rows(activated, outer_low)
    inner_low = (times_transposed(outer_low, outer) * slope).astype(jnp.bfloat16)
    widened_g = jnp.sum(inner_low.astype(jnp.float32), axis=0)
    inner_g = contract_rows(first_low, inner_low)
    first_total = second_grad + times_transposed(inner_low, inner)
    _, first_pull = jax.vjp(normalize, first_sum, vectors[3], vectors[4])
    first_grad, first_gain_g, first_shift_g = first_pull(first_total)
    attended_low = first_grad.astype(jnp.bfloat16)
    attn_bias_g = jnp.sum(attended_low.astype(jnp.float32), axis=0)
    attn_g = contract_rows(context, attended_low)
    context_low = times_transposed(attended_low, attn).astype(jnp.bfloat16)
    merged_low = attention_back(projected, probs, context_low, (width // HEADS) ** (-0.5))
    merged_g = contract_rows(states, merged_low)
    merged_bias_g = jnp.sum(merged_low.astype(jnp.float32), axis=0)
    states_part = first_grad + times_transposed(merged_low, merged)
    vector_g = jnp.stack((merged_bias_g[:width], merged_bias_g[2 * width :], attn_bias_g, first_gain_g, first_shift_g,
                          sums[5], sums[6], sums[7]), axis=1)
    low = [
        part.astype(jnp.bfloat16).reshape(4, depth, 2, part.shape[0] // places, part.shape[1])
        for part in (outer_g, inner_g, merged_g, attn_g)
    ]
    table_g = jnp.concatenate(
        (vector_g.reshape(places, block, 8).transpose(0, 2, 1).reshape(places, -1), widened_g.reshape(places, -1)), axis=1
    )
    table_g = jnp.pad(table_g, ((0, 0), (0, 1024 - table_g.shape[1]))).reshape(4, depth, 2, 8, 128)
    outer_sum, inner_sum, merged_sum, attn_sum, table_sum = scatter_all(depth, low + [table_g])
    flat = table_sum.reshape(-1)
    vector_sum = flat[: 8 * block].reshape(8, block)
    widened_sum = flat[8 * block : 8 * block + long_block]
    return ordered(encoded, states_part, merged_sum, attn_sum, inner_sum, outer_sum, vector_sum, widened_sum)


def solution(mesh):
    dps, others = mesh.shape["dp"], mesh.shape["fsdp"]
    matrix = P(("dp", "fsdp"), None)
    vector = P(("dp", "fsdp"))

    def whole(*arrays):
        rows = arrays[2].shape[0] // (dps * others)
        depth = others // 2 if rows % 16 == 0 and dps == 4 and others % 2 == 0 else 0
        return jax.shard_map(
            functools.partial(shards, depth),
            mesh=mesh,
            in_specs=(matrix,) * 6 + (vector,) * 5 + (matrix, vector, matrix) + (vector,) * 3 + (matrix,),
            out_specs=(matrix,) * 6 + (vector,) * 5 + (matrix, vector, matrix) + (vector,) * 3,
            check_vma=False,
        )(*arrays)

    return whole
```

```python
import functools

import jax
import jax.numpy as jnp
from jax import lax
from jax.experimental import pallas as pl
from jax.experimental.pallas import tpu as pltpu
from jax.sharding import PartitionSpec as P

HEADS = 16
MESH = pl.DeviceIdType.MESH

epsilon = 1e-05
neg_fill = -1e30


class Place:
    def __init__(self, depth):
        dp = lax.axis_index("dp")
        fsdp = lax.axis_index("fsdp")
        self.depth = depth
        self.dp = dp
        self.z = fsdp // 2
        self.core = lax.rem(fsdp, 2)
        flip_x = dp + 1 - 2 * lax.rem(dp, 2)
        flip_y = lax.rem(dp + 2, 4)
        self.near = flip_x + self.core * (flip_y - flip_x)
        self.far = flip_y + self.core * (flip_x - flip_y)
        self.both = lax.rem(flip_x + 2, 4)
        self.fsdp = fsdp
        self.sibling = fsdp + 1 - 2 * self.core

    def up(self, step):
        return lax.rem(self.z + step, self.depth)

    def down(self, step):
        return lax.rem(self.z + self.depth - step, self.depth)

    def along(self, z):
        return (self.dp, z * 2 + self.core)

    def greet(self):
        barrier = pltpu.get_barrier_semaphore()
        others = [self.along(self.up(step)) for step in range(1, self.depth)]
        others += [(self.near, self.fsdp), (self.far, self.fsdp), (self.dp, self.sibling)]
        for other in others:
            pl.semaphore_signal(barrier, inc=1, device_id=other, device_id_type=MESH)
        pl.semaphore_wait(barrier, len(others))


def remote(source, target, send, recv, device):
    return pltpu.make_async_remote_copy(
        src_ref=source, dst_ref=target, send_sem=send, recv_sem=recv, device_id=device, device_id_type=MESH
    )


class Gather:
    def __init__(self, place, full, own, sems, piece):
        self.place, self.full, self.own, self.piece = place, full, own, piece
        self.su, self.ru, self.sd, self.rd, self.sb, self.rb, self.sa, self.ra, self.sc, self.rc, self.so = sems

    def copy_own(self):
        p = self.place
        return pltpu.make_async_copy(self.own, self.full.at[p.dp, p.z, p.core], self.so.at[self.piece])

    def copy_up(self, z, first=False):
        p = self.place
        block = self.full.at[p.dp, z, p.core]
        source = self.own if first else block
        return remote(source, block, self.su.at[self.piece, z], self.ru.at[self.piece, z], p.along(p.z + 1))

    def copy_down(self, z, first=False):
        p = self.place
        block = self.full.at[p.dp, z, p.core]
        source = self.own if first else block
        return remote(source, block, self.sd.at[self.piece, z], self.rd.at[self.piece, z], p.along(p.z - 1))

    def copy_near(self, z, first=False, arriving=False):
        p = self.place
        block = self.full.at[p.near if arriving else p.dp, z, p.core]
        source = self.own if first else block
        return remote(source, block, self.sb.at[self.piece, z], self.rb.at[self.piece, z], (p.near, p.fsdp))

    def copy_far(self, half, z, first=False, arriving=False):
        p = self.place
        row = (p.both if half else p.far) if arriving else (p.near if half else p.dp)
        block = self.full.at[row, z, p.core]
        source = self.own if first else block
        at = half * p.depth + z
        return remote(source, block, self.sa.at[self.piece, at], self.ra.at[self.piece, at], (p.far, p.fsdp))

    def copy_core(self, part, arriving=False):
        p = self.place
        if arriving:
            row = (p.dp, p.far, p.near, p.both)[part]
            block = self.full.at[row, :, 1 - p.core]
        else:
            row = (p.dp, p.near, p.far, p.both)[part]
            block = self.full.at[row, :, p.core]
        return remote(block, block, self.sc.at[self.piece, part], self.rc.at[self.piece, part], (p.dp, p.sibling))

    def start(self):
        p = self.place
        pl.when(p.z < p.depth - 1)(lambda: self.copy_up(p.z, True).start())
        pl.when(p.z > 0)(lambda: self.copy_down(p.z, True).start())
        self.copy_near(p.z, True).start()
        self.copy_far(0, p.z, True).start()
        self.copy_own().start()

    def hop(self, step):
        p = self.place

        @pl.when(p.z >= step)
        def _():
            z = p.z - step
            self.copy_up(z).wait_recv()
            pl.when(p.z < p.depth - 1)(lambda: self.copy_up(z).start())
            self.copy_near(z).start()
            self.copy_far(0, z).start()

        @pl.when(p.z + step < p.depth)
        def _():
            z = p.z + step
            self.copy_down(z).wait_recv()
            pl.when(p.z > 0)(lambda: self.copy_down(z).start())
            self.copy_near(z).start()
            self.copy_far(0, z).start()

    def last_hop(self):
        self.hop(self.place.depth - 1)
        self.copy_own().wait()
        self.copy_core(0).start()

    def spread(self, step):
        p = self.place

        def act(z):
            self.copy_near(z, arriving=True).wait_recv()
            self.copy_far(1, z).start()

        if step == 0:
            act(p.z)
        else:
            pl.when(p.z >= step)(lambda: act(p.z - step))
            pl.when(p.z + step < p.depth)(lambda: act(p.z + step))
        if step == p.depth - 1:
            self.copy_core(1).start()

    def arrive_far(self, half):
        p = self.place
        for z in range(p.depth):
            self.copy_far(half, z, arriving=True).wait_recv()
        self.copy_core(2 + half).start()

    def arrive_core(self, *parts):
        for part in parts:
            self.copy_core(part, arriving=True).wait_recv()

    def drain(self):
        p = self.place
        for z in range(p.depth):
            pl.when((p.z < p.depth - 1) & (z <= p.z))(lambda: self.copy_up(z).wait_send())
            pl.when((p.z > 0) & (z >= p.z))(lambda: self.copy_down(z).wait_send())
            self.copy_near(z).wait_send()
            self.copy_far(0, z).wait_send()
            self.copy_far(1, z).wait_send()
        for part in range(4):
            self.copy_core(part).wait_send()


def gather_sems(pieces, depth):
    dma = pltpu.SemaphoreType.DMA
    counts = (depth, depth, depth, depth, depth, depth, 2 * depth, 2 * depth, 4, 4)
    return [dma((pieces, count)) for count in counts] + [dma((pieces,))]


def matmul(left, right):
    return lax.dot_general(left, right, (((1,), (0,)), ((), ())), preferred_element_type=jnp.float32)


def matmul_nt(left, right):
    return lax.dot_general(left, right, (((1,), (1,)), ((), ())), preferred_element_type=jnp.float32)


def matmul_tn(left, right):
    return lax.dot_general(left, right, (((0,), (0,)), ((), ())), preferred_element_type=jnp.float32)


def flat(value):
    return value.reshape(-1, value.shape[-1])


def span(index, size):
    return pl.ds(pl.multiple_of(index * size, size), size)


def unpack_table(table, block, vectors):
    places = table.shape[0] * table.shape[1] * table.shape[2]
    width = vectors.shape[1]
    per_row = 128 // block
    lane = lax.broadcasted_iota(jnp.int32, (128, width), 1)
    source = lax.broadcasted_iota(jnp.int32, (128, width), 0)
    owner = lax.broadcasted_iota(jnp.int32, (places, width), 1) // block
    mine = owner == lax.broadcasted_iota(jnp.int32, (places, width), 0)
    for vector in range(8):
        row = table[:, :, :, vector // per_row, :].reshape(places, 128).astype(jnp.bfloat16)
        pick = jnp.where(source == lax.rem(lane, block) + block * (vector % per_row), 1.0, 0.0).astype(jnp.bfloat16)
        spread = jnp.where(mine, matmul(row, pick), 0.0)
        vectors[vector : vector + 1, :] = jnp.sum(spread, axis=0, keepdims=True)


def project(rows, weights, vectors, projected):
    width = rows.shape[1]
    for part, bias in ((0, 0), (1, None), (2, 1)):

        def one(index, _):
            at = span(index, 256)
            weight = flat(weights[:, :, :, :, part * width : (part + 1) * width])
            total = matmul(rows[at, :], weight)
            if bias is not None:
                total = total + vectors[bias : bias + 1, :]
            projected[at, part * width : (part + 1) * width] = total.astype(jnp.bfloat16)
            return 0

        lax.fori_loop(0, rows.shape[0] // 256, one, 0)


def head_lanes(heads, rows, size):
    lane = lax.broadcasted_iota(jnp.int32, (rows, heads * size), 1) // size
    return [lane == head for head in range(heads)]


def stack_heads(value, lanes):
    return jnp.concatenate([jnp.where(lane, value, jnp.zeros_like(value)) for lane in lanes], axis=0)


def merge_heads(value, lanes):
    rows = value.shape[0] // len(lanes)
    result = value[:rows]
    for head in range(1, len(lanes)):
        result = jnp.where(lanes[head], value[head * rows : (head + 1) * rows], result)
    return result


QUAD = 4


def attend(projected, keep, probs, context):
    width = context.shape[1]
    size = width // HEADS
    segments, length = keep.shape
    scale = size ** (-0.5)
    lanes = head_lanes(QUAD, length, size)
    quads = HEADS // QUAD

    def one(index, _):
        segment = index // quads
        quad = lax.rem(index, quads)
        at = span(segment, length)
        queries = projected[at, span(quad, QUAD * size)]
        keysets = projected[at, span(quad + quads, QUAD * size)]
        valuesets = projected[at, span(quad + 2 * quads, QUAD * size)]
        scores = matmul_nt(stack_heads(queries, lanes), keysets) * scale
        mask = keep[pl.ds(segment, 1), :] > 0
        scores = jnp.where(mask, scores, neg_fill)
        raised = jnp.exp(scores - jnp.max(scores, axis=1, keepdims=True))
        low = (raised / jnp.sum(raised, axis=1, keepdims=True)).astype(jnp.bfloat16)
        probs[index] = low
        context[at, span(quad, QUAD * size)] = merge_heads(matmul(low, valuesets), lanes).astype(jnp.bfloat16)
        return 0

    lax.fori_loop(0, segments * quads, one, 0)


def center_scale(hidden):
    center = hidden - jnp.mean(hidden, axis=1, keepdims=True)
    spread = jnp.mean(center * center, axis=1, keepdims=True)
    rate = lax.rsqrt(spread + epsilon)
    return center * rate, rate


def first_block(rows, context, weights, vectors, first_sum, first_norm, first_low):

    def one(index, _):
        at = span(index, 128)
        weight = flat(weights[...])
        total = rows[at, :].astype(jnp.float32) + (matmul(context[at, :], weight) + vectors[2:3, :])
        first_sum[at, :] = total
        normed, _ = center_scale(total)
        result = normed * vectors[3:4, :] + vectors[4:5, :]
        first_norm[at, :] = result
        first_low[at, :] = result.astype(jnp.bfloat16)
        return 0

    lax.fori_loop(0, rows.shape[0] // 128, one, 0)


def inner_block(first_low, weights, table, row_at, activated, slope):
    count = first_low.shape[0]
    biases = table.shape[0] * table.shape[1] * table.shape[2]
    chunks = weights.shape[4] // 512
    per_chunk = biases // chunks
    rows_of = table[:, :, :, row_at, :].reshape(biases, 128)
    for chunk in range(chunks):
        columns = slice(chunk * 512, (chunk + 1) * 512)
        first = chunk * per_chunk
        bias = jnp.concatenate([rows_of[first + part : first + part + 1] for part in range(per_chunk)], axis=1)

        def one(index, _):
            at = span(index, 128)
            value = matmul(first_low[at, :], flat(weights[:, :, :, :, columns])) + bias
            share = 0.5 * (1.0 + lax.erf(value * (0.5**0.5)))
            bell = jnp.exp(-0.5 * value * value) * ((0.5 / jnp.pi) ** 0.5)
            activated[at, columns] = (value * share).astype(jnp.bfloat16)
            slope[at, columns] = (share + value * bell).astype(jnp.bfloat16)
            return 0

        lax.fori_loop(0, count // 128, one, 0)


def outer_part(activated, weights, row, total, fresh):
    size = weights.shape[1] * weights.shape[2] * weights.shape[3]

    def one(index, _):
        at = span(index, 256)
        value = matmul(activated[at, span(row, size)], flat(weights[row]))
        total[at, :] = value if fresh else total[at, :] + value
        return 0

    lax.fori_loop(0, activated.shape[0] // 256, one, 0)


def norm_back(grad, normed, rate, gain):
    scaled = grad * gain
    mean = jnp.mean(scaled, axis=1, keepdims=True)
    along = jnp.mean(scaled * normed, axis=1, keepdims=True)
    return rate * (scaled - mean - normed * along)


def second_block(first_norm, total, cotangent, vectors, encoded, second_grad, outer_low, sums):
    sums[...] = jnp.zeros_like(sums)

    def one(index, _):
        at = span(index, 128)
        normed, rate = center_scale(first_norm[at, :] + (total[at, :] + vectors[5:6, :]))
        gain = vectors[6:7, :]
        encoded[at, :] = (normed * gain + vectors[7:8, :]).astype(jnp.bfloat16)
        grad = cotangent[at, :].astype(jnp.float32)
        back = norm_back(grad, normed, rate, gain)
        low = back.astype(jnp.bfloat16)
        second_grad[at, :] = back
        outer_low[at, :] = low
        sums[5:6, :] += jnp.sum(low.astype(jnp.float32), axis=0, keepdims=True)
        sums[6:7, :] += jnp.sum(grad * normed, axis=0, keepdims=True)
        sums[7:8, :] += jnp.sum(grad, axis=0, keepdims=True)
        return 0

    lax.fori_loop(0, first_norm.shape[0] // 128, one, 0)


def forward_kernel(depth, block, *refs):
    (rows, keep, cotangent, query_own, key_own, value_own, attn_own, inner_own, outer_own, table_own) = refs[:10]
    merged_out, attn_out, inner_out, outer_out = refs[10:14]
    (encoded_out, projected_out, probs_out, context_out, first_sum_out, first_low_out, activated_out, slope_out,
     second_grad_out, outer_low_out, vectors, sums) = refs[14:26]
    (merged_own, table, merged, attn, inner, outer, projected, probs, context, first_sum, first_norm, first_low, activated,
     slope, total, encoded, second_grad, outer_low, save_sem) = refs[26:45]
    sems = refs[45:]
    place = Place(depth)
    width = rows.shape[1]
    for part, own in enumerate((query_own, key_own, value_own)):
        merged_own[:, part * width : (part + 1) * width] = own[...]
    net_table = Gather(place, table, table_own, sems, 0)
    net_merged = Gather(place, merged, merged_own, sems, 1)
    net_attn = Gather(place, attn, attn_own, sems, 2)
    net_inner = Gather(place, inner, inner_own, sems, 3)
    net_outer = Gather(place, outer, outer_own, sems, 4)
    nets = (net_table, net_merged, net_attn, net_inner, net_outer)
    front = nets[:3]
    place.greet()
    saves = []

    def save(source, target):
        copy = pltpu.make_async_copy(source, target, save_sem.at[len(saves)])
        copy.start()
        saves.append(copy)

    def hop(net, step):
        if step == depth - 1:
            net.last_hop()
        else:
            net.hop(step)

    for net in front:
        net.start()
    for step in range(1, depth):
        for net in front:
            hop(net, step)
        if step == 1:
            net_inner.start()
        for net in front:
            net.spread(step - 1)
    for net in front:
        net.spread(depth - 1)
    hop(net_inner, 1)
    net_inner.spread(0)
    net_outer.start()
    for net in front:
        net.arrive_far(0)
        net.arrive_far(1)
        net.arrive_core(0, 1, 2, 3)
    save(merged, merged_out)
    save(attn, attn_out)
    unpack_table(table, block, vectors)
    project(rows, merged, vectors, projected)
    save(projected, projected_out)
    for step in range(2, depth):
        hop(net_inner, step)
        net_inner.spread(step - 1)
    net_inner.spread(depth - 1)
    attend(projected, keep, probs, context)
    save(probs, probs_out)
    save(context, context_out)
    hop(net_outer, 1)
    net_outer.spread(0)
    first_block(rows, context, attn, vectors, first_sum, first_norm, first_low)
    save(first_sum, first_sum_out)
    save(first_low, first_low_out)
    for step in range(2, depth):
        hop(net_outer, step)
        net_outer.spread(step - 1)
    net_outer.spread(depth - 1)
    net_inner.arrive_far(0)
    net_inner.arrive_far(1)
    net_inner.arrive_core(0, 1, 2, 3)
    save(inner, inner_out)
    inner_block(first_low, inner, table, 8 * block // 128, activated, slope)
    save(activated, activated_out)
    save(slope, slope_out)
    net_outer.arrive_core(0)
    outer_part(activated, outer, place.dp, total, True)
    net_outer.arrive_far(0)
    net_outer.arrive_core(1, 2)
    outer_part(activated, outer, place.near, total, False)
    outer_part(activated, outer, place.far, total, False)
    net_outer.arrive_far(1)
    net_outer.arrive_core(3)
    save(outer, outer_out)
    outer_part(activated, outer, place.both, total, False)
    second_block(first_norm, total, cotangent, vectors, encoded, second_grad, outer_low, sums)
    save(encoded, encoded_out)
    save(second_grad, second_grad_out)
    save(outer_low, outer_low_out)
    for net in nets:
        net.drain()
    for copy in saves:
        copy.wait()


def forward_all(depth, block, rows, keep, cotangent, owns):
    query_own, _, _, attn_own, inner_own, outer_own, table_own = owns
    tokens, width = rows.shape
    hidden = inner_own.shape[1]
    segments, length = keep.shape
    low, high = jnp.bfloat16, jnp.float32

    def fulls(own, columns):
        return (4, depth, 2, own.shape[0], columns)

    full_shapes = [fulls(query_own, 3 * width), fulls(attn_own, width), fulls(inner_own, hidden), fulls(outer_own, width)]
    kept = [
        ((tokens, width), low),
        ((tokens, 3 * width), low),
        ((segments * HEADS // QUAD, QUAD * length, length), low),
        ((tokens, width), low),
        ((tokens, width), high),
        ((tokens, width), low),
        ((tokens, hidden), low),
        ((tokens, hidden), low),
        ((tokens, width), high),
        ((tokens, width), low),
    ]
    small = [((8, width), high), ((8, width), high)]
    shapes = [jax.ShapeDtypeStruct(shape, low) for shape in full_shapes]
    shapes += [jax.ShapeDtypeStruct(*one) for one in kept + small]
    held = {name: pltpu.VMEM(*one) for name, one in zip(
        ("encoded", "projected", "probs", "context", "first_sum", "first_low", "activated", "slope", "second_grad", "outer_low"),
        kept)}
    scratch = [pltpu.VMEM((query_own.shape[0], 3 * width), low), pltpu.VMEM(fulls(table_own, 128), high)]
    scratch += [pltpu.VMEM(shape, low) for shape in full_shapes]
    scratch += [held[name] for name in ("projected", "probs", "context", "first_sum")]
    scratch += [pltpu.VMEM((tokens, width), high)]
    scratch += [held[name] for name in ("first_low", "activated", "slope")]
    scratch += [pltpu.VMEM((tokens, width), high)]
    scratch += [held[name] for name in ("encoded", "second_grad", "outer_low")]
    scratch += [pltpu.SemaphoreType.DMA((len(full_shapes) + len(kept),))]
    here = pl.BlockSpec(memory_space=pltpu.VMEM)
    away = pl.BlockSpec(memory_space=pl.ANY)
    return pl.pallas_call(
        functools.partial(forward_kernel, depth, block),
        out_shape=shapes,
        in_specs=[here] * 10,
        out_specs=[away] * (len(full_shapes) + len(kept)) + [here] * 2,
        scratch_shapes=scratch + gather_sems(5, depth),
        compiler_params=pltpu.CompilerParams(
            collective_id=0, has_side_effects=True, vmem_limit_bytes=60 * 1024 * 1024
        ),
        name="forward",
    )(rows, keep, cotangent, *owns)


SUBS = 4


class Slots:
    def __init__(self, core, far, near, along):
        self.core, self.far, self.near, self.along = core, far, near, along


class Scatter:
    def __init__(self, place, whole, slots, sems, credits, number, lot, first, count, after=False, before=False,
                 late_after=False, late_before=False):
        self.place, self.whole, self.slots = place, whole, slots
        self.sc, self.rc, self.sa, self.ra, self.sb, self.rb, self.sz, self.rz = sems
        self.core_free, self.far_free, self.near_free, self.z_free = credits
        self.number, self.lot, self.first, self.count = number, lot, first, count
        self.sub = first // count
        self.after, self.before, self.late_after, self.late_before = after, before, late_after, late_before
        self.tile = 8 if whole.dtype == jnp.float32 else 16

    def lines(self):
        return pl.ds(self.first, self.count)

    def mine(self, row):
        return self.whole.at[row, :, self.place.core, self.lines()]

    def sent_row(self, at):
        p = self.place
        return (p.both, p.near, p.far, p.dp)[at]

    def got_row(self, at):
        p = self.place
        return (p.both, p.far, p.near, p.dp)[at]

    def copy_core(self, at):
        p = self.place
        return remote(
            self.whole.at[self.sent_row(at), :, 1 - p.core, self.lines()], self.slots.core.at[at, :, self.lines()],
            self.sc.at[self.number, at], self.rc.at[self.number, at], (p.dp, p.sibling),
        )

    def copy_far(self, half):
        p = self.place
        return remote(
            self.mine(p.both if half else p.far), self.slots.far.at[self.lot, half, :, self.lines()],
            self.sa.at[self.number, half], self.ra.at[self.number, half], (p.far, p.fsdp),
        )

    def copy_near(self):
        p = self.place
        return remote(
            self.mine(p.near), self.slots.near.at[self.lot, :, self.lines()], self.sb.at[self.number],
            self.rb.at[self.number], (p.near, p.fsdp),
        )

    def copy_z(self, step):
        p = self.place
        return remote(
            self.whole.at[p.dp, p.up(step), p.core, self.lines()], self.slots.along.at[self.lot, step - 1, self.lines()],
            self.sz.at[self.number, step - 1], self.rz.at[self.number, step - 1], p.along(p.up(step)),
        )

    def add(self, row, slot):
        p = self.place
        tiles = self.count // self.tile

        def one(index, _):
            z = index // tiles
            at = pl.ds(pl.multiple_of(self.first + lax.rem(index, tiles) * self.tile, self.tile), self.tile)
            self.whole[row, z, p.core, at, :] = self.whole[row, z, p.core, at, :] + slot[z, at, :]
            return 0

        lax.fori_loop(0, p.depth * tiles, one, 0)

    def start_core(self, at):
        if self.after:
            pl.semaphore_wait(self.core_free.at[at, self.sub], 1)
        self.copy_core(at).start()

    def add_core(self, at):
        p = self.place
        self.copy_core(at).wait_recv()
        self.add(self.got_row(at), self.slots.core.at[at])
        if self.before:
            pl.semaphore_signal(self.core_free.at[at, self.sub], inc=1, device_id=(p.dp, p.sibling), device_id_type=MESH)
        if at < 2:
            if self.late_after:
                pl.semaphore_wait(self.far_free.at[1 - at, self.sub], 1)
            self.copy_far(1 - at).start()

    def add_far(self, half):
        p = self.place
        self.copy_far(half).wait_recv()
        self.add(p.near if half else p.dp, self.slots.far.at[self.lot, half])
        if self.late_before:
            pl.semaphore_signal(self.far_free.at[half, self.sub], inc=1, device_id=(p.far, p.fsdp), device_id_type=MESH)
        if half:
            if self.late_after:
                pl.semaphore_wait(self.near_free.at[self.sub], 1)
            self.copy_near().start()

    def add_near(self):
        p = self.place
        self.copy_near().wait_recv()
        self.add(p.dp, self.slots.near.at[self.lot])
        if self.late_before:
            pl.semaphore_signal(self.near_free.at[self.sub], inc=1, device_id=(p.near, p.fsdp), device_id_type=MESH)
        for step in range(1, p.depth):
            if self.late_after:
                pl.semaphore_wait(self.z_free.at[self.sub, step - 1], 1)
            self.copy_z(step).start()

    def finish(self, out):
        p = self.place
        for step in range(1, p.depth):
            self.copy_z(step).wait_recv()

        def one(index, _):
            start = pl.multiple_of(index * self.tile, self.tile)
            at = pl.ds(pl.multiple_of(self.first + start, self.tile), self.tile)
            total = self.whole[p.dp, p.z, p.core, at, :].astype(jnp.float32)
            for step in range(p.depth - 1):
                total = total + self.slots.along[self.lot, step, at, :].astype(jnp.float32)
            out[pl.ds(start, self.tile), :] = total
            return 0

        lax.fori_loop(0, self.count // self.tile, one, 0)
        if self.late_before:
            for step in range(1, p.depth):
                pl.semaphore_signal(
                    self.z_free.at[self.sub, step - 1], inc=1, device_id=p.along(p.down(step)), device_id_type=MESH
                )

    def drain(self):
        for at in range(4):
            self.copy_core(at).wait_send()
        self.copy_far(1).wait_send()
        self.copy_far(0).wait_send()
        self.copy_near().wait_send()
        for step in range(1, self.place.depth):
            self.copy_z(step).wait_send()


def outer_gradient(acts, low, grads, row):
    depth, cores, count, _ = grads.shape[1:]
    size = cores * count

    def one(z, _):
        value = matmul_tn(acts[row, :, span(z, size)], low[...])
        grads[row, z] = value.astype(jnp.bfloat16).reshape(grads.shape[2:])
        return 0

    lax.fori_loop(0, depth, one, 0)


def input_gradient(inputs, low, grads, row, part):
    depth, cores, count, width = grads.shape[1:]
    size = inputs.shape[1] // grads.shape[0]
    lines = count // SUBS
    value = matmul_tn(inputs[:, span(row, size)], low)
    grads[row, :, :, part * lines : (part + 1) * lines, :] = value.astype(jnp.bfloat16).reshape(depth, cores, lines, width)


def hidden_back(low, weights, slopes, bias_sum):
    width = low.shape[1]
    for part in range(SUBS):
        bias_sum[:, part * width : (part + 1) * width] = jnp.zeros((1, width), jnp.float32)

        def one(index, _):
            at = span(index, 128)
            value = matmul_nt(low[at, :], flat(weights[part])) * slopes[SUBS + part, at, :].astype(jnp.float32)
            rounded = value.astype(jnp.bfloat16)
            slopes[SUBS + part, at, :] = rounded
            bias_sum[:, part * width : (part + 1) * width] += jnp.sum(rounded.astype(jnp.float32), axis=0, keepdims=True)
            return 0

        lax.fori_loop(0, low.shape[0] // 128, one, 0)


def first_total_part(grad, inner_low, weights, part):
    lines = weights.shape[3] // SUBS

    def one(index, _):
        at = span(index, 128)
        weight = flat(weights[:, :, :, part * lines : (part + 1) * lines, :])
        grad[at, :] += matmul_nt(inner_low[SUBS + part, at, :], weight)
        return 0

    lax.fori_loop(0, grad.shape[0] // 128, one, 0)


def first_back(first_sum, grad, low, vectors, sums):
    for row in (2, 3, 4):
        sums[row : row + 1, :] = jnp.zeros((1, grad.shape[1]), jnp.float32)

    def one(index, _):
        at = span(index, 64)
        normed, rate = center_scale(first_sum[at, :])
        upper = grad[at, :]
        back = norm_back(upper, normed, rate, vectors[3:4, :])
        rounded = back.astype(jnp.bfloat16)
        grad[at, :] = back
        low[at, :] = rounded
        sums[2:3, :] += jnp.sum(rounded.astype(jnp.float32), axis=0, keepdims=True)
        sums[3:4, :] += jnp.sum(upper * normed, axis=0, keepdims=True)
        sums[4:5, :] += jnp.sum(upper, axis=0, keepdims=True)
        return 0

    lax.fori_loop(0, grad.shape[0] // 64, one, 0)


def context_back(low, weights, context):
    def one(index, _):
        at = span(index, 128)
        context[at, :] = matmul_nt(low[at, :], flat(weights[0:2])).astype(jnp.bfloat16)
        return 0

    lax.fori_loop(0, low.shape[0] // 128, one, 0)


def attend_back(projected, probs, context_low, sums, first, last):
    width = context_low.shape[1]
    size = width // HEADS
    length = probs.shape[2]
    scale = size ** (-0.5)
    lanes = head_lanes(QUAD, length, size)
    quads = HEADS // QUAD

    def one(index, _):
        segment = index // quads
        quad = lax.rem(index, quads)
        at = span(segment, length)
        columns = [span(quad + part * quads, QUAD * size) for part in range(3)]
        queries, keysets, valuesets = [projected[at, column] for column in columns]
        low = probs[index]
        wide = low.astype(jnp.float32)
        upper = stack_heads(context_low[at, columns[0]], lanes)
        prob_grad = matmul_nt(upper, valuesets)
        score_low = (wide * (prob_grad - jnp.sum(wide * prob_grad, axis=1, keepdims=True))).astype(jnp.bfloat16)
        value_low = matmul_tn(low, upper).astype(jnp.bfloat16)
        query_low = (merge_heads(matmul(score_low, keysets), lanes) * scale).astype(jnp.bfloat16)
        key_low = (matmul_tn(score_low, stack_heads(queries, lanes)) * scale).astype(jnp.bfloat16)
        projected[at, columns[0]] = query_low
        projected[at, columns[1]] = key_low
        projected[at, columns[2]] = value_low
        sums[0:1, columns[0]] += jnp.sum(query_low.astype(jnp.float32), axis=0, keepdims=True)
        sums[1:2, columns[0]] += jnp.sum(value_low.astype(jnp.float32), axis=0, keepdims=True)
        return 0

    lax.fori_loop(first, last, one, 0)


def states_back(grad, projected, weights):
    width = grad.shape[1]

    def one(index, _):
        at = span(index, 128)
        total = grad[at, :]
        for part in range(3):
            weight = flat(weights[2 + 2 * part : 4 + 2 * part])
            total = total + matmul_nt(projected[at, part * width : (part + 1) * width], weight)
        grad[at, :] = total
        return 0

    lax.fori_loop(0, grad.shape[0] // 128, one, 0)


def pack_sums(sums, bias_sum, block, table):
    dps, depth, cores = table.shape[:3]
    places = dps * depth * cores
    width = sums.shape[1]
    per_row = 128 // block
    lane = lax.broadcasted_iota(jnp.int32, (width, 128), 1)
    source = lax.broadcasted_iota(jnp.int32, (width, 128), 0)
    owner = lax.broadcasted_iota(jnp.int32, (places, width), 1) // block
    mine = owner == lax.broadcasted_iota(jnp.int32, (places, width), 0)
    table[...] = jnp.zeros_like(table)
    for row in range(8 // per_row):
        total = jnp.zeros((places, 128), jnp.float32)
        for part in range(per_row):
            vector = row * per_row + part
            pick = jnp.where(lane == lax.rem(source, block) + block * part, 1.0, 0.0).astype(jnp.bfloat16)
            value = jnp.where(mine, sums[vector : vector + 1, :], 0.0)
            upper = value.astype(jnp.bfloat16)
            lower = (value - upper.astype(jnp.float32)).astype(jnp.bfloat16)
            both = matmul(jnp.concatenate((upper, lower), axis=0), pick)
            total = total + (both[:places] + both[places:])
        table[:, :, :, row, :] = total.reshape(dps, depth, cores, 128)
    row = 8 * block // 128
    for index in range(places):
        dp, z, core = index // (depth * cores), index // cores % depth, index % cores
        table[dp, z, core, row : row + 1, :] = bias_sum[:, index * 128 : (index + 1) * 128]


def backward_kernel(depth, block, *refs):
    (vectors, known, rows_in, activated_in, slope_in, outer_low_in, second_grad_in, first_sum_in, first_low_in, context_in,
     projected_in, probs_in, merged_in, attn_in, inner_in, outer_in) = refs[:16]
    states_out, outer_out, inner_out, query_out, key_out, value_out, attn_out, table_out = refs[16:24]
    (first_buffer, second_buffer, outer_grads, wide, from_core, from_far, from_near, from_z, low, first_low, grad, first_sum,
     context, projected, probs, rows, sums, bias_sum, table, table_core, table_far, table_near, table_z) = refs[24:47]
    load_sem, save_sem = refs[47:49]
    sems = refs[49:57]
    credits = refs[57:61]
    place = Place(depth)
    width = rows.shape[1]
    tokens = rows.shape[0]
    lines = outer_grads.shape[3] // SUBS
    loads = []

    def load(source, target):
        copy = pltpu.make_async_copy(source, target, load_sem.at[len(loads)])
        copy.start()
        loads.append(copy)
        return copy

    def load_columns(source, targets):
        return [load(source.at[:, part * width : (part + 1) * width], target) for part, target in enumerate(targets)]

    low_load = load(outer_low_in, low)
    act_loads = load_columns(activated_in, [wide.at[part] for part in range(SUBS)])
    outer_load = load(outer_in, first_buffer)
    slope_loads = load_columns(slope_in, [wide.at[SUBS + part] for part in range(SUBS)])
    first_low_load = load(first_low_in, first_low)
    grad_load = load(second_grad_in, grad)
    inner_loads = [
        load(inner_in.at[:, :, :, :, part * width : (part + 1) * width],
             second_buffer.at[:, :, :, part * lines : (part + 1) * lines, :])
        for part in range(SUBS)
    ]
    first_sum_load = load(first_sum_in, first_sum)
    context_load = load(context_in, context)
    projected_load = load(projected_in, projected)
    probs_load = load(probs_in, probs)
    rows_load = load(rows_in, rows)

    slots = Slots(from_core, from_far, from_near, from_z)
    table_slots = Slots(table_core, table_far, table_near, table_z)
    outers = [
        Scatter(place, outer_grads, slots, sems, credits, sub, 0, sub * lines, lines, before=True, late_before=True)
        for sub in range(SUBS)
    ]
    inner_grads = first_buffer
    inners = [
        Scatter(place, inner_grads, slots, sems, credits, SUBS + sub, 1, sub * lines, lines, after=True, before=True)
        for sub in range(SUBS)
    ]
    other_grads = second_buffer
    others = [
        Scatter(place, other_grads, slots, sems, credits, 2 * SUBS + sub, 0, sub * lines, lines, after=True, late_after=True)
        for sub in range(SUBS)
    ]
    attn_net = others[3]
    mergeds = others[:3]
    small = Scatter(place, table, table_slots, sems, credits, 3 * SUBS, 0, 0, 8)
    row_order = (place.both, place.near, place.far, place.dp)
    sums[...] = known[...]
    sums[0:2, :] = jnp.zeros((2, width), jnp.float32)
    place.greet()

    def pieces(nets, compute):
        for at in range(4):
            compute(row_order[at])
            for net in nets:
                net.start_core(at)
            if at:
                for net in nets:
                    net.add_core(at - 1)
        for net in nets:
            net.add_core(3)

    low_load.wait()
    for copy in act_loads:
        copy.wait()
    pieces(outers, lambda row: outer_gradient(wide, low, outer_grads, row))
    half = tokens
    attn_loads = [load(attn_in.at[part * half : (part + 1) * half], wide.at[part]) for part in range(2)]

    def load_merged(part):
        return [
            load(merged_in.at[at * half : (at + 1) * half, part * width : (part + 1) * width], wide.at[2 + 2 * part + at])
            for at in range(2)
        ]

    merged_loads = load_merged(0)
    outer_load.wait()
    for copy in slope_loads:
        copy.wait()
    hidden_back(low, first_buffer, wide, bias_sum)
    first_low_load.wait()

    def inner_rows(row):
        for part in range(SUBS):
            input_gradient(first_low, wide[SUBS + part], inner_grads, row, part)

    pieces(inners, inner_rows)
    for net in outers:
        net.add_far(1)
    grad_load.wait()
    for copy in inner_loads:
        copy.wait()
    for part in range(SUBS):
        first_total_part(grad, wide, second_buffer, part)
    merged_loads += load_merged(1) + load_merged(2)
    for net in outers:
        net.add_far(0)
    first_sum_load.wait()
    first_back(first_sum, grad, low, vectors, sums)
    context_load.wait()
    pieces([attn_net], lambda row: input_gradient(context, low[...], other_grads, row, 3))
    for copy in attn_loads:
        copy.wait()
    context_back(low, wide, context)
    for net in outers:
        net.add_near()
    projected_load.wait()
    probs_load.wait()
    count = probs.shape[0]
    attend_back(projected, probs, context, sums, 0, count // 2)
    for net in inners:
        net.add_far(1)
    attend_back(projected, probs, context, sums, count // 2, count)
    rows_load.wait()

    def merged_rows(row):
        for part in range(3):
            input_gradient(rows, projected[:, part * width : (part + 1) * width], other_grads, row, part)

    for sub, net in enumerate(outers):
        net.finish(outer_out.at[pl.ds(sub * lines, lines), :])
    pieces(mergeds, merged_rows)
    for net in inners:
        net.add_far(0)
    pack_sums(sums, bias_sum, block, table)
    pieces([small], lambda row: None)
    for copy in merged_loads:
        copy.wait()
    states_back(grad, projected, wide)
    save = pltpu.make_async_copy(grad, states_out, save_sem)
    save.start()
    for net in inners:
        net.add_near()
    last = [attn_net] + mergeds + [small]
    for net in last:
        net.add_far(1)
    for net in last:
        net.add_far(0)
        net.add_near()
    for sub, net in enumerate(inners):
        net.finish(inner_out.at[:, pl.ds(sub * width, width)])
    for net, out in zip(last, (attn_out, query_out, key_out, value_out, table_out)):
        net.finish(out)
    for net in outers + inners + last:
        net.drain()
    save.wait()


def backward_all(depth, block, vectors, known, kept):
    low, high = jnp.bfloat16, jnp.float32
    (rows, activated, _, _, _, first_sum, _, _, projected, probs, _, _, inner, outer) = kept
    tokens, width = rows.shape
    hidden = activated.shape[1]
    unit = outer.shape
    lines = unit[3]
    own_rows = lines // SUBS
    dma, regular = pltpu.SemaphoreType.DMA, pltpu.SemaphoreType.REGULAR
    nets = 3 * SUBS + 1
    scratch = [
        pltpu.VMEM(unit, low),
        pltpu.VMEM(unit, low),
        pltpu.VMEM(unit, low),
        pltpu.VMEM((2 * SUBS, tokens, width), low),
        pltpu.VMEM((4, depth, lines, width), low),
        pltpu.VMEM((2, 2, depth, lines, width), low),
        pltpu.VMEM((2, depth, lines, width), low),
        pltpu.VMEM((2, depth - 1, lines, width), low),
        pltpu.VMEM((tokens, width), low),
        pltpu.VMEM((tokens, width), low),
        pltpu.VMEM((tokens, width), high),
        pltpu.VMEM((tokens, width), high),
        pltpu.VMEM((tokens, width), low),
        pltpu.VMEM(projected.shape, low),
        pltpu.VMEM(probs.shape, low),
        pltpu.VMEM((tokens, width), low),
        pltpu.VMEM((8, width), high),
        pltpu.VMEM((1, hidden), high),
        pltpu.VMEM((4, depth, 2, 8, 128), high),
        pltpu.VMEM((4, depth, 8, 128), high),
        pltpu.VMEM((1, 2, depth, 8, 128), high),
        pltpu.VMEM((1, depth, 8, 128), high),
        pltpu.VMEM((1, depth - 1, 8, 128), high),
        dma((40,)),
        dma,
        dma((nets, 4)), dma((nets, 4)), dma((nets, 2)), dma((nets, 2)), dma((nets,)), dma((nets,)),
        dma((nets, depth - 1)), dma((nets, depth - 1)),
        regular((4, SUBS)), regular((2, SUBS)), regular((SUBS,)), regular((SUBS, depth - 1)),
    ]
    shapes = [(tokens, width), (lines, width), (own_rows, hidden)] + [(own_rows, width)] * 4 + [(8, 128)]
    here = pl.BlockSpec(memory_space=pltpu.VMEM)
    away = pl.BlockSpec(memory_space=pl.ANY)
    return pl.pallas_call(
        functools.partial(backward_kernel, depth, block),
        out_shape=[jax.ShapeDtypeStruct(shape, high) for shape in shapes],
        in_specs=[here] * 2 + [away] * len(kept),
        out_specs=[away] + [here] * 7,
        scratch_shapes=scratch,
        compiler_params=pltpu.CompilerParams(
            collective_id=1, has_side_effects=True, vmem_limit_bytes=62 * 1024 * 1024
        ),
        name="backward",
    )(vectors, known, *kept)


def normalize(hidden, gain, shift):
    center = hidden - jnp.mean(hidden, axis=-1, keepdims=True)
    spread = jnp.mean(center * center, axis=-1, keepdims=True)
    return center * lax.rsqrt(spread + epsilon) * gain + shift


def exact_gelu(value):
    return jax.nn.gelu(value, approximate=False)


def contract_rows(left, right):
    return lax.dot_general(
        left, right, (((0,), (0,)), ((), ())), preferred_element_type=jnp.float32
    )


def times_transposed(left, right):
    return lax.dot_general(
        left, right, (((1,), (1,)), ((), ())), preferred_element_type=jnp.float32
    )


def collect(merged, attn, inner, outer, vectors, widened):
    return (
        lax.all_gather(merged, ("dp", "fsdp"), axis=0, tiled=True),
        lax.all_gather(attn, ("dp", "fsdp"), axis=0, tiled=True),
        lax.all_gather(inner, ("dp", "fsdp"), axis=0, tiled=True),
        lax.all_gather(outer, ("dp", "fsdp"), axis=0, tiled=True),
        lax.all_gather(vectors, ("dp", "fsdp"), axis=0, tiled=True),
        lax.all_gather(widened, ("dp", "fsdp"), axis=0, tiled=True),
    )


def reduce_grads(merged, attn, inner, outer, vectors, widened):
    return (
        lax.psum_scatter(merged, ("dp", "fsdp"), scatter_dimension=0, tiled=True),
        lax.psum_scatter(attn, ("dp", "fsdp"), scatter_dimension=0, tiled=True),
        lax.psum_scatter(inner, ("dp", "fsdp"), scatter_dimension=0, tiled=True),
        lax.psum_scatter(outer, ("dp", "fsdp"), scatter_dimension=0, tiled=True),
        lax.psum_scatter(vectors, ("dp", "fsdp"), scatter_dimension=0, tiled=True),
        lax.psum_scatter(widened, ("dp", "fsdp"), scatter_dimension=0, tiled=True),
    )


def split_heads(projected, segments):
    total_rows, triple = projected.shape
    width = triple // 3
    return projected.reshape(segments, total_rows // segments, 3, HEADS, width // HEADS)


def attention_probs(queries, keysets, keep, scale):
    scores = (
        jnp.einsum("sqhd,skhd->shqk", queries, keysets, preferred_element_type=jnp.float32) * scale
    )
    scores = jnp.where(keep[:, None, None, :] > 0, scores, neg_fill)
    peaks = jnp.max(scores, axis=-1, keepdims=True)
    raised = jnp.exp(scores - peaks)
    return raised / jnp.sum(raised, axis=-1, keepdims=True)


def forward_pass(rows, keep, weights):
    merged, attn, inner, outer, vectors, widened = weights
    vector_full = vectors.astype(jnp.float32)
    width = rows.shape[1]
    scale = (width // HEADS) ** (-0.5)
    merged_bias = jnp.concatenate(
        (vector_full[:, 0], jnp.zeros((width,), jnp.float32), vector_full[:, 1])
    )
    projected = (jnp.dot(rows, merged, preferred_element_type=jnp.float32) + merged_bias).astype(
        jnp.bfloat16
    )
    split = split_heads(projected, keep.shape[0])
    probs = attention_probs(split[:, :, 0], split[:, :, 1], keep, scale).astype(jnp.bfloat16)
    context = jnp.einsum(
        "shqk,skhd->sqhd", probs, split[:, :, 2], preferred_element_type=jnp.float32
    )
    context = context.reshape(rows.shape[0], width).astype(jnp.bfloat16)
    attended = jnp.dot(context, attn, preferred_element_type=jnp.float32) + vector_full[:, 2]
    first_sum = rows.astype(jnp.float32) + attended
    first_norm = normalize(first_sum, vector_full[:, 3], vector_full[:, 4])
    first_low = first_norm.astype(jnp.bfloat16)
    inner_act = jnp.dot(first_low, inner, preferred_element_type=jnp.float32) + widened.astype(
        jnp.float32
    )
    activated = exact_gelu(inner_act).astype(jnp.bfloat16)
    outer_act = jnp.dot(activated, outer, preferred_element_type=jnp.float32) + vector_full[:, 5]
    second_sum = first_norm + outer_act
    encoded = normalize(second_sum, vector_full[:, 6], vector_full[:, 7]).astype(jnp.bfloat16)
    return (encoded, (projected, context, first_sum, first_low, inner_act, activated, second_sum))


def backward_pass(rows, keep, cotangent, weights, kept):
    merged, attn, inner, outer, vectors, widened = weights
    projected, context, first_sum, first_low, inner_act, activated, second_sum = kept
    vector_full = vectors.astype(jnp.float32)
    width = rows.shape[1]
    scale = (width // HEADS) ** (-0.5)
    second_out, second_pull = jax.vjp(normalize, second_sum, vector_full[:, 6], vector_full[:, 7])
    second_grad, second_gain_g, second_shift_g = second_pull(cotangent.astype(jnp.float32))
    outer_low = second_grad.astype(jnp.bfloat16)
    outer_bias_g = jnp.sum(outer_low.astype(jnp.float32), axis=0)
    outer_weight_g = contract_rows(activated, outer_low)
    act_grad = times_transposed(outer_low, outer)
    gelu_out, gelu_pull = jax.vjp(exact_gelu, inner_act)
    inner_low = gelu_pull(act_grad)[0].astype(jnp.bfloat16)
    inner_bias_g = jnp.sum(inner_low.astype(jnp.float32), axis=0)
    inner_weight_g = contract_rows(first_low, inner_low)
    first_total = second_grad + times_transposed(inner_low, inner)
    first_out, first_pull = jax.vjp(normalize, first_sum, vector_full[:, 3], vector_full[:, 4])
    first_grad, first_gain_g, first_shift_g = first_pull(first_total)
    attended_low = first_grad.astype(jnp.bfloat16)
    attn_bias_g = jnp.sum(attended_low.astype(jnp.float32), axis=0)
    attn_weight_g = contract_rows(context, attended_low)
    context_low = times_transposed(attended_low, attn).astype(jnp.bfloat16)
    split = split_heads(projected, keep.shape[0])
    queries = split[:, :, 0]
    keysets = split[:, :, 1]
    valuesets = split[:, :, 2]
    probs = attention_probs(queries, keysets, keep, scale)
    probs_low = probs.astype(jnp.bfloat16)
    context_heads = context_low.reshape(queries.shape)
    prob_grad = jnp.einsum(
        "sqhd,skhd->shqk", context_heads, valuesets, preferred_element_type=jnp.float32
    )
    value_grad = jnp.einsum(
        "shqk,sqhd->skhd", probs_low, context_heads, preferred_element_type=jnp.float32
    )
    score_low = (probs * (prob_grad - jnp.sum(probs * prob_grad, axis=-1, keepdims=True))).astype(
        jnp.bfloat16
    )
    query_grad = (
        jnp.einsum("shqk,skhd->sqhd", score_low, keysets, preferred_element_type=jnp.float32)
        * scale
    )
    key_grad = (
        jnp.einsum("shqk,sqhd->skhd", score_low, queries, preferred_element_type=jnp.float32)
        * scale
    )
    merged_low = jnp.stack((query_grad, key_grad, value_grad), axis=2).astype(jnp.bfloat16)
    merged_low = merged_low.reshape(rows.shape[0], 3 * width)
    merged_weight_g = contract_rows(rows, merged_low)
    merged_bias_g = jnp.sum(merged_low.astype(jnp.float32), axis=0)
    states_part = first_grad + times_transposed(merged_low, merged)
    vector_grads = jnp.stack(
        (
            merged_bias_g[:width],
            merged_bias_g[2 * width :],
            attn_bias_g,
            first_gain_g,
            first_shift_g,
            outer_bias_g,
            second_gain_g,
            second_shift_g,
        ),
        axis=1,
    )
    return (
        states_part,
        (
            merged_weight_g,
            attn_weight_g,
            inner_weight_g,
            outer_weight_g,
            vector_grads,
            inner_bias_g,
        ),
    )


def pack_vectors(vectors, widened):
    joined = jnp.concatenate(list(vectors) + [widened]).astype(jnp.float32)
    rows = joined.shape[0] // 128
    return jnp.pad(joined.reshape(rows, 128), ((0, 8 - rows), (0, 0)))


def shards(depth, *arrays):
    (states, pad_mask, query_proj, key_proj, value_proj, attn_proj, query_bias, value_bias, attn_bias, first_gain,
     first_shift, inner_proj, inner_bias, outer_proj, outer_bias, second_gain, second_shift, out_grad) = arrays
    width = states.shape[1]
    short = (query_bias, value_bias, attn_bias, first_gain, first_shift, outer_bias, second_gain, second_shift)
    if depth:
        return kernel_shards(depth, short, states, pad_mask, query_proj, key_proj, value_proj, attn_proj, inner_proj,
                             inner_bias, outer_proj, out_grad)
    merged_shard = jnp.concatenate((query_proj, key_proj, value_proj), axis=1)
    fetched = collect(merged_shard, attn_proj, inner_proj, outer_proj, jnp.stack(short, axis=1), inner_bias)
    encoded, kept = forward_pass(states, pad_mask, fetched)
    states_part, totals = backward_pass(states, pad_mask, out_grad, fetched, kept)
    merged_sum, attn_sum, inner_sum, outer_sum, vector_sum, widened_sum = reduce_grads(*totals)
    return ordered(encoded, states_part, merged_sum, attn_sum, inner_sum, outer_sum, vector_sum.T, widened_sum)


def ordered(encoded, states_part, merged_sum, attn_sum, inner_sum, outer_sum, vectors, widened_sum):
    width = attn_sum.shape[1]
    return (encoded, states_part, merged_sum[:, :width], merged_sum[:, width : 2 * width], merged_sum[:, 2 * width :],
            attn_sum, vectors[0], vectors[1], vectors[2], vectors[3], vectors[4], inner_sum, widened_sum, outer_sum,
            vectors[5], vectors[6], vectors[7])


def kernel_shards(depth, short, states, pad_mask, query_proj, key_proj, value_proj, attn_proj, inner_proj, inner_bias,
                  outer_proj, out_grad):
    width = states.shape[1]
    block = short[0].shape[0]
    long_block = inner_bias.shape[0]
    packed = pack_vectors(short, inner_bias)
    (merged, attn, inner, outer, encoded, projected, probs, context, first_sum, first_low, activated, slope, second_grad,
     outer_low, vectors, sums) = forward_all(
        depth, block, states, pad_mask, out_grad,
        (query_proj, key_proj, value_proj, attn_proj, inner_proj, outer_proj, packed))
    states_part, outer_sum, inner_sum, query_sum, key_sum, value_sum, attn_sum, table_sum = backward_all(
        depth, block, vectors, sums,
        (states, activated, slope, outer_low, second_grad, first_sum, first_low, context, projected, probs,
         merged.reshape(width, -1), attn.reshape(width, -1), inner, outer))
    joined = table_sum.reshape(-1)
    vector_sum = joined[: 8 * block].reshape(8, block)
    widened_sum = joined[8 * block : 8 * block + long_block]
    return (encoded, states_part, query_sum, key_sum, value_sum, attn_sum, vector_sum[0], vector_sum[1], vector_sum[2],
            vector_sum[3], vector_sum[4], inner_sum, widened_sum, outer_sum, vector_sum[5], vector_sum[6], vector_sum[7])


def solution(mesh):
    dps, others = mesh.shape["dp"], mesh.shape["fsdp"]
    matrix = P(("dp", "fsdp"), None)
    vector = P(("dp", "fsdp"))

    def whole(*arrays):
        rows = arrays[2].shape[0] // (dps * others)
        depth = others // 2 if rows % 16 == 0 and dps == 4 and others % 2 == 0 else 0
        return jax.shard_map(
            functools.partial(shards, depth),
            mesh=mesh,
            in_specs=(matrix,) * 6 + (vector,) * 5 + (matrix, vector, matrix) + (vector,) * 3 + (matrix,),
            out_specs=(matrix,) * 6 + (vector,) * 5 + (matrix, vector, matrix) + (vector,) * 3,
            check_vma=False,
        )(*arrays)

    return whole
```

```python
import functools

import jax
import jax.numpy as jnp
from jax import lax
from jax.experimental import pallas as pl
from jax.experimental.pallas import tpu as pltpu
from jax.sharding import PartitionSpec as P

HEADS = 16
MESH = pl.DeviceIdType.MESH

epsilon = 1e-05
neg_fill = -1e30


class Place:
    def __init__(self, depth):
        dp = lax.axis_index("dp")
        fsdp = lax.axis_index("fsdp")
        self.depth = depth
        self.dp = dp
        self.z = fsdp // 2
        self.core = lax.rem(fsdp, 2)
        flip_x = dp + 1 - 2 * lax.rem(dp, 2)
        flip_y = lax.rem(dp + 2, 4)
        self.near = flip_x + self.core * (flip_y - flip_x)
        self.far = flip_y + self.core * (flip_x - flip_y)
        self.both = lax.rem(flip_x + 2, 4)
        self.fsdp = fsdp
        self.sibling = fsdp + 1 - 2 * self.core

    def up(self, step):
        return lax.rem(self.z + step, self.depth)

    def down(self, step):
        return lax.rem(self.z + self.depth - step, self.depth)

    def along(self, z):
        return (self.dp, z * 2 + self.core)

    def greet(self):
        barrier = pltpu.get_barrier_semaphore()
        others = [self.along(self.up(step)) for step in range(1, self.depth)]
        others += [(self.near, self.fsdp), (self.far, self.fsdp), (self.dp, self.sibling)]
        for other in others:
            pl.semaphore_signal(barrier, inc=1, device_id=other, device_id_type=MESH)
        pl.semaphore_wait(barrier, len(others))


def remote(source, target, send, recv, device):
    return pltpu.make_async_remote_copy(
        src_ref=source, dst_ref=target, send_sem=send, recv_sem=recv, device_id=device, device_id_type=MESH
    )


class Gather:
    def __init__(self, place, full, own, sems, piece):
        self.place, self.full, self.own, self.piece = place, full, own, piece
        self.su, self.ru, self.sd, self.rd, self.sb, self.rb, self.sa, self.ra, self.sc, self.rc, self.so = sems

    def copy_own(self):
        p = self.place
        return pltpu.make_async_copy(self.own, self.full.at[p.dp, p.z, p.core], self.so.at[self.piece])

    def copy_up(self, z, first=False):
        p = self.place
        block = self.full.at[p.dp, z, p.core]
        source = self.own if first else block
        return remote(source, block, self.su.at[self.piece, z], self.ru.at[self.piece, z], p.along(p.z + 1))

    def copy_down(self, z, first=False):
        p = self.place
        block = self.full.at[p.dp, z, p.core]
        source = self.own if first else block
        return remote(source, block, self.sd.at[self.piece, z], self.rd.at[self.piece, z], p.along(p.z - 1))

    def copy_near(self, z, first=False, arriving=False):
        p = self.place
        block = self.full.at[p.near if arriving else p.dp, z, p.core]
        source = self.own if first else block
        return remote(source, block, self.sb.at[self.piece, z], self.rb.at[self.piece, z], (p.near, p.fsdp))

    def copy_far(self, half, z, first=False, arriving=False):
        p = self.place
        row = (p.both if half else p.far) if arriving else (p.near if half else p.dp)
        block = self.full.at[row, z, p.core]
        source = self.own if first else block
        at = half * p.depth + z
        return remote(source, block, self.sa.at[self.piece, at], self.ra.at[self.piece, at], (p.far, p.fsdp))

    def copy_core(self, part, arriving=False):
        p = self.place
        if arriving:
            row = (p.dp, p.far, p.near, p.both)[part]
            block = self.full.at[row, :, 1 - p.core]
        else:
            row = (p.dp, p.near, p.far, p.both)[part]
            block = self.full.at[row, :, p.core]
        return remote(block, block, self.sc.at[self.piece, part], self.rc.at[self.piece, part], (p.dp, p.sibling))

    def start(self):
        p = self.place
        pl.when(p.z < p.depth - 1)(lambda: self.copy_up(p.z, True).start())
        pl.when(p.z > 0)(lambda: self.copy_down(p.z, True).start())
        self.copy_own().start()

    def send(self, step):
        p = self.place

        def act(z, first=False):
            self.copy_near(z, first).start()
            self.copy_far(0, z, first).start()

        if step == 0:
            act(p.z, True)
        else:
            pl.when(p.z >= step)(lambda: act(p.z - step))
            pl.when(p.z + step < p.depth)(lambda: act(p.z + step))

    def hop(self, step):
        p = self.place

        @pl.when(p.z >= step)
        def _():
            z = p.z - step
            self.copy_up(z).wait_recv()
            pl.when(p.z < p.depth - 1)(lambda: self.copy_up(z).start())

        @pl.when(p.z + step < p.depth)
        def _():
            z = p.z + step
            self.copy_down(z).wait_recv()
            pl.when(p.z > 0)(lambda: self.copy_down(z).start())

    def last_hop(self):
        self.hop(self.place.depth - 1)
        self.copy_own().wait()
        self.copy_core(0).start()

    def spread(self, step):
        p = self.place

        def act(z):
            self.copy_near(z, arriving=True).wait_recv()
            self.copy_far(1, z).start()

        if step == 0:
            act(p.z)
        else:
            pl.when(p.z >= step)(lambda: act(p.z - step))
            pl.when(p.z + step < p.depth)(lambda: act(p.z + step))
        if step == p.depth - 1:
            self.copy_core(1).start()

    def arrive_far(self, half):
        p = self.place
        for z in range(p.depth):
            self.copy_far(half, z, arriving=True).wait_recv()
        self.copy_core(2 + half).start()

    def arrive_core(self, *parts):
        for part in parts:
            self.copy_core(part, arriving=True).wait_recv()

    def drain(self):
        p = self.place
        for z in range(p.depth):
            pl.when((p.z < p.depth - 1) & (z <= p.z))(lambda: self.copy_up(z).wait_send())
            pl.when((p.z > 0) & (z >= p.z))(lambda: self.copy_down(z).wait_send())
            self.copy_near(z).wait_send()
            self.copy_far(0, z).wait_send()
            self.copy_far(1, z).wait_send()
        for part in range(4):
            self.copy_core(part).wait_send()


def gather_sems(pieces, depth):
    dma = pltpu.SemaphoreType.DMA
    counts = (depth, depth, depth, depth, depth, depth, 2 * depth, 2 * depth, 4, 4)
    return [dma((pieces, count)) for count in counts] + [dma((pieces,))]


def matmul(left, right):
    return lax.dot_general(left, right, (((1,), (0,)), ((), ())), preferred_element_type=jnp.float32)


def matmul_nt(left, right):
    return lax.dot_general(left, right, (((1,), (1,)), ((), ())), preferred_element_type=jnp.float32)


def matmul_tn(left, right):
    return lax.dot_general(left, right, (((0,), (0,)), ((), ())), preferred_element_type=jnp.float32)


def flat(value):
    return value.reshape(-1, value.shape[-1])


def span(index, size):
    return pl.ds(pl.multiple_of(index * size, size), size)


def unpack_table(table, block, vectors, long_bias):
    dps, depth, cores = table.shape[:3]
    places = dps * depth * cores
    width = vectors.shape[1]
    lane = lax.broadcasted_iota(jnp.int32, (128, width), 1)
    source = lax.broadcasted_iota(jnp.int32, (128, width), 0)
    pick = jnp.where(source == lax.rem(lane, block), 1.0, 0.0).astype(jnp.bfloat16)
    owner = lax.broadcasted_iota(jnp.int32, (places, width), 1) // block
    mine = owner == lax.broadcasted_iota(jnp.int32, (places, width), 0)
    blocks = [table[:, :, :, vector, :].reshape(places, 128) for vector in range(8)]
    spread = matmul(jnp.concatenate(blocks, axis=0).astype(jnp.bfloat16), pick)
    for vector in range(8):
        own = jnp.where(mine, spread[vector * places : (vector + 1) * places], 0.0)
        vectors[vector : vector + 1, :] = jnp.sum(own, axis=0, keepdims=True)
    for index in range(places):
        dp, z, core = index // (depth * cores), index // cores % depth, index % cores
        long_bias[:, index * 128 : (index + 1) * 128] = table[dp, z, core, 8:9, :]


CHUNK = 256


def project(rows, weights, vectors, projected):
    chunks = rows.shape[1] // CHUNK
    for part, bias in ((0, 0), (1, None), (2, 1)):

        def one(index, _):
            at = span(part * chunks + index, CHUNK)
            total = matmul(rows[...], flat(weights[:, :, :, :, at]))
            if bias is not None:
                total = total + vectors[bias : bias + 1, span(index, CHUNK)]
            projected[:, at] = total.astype(jnp.bfloat16)
            return 0

        lax.fori_loop(0, chunks, one, 0)


def head_lanes(heads, rows, size):
    lane = lax.broadcasted_iota(jnp.int32, (rows, heads * size), 1) // size
    return [lane == head for head in range(heads)]


def stack_heads(value, lanes):
    return jnp.concatenate([jnp.where(lane, value, jnp.zeros_like(value)) for lane in lanes], axis=0)


def merge_heads(value, lanes):
    rows = value.shape[0] // len(lanes)
    result = value[:rows]
    for head in range(1, len(lanes)):
        result = jnp.where(lanes[head], value[head * rows : (head + 1) * rows], result)
    return result


QUAD = 4


def attend(projected, keep, probs, context, first, last):
    width = context.shape[1]
    size = width // HEADS
    length = keep.shape[1]
    scale = size ** (-0.5)
    lanes = head_lanes(QUAD, length, size)
    quads = HEADS // QUAD

    def one(index, _):
        segment = index // quads
        quad = lax.rem(index, quads)
        at = span(segment, length)
        queries = projected[at, span(quad, QUAD * size)]
        keysets = projected[at, span(quad + quads, QUAD * size)]
        valuesets = projected[at, span(quad + 2 * quads, QUAD * size)]
        scores = matmul_nt(stack_heads(queries, lanes), keysets) * scale
        mask = keep[pl.ds(segment, 1), :] > 0
        scores = jnp.where(mask, scores, neg_fill)
        raised = jnp.exp(scores - jnp.max(scores, axis=1, keepdims=True))
        low = (raised / jnp.sum(raised, axis=1, keepdims=True)).astype(jnp.bfloat16)
        probs[index] = low
        context[at, span(quad, QUAD * size)] = merge_heads(matmul(low, valuesets), lanes).astype(jnp.bfloat16)
        return 0

    lax.fori_loop(first, last, one, 0)


def center_scale(hidden):
    center = hidden - jnp.mean(hidden, axis=1, keepdims=True)
    spread = jnp.mean(center * center, axis=1, keepdims=True)
    rate = lax.rsqrt(spread + epsilon)
    return center * rate, rate


def first_block(rows, context, weights, vectors, first_sum, first_norm, first_low):
    def product(index, _):
        at = span(index, CHUNK)
        attended = matmul(context[...], flat(weights[:, :, :, :, at])) + vectors[2:3, at]
        first_sum[:, at] = rows[:, at].astype(jnp.float32) + attended
        return 0

    lax.fori_loop(0, rows.shape[1] // CHUNK, product, 0)

    def one(index, _):
        at = span(index, 64)
        normed, _ = center_scale(first_sum[at, :])
        result = normed * vectors[3:4, :] + vectors[4:5, :]
        first_norm[at, :] = result
        first_low[at, :] = result.astype(jnp.bfloat16)
        return 0

    lax.fori_loop(0, rows.shape[0] // 64, one, 0)


def inner_block(first_low, weights, long_bias, activated, slope, first, last):
    def one(index, _):
        at = span(index, CHUNK)
        value = matmul(first_low[...], flat(weights[:, :, :, :, at])) + long_bias[:, at]
        share = 0.5 * (1.0 + lax.erf(value * (0.5**0.5)))
        bell = jnp.exp(-0.5 * value * value) * ((0.5 / jnp.pi) ** 0.5)
        activated[:, at] = (value * share).astype(jnp.bfloat16)
        slope[:, at] = (share + value * bell).astype(jnp.bfloat16)
        return 0

    lax.fori_loop(first, last, one, 0)


def outer_part(activated, weights, row, total, fresh):
    size = weights.shape[1] * weights.shape[2] * weights.shape[3]

    def one(index, _):
        at = span(index, CHUNK)
        value = matmul(activated[:, span(row, size)], flat(weights[row, :, :, :, at]))
        total[:, at] = value if fresh else total[:, at] + value
        return 0

    lax.fori_loop(0, total.shape[1] // CHUNK, one, 0)


def norm_back(grad, normed, rate, gain):
    scaled = grad * gain
    mean = jnp.mean(scaled, axis=1, keepdims=True)
    along = jnp.mean(scaled * normed, axis=1, keepdims=True)
    return rate * (scaled - mean - normed * along)


def second_block(first_norm, total, cotangent, vectors, encoded, second_grad, outer_low, sums):
    sums[...] = jnp.zeros_like(sums)

    def one(index, _):
        at = span(index, 64)
        normed, rate = center_scale(first_norm[at, :] + (total[at, :] + vectors[5:6, :]))
        gain = vectors[6:7, :]
        encoded[at, :] = (normed * gain + vectors[7:8, :]).astype(jnp.bfloat16)
        grad = cotangent[at, :].astype(jnp.float32)
        back = norm_back(grad, normed, rate, gain)
        low = back.astype(jnp.bfloat16)
        second_grad[at, :] = back
        outer_low[at, :] = low
        sums[5:6, :] += jnp.sum(low.astype(jnp.float32), axis=0, keepdims=True)
        sums[6:7, :] += jnp.sum(grad * normed, axis=0, keepdims=True)
        sums[7:8, :] += jnp.sum(grad, axis=0, keepdims=True)
        return 0

    lax.fori_loop(0, first_norm.shape[0] // 64, one, 0)


def forward_kernel(depth, block, *refs):
    (rows, keep, cotangent, query_own, key_own, value_own, attn_own, inner_own, outer_own, table_own) = refs[:10]
    merged_out, attn_out, inner_out, outer_out = refs[10:14]
    (encoded_out, projected_out, probs_out, context_out, first_sum_out, first_low_out, activated_out, slope_out,
     second_grad_out, outer_low_out, vectors, sums) = refs[14:26]
    (merged_own, table, merged, attn, inner, outer, projected, probs, context, first_sum, first_norm, first_low, activated,
     slope, total, encoded, second_grad, outer_low, long_bias, save_sem) = refs[26:46]
    sems = refs[46:]
    place = Place(depth)
    width = rows.shape[1]
    for part, own in enumerate((query_own, key_own, value_own)):
        merged_own[:, part * width : (part + 1) * width] = own[...]
    net_table = Gather(place, table, table_own, sems, 0)
    net_merged = Gather(place, merged, merged_own, sems, 1)
    net_attn = Gather(place, attn, attn_own, sems, 2)
    net_inner = Gather(place, inner, inner_own, sems, 3)
    net_outer = Gather(place, outer, outer_own, sems, 4)
    nets = (net_table, net_merged, net_attn, net_inner, net_outer)
    front = nets[:3]
    place.greet()
    saves = []

    def save(source, target):
        copy = pltpu.make_async_copy(source, target, save_sem.at[len(saves)])
        copy.start()
        saves.append(copy)

    def hop(net, step):
        if step == depth - 1:
            net.last_hop()
        else:
            net.hop(step)

    def each(nets_of, *names, step):
        for name in names:
            for net in nets_of:
                hop(net, step) if name == "hop" else getattr(net, name)(step)

    for net in front:
        net.start()
    each(front, "send", step=0)
    each(front, "hop", "send", step=1)
    net_inner.start()
    each(front, "spread", step=0)
    for step in range(2, depth):
        each(front, "hop", "send", step=step)
        each(front, "spread", step=step - 1)
    net_inner.send(0)
    net_outer.start()
    net_inner.hop(1)
    net_inner.send(1)
    each(front, "spread", step=depth - 1)
    net_inner.spread(0)
    net_outer.hop(1)
    for step in range(2, depth - 1):
        net_inner.hop(step)
        net_inner.send(step)
        net_inner.spread(step - 1)
    for net in front:
        net.arrive_far(0)
        net.arrive_far(1)
        net.arrive_core(0, 1, 2, 3)
    save(merged, merged_out)
    save(attn, attn_out)
    unpack_table(table, block, vectors, long_bias)
    project(rows, merged, vectors, projected)
    save(projected, projected_out)
    for step in range(2, depth - 1):
        net_outer.hop(step)
    net_inner.last_hop()
    net_inner.send(depth - 1)
    net_inner.spread(depth - 2)
    count = probs.shape[0]
    attend(projected, keep, probs, context, 0, count // 2)
    net_outer.last_hop()
    net_inner.spread(depth - 1)
    attend(projected, keep, probs, context, count // 2, count)
    save(probs, probs_out)
    save(context, context_out)
    first_block(rows, context, attn, vectors, first_sum, first_norm, first_low)
    save(first_sum, first_sum_out)
    save(first_low, first_low_out)
    net_inner.arrive_far(0)
    for step in range(depth):
        net_outer.send(step)
    net_inner.arrive_far(1)
    net_inner.arrive_core(0, 1, 2, 3)
    save(inner, inner_out)
    chunks = inner.shape[4] // CHUNK
    inner_block(first_low, inner, long_bias, activated, slope, 0, chunks // 2)
    for step in range(depth // 2):
        net_outer.spread(step)
    inner_block(first_low, inner, long_bias, activated, slope, chunks // 2, chunks)
    for step in range(depth // 2, depth):
        net_outer.spread(step)
    save(activated, activated_out)
    save(slope, slope_out)
    net_outer.arrive_core(0)
    outer_part(activated, outer, place.dp, total, True)
    net_outer.arrive_far(0)
    net_outer.arrive_core(1, 2)
    outer_part(activated, outer, place.near, total, False)
    outer_part(activated, outer, place.far, total, False)
    net_outer.arrive_far(1)
    net_outer.arrive_core(3)
    save(outer, outer_out)
    outer_part(activated, outer, place.both, total, False)
    second_block(first_norm, total, cotangent, vectors, encoded, second_grad, outer_low, sums)
    save(encoded, encoded_out)
    save(second_grad, second_grad_out)
    save(outer_low, outer_low_out)
    for net in nets:
        net.drain()
    for copy in saves:
        copy.wait()


def forward_all(depth, block, rows, keep, cotangent, owns):
    query_own, _, _, attn_own, inner_own, outer_own, table_own = owns
    tokens, width = rows.shape
    hidden = inner_own.shape[1]
    segments, length = keep.shape
    low, high = jnp.bfloat16, jnp.float32

    def fulls(own, columns):
        return (4, depth, 2, own.shape[0], columns)

    full_shapes = [fulls(query_own, 3 * width), fulls(attn_own, width), fulls(inner_own, hidden), fulls(outer_own, width)]
    kept = [
        ((tokens, width), low),
        ((tokens, 3 * width), low),
        ((segments * HEADS // QUAD, QUAD * length, length), low),
        ((tokens, width), low),
        ((tokens, width), high),
        ((tokens, width), low),
        ((tokens, hidden), low),
        ((tokens, hidden), low),
        ((tokens, width), high),
        ((tokens, width), low),
    ]
    small = [((8, width), high), ((8, width), high)]
    shapes = [jax.ShapeDtypeStruct(shape, low) for shape in full_shapes]
    shapes += [jax.ShapeDtypeStruct(*one) for one in kept + small]
    held = {name: pltpu.VMEM(*one) for name, one in zip(
        ("encoded", "projected", "probs", "context", "first_sum", "first_low", "activated", "slope", "second_grad", "outer_low"),
        kept)}
    scratch = [pltpu.VMEM((query_own.shape[0], 3 * width), low), pltpu.VMEM(fulls(table_own, 128), high)]
    scratch += [pltpu.VMEM(shape, low) for shape in full_shapes]
    scratch += [held[name] for name in ("projected", "probs", "context", "first_sum")]
    scratch += [pltpu.VMEM((tokens, width), high)]
    scratch += [held[name] for name in ("first_low", "activated", "slope")]
    scratch += [pltpu.VMEM((tokens, width), high)]
    scratch += [held[name] for name in ("encoded", "second_grad", "outer_low")]
    scratch += [pltpu.VMEM((1, hidden), high)]
    scratch += [pltpu.SemaphoreType.DMA((len(full_shapes) + len(kept),))]
    here = pl.BlockSpec(memory_space=pltpu.VMEM)
    away = pl.BlockSpec(memory_space=pl.ANY)
    return pl.pallas_call(
        functools.partial(forward_kernel, depth, block),
        out_shape=shapes,
        in_specs=[here] * 10,
        out_specs=[away] * (len(full_shapes) + len(kept)) + [here] * 2,
        scratch_shapes=scratch + gather_sems(5, depth),
        compiler_params=pltpu.CompilerParams(
            collective_id=0, has_side_effects=True, vmem_limit_bytes=60 * 1024 * 1024
        ),
        name="forward",
    )(rows, keep, cotangent, *owns)


SUBS = 4


class Slots:
    def __init__(self, core, far, near, along):
        self.core, self.far, self.near, self.along = core, far, near, along


class Scatter:
    def __init__(self, place, whole, slots, sems, credits, number, lot, first, count, after=False, before=False,
                 late_after=False, late_before=False):
        self.place, self.whole, self.slots = place, whole, slots
        self.sc, self.rc, self.sa, self.ra, self.sb, self.rb, self.sz, self.rz = sems
        self.core_free, self.far_free, self.near_free, self.z_free = credits
        self.number, self.lot, self.first, self.count = number, lot, first, count
        self.sub = first // count
        self.after, self.before, self.late_after, self.late_before = after, before, late_after, late_before
        self.tile = 8 if whole.dtype == jnp.float32 else 16

    def lines(self):
        return pl.ds(self.first, self.count)

    def mine(self, row):
        return self.whole.at[row, :, self.place.core, self.lines()]

    def sent_row(self, at):
        p = self.place
        return (p.both, p.near, p.far, p.dp)[at]

    def got_row(self, at):
        p = self.place
        return (p.both, p.far, p.near, p.dp)[at]

    def copy_core(self, at):
        p = self.place
        return remote(
            self.whole.at[self.sent_row(at), :, 1 - p.core, self.lines()], self.slots.core.at[at, :, self.lines()],
            self.sc.at[self.number, at], self.rc.at[self.number, at], (p.dp, p.sibling),
        )

    def copy_far(self, half):
        p = self.place
        return remote(
            self.mine(p.both if half else p.far), self.slots.far.at[self.lot, half, :, self.lines()],
            self.sa.at[self.number, half], self.ra.at[self.number, half], (p.far, p.fsdp),
        )

    def copy_near(self):
        p = self.place
        return remote(
            self.mine(p.near), self.slots.near.at[self.lot, :, self.lines()], self.sb.at[self.number],
            self.rb.at[self.number], (p.near, p.fsdp),
        )

    def copy_z(self, step):
        p = self.place
        return remote(
            self.whole.at[p.dp, p.up(step), p.core, self.lines()], self.slots.along.at[self.lot, step - 1, self.lines()],
            self.sz.at[self.number, step - 1], self.rz.at[self.number, step - 1], p.along(p.up(step)),
        )

    def add(self, row, slot):
        p = self.place
        tiles = self.count // self.tile

        def one(index, _):
            z = index // tiles
            at = pl.ds(pl.multiple_of(self.first + lax.rem(index, tiles) * self.tile, self.tile), self.tile)
            self.whole[row, z, p.core, at, :] = self.whole[row, z, p.core, at, :] + slot[z, at, :]
            return 0

        lax.fori_loop(0, p.depth * tiles, one, 0)

    def start_core(self, at):
        if self.after:
            pl.semaphore_wait(self.core_free.at[at, self.sub], 1)
        self.copy_core(at).start()

    def add_core(self, at):
        p = self.place
        self.copy_core(at).wait_recv()
        self.add(self.got_row(at), self.slots.core.at[at])
        if self.before:
            pl.semaphore_signal(self.core_free.at[at, self.sub], inc=1, device_id=(p.dp, p.sibling), device_id_type=MESH)

    def start_far(self, half):
        if self.late_after:
            pl.semaphore_wait(self.far_free.at[half, self.sub], 1)
        self.copy_far(half).start()

    def add_far(self, half):
        p = self.place
        self.copy_far(half).wait_recv()
        self.add(p.near if half else p.dp, self.slots.far.at[self.lot, half])
        if self.late_before:
            pl.semaphore_signal(self.far_free.at[half, self.sub], inc=1, device_id=(p.far, p.fsdp), device_id_type=MESH)
        if half:
            if self.late_after:
                pl.semaphore_wait(self.near_free.at[self.sub], 1)
            self.copy_near().start()

    def add_near(self):
        p = self.place
        self.copy_near().wait_recv()
        self.add(p.dp, self.slots.near.at[self.lot])
        if self.late_before:
            pl.semaphore_signal(self.near_free.at[self.sub], inc=1, device_id=(p.near, p.fsdp), device_id_type=MESH)
        for step in range(1, p.depth):
            if self.late_after:
                pl.semaphore_wait(self.z_free.at[self.sub, step - 1], 1)
            self.copy_z(step).start()

    def finish(self, out):
        p = self.place
        for step in range(1, p.depth):
            self.copy_z(step).wait_recv()

        def one(index, _):
            start = pl.multiple_of(index * self.tile, self.tile)
            at = pl.ds(pl.multiple_of(self.first + start, self.tile), self.tile)
            total = self.whole[p.dp, p.z, p.core, at, :].astype(jnp.float32)
            for step in range(p.depth - 1):
                total = total + self.slots.along[self.lot, step, at, :].astype(jnp.float32)
            out[pl.ds(start, self.tile), :] = total
            return 0

        lax.fori_loop(0, self.count // self.tile, one, 0)
        if self.late_before:
            for step in range(1, p.depth):
                pl.semaphore_signal(
                    self.z_free.at[self.sub, step - 1], inc=1, device_id=p.along(p.down(step)), device_id_type=MESH
                )

    def drain(self):
        for at in range(4):
            self.copy_core(at).wait_send()
        self.copy_far(1).wait_send()
        self.copy_far(0).wait_send()
        self.copy_near().wait_send()
        for step in range(1, self.place.depth):
            self.copy_z(step).wait_send()


def outer_gradient(acts, low, grads, row):
    depth, cores, count, _ = grads.shape[1:]
    size = cores * count

    def one(z, _):
        value = matmul_tn(acts[row, :, span(z, size)], low[...])
        grads[row, z] = value.astype(jnp.bfloat16).reshape(grads.shape[2:])
        return 0

    lax.fori_loop(0, depth, one, 0)


def input_gradient(inputs, low, grads, row, part):
    depth, cores, count, width = grads.shape[1:]
    size = inputs.shape[1] // grads.shape[0]
    lines = count // SUBS
    value = matmul_tn(inputs[:, span(row, size)], low)
    grads[row, :, :, part * lines : (part + 1) * lines, :] = value.astype(jnp.bfloat16).reshape(depth, cores, lines, width)


def hidden_back(low, weights, slopes, bias_sum, part):
    depth, cores, count, width = weights.shape[1:]
    size = cores * count

    def one(index, _):
        at = span(index, size)
        value = matmul_nt(low[...], flat(weights[part, index])) * slopes[SUBS + part, :, at].astype(jnp.float32)
        rounded = value.astype(jnp.bfloat16)
        slopes[SUBS + part, :, at] = rounded
        total = jnp.sum(rounded.astype(jnp.float32), axis=0, keepdims=True)
        bias_sum[:, pl.ds(pl.multiple_of(part * width + index * size, size), size)] = total
        return 0

    lax.fori_loop(0, depth, one, 0)


def first_total_rows(grad, inner_low, weights):
    lines = weights.shape[3] // SUBS
    size = grad.shape[1] // weights.shape[0]

    def one(index, _):
        at = span(index, size)
        total = grad[:, at]
        for part in range(SUBS):
            weight = flat(weights[index, :, :, part * lines : (part + 1) * lines, :])
            total = total + matmul_nt(inner_low[SUBS + part], weight)
        grad[:, at] = total
        return 0

    lax.fori_loop(0, weights.shape[0], one, 0)


def first_back(first_sum, grad, low, vectors, sums):
    for row in (2, 3, 4):
        sums[row : row + 1, :] = jnp.zeros((1, grad.shape[1]), jnp.float32)

    def one(index, _):
        at = span(index, 64)
        normed, rate = center_scale(first_sum[at, :])
        upper = grad[at, :]
        back = norm_back(upper, normed, rate, vectors[3:4, :])
        rounded = back.astype(jnp.bfloat16)
        grad[at, :] = back
        low[at, :] = rounded
        sums[2:3, :] += jnp.sum(rounded.astype(jnp.float32), axis=0, keepdims=True)
        sums[3:4, :] += jnp.sum(upper * normed, axis=0, keepdims=True)
        sums[4:5, :] += jnp.sum(upper, axis=0, keepdims=True)
        return 0

    lax.fori_loop(0, grad.shape[0] // 64, one, 0)


def context_back(low, weights, context):
    halves = weights.shape[1] // CHUNK

    def one(index, _):
        weight = weights[index // halves, span(lax.rem(index, halves), CHUNK), :]
        context[:, span(index, CHUNK)] = matmul_nt(low[...], weight).astype(jnp.bfloat16)
        return 0

    lax.fori_loop(0, context.shape[1] // CHUNK, one, 0)


def attend_back(projected, probs, context_low, sums, first, last):
    width = context_low.shape[1]
    size = width // HEADS
    length = probs.shape[2]
    scale = size ** (-0.5)
    lanes = head_lanes(QUAD, length, size)
    quads = HEADS // QUAD

    def one(index, _):
        segment = index // quads
        quad = lax.rem(index, quads)
        at = span(segment, length)
        columns = [span(quad + part * quads, QUAD * size) for part in range(3)]
        queries, keysets, valuesets = [projected[at, column] for column in columns]
        low = probs[index]
        wide = low.astype(jnp.float32)
        upper = stack_heads(context_low[at, columns[0]], lanes)
        prob_grad = matmul_nt(upper, valuesets)
        score_low = (wide * (prob_grad - jnp.sum(wide * prob_grad, axis=1, keepdims=True))).astype(jnp.bfloat16)
        value_low = matmul_tn(low, upper).astype(jnp.bfloat16)
        query_low = (merge_heads(matmul(score_low, keysets), lanes) * scale).astype(jnp.bfloat16)
        key_low = (matmul_tn(score_low, stack_heads(queries, lanes)) * scale).astype(jnp.bfloat16)
        projected[at, columns[0]] = query_low
        projected[at, columns[1]] = key_low
        projected[at, columns[2]] = value_low
        sums[0:1, columns[0]] += jnp.sum(query_low.astype(jnp.float32), axis=0, keepdims=True)
        sums[1:2, columns[0]] += jnp.sum(value_low.astype(jnp.float32), axis=0, keepdims=True)
        return 0

    lax.fori_loop(first, last, one, 0)


def states_back(grad, projected, weights):
    width = grad.shape[1]
    halves = weights.shape[1] // CHUNK

    def one(index, _):
        at = span(index, CHUNK)
        total = grad[:, at]
        for part in range(3):
            weight = weights[2 + 2 * part + index // halves, span(lax.rem(index, halves), CHUNK), :]
            total = total + matmul_nt(projected[:, part * width : (part + 1) * width], weight)
        grad[:, at] = total
        return 0

    lax.fori_loop(0, width // CHUNK, one, 0)


def pack_sums(sums, bias_sum, block, table):
    dps, depth, cores = table.shape[:3]
    places = dps * depth * cores
    width = sums.shape[1]
    lane = lax.broadcasted_iota(jnp.int32, (width, 128), 1)
    source = lax.broadcasted_iota(jnp.int32, (width, 128), 0)
    pick = jnp.where(lane == lax.rem(source, block), 1.0, 0.0).astype(jnp.bfloat16)
    owner = lax.broadcasted_iota(jnp.int32, (places, width), 1) // block
    mine = owner == lax.broadcasted_iota(jnp.int32, (places, width), 0)
    values = jnp.concatenate([jnp.where(mine, sums[vector : vector + 1, :], 0.0) for vector in range(8)], axis=0)
    upper = values.astype(jnp.bfloat16)
    lower = (values - upper.astype(jnp.float32)).astype(jnp.bfloat16)
    total = matmul(upper, pick) + matmul(lower, pick)
    table[...] = jnp.zeros_like(table)
    for vector in range(8):
        table[:, :, :, vector, :] = total[vector * places : (vector + 1) * places].reshape(dps, depth, cores, 128)
    for index in range(places):
        dp, z, core = index // (depth * cores), index // cores % depth, index % cores
        table[dp, z, core, 8:9, :] = bias_sum[:, index * 128 : (index + 1) * 128]


def backward_kernel(depth, block, *refs):
    (vectors, known, rows_in, activated_in, slope_in, outer_low_in, second_grad_in, first_sum_in, first_low_in, context_in,
     projected_in, probs_in, merged_in, attn_in, inner_in, outer_in) = refs[:16]
    states_out, outer_out, inner_out, query_out, key_out, value_out, attn_out, table_out = refs[16:24]
    (first_buffer, second_buffer, outer_grads, wide, from_core, from_far, from_near, from_z, low, first_low, grad, first_sum,
     context, projected, probs, rows, sums, bias_sum, table, table_core, table_far, table_near, table_z) = refs[24:47]
    load_sem, save_sem = refs[47:49]
    sems = refs[49:57]
    credits = refs[57:61]
    place = Place(depth)
    width = rows.shape[1]
    tokens = rows.shape[0]
    lines = outer_grads.shape[3] // SUBS
    loads = []

    def load(source, target):
        copy = pltpu.make_async_copy(source, target, load_sem.at[len(loads)])
        copy.start()
        loads.append(copy)
        return copy

    def load_columns(source, targets):
        return [load(source.at[:, part * width : (part + 1) * width], target) for part, target in enumerate(targets)]

    low_load = load(outer_low_in, low)
    act_loads = load_columns(activated_in, [wide.at[part] for part in range(SUBS)])
    outer_load = load(outer_in, first_buffer)
    slope_loads = load_columns(slope_in, [wide.at[SUBS + part] for part in range(SUBS)])
    first_low_load = load(first_low_in, first_low)
    grad_load = load(second_grad_in, grad)
    inner_loads = [
        load(inner_in.at[:, :, :, :, part * width : (part + 1) * width],
             second_buffer.at[:, :, :, part * lines : (part + 1) * lines, :])
        for part in range(SUBS)
    ]
    first_sum_load = load(first_sum_in, first_sum)
    context_load = load(context_in, context)
    projected_load = load(projected_in, projected)
    probs_load = load(probs_in, probs)
    rows_load = load(rows_in, rows)

    slots = Slots(from_core, from_far, from_near, from_z)
    table_slots = Slots(table_core, table_far, table_near, table_z)
    outers = [
        Scatter(place, outer_grads, slots, sems, credits, sub, 0, sub * lines, lines, before=True, late_before=True)
        for sub in range(SUBS)
    ]
    inner_grads = first_buffer
    inners = [
        Scatter(place, inner_grads, slots, sems, credits, SUBS + sub, 1, sub * lines, lines, after=True, before=True)
        for sub in range(SUBS)
    ]
    other_grads = second_buffer
    others = [
        Scatter(place, other_grads, slots, sems, credits, 2 * SUBS + sub, 0, sub * lines, lines, after=True, late_after=True)
        for sub in range(SUBS)
    ]
    attn_net = others[3]
    mergeds = others[:3]
    small = Scatter(place, table, table_slots, sems, credits, 3 * SUBS, 0, 0, 16)
    row_order = (place.both, place.near, place.far, place.dp)
    sums[...] = known[...]
    sums[0:2, :] = jnp.zeros((2, width), jnp.float32)
    place.greet()

    def pieces(nets, compute, early=()):
        def added(at):
            for net in nets:
                net.add_core(at)
            if at < 2:
                for net in early:
                    net.start_far(1 - at)

        for at in range(4):
            compute(row_order[at])
            for net in nets:
                net.start_core(at)
            if at:
                added(at - 1)
        added(3)

    order = outers + inners + [attn_net] + mergeds + [small]
    outs = [outer_out.at[pl.ds(sub * lines, lines), :] for sub in range(SUBS)]
    outs += [inner_out.at[:, pl.ds(sub * width, width)] for sub in range(SUBS)]
    outs += [attn_out, query_out, key_out, value_out, table_out]
    window = 3

    def pump(number):
        if number < len(order):
            order[number].add_far(1)
            order[number].add_far(0)
        if number + window < len(order):
            order[number + window].start_far(1)
            order[number + window].start_far(0)
        if 1 <= number <= len(order):
            order[number - 1].add_near()
        if 3 <= number:
            order[number - 3].finish(outs[number - 3])

    low_load.wait()
    for copy in act_loads:
        copy.wait()
    pieces(outers, lambda row: outer_gradient(wide, low, outer_grads, row), outers[:window])
    attn_loads = [load(attn_in.at[part * tokens : (part + 1) * tokens], wide.at[part]) for part in range(2)]

    def load_merged(part):
        return [
            load(merged_in.at[at * tokens : (at + 1) * tokens, part * width : (part + 1) * width], wide.at[2 + 2 * part + at])
            for at in range(2)
        ]

    merged_loads = load_merged(0)
    outer_load.wait()
    for copy in slope_loads:
        copy.wait()
    for part in range(SUBS):
        hidden_back(low, first_buffer, wide, bias_sum, part)
    first_low_load.wait()

    def inner_rows(row):
        for part in range(SUBS):
            input_gradient(first_low, wide[SUBS + part], inner_grads, row, part)

    pump(0)
    pieces(inners, inner_rows)
    pump(1)
    grad_load.wait()
    for copy in inner_loads:
        copy.wait()
    first_total_rows(grad, wide, second_buffer)
    merged_loads += load_merged(1) + load_merged(2)
    first_sum_load.wait()
    first_back(first_sum, grad, low, vectors, sums)
    pump(2)
    context_load.wait()
    pieces([attn_net], lambda row: input_gradient(context, low[...], other_grads, row, 3))
    for copy in attn_loads:
        copy.wait()
    context_back(low, wide, context)
    projected_load.wait()
    probs_load.wait()
    pump(3)
    count = probs.shape[0]
    attend_back(projected, probs, context, sums, 0, count // 2)
    pump(4)
    attend_back(projected, probs, context, sums, count // 2, count)
    rows_load.wait()

    def merged_rows(row):
        for part in range(3):
            input_gradient(rows, projected[:, part * width : (part + 1) * width], other_grads, row, part)

    pieces(mergeds, merged_rows)
    pump(5)
    pack_sums(sums, bias_sum, block, table)
    pieces([small], lambda row: None)
    pump(6)
    for copy in merged_loads:
        copy.wait()
    states_back(grad, projected, wide)
    save = pltpu.make_async_copy(grad, states_out, save_sem)
    save.start()
    for number in range(7, len(order) + 3):
        pump(number)
    for net in order:
        net.drain()
    save.wait()


def backward_all(depth, block, vectors, known, kept):
    low, high = jnp.bfloat16, jnp.float32
    (rows, activated, _, _, _, first_sum, _, _, projected, probs, _, _, inner, outer) = kept
    tokens, width = rows.shape
    hidden = activated.shape[1]
    unit = outer.shape
    lines = unit[3]
    own_rows = lines // SUBS
    dma, regular = pltpu.SemaphoreType.DMA, pltpu.SemaphoreType.REGULAR
    nets = 3 * SUBS + 1
    scratch = [
        pltpu.VMEM(unit, low),
        pltpu.VMEM(unit, low),
        pltpu.VMEM(unit, low),
        pltpu.VMEM((2 * SUBS, tokens, width), low),
        pltpu.VMEM((4, depth, lines, width), low),
        pltpu.VMEM((2, 2, depth, lines, width), low),
        pltpu.VMEM((2, depth, lines, width), low),
        pltpu.VMEM((2, depth - 1, lines, width), low),
        pltpu.VMEM((tokens, width), low),
        pltpu.VMEM((tokens, width), low),
        pltpu.VMEM((tokens, width), high),
        pltpu.VMEM((tokens, width), high),
        pltpu.VMEM((tokens, width), low),
        pltpu.VMEM(projected.shape, low),
        pltpu.VMEM(probs.shape, low),
        pltpu.VMEM((tokens, width), low),
        pltpu.VMEM((8, width), high),
        pltpu.VMEM((1, hidden), high),
        pltpu.VMEM((4, depth, 2, 16, 128), high),
        pltpu.VMEM((4, depth, 16, 128), high),
        pltpu.VMEM((1, 2, depth, 16, 128), high),
        pltpu.VMEM((1, depth, 16, 128), high),
        pltpu.VMEM((1, depth - 1, 16, 128), high),
        dma((40,)),
        dma,
        dma((nets, 4)), dma((nets, 4)), dma((nets, 2)), dma((nets, 2)), dma((nets,)), dma((nets,)),
        dma((nets, depth - 1)), dma((nets, depth - 1)),
        regular((4, SUBS)), regular((2, SUBS)), regular((SUBS,)), regular((SUBS, depth - 1)),
    ]
    shapes = [(tokens, width), (lines, width), (own_rows, hidden)] + [(own_rows, width)] * 4 + [(16, 128)]
    here = pl.BlockSpec(memory_space=pltpu.VMEM)
    away = pl.BlockSpec(memory_space=pl.ANY)
    return pl.pallas_call(
        functools.partial(backward_kernel, depth, block),
        out_shape=[jax.ShapeDtypeStruct(shape, high) for shape in shapes],
        in_specs=[here] * 2 + [away] * len(kept),
        out_specs=[away] + [here] * 7,
        scratch_shapes=scratch,
        compiler_params=pltpu.CompilerParams(
            collective_id=1, has_side_effects=True, vmem_limit_bytes=62 * 1024 * 1024
        ),
        name="backward",
    )(vectors, known, *kept)


def normalize(hidden, gain, shift):
    center = hidden - jnp.mean(hidden, axis=-1, keepdims=True)
    spread = jnp.mean(center * center, axis=-1, keepdims=True)
    return center * lax.rsqrt(spread + epsilon) * gain + shift


def exact_gelu(value):
    return jax.nn.gelu(value, approximate=False)


def contract_rows(left, right):
    return lax.dot_general(
        left, right, (((0,), (0,)), ((), ())), preferred_element_type=jnp.float32
    )


def times_transposed(left, right):
    return lax.dot_general(
        left, right, (((1,), (1,)), ((), ())), preferred_element_type=jnp.float32
    )


def collect(merged, attn, inner, outer, vectors, widened):
    return (
        lax.all_gather(merged, ("dp", "fsdp"), axis=0, tiled=True),
        lax.all_gather(attn, ("dp", "fsdp"), axis=0, tiled=True),
        lax.all_gather(inner, ("dp", "fsdp"), axis=0, tiled=True),
        lax.all_gather(outer, ("dp", "fsdp"), axis=0, tiled=True),
        lax.all_gather(vectors, ("dp", "fsdp"), axis=0, tiled=True),
        lax.all_gather(widened, ("dp", "fsdp"), axis=0, tiled=True),
    )


def reduce_grads(merged, attn, inner, outer, vectors, widened):
    return (
        lax.psum_scatter(merged, ("dp", "fsdp"), scatter_dimension=0, tiled=True),
        lax.psum_scatter(attn, ("dp", "fsdp"), scatter_dimension=0, tiled=True),
        lax.psum_scatter(inner, ("dp", "fsdp"), scatter_dimension=0, tiled=True),
        lax.psum_scatter(outer, ("dp", "fsdp"), scatter_dimension=0, tiled=True),
        lax.psum_scatter(vectors, ("dp", "fsdp"), scatter_dimension=0, tiled=True),
        lax.psum_scatter(widened, ("dp", "fsdp"), scatter_dimension=0, tiled=True),
    )


def split_heads(projected, segments):
    total_rows, triple = projected.shape
    width = triple // 3
    return projected.reshape(segments, total_rows // segments, 3, HEADS, width // HEADS)


def attention_probs(queries, keysets, keep, scale):
    scores = (
        jnp.einsum("sqhd,skhd->shqk", queries, keysets, preferred_element_type=jnp.float32) * scale
    )
    scores = jnp.where(keep[:, None, None, :] > 0, scores, neg_fill)
    peaks = jnp.max(scores, axis=-1, keepdims=True)
    raised = jnp.exp(scores - peaks)
    return raised / jnp.sum(raised, axis=-1, keepdims=True)


def forward_pass(rows, keep, weights):
    merged, attn, inner, outer, vectors, widened = weights
    vector_full = vectors.astype(jnp.float32)
    width = rows.shape[1]
    scale = (width // HEADS) ** (-0.5)
    merged_bias = jnp.concatenate(
        (vector_full[:, 0], jnp.zeros((width,), jnp.float32), vector_full[:, 1])
    )
    projected = (jnp.dot(rows, merged, preferred_element_type=jnp.float32) + merged_bias).astype(
        jnp.bfloat16
    )
    split = split_heads(projected, keep.shape[0])
    probs = attention_probs(split[:, :, 0], split[:, :, 1], keep, scale).astype(jnp.bfloat16)
    context = jnp.einsum(
        "shqk,skhd->sqhd", probs, split[:, :, 2], preferred_element_type=jnp.float32
    )
    context = context.reshape(rows.shape[0], width).astype(jnp.bfloat16)
    attended = jnp.dot(context, attn, preferred_element_type=jnp.float32) + vector_full[:, 2]
    first_sum = rows.astype(jnp.float32) + attended
    first_norm = normalize(first_sum, vector_full[:, 3], vector_full[:, 4])
    first_low = first_norm.astype(jnp.bfloat16)
    inner_act = jnp.dot(first_low, inner, preferred_element_type=jnp.float32) + widened.astype(
        jnp.float32
    )
    activated = exact_gelu(inner_act).astype(jnp.bfloat16)
    outer_act = jnp.dot(activated, outer, preferred_element_type=jnp.float32) + vector_full[:, 5]
    second_sum = first_norm + outer_act
    encoded = normalize(second_sum, vector_full[:, 6], vector_full[:, 7]).astype(jnp.bfloat16)
    return (encoded, (projected, context, first_sum, first_low, inner_act, activated, second_sum))


def backward_pass(rows, keep, cotangent, weights, kept):
    merged, attn, inner, outer, vectors, widened = weights
    projected, context, first_sum, first_low, inner_act, activated, second_sum = kept
    vector_full = vectors.astype(jnp.float32)
    width = rows.shape[1]
    scale = (width // HEADS) ** (-0.5)
    second_out, second_pull = jax.vjp(normalize, second_sum, vector_full[:, 6], vector_full[:, 7])
    second_grad, second_gain_g, second_shift_g = second_pull(cotangent.astype(jnp.float32))
    outer_low = second_grad.astype(jnp.bfloat16)
    outer_bias_g = jnp.sum(outer_low.astype(jnp.float32), axis=0)
    outer_weight_g = contract_rows(activated, outer_low)
    act_grad = times_transposed(outer_low, outer)
    gelu_out, gelu_pull = jax.vjp(exact_gelu, inner_act)
    inner_low = gelu_pull(act_grad)[0].astype(jnp.bfloat16)
    inner_bias_g = jnp.sum(inner_low.astype(jnp.float32), axis=0)
    inner_weight_g = contract_rows(first_low, inner_low)
    first_total = second_grad + times_transposed(inner_low, inner)
    first_out, first_pull = jax.vjp(normalize, first_sum, vector_full[:, 3], vector_full[:, 4])
    first_grad, first_gain_g, first_shift_g = first_pull(first_total)
    attended_low = first_grad.astype(jnp.bfloat16)
    attn_bias_g = jnp.sum(attended_low.astype(jnp.float32), axis=0)
    attn_weight_g = contract_rows(context, attended_low)
    context_low = times_transposed(attended_low, attn).astype(jnp.bfloat16)
    split = split_heads(projected, keep.shape[0])
    queries = split[:, :, 0]
    keysets = split[:, :, 1]
    valuesets = split[:, :, 2]
    probs = attention_probs(queries, keysets, keep, scale)
    probs_low = probs.astype(jnp.bfloat16)
    context_heads = context_low.reshape(queries.shape)
    prob_grad = jnp.einsum(
        "sqhd,skhd->shqk", context_heads, valuesets, preferred_element_type=jnp.float32
    )
    value_grad = jnp.einsum(
        "shqk,sqhd->skhd", probs_low, context_heads, preferred_element_type=jnp.float32
    )
    score_low = (probs * (prob_grad - jnp.sum(probs * prob_grad, axis=-1, keepdims=True))).astype(
        jnp.bfloat16
    )
    query_grad = (
        jnp.einsum("shqk,skhd->sqhd", score_low, keysets, preferred_element_type=jnp.float32)
        * scale
    )
    key_grad = (
        jnp.einsum("shqk,sqhd->skhd", score_low, queries, preferred_element_type=jnp.float32)
        * scale
    )
    merged_low = jnp.stack((query_grad, key_grad, value_grad), axis=2).astype(jnp.bfloat16)
    merged_low = merged_low.reshape(rows.shape[0], 3 * width)
    merged_weight_g = contract_rows(rows, merged_low)
    merged_bias_g = jnp.sum(merged_low.astype(jnp.float32), axis=0)
    states_part = first_grad + times_transposed(merged_low, merged)
    vector_grads = jnp.stack(
        (
            merged_bias_g[:width],
            merged_bias_g[2 * width :],
            attn_bias_g,
            first_gain_g,
            first_shift_g,
            outer_bias_g,
            second_gain_g,
            second_shift_g,
        ),
        axis=1,
    )
    return (
        states_part,
        (
            merged_weight_g,
            attn_weight_g,
            inner_weight_g,
            outer_weight_g,
            vector_grads,
            inner_bias_g,
        ),
    )


def pack_vectors(vectors):
    row = lax.broadcasted_iota(jnp.int32, (16, 128), 0)
    table = jnp.zeros((16, 128), jnp.float32)
    for index, vector in enumerate(vectors):
        padded = jnp.pad(vector.astype(jnp.float32), (0, 128 - vector.shape[0]))
        table = jnp.where(row == index, padded[None, :], table)
    return table


def shards(depth, *arrays):
    (states, pad_mask, query_proj, key_proj, value_proj, attn_proj, query_bias, value_bias, attn_bias, first_gain,
     first_shift, inner_proj, inner_bias, outer_proj, outer_bias, second_gain, second_shift, out_grad) = arrays
    width = states.shape[1]
    short = (query_bias, value_bias, attn_bias, first_gain, first_shift, outer_bias, second_gain, second_shift)
    if depth:
        return kernel_shards(depth, short, states, pad_mask, query_proj, key_proj, value_proj, attn_proj, inner_proj,
                             inner_bias, outer_proj, out_grad)
    merged_shard = jnp.concatenate((query_proj, key_proj, value_proj), axis=1)
    fetched = collect(merged_shard, attn_proj, inner_proj, outer_proj, jnp.stack(short, axis=1), inner_bias)
    encoded, kept = forward_pass(states, pad_mask, fetched)
    states_part, totals = backward_pass(states, pad_mask, out_grad, fetched, kept)
    merged_sum, attn_sum, inner_sum, outer_sum, vector_sum, widened_sum = reduce_grads(*totals)
    return ordered(encoded, states_part, merged_sum, attn_sum, inner_sum, outer_sum, vector_sum.T, widened_sum)


def ordered(encoded, states_part, merged_sum, attn_sum, inner_sum, outer_sum, vectors, widened_sum):
    width = attn_sum.shape[1]
    return (encoded, states_part, merged_sum[:, :width], merged_sum[:, width : 2 * width], merged_sum[:, 2 * width :],
            attn_sum, vectors[0], vectors[1], vectors[2], vectors[3], vectors[4], inner_sum, widened_sum, outer_sum,
            vectors[5], vectors[6], vectors[7])


def kernel_shards(depth, short, states, pad_mask, query_proj, key_proj, value_proj, attn_proj, inner_proj, inner_bias,
                  outer_proj, out_grad):
    width = states.shape[1]
    block = short[0].shape[0]
    packed = pack_vectors(short + (inner_bias,))
    (merged, attn, inner, outer, encoded, projected, probs, context, first_sum, first_low, activated, slope, second_grad,
     outer_low, vectors, sums) = forward_all(
        depth, block, states, pad_mask, out_grad,
        (query_proj, key_proj, value_proj, attn_proj, inner_proj, outer_proj, packed))
    states_part, outer_sum, inner_sum, query_sum, key_sum, value_sum, attn_sum, table_sum = backward_all(
        depth, block, vectors, sums,
        (states, activated, slope, outer_low, second_grad, first_sum, first_low, context, projected, probs,
         merged.reshape(width, -1), attn.reshape(width, -1), inner, outer))
    short_sums = [table_sum[index, :block] for index in range(8)]
    widened_sum = table_sum[8, : inner_bias.shape[0]]
    return (encoded, states_part, query_sum, key_sum, value_sum, attn_sum, *short_sums[:5], inner_sum, widened_sum,
            outer_sum, *short_sums[5:])


def solution(mesh):
    dps, others = mesh.shape["dp"], mesh.shape["fsdp"]
    matrix = P(("dp", "fsdp"), None)
    vector = P(("dp", "fsdp"))

    def whole(*arrays):
        rows = arrays[2].shape[0] // (dps * others)
        tiles = rows % 16 == 0 and arrays[12].shape[0] == 128 * dps * others
        depth = others // 2 if tiles and dps == 4 and others % 2 == 0 else 0
        return jax.shard_map(
            functools.partial(shards, depth),
            mesh=mesh,
            in_specs=(matrix,) * 6 + (vector,) * 5 + (matrix, vector, matrix) + (vector,) * 3 + (matrix,),
            out_specs=(matrix,) * 6 + (vector,) * 5 + (matrix, vector, matrix) + (vector,) * 3,
            check_vma=False,
        )(*arrays)

    return whole
```

```python
import functools

import jax
import jax.numpy as jnp
from jax import lax
from jax.experimental import pallas as pl
from jax.experimental.pallas import tpu as pltpu
from jax.sharding import PartitionSpec as P

HEADS = 16
MESH = pl.DeviceIdType.MESH

epsilon = 1e-05
neg_fill = -1e30


class Place:
    def __init__(self, depth):
        dp = lax.axis_index("dp")
        fsdp = lax.axis_index("fsdp")
        self.depth = depth
        self.dp = dp
        self.z = fsdp // 2
        self.core = lax.rem(fsdp, 2)
        flip_x = dp + 1 - 2 * lax.rem(dp, 2)
        flip_y = lax.rem(dp + 2, 4)
        self.near = flip_x + self.core * (flip_y - flip_x)
        self.far = flip_y + self.core * (flip_x - flip_y)
        self.both = lax.rem(flip_x + 2, 4)
        self.fsdp = fsdp
        self.sibling = fsdp + 1 - 2 * self.core
        self.pair = self.z + 1 - 2 * lax.rem(self.z, 2)
        self.jump = self.up(2)
        self.cross = 3 - self.z

    def up(self, step):
        return lax.rem(self.z + step, self.depth)

    def down(self, step):
        return lax.rem(self.z + self.depth - step, self.depth)

    def along(self, z):
        return (self.dp, z * 2 + self.core)

    def greet(self):
        barrier = pltpu.get_barrier_semaphore()
        others = [self.along(self.up(step)) for step in range(1, self.depth)]
        others += [(self.near, self.fsdp), (self.far, self.fsdp), (self.dp, self.sibling)]
        for other in others:
            pl.semaphore_signal(barrier, inc=1, device_id=other, device_id_type=MESH)
        pl.semaphore_wait(barrier, len(others))


def remote(source, target, send, recv, device):
    return pltpu.make_async_remote_copy(
        src_ref=source, dst_ref=target, send_sem=send, recv_sem=recv, device_id=device, device_id_type=MESH
    )


class Gather:
    def __init__(self, place, full, own, sems, piece, lines=None):
        self.lines = pl.ds(0, full.shape[3]) if lines is None else lines
        self.place, self.full, self.own, self.piece = place, full, own.at[self.lines], piece
        self.su, self.ru, self.sd, self.rd, self.sb, self.rb, self.sa, self.ra, self.sc, self.rc, self.so = sems

    def copy_own(self):
        p = self.place
        return pltpu.make_async_copy(self.own, self.full.at[p.dp, p.z, p.core, self.lines], self.so.at[self.piece])

    def copy_up(self, z, first=False):
        p = self.place
        block = self.full.at[p.dp, z, p.core, self.lines]
        source = self.own if first else block
        return remote(source, block, self.su.at[self.piece, z], self.ru.at[self.piece, z], p.along(p.z + 1))

    def copy_down(self, z, first=False):
        p = self.place
        block = self.full.at[p.dp, z, p.core, self.lines]
        source = self.own if first else block
        return remote(source, block, self.sd.at[self.piece, z], self.rd.at[self.piece, z], p.along(p.z - 1))

    def copy_near(self, z, first=False, arriving=False):
        p = self.place
        block = self.full.at[p.near if arriving else p.dp, z, p.core, self.lines]
        source = self.own if first else block
        return remote(source, block, self.sb.at[self.piece, z], self.rb.at[self.piece, z], (p.near, p.fsdp))

    def copy_far(self, half, z, first=False, arriving=False):
        p = self.place
        row = (p.both if half else p.far) if arriving else (p.near if half else p.dp)
        block = self.full.at[row, z, p.core, self.lines]
        source = self.own if first else block
        at = half * p.depth + z
        return remote(source, block, self.sa.at[self.piece, at], self.ra.at[self.piece, at], (p.far, p.fsdp))

    def copy_core(self, part, arriving=False):
        p = self.place
        if arriving:
            row = (p.dp, p.far, p.near, p.both)[part]
            block = self.full.at[row, :, 1 - p.core, self.lines]
        else:
            row = (p.dp, p.near, p.far, p.both)[part]
            block = self.full.at[row, :, p.core, self.lines]
        return remote(block, block, self.sc.at[self.piece, part], self.rc.at[self.piece, part], (p.dp, p.sibling))

    def start(self):
        p = self.place
        pl.when(p.z < p.depth - 1)(lambda: self.copy_up(p.z, True).start())
        pl.when(p.z > 0)(lambda: self.copy_down(p.z, True).start())
        self.copy_own().start()

    def send(self, step):
        p = self.place

        def act(z, first=False):
            self.copy_near(z, first).start()
            self.copy_far(0, z, first).start()

        if step == 0:
            act(p.z, True)
        else:
            pl.when(p.z >= step)(lambda: act(p.z - step))
            pl.when(p.z + step < p.depth)(lambda: act(p.z + step))

    def hop(self, step):
        p = self.place

        @pl.when(p.z >= step)
        def _():
            z = p.z - step
            self.copy_up(z).wait_recv()
            pl.when(p.z < p.depth - 1)(lambda: self.copy_up(z).start())

        @pl.when(p.z + step < p.depth)
        def _():
            z = p.z + step
            self.copy_down(z).wait_recv()
            pl.when(p.z > 0)(lambda: self.copy_down(z).start())

    def last_hop(self):
        self.hop(self.place.depth - 1)
        self.copy_own().wait()
        self.copy_core(0).start()

    def spread(self, step):
        p = self.place

        def act(z):
            self.copy_near(z, arriving=True).wait_recv()
            self.copy_far(1, z).start()

        if step == 0:
            act(p.z)
        else:
            pl.when(p.z >= step)(lambda: act(p.z - step))
            pl.when(p.z + step < p.depth)(lambda: act(p.z + step))
        if step == p.depth - 1:
            self.copy_core(1).start()

    def arrive_far(self, half):
        p = self.place
        for z in range(p.depth):
            self.copy_far(half, z, arriving=True).wait_recv()
        self.copy_core(2 + half).start()

    def arrive_core(self, *parts):
        for part in parts:
            self.copy_core(part, arriving=True).wait_recv()

    def drain(self):
        p = self.place
        for z in range(p.depth):
            pl.when((p.z < p.depth - 1) & (z <= p.z))(lambda: self.copy_up(z).wait_send())
            pl.when((p.z > 0) & (z >= p.z))(lambda: self.copy_down(z).wait_send())
            self.copy_near(z).wait_send()
            self.copy_far(0, z).wait_send()
            self.copy_far(1, z).wait_send()
        for part in range(4):
            self.copy_core(part).wait_send()


class GatherLine:
    def __init__(self, place, full, own, sems, piece, lines):
        self.place, self.full, self.own, self.piece, self.lines = place, full, own.at[lines], piece, lines
        self.sj, self.rj, self.sp, self.rp, self.sb, self.rb, self.sa, self.ra, self.sc, self.rc, self.so = sems

    def block(self, row):
        return self.full.at[row, self.place.z, self.place.core, self.lines]

    def column(self, z, core):
        return self.full.at[:, z, core, self.lines]

    def copy_own(self):
        return pltpu.make_async_copy(self.own, self.block(self.place.dp), self.so.at[self.piece])

    def copy_near(self, arriving=False):
        p = self.place
        target = self.block(p.near if arriving else p.dp)
        return remote(self.own, target, self.sb.at[self.piece, 0], self.rb.at[self.piece, 0], (p.near, p.fsdp))

    def copy_far(self, half, arriving=False):
        p = self.place
        target = self.block((p.both if half else p.far) if arriving else (p.near if half else p.dp))
        source = target if half else self.own
        return remote(source, target, self.sa.at[self.piece, half], self.ra.at[self.piece, half], (p.far, p.fsdp))

    def copy_jump(self, arriving=False):
        p = self.place
        column = self.column(p.jump if arriving else p.z, p.core)
        return remote(column, column, self.sj.at[self.piece, 0], self.rj.at[self.piece, 0], p.along(p.jump))

    def copy_pair(self, part, arriving=False):
        p = self.place
        z = (p.cross if part else p.pair) if arriving else (p.jump if part else p.z)
        column = self.column(z, p.core)
        return remote(column, column, self.sp.at[self.piece, part], self.rp.at[self.piece, part], p.along(p.pair))

    def copy_core(self, part, arriving=False):
        p = self.place
        column = self.column((p.z, p.jump, p.pair, p.cross)[part], 1 - p.core if arriving else p.core)
        return remote(column, column, self.sc.at[self.piece, part], self.rc.at[self.piece, part], (p.dp, p.sibling))

    def start(self):
        self.copy_near().start()
        self.copy_far(0).start()
        self.copy_own().start()

    def spread(self):
        self.copy_near(arriving=True).wait_recv()
        self.copy_far(1).start()

    def join(self):
        self.copy_own().wait()
        for half in range(2):
            self.copy_far(half, arriving=True).wait_recv()
        self.copy_jump().start()
        self.copy_pair(0).start()
        self.copy_core(0).start()

    def relay(self):
        self.copy_jump(arriving=True).wait_recv()
        self.copy_pair(1).start()
        self.copy_core(1).start()

    def arrive(self):
        for part in range(2):
            self.copy_pair(part, arriving=True).wait_recv()
            self.copy_core(2 + part).start()

    def arrive_core(self):
        for part in range(4):
            self.copy_core(part, arriving=True).wait_recv()

    def drain(self):
        self.copy_near().wait_send()
        self.copy_jump().wait_send()
        for part in range(2):
            self.copy_far(part).wait_send()
            self.copy_pair(part).wait_send()
        for part in range(4):
            self.copy_core(part).wait_send()


def gather_sems(pieces, depth):
    dma = pltpu.SemaphoreType.DMA
    counts = (depth, depth, depth, depth, depth, depth, 2 * depth, 2 * depth, 4, 4)
    return [dma((pieces, count)) for count in counts] + [dma((pieces,))]


def matmul(left, right):
    return lax.dot_general(left, right, (((1,), (0,)), ((), ())), preferred_element_type=jnp.float32)


def matmul_nt(left, right):
    return lax.dot_general(left, right, (((1,), (1,)), ((), ())), preferred_element_type=jnp.float32)


def matmul_tn(left, right):
    return lax.dot_general(left, right, (((0,), (0,)), ((), ())), preferred_element_type=jnp.float32)


def flat(value):
    return value.reshape(-1, value.shape[-1])


def span(index, size):
    return pl.ds(pl.multiple_of(index * size, size), size)


def unpack_table(table, block, vectors, long_bias):
    dps, depth, cores = table.shape[:3]
    places = dps * depth * cores
    width = vectors.shape[1]
    lane = lax.broadcasted_iota(jnp.int32, (128, width), 1)
    source = lax.broadcasted_iota(jnp.int32, (128, width), 0)
    pick = jnp.where(source == lax.rem(lane, block), 1.0, 0.0).astype(jnp.bfloat16)
    owner = lax.broadcasted_iota(jnp.int32, (places, width), 1) // block
    mine = owner == lax.broadcasted_iota(jnp.int32, (places, width), 0)
    blocks = [table[:, :, :, vector, :].reshape(places, 128) for vector in range(8)]
    spread = matmul(jnp.concatenate(blocks, axis=0).astype(jnp.bfloat16), pick)
    for vector in range(8):
        own = jnp.where(mine, spread[vector * places : (vector + 1) * places], 0.0)
        vectors[vector : vector + 1, :] = jnp.sum(own, axis=0, keepdims=True)
    for index in range(places):
        dp, z, core = index // (depth * cores), index // cores % depth, index % cores
        long_bias[:, index * 128 : (index + 1) * 128] = table[dp, z, core, 8:9, :]


CHUNK = 256


def project(rows, weights, vectors, projected):
    chunks = rows.shape[1] // CHUNK
    for part, bias in ((0, 0), (1, None), (2, 1)):

        def one(index, _):
            at = span(part * chunks + index, CHUNK)
            total = matmul(rows[...], flat(weights[:, :, :, :, at]))
            if bias is not None:
                total = total + vectors[bias : bias + 1, span(index, CHUNK)]
            projected[:, at] = total.astype(jnp.bfloat16)
            return 0

        lax.fori_loop(0, chunks, one, 0)


def head_lanes(heads, rows, size):
    lane = lax.broadcasted_iota(jnp.int32, (rows, heads * size), 1) // size
    return [lane == head for head in range(heads)]


def stack_heads(value, lanes):
    return jnp.concatenate([jnp.where(lane, value, jnp.zeros_like(value)) for lane in lanes], axis=0)


def merge_heads(value, lanes):
    rows = value.shape[0] // len(lanes)
    result = value[:rows]
    for head in range(1, len(lanes)):
        result = jnp.where(lanes[head], value[head * rows : (head + 1) * rows], result)
    return result


QUAD = 4


def attend(projected, keep, probs, context, first, last):
    width = context.shape[1]
    size = width // HEADS
    length = keep.shape[1]
    scale = size ** (-0.5)
    lanes = head_lanes(QUAD, length, size)
    quads = HEADS // QUAD

    def one(index, _):
        segment = index // quads
        quad = lax.rem(index, quads)
        at = span(segment, length)
        queries = projected[at, span(quad, QUAD * size)]
        keysets = projected[at, span(quad + quads, QUAD * size)]
        valuesets = projected[at, span(quad + 2 * quads, QUAD * size)]
        scores = matmul_nt(stack_heads(queries, lanes), keysets) * scale
        mask = keep[pl.ds(segment, 1), :] > 0
        scores = jnp.where(mask, scores, neg_fill)
        raised = jnp.exp(scores - jnp.max(scores, axis=1, keepdims=True))
        low = (raised / jnp.sum(raised, axis=1, keepdims=True)).astype(jnp.bfloat16)
        probs[index] = low
        context[at, span(quad, QUAD * size)] = merge_heads(matmul(low, valuesets), lanes).astype(jnp.bfloat16)
        return 0

    lax.fori_loop(first, last, one, 0)


def center_scale(hidden):
    center = hidden - jnp.mean(hidden, axis=1, keepdims=True)
    spread = jnp.mean(center * center, axis=1, keepdims=True)
    rate = lax.rsqrt(spread + epsilon)
    return center * rate, rate


def first_block(rows, context, weights, vectors, first_sum, first_norm, first_low):
    def product(index, _):
        at = span(index, CHUNK)
        attended = matmul(context[...], flat(weights[:, :, :, :, at])) + vectors[2:3, at]
        first_sum[:, at] = rows[:, at].astype(jnp.float32) + attended
        return 0

    lax.fori_loop(0, rows.shape[1] // CHUNK, product, 0)

    def one(index, _):
        at = span(index, 64)
        normed, _ = center_scale(first_sum[at, :])
        result = normed * vectors[3:4, :] + vectors[4:5, :]
        first_norm[at, :] = result
        first_low[at, :] = result.astype(jnp.bfloat16)
        return 0

    lax.fori_loop(0, rows.shape[0] // 64, one, 0)


def inner_block(first_low, weights, long_bias, activated, slope, first, last):
    def one(index, _):
        at = span(index, CHUNK)
        value = matmul(first_low[...], flat(weights[:, :, :, :, at])) + long_bias[:, at]
        share = 0.5 * (1.0 + lax.erf(value * (0.5**0.5)))
        bell = jnp.exp(-0.5 * value * value) * ((0.5 / jnp.pi) ** 0.5)
        activated[:, at] = (value * share).astype(jnp.bfloat16)
        slope[:, at] = (share + value * bell).astype(jnp.bfloat16)
        return 0

    lax.fori_loop(first, last, one, 0)


def outer_part(activated, weights, row, total, fresh):
    size = weights.shape[1] * weights.shape[2] * weights.shape[3]

    def one(index, _):
        at = span(index, CHUNK)
        value = matmul(activated[:, span(row, size)], flat(weights[row, :, :, :, at]))
        total[:, at] = value if fresh else total[:, at] + value
        return 0

    lax.fori_loop(0, total.shape[1] // CHUNK, one, 0)


def norm_back(grad, normed, rate, gain):
    scaled = grad * gain
    mean = jnp.mean(scaled, axis=1, keepdims=True)
    along = jnp.mean(scaled * normed, axis=1, keepdims=True)
    return rate * (scaled - mean - normed * along)


def second_block(first_norm, total, cotangent, vectors, encoded, second_grad, outer_low, sums):
    sums[...] = jnp.zeros_like(sums)

    def one(index, _):
        at = span(index, 64)
        normed, rate = center_scale(first_norm[at, :] + (total[at, :] + vectors[5:6, :]))
        gain = vectors[6:7, :]
        encoded[at, :] = (normed * gain + vectors[7:8, :]).astype(jnp.bfloat16)
        grad = cotangent[at, :].astype(jnp.float32)
        back = norm_back(grad, normed, rate, gain)
        low = back.astype(jnp.bfloat16)
        second_grad[at, :] = back
        outer_low[at, :] = low
        sums[5:6, :] += jnp.sum(low.astype(jnp.float32), axis=0, keepdims=True)
        sums[6:7, :] += jnp.sum(grad * normed, axis=0, keepdims=True)
        sums[7:8, :] += jnp.sum(grad, axis=0, keepdims=True)
        return 0

    lax.fori_loop(0, first_norm.shape[0] // 64, one, 0)


def forward_kernel(depth, block, *refs):
    (rows, keep, cotangent, query_own, key_own, value_own, attn_own, inner_own, outer_own) = refs[:9]
    short_vectors = refs[9:18]
    merged_out, attn_out, inner_out, outer_out = refs[18:22]
    (encoded_out, projected_out, probs_out, context_out, first_sum_out, first_low_out, activated_out, slope_out,
     second_grad_out, outer_low_out, vectors, sums) = refs[22:34]
    (table_own, merged_own, table, merged, attn, inner, outer, projected, probs, context, first_sum, first_norm, first_low,
     activated, slope, total, encoded, second_grad, outer_low, long_bias, save_sem) = refs[34:55]
    sems = refs[55:]
    table_own[...] = jnp.zeros_like(table_own)
    for index, vector in enumerate(short_vectors):
        table_own[index, : vector.shape[0]] = vector[...].astype(jnp.float32)
    place = Place(depth)
    width = rows.shape[1]
    for part, own in enumerate((query_own, key_own, value_own)):
        merged_own[:, part * width : (part + 1) * width] = own[...]
    net_table = Gather(place, table, table_own, sems, 0)
    net_merged = Gather(place, merged, merged_own, sems, 1)
    net_attn = Gather(place, attn, attn_own, sems, 2)
    net_inner = Gather(place, inner, inner_own, sems, 3)
    half = outer.shape[3] // 2
    net_outer = Gather(place, outer, outer_own, sems, 4, pl.ds(0, half))
    line = GatherLine(place, outer, outer_own, sems, 5, pl.ds(half, half))
    nets = (net_table, net_merged, net_attn, net_inner, net_outer, line)
    front = nets[:3]
    place.greet()
    saves = []

    def save(source, target):
        copy = pltpu.make_async_copy(source, target, save_sem.at[len(saves)])
        copy.start()
        saves.append(copy)

    def hop(net, step):
        if step == depth - 1:
            net.last_hop()
        else:
            net.hop(step)

    def each(nets_of, *names, step):
        for name in names:
            for net in nets_of:
                hop(net, step) if name == "hop" else getattr(net, name)(step)

    for net in front:
        net.start()
    each(front, "send", step=0)
    line.start()
    each(front, "hop", "send", step=1)
    line.spread()
    net_inner.start()
    each(front, "spread", step=0)
    for step in range(2, depth):
        each(front, "hop", "send", step=step)
        each(front, "spread", step=step - 1)
    net_inner.send(0)
    net_outer.start()
    net_inner.hop(1)
    net_inner.send(1)
    each(front, "spread", step=depth - 1)
    net_inner.spread(0)
    net_outer.hop(1)
    for step in range(2, depth - 1):
        net_inner.hop(step)
        net_inner.send(step)
        net_inner.spread(step - 1)
    line.join()
    for net in front:
        net.arrive_far(0)
        net.arrive_far(1)
        net.arrive_core(0, 1, 2, 3)
    save(merged, merged_out)
    save(attn, attn_out)
    unpack_table(table, block, vectors, long_bias)
    project(rows, merged, vectors, projected)
    save(projected, projected_out)
    for step in range(2, depth - 1):
        net_outer.hop(step)
    net_inner.last_hop()
    net_inner.send(depth - 1)
    net_inner.spread(depth - 2)
    line.relay()
    count = probs.shape[0]
    attend(projected, keep, probs, context, 0, count // 2)
    net_outer.last_hop()
    net_inner.spread(depth - 1)
    attend(projected, keep, probs, context, count // 2, count)
    save(probs, probs_out)
    save(context, context_out)
    first_block(rows, context, attn, vectors, first_sum, first_norm, first_low)
    save(first_sum, first_sum_out)
    save(first_low, first_low_out)
    net_inner.arrive_far(0)
    for step in range(depth):
        net_outer.send(step)
    net_inner.arrive_far(1)
    net_inner.arrive_core(0, 1, 2, 3)
    save(inner, inner_out)
    quarter = inner.shape[4] // CHUNK // 4

    def inner_quarter(index):
        inner_block(first_low, inner, long_bias, activated, slope, index * quarter, (index + 1) * quarter)

    inner_quarter(0)
    net_outer.spread(0)
    inner_quarter(1)
    for step in range(1, depth - 1):
        net_outer.spread(step)
    inner_quarter(2)
    net_outer.spread(depth - 1)
    line.arrive()
    inner_quarter(3)
    save(activated, activated_out)
    save(slope, slope_out)
    line.arrive_core()
    net_outer.arrive_core(0)
    outer_part(activated, outer, place.dp, total, True)
    net_outer.arrive_far(0)
    net_outer.arrive_core(1, 2)
    outer_part(activated, outer, place.near, total, False)
    outer_part(activated, outer, place.far, total, False)
    net_outer.arrive_far(1)
    net_outer.arrive_core(3)
    save(outer, outer_out)
    outer_part(activated, outer, place.both, total, False)
    second_block(first_norm, total, cotangent, vectors, encoded, second_grad, outer_low, sums)
    save(encoded, encoded_out)
    save(second_grad, second_grad_out)
    save(outer_low, outer_low_out)
    for net in nets:
        net.drain()
    for copy in saves:
        copy.wait()


def forward_all(depth, block, rows, keep, cotangent, owns):
    query_own, _, _, attn_own, inner_own, outer_own = owns[:6]
    tokens, width = rows.shape
    hidden = inner_own.shape[1]
    segments, length = keep.shape
    low, high = jnp.bfloat16, jnp.float32

    def fulls(own, columns):
        return (4, depth, 2, own.shape[0], columns)

    full_shapes = [fulls(query_own, 3 * width), fulls(attn_own, width), fulls(inner_own, hidden), fulls(outer_own, width)]
    kept = [
        ((tokens, width), low),
        ((tokens, 3 * width), low),
        ((segments * HEADS // QUAD, QUAD * length, length), low),
        ((tokens, width), low),
        ((tokens, width), high),
        ((tokens, width), low),
        ((tokens, hidden), low),
        ((tokens, hidden), low),
        ((tokens, width), high),
        ((tokens, width), low),
    ]
    small = [((8, width), high), ((8, width), high)]
    shapes = [jax.ShapeDtypeStruct(shape, low) for shape in full_shapes]
    shapes += [jax.ShapeDtypeStruct(*one) for one in kept + small]
    held = {name: pltpu.VMEM(*one) for name, one in zip(
        ("encoded", "projected", "probs", "context", "first_sum", "first_low", "activated", "slope", "second_grad", "outer_low"),
        kept)}
    scratch = [pltpu.VMEM((16, 128), high), pltpu.VMEM((query_own.shape[0], 3 * width), low)]
    scratch += [pltpu.VMEM((4, depth, 2, 16, 128), high)]
    scratch += [pltpu.VMEM(shape, low) for shape in full_shapes]
    scratch += [held[name] for name in ("projected", "probs", "context", "first_sum")]
    scratch += [pltpu.VMEM((tokens, width), high)]
    scratch += [held[name] for name in ("first_low", "activated", "slope")]
    scratch += [pltpu.VMEM((tokens, width), high)]
    scratch += [held[name] for name in ("encoded", "second_grad", "outer_low")]
    scratch += [pltpu.VMEM((1, hidden), high)]
    scratch += [pltpu.SemaphoreType.DMA((len(full_shapes) + len(kept),))]
    here = pl.BlockSpec(memory_space=pltpu.VMEM)
    away = pl.BlockSpec(memory_space=pl.ANY)
    return pl.pallas_call(
        functools.partial(forward_kernel, depth, block),
        out_shape=shapes,
        in_specs=[here] * (3 + len(owns)),
        out_specs=[away] * (len(full_shapes) + len(kept)) + [here] * 2,
        scratch_shapes=scratch + gather_sems(6, depth),
        compiler_params=pltpu.CompilerParams(
            collective_id=0, has_side_effects=True, vmem_limit_bytes=60 * 1024 * 1024
        ),
        name="forward",
    )(rows, keep, cotangent, *owns)


SUBS = 4


class Slots:
    def __init__(self, core, far, near, along):
        self.core, self.far, self.near, self.along = core, far, near, along


class Scatter:
    def __init__(self, place, whole, slots, sems, credits, number, lot, first, count, after=False, before=False,
                 late_after=False, late_before=False):
        self.place, self.whole, self.slots = place, whole, slots
        self.sc, self.rc, self.sa, self.ra, self.sb, self.rb, self.sz, self.rz = sems
        self.core_free, self.far_free, self.near_free, self.z_free = credits
        self.number, self.lot, self.first, self.count = number, lot, first, count
        self.sub = first // count
        self.after, self.before, self.late_after, self.late_before = after, before, late_after, late_before
        self.tile = 8 if whole.dtype == jnp.float32 else 16

    def lines(self):
        return pl.ds(self.first, self.count)

    def mine(self, row):
        return self.whole.at[row, :, self.place.core, self.lines()]

    def sent_row(self, at):
        p = self.place
        return (p.both, p.near, p.far, p.dp)[at]

    def got_row(self, at):
        p = self.place
        return (p.both, p.far, p.near, p.dp)[at]

    def copy_core(self, at):
        p = self.place
        return remote(
            self.whole.at[self.sent_row(at), :, 1 - p.core, self.lines()], self.slots.core.at[at, :, self.lines()],
            self.sc.at[self.number, at], self.rc.at[self.number, at], (p.dp, p.sibling),
        )

    def copy_far(self, half):
        p = self.place
        return remote(
            self.mine(p.both if half else p.far), self.slots.far.at[self.lot, half, :, self.lines()],
            self.sa.at[self.number, half], self.ra.at[self.number, half], (p.far, p.fsdp),
        )

    def copy_near(self):
        p = self.place
        return remote(
            self.mine(p.near), self.slots.near.at[self.lot, :, self.lines()], self.sb.at[self.number],
            self.rb.at[self.number], (p.near, p.fsdp),
        )

    def copy_z(self, step):
        p = self.place
        return remote(
            self.whole.at[p.dp, p.up(step), p.core, self.lines()], self.slots.along.at[self.lot, step - 1, self.lines()],
            self.sz.at[self.number, step - 1], self.rz.at[self.number, step - 1], p.along(p.up(step)),
        )

    def add(self, row, slot):
        p = self.place
        tiles = self.count // self.tile

        def one(index, _):
            z = index // tiles
            at = pl.ds(pl.multiple_of(self.first + lax.rem(index, tiles) * self.tile, self.tile), self.tile)
            self.whole[row, z, p.core, at, :] = self.whole[row, z, p.core, at, :] + slot[z, at, :]
            return 0

        lax.fori_loop(0, p.depth * tiles, one, 0)

    def start_core(self, at):
        if self.after:
            pl.semaphore_wait(self.core_free.at[at, self.sub], 1)
        self.copy_core(at).start()

    def add_core(self, at):
        p = self.place
        self.copy_core(at).wait_recv()
        self.add(self.got_row(at), self.slots.core.at[at])
        if self.before:
            pl.semaphore_signal(self.core_free.at[at, self.sub], inc=1, device_id=(p.dp, p.sibling), device_id_type=MESH)

    def start_far(self, half):
        if self.late_after:
            pl.semaphore_wait(self.far_free.at[half, self.sub], 1)
        self.copy_far(half).start()

    def add_far(self, half):
        p = self.place
        self.copy_far(half).wait_recv()
        self.add(p.near if half else p.dp, self.slots.far.at[self.lot, half])
        if self.late_before:
            pl.semaphore_signal(self.far_free.at[half, self.sub], inc=1, device_id=(p.far, p.fsdp), device_id_type=MESH)
        if half:
            if self.late_after:
                pl.semaphore_wait(self.near_free.at[self.sub], 1)
            self.copy_near().start()

    def add_near(self):
        p = self.place
        self.copy_near().wait_recv()
        self.add(p.dp, self.slots.near.at[self.lot])
        if self.late_before:
            pl.semaphore_signal(self.near_free.at[self.sub], inc=1, device_id=(p.near, p.fsdp), device_id_type=MESH)
        for step in range(1, p.depth):
            if self.late_after:
                pl.semaphore_wait(self.z_free.at[self.sub, step - 1], 1)
            self.copy_z(step).start()

    def finish(self, out):
        p = self.place
        for step in range(1, p.depth):
            self.copy_z(step).wait_recv()

        def one(index, _):
            start = pl.multiple_of(index * self.tile, self.tile)
            at = pl.ds(pl.multiple_of(self.first + start, self.tile), self.tile)
            total = self.whole[p.dp, p.z, p.core, at, :].astype(jnp.float32)
            for step in range(p.depth - 1):
                total = total + self.slots.along[self.lot, step, at, :].astype(jnp.float32)
            out[pl.ds(start, self.tile), :] = total
            return 0

        lax.fori_loop(0, self.count // self.tile, one, 0)
        if self.late_before:
            for step in range(1, p.depth):
                pl.semaphore_signal(
                    self.z_free.at[self.sub, step - 1], inc=1, device_id=p.along(p.down(step)), device_id_type=MESH
                )

    def drain(self):
        for at in range(4):
            self.copy_core(at).wait_send()
        self.copy_far(1).wait_send()
        self.copy_far(0).wait_send()
        self.copy_near().wait_send()
        for step in range(1, self.place.depth):
            self.copy_z(step).wait_send()


class ScatterLine(Scatter):
    def column(self, z):
        return self.whole.at[:, z, self.place.core, self.lines()]

    def copy_pair(self, part):
        p = self.place
        return remote(
            self.column(p.cross if part else p.pair), self.slots.far.at[0, part, :, self.lines()],
            self.sa.at[self.number, part], self.ra.at[self.number, part], p.along(p.pair),
        )

    def copy_jump(self):
        p = self.place
        return remote(
            self.column(p.jump), self.slots.near.at[0, :, self.lines()], self.sb.at[self.number], self.rb.at[self.number],
            p.along(p.jump),
        )

    def copy_axis(self, part):
        p = self.place
        row = (p.both, p.far, p.near)[part]
        target = p.near if part == 2 else p.far
        return remote(
            self.whole.at[row, p.z, p.core, self.lines()], self.slots.along.at[0, part, self.lines()],
            self.sz.at[self.number, part], self.rz.at[self.number, part], (target, p.fsdp),
        )

    def add_column(self, z, slot):
        p = self.place
        tiles = self.count // self.tile

        def one(index, _):
            row = index // tiles
            at = pl.ds(pl.multiple_of(self.first + lax.rem(index, tiles) * self.tile, self.tile), self.tile)
            self.whole[row, z, p.core, at, :] = self.whole[row, z, p.core, at, :] + slot[row, at, :]
            return 0

        lax.fori_loop(0, self.whole.shape[0] * tiles, one, 0)

    def add_block(self, row, part):
        p = self.place

        def one(index, _):
            at = pl.ds(pl.multiple_of(self.first + index * self.tile, self.tile), self.tile)
            self.whole[row, p.z, p.core, at, :] = self.whole[row, p.z, p.core, at, :] + self.slots.along[0, part, at, :]
            return 0

        lax.fori_loop(0, self.count // self.tile, one, 0)

    def tell(self, semaphore, device):
        pl.semaphore_signal(semaphore, inc=1, device_id=device, device_id_type=MESH)

    def add_core(self, at):
        p = self.place
        self.copy_core(at).wait_recv()
        self.add(self.got_row(at), self.slots.core.at[at])
        for sub in range(SUBS // 2, SUBS):
            self.tell(self.core_free.at[at, sub], (p.dp, p.sibling))

    def start_pair(self):
        self.copy_pair(1).start()
        self.copy_pair(0).start()

    def add_pair(self, part):
        p = self.place
        self.copy_pair(part).wait_recv()
        self.add_column(p.jump if part else p.z, self.slots.far.at[0, part])
        if part:
            self.copy_jump().start()
        for sub in range(SUBS // 2, SUBS):
            self.tell(self.far_free.at[part, sub], (p.far, p.fsdp))

    def add_jump(self):
        p = self.place
        self.copy_jump().wait_recv()
        self.add_column(p.z, self.slots.near.at[0])
        for sub in range(SUBS // 2, SUBS):
            self.tell(self.near_free.at[sub], (p.near, p.fsdp))
        self.copy_axis(0).start()
        self.copy_axis(1).start()

    def add_far_axis(self):
        p = self.place
        for part in range(2):
            self.copy_axis(part).wait_recv()
            self.add_block(p.dp if part else p.near, part)
        self.copy_axis(2).start()

    def finish(self, out):
        p = self.place
        self.copy_axis(2).wait_recv()

        def one(index, _):
            start = pl.multiple_of(index * self.tile, self.tile)
            at = pl.ds(pl.multiple_of(self.first + start, self.tile), self.tile)
            total = self.whole[p.dp, p.z, p.core, at, :].astype(jnp.float32)
            out[pl.ds(start, self.tile), :] = total + self.slots.along[0, 2, at, :].astype(jnp.float32)
            return 0

        lax.fori_loop(0, self.count // self.tile, one, 0)
        for sub in range(SUBS // 2, SUBS):
            for step in range(1, p.depth):
                self.tell(self.z_free.at[sub, step - 1], p.along(p.down(step)))

    def drain(self):
        for at in range(4):
            self.copy_core(at).wait_send()
        for part in range(2):
            self.copy_pair(part).wait_send()
        self.copy_jump().wait_send()
        for part in range(3):
            self.copy_axis(part).wait_send()


def outer_gradient(acts, low, grads, row):
    depth, cores, count, _ = grads.shape[1:]
    size = cores * count

    def one(z, _):
        value = matmul_tn(acts[row, :, span(z, size)], low[...])
        grads[row, z] = value.astype(jnp.bfloat16).reshape(grads.shape[2:])
        return 0

    lax.fori_loop(0, depth, one, 0)


def input_gradient(inputs, low, grads, row, part):
    depth, cores, count, width = grads.shape[1:]
    size = inputs.shape[1] // grads.shape[0]
    lines = count // SUBS
    value = matmul_tn(inputs[:, span(row, size)], low)
    grads[row, :, :, part * lines : (part + 1) * lines, :] = value.astype(jnp.bfloat16).reshape(depth, cores, lines, width)


def hidden_back(low, weights, slopes, bias_sum, part):
    depth, cores, count, width = weights.shape[1:]
    size = cores * count

    def one(index, _):
        at = span(index, size)
        value = matmul_nt(low[...], flat(weights[part, index])) * slopes[SUBS + part, :, at].astype(jnp.float32)
        rounded = value.astype(jnp.bfloat16)
        slopes[SUBS + part, :, at] = rounded
        total = jnp.sum(rounded.astype(jnp.float32), axis=0, keepdims=True)
        bias_sum[:, pl.ds(pl.multiple_of(part * width + index * size, size), size)] = total
        return 0

    lax.fori_loop(0, depth, one, 0)


def first_total_rows(grad, inner_low, weights):
    lines = weights.shape[3] // SUBS
    size = grad.shape[1] // weights.shape[0]

    def one(index, _):
        at = span(index, size)
        total = grad[:, at]
        for part in range(SUBS):
            weight = flat(weights[index, :, :, part * lines : (part + 1) * lines, :])
            total = total + matmul_nt(inner_low[SUBS + part], weight)
        grad[:, at] = total
        return 0

    lax.fori_loop(0, weights.shape[0], one, 0)


def first_back(first_sum, grad, low, vectors, sums):
    for row in (2, 3, 4):
        sums[row : row + 1, :] = jnp.zeros((1, grad.shape[1]), jnp.float32)

    def one(index, _):
        at = span(index, 64)
        normed, rate = center_scale(first_sum[at, :])
        upper = grad[at, :]
        back = norm_back(upper, normed, rate, vectors[3:4, :])
        rounded = back.astype(jnp.bfloat16)
        grad[at, :] = back
        low[at, :] = rounded
        sums[2:3, :] += jnp.sum(rounded.astype(jnp.float32), axis=0, keepdims=True)
        sums[3:4, :] += jnp.sum(upper * normed, axis=0, keepdims=True)
        sums[4:5, :] += jnp.sum(upper, axis=0, keepdims=True)
        return 0

    lax.fori_loop(0, grad.shape[0] // 64, one, 0)


def context_back(low, weights, context):
    halves = weights.shape[1] // CHUNK

    def one(index, _):
        weight = weights[index // halves, span(lax.rem(index, halves), CHUNK), :]
        context[:, span(index, CHUNK)] = matmul_nt(low[...], weight).astype(jnp.bfloat16)
        return 0

    lax.fori_loop(0, context.shape[1] // CHUNK, one, 0)


def attend_back(projected, probs, context_low, sums, first, last):
    width = context_low.shape[1]
    size = width // HEADS
    length = probs.shape[2]
    scale = size ** (-0.5)
    lanes = head_lanes(QUAD, length, size)
    quads = HEADS // QUAD

    def one(index, _):
        segment = index // quads
        quad = lax.rem(index, quads)
        at = span(segment, length)
        columns = [span(quad + part * quads, QUAD * size) for part in range(3)]
        queries, keysets, valuesets = [projected[at, column] for column in columns]
        low = probs[index]
        wide = low.astype(jnp.float32)
        upper = stack_heads(context_low[at, columns[0]], lanes)
        prob_grad = matmul_nt(upper, valuesets)
        score_low = (wide * (prob_grad - jnp.sum(wide * prob_grad, axis=1, keepdims=True))).astype(jnp.bfloat16)
        value_low = matmul_tn(low, upper).astype(jnp.bfloat16)
        query_low = (merge_heads(matmul(score_low, keysets), lanes) * scale).astype(jnp.bfloat16)
        key_low = (matmul_tn(score_low, stack_heads(queries, lanes)) * scale).astype(jnp.bfloat16)
        projected[at, columns[0]] = query_low
        projected[at, columns[1]] = key_low
        projected[at, columns[2]] = value_low
        sums[0:1, columns[0]] += jnp.sum(query_low.astype(jnp.float32), axis=0, keepdims=True)
        sums[1:2, columns[0]] += jnp.sum(value_low.astype(jnp.float32), axis=0, keepdims=True)
        return 0

    lax.fori_loop(first, last, one, 0)


def states_back(grad, projected, weights):
    width = grad.shape[1]
    halves = weights.shape[1] // CHUNK

    def one(index, _):
        at = span(index, CHUNK)
        total = grad[:, at]
        for part in range(3):
            weight = weights[2 + 2 * part + index // halves, span(lax.rem(index, halves), CHUNK), :]
            total = total + matmul_nt(projected[:, part * width : (part + 1) * width], weight)
        grad[:, at] = total
        return 0

    lax.fori_loop(0, width // CHUNK, one, 0)


def pack_sums(sums, bias_sum, block, table):
    dps, depth, cores = table.shape[:3]
    places = dps * depth * cores
    width = sums.shape[1]
    lane = lax.broadcasted_iota(jnp.int32, (width, 128), 1)
    source = lax.broadcasted_iota(jnp.int32, (width, 128), 0)
    pick = jnp.where(lane == lax.rem(source, block), 1.0, 0.0).astype(jnp.bfloat16)
    owner = lax.broadcasted_iota(jnp.int32, (places, width), 1) // block
    mine = owner == lax.broadcasted_iota(jnp.int32, (places, width), 0)
    values = jnp.concatenate([jnp.where(mine, sums[vector : vector + 1, :], 0.0) for vector in range(8)], axis=0)
    upper = values.astype(jnp.bfloat16)
    lower = (values - upper.astype(jnp.float32)).astype(jnp.bfloat16)
    total = matmul(upper, pick) + matmul(lower, pick)
    table[...] = jnp.zeros_like(table)
    for vector in range(8):
        table[:, :, :, vector, :] = total[vector * places : (vector + 1) * places].reshape(dps, depth, cores, 128)
    for index in range(places):
        dp, z, core = index // (depth * cores), index // cores % depth, index % cores
        table[dp, z, core, 8:9, :] = bias_sum[:, index * 128 : (index + 1) * 128]


EARLY = 2
SCHEDULE = (
    ("outer",), ("hidden",), ("far", 0), ("inner",), ("far", 1), ("line", 0), ("near", 0), ("total",), ("line", 1),
    ("go", 4), ("far", 2), ("near", 1), ("norm",), ("go", 5), ("attn",), ("context",), ("far", 3), ("go", 6),
    ("near", 2), ("heads", 0), ("heads", 1), ("line", 2), ("merged",), ("go", 7), ("far", 4), ("near", 3), ("end", 0),
    ("far", 5), ("go", 8), ("near", 4), ("end", 1), ("line", 3), ("pack",), ("states",), ("far", 6), ("go", 9),
    ("near", 5), ("line", 4), ("end", 2), ("go", 10), ("far", 7), ("near", 6), ("end", 3), ("far", 8), ("near", 7),
    ("end", 4), ("far", 9), ("near", 8), ("end", 5), ("far", 10), ("near", 9), ("end", 6), ("near", 10), ("end", 7),
    ("end", 8), ("end", 9), ("end", 10),
)


def backward_kernel(depth, block, *refs):
    (vectors, known, rows_in, activated_in, slope_in, outer_low_in, second_grad_in, first_sum_in, first_low_in, context_in,
     projected_in, probs_in, merged_in, attn_in, inner_in, outer_in) = refs[:16]
    states_out, outer_out, inner_out, query_out, key_out, value_out, attn_out, table_out = refs[16:24]
    (first_buffer, second_buffer, outer_grads, wide, from_core, from_far, from_near, from_z, low, first_low, grad, first_sum,
     context, projected, probs, rows, sums, bias_sum, table, table_core, table_far, table_near, table_z) = refs[24:47]
    load_sem, save_sem = refs[47:49]
    sems = refs[49:57]
    credits = refs[57:61]
    place = Place(depth)
    width = rows.shape[1]
    tokens = rows.shape[0]
    lines = outer_grads.shape[3] // SUBS
    loads = []

    def load(source, target):
        copy = pltpu.make_async_copy(source, target, load_sem.at[len(loads)])
        copy.start()
        loads.append(copy)
        return copy

    def load_columns(source, targets):
        return [load(source.at[:, part * width : (part + 1) * width], target) for part, target in enumerate(targets)]

    low_load = load(outer_low_in, low)
    act_loads = load_columns(activated_in, [wide.at[part] for part in range(SUBS)])
    outer_load = load(outer_in, first_buffer)
    slope_loads = load_columns(slope_in, [wide.at[SUBS + part] for part in range(SUBS)])
    first_low_load = load(first_low_in, first_low)
    grad_load = load(second_grad_in, grad)
    inner_loads = [
        load(inner_in.at[:, :, :, :, part * width : (part + 1) * width],
             second_buffer.at[:, :, :, part * lines : (part + 1) * lines, :])
        for part in range(SUBS)
    ]
    first_sum_load = load(first_sum_in, first_sum)
    context_load = load(context_in, context)
    projected_load = load(projected_in, projected)
    probs_load = load(probs_in, probs)
    rows_load = load(rows_in, rows)

    slots = Slots(from_core, from_far, from_near, from_z)
    table_slots = Slots(table_core, table_far, table_near, table_z)
    outers = [
        Scatter(place, outer_grads, slots, sems, credits, sub, 0, sub * lines, lines, before=True, late_before=True)
        for sub in range(SUBS // 2)
    ]
    line = ScatterLine(place, outer_grads, slots, sems, credits, SUBS - 1, 0, SUBS // 2 * lines, SUBS // 2 * lines)
    inner_grads = first_buffer
    inners = [
        Scatter(place, inner_grads, slots, sems, credits, SUBS + sub, 1, sub * lines, lines, after=True, before=True)
        for sub in range(SUBS)
    ]
    other_grads = second_buffer
    others = [
        Scatter(place, other_grads, slots, sems, credits, 2 * SUBS + sub, 0, sub * lines, lines, after=True, late_after=True)
        for sub in range(SUBS)
    ]
    attn_net = others[0]
    mergeds = others[1:]
    small = Scatter(place, table, table_slots, sems, credits, 3 * SUBS, 0, 0, 16)
    row_order = (place.both, place.near, place.far, place.dp)
    sums[...] = known[...]
    sums[0:2, :] = jnp.zeros((2, width), jnp.float32)
    place.greet()

    def pieces(nets, compute, early=()):
        def added(at):
            for net in nets:
                net.add_core(at)
            if at < 2:
                for net in early:
                    net.start_far(1 - at)

        for at in range(4):
            compute(row_order[at])
            for net in nets:
                net.start_core(at)
            if at:
                added(at - 1)
        added(3)

    order = outers + inners + [attn_net] + mergeds + [small]
    outs = [outer_out.at[pl.ds(sub * lines, lines), :] for sub in range(SUBS // 2)]
    outs += [inner_out.at[:, pl.ds(sub * width, width)] for sub in range(SUBS)]
    outs += [attn_out, query_out, key_out, value_out, table_out]
    def far(number):
        order[number].add_far(1)
        order[number].add_far(0)

    def go(number):
        order[number].start_far(1)
        order[number].start_far(0)

    def near(number):
        order[number].add_near()

    def end(number):
        order[number].finish(outs[number])

    def ready(copies):
        for copy in copies:
            copy.wait()

    def load_merged(part):
        return [
            load(merged_in.at[at * tokens : (at + 1) * tokens, part * width : (part + 1) * width], wide.at[2 + 2 * part + at])
            for at in range(2)
        ]

    late_loads = []

    def outer_step():
        ready([low_load] + act_loads)
        pieces(outers + [line], lambda row: outer_gradient(wide, low, outer_grads, row), outers)
        line.start_pair()
        late_loads.append(load(attn_in.at[:tokens], wide.at[0]))
        late_loads.append(load(attn_in.at[tokens:], wide.at[1]))
        late_loads.extend(load_merged(0))

    def hidden_step():
        ready([outer_load] + slope_loads)
        for part in range(SUBS):
            hidden_back(low, first_buffer, wide, bias_sum, part)

    def inner_step():
        def compute(row):
            for part in range(SUBS):
                input_gradient(first_low, wide[SUBS + part], inner_grads, row, part)

        ready([first_low_load])
        pieces(inners, compute, inners[:EARLY])

    def total_step():
        ready([grad_load] + inner_loads)
        first_total_rows(grad, wide, second_buffer)
        late_loads.extend(load_merged(1) + load_merged(2))

    def norm_step():
        ready([first_sum_load])
        first_back(first_sum, grad, low, vectors, sums)

    def attn_step():
        ready([context_load])
        pieces([attn_net], lambda row: input_gradient(context, low[...], other_grads, row, 0))

    def context_step():
        ready(late_loads[:2])
        context_back(low, wide, context)

    def heads_step(part):
        if part == 0:
            ready([projected_load, probs_load])
        count = probs.shape[0]
        attend_back(projected, probs, context, sums, part * count // 2, (part + 1) * count // 2)

    def merged_step():
        def compute(row):
            for part in range(3):
                input_gradient(rows, projected[:, part * width : (part + 1) * width], other_grads, row, 1 + part)

        ready([rows_load])
        pieces(mergeds, compute)

    def pack_step():
        pack_sums(sums, bias_sum, block, table)
        pieces([small], lambda row: None)

    save = pltpu.make_async_copy(grad, states_out, save_sem)

    def states_step():
        ready(late_loads[2:])
        states_back(grad, projected, wide)
        save.start()

    def line_step(part):
        (line.add_pair, line.add_jump, line.add_far_axis, line.finish)[max(part - 1, 0)](
            *(((1,), (0,), (), (), (outer_out.at[pl.ds(SUBS // 2 * lines, SUBS // 2 * lines), :],))[part])
        )

    steps = {
        "outer": outer_step, "hidden": hidden_step, "inner": inner_step, "total": total_step, "norm": norm_step,
        "attn": attn_step, "context": context_step, "heads": heads_step, "merged": merged_step, "pack": pack_step,
        "states": states_step, "line": line_step, "go": go, "far": far, "near": near, "end": end,
    }
    for entry in SCHEDULE:
        steps[entry[0]](*entry[1:])
    for net in order + [line]:
        net.drain()
    save.wait()


def backward_all(depth, block, vectors, known, kept):
    low, high = jnp.bfloat16, jnp.float32
    (rows, activated, _, _, _, first_sum, _, _, projected, probs, _, _, inner, outer) = kept
    tokens, width = rows.shape
    hidden = activated.shape[1]
    unit = outer.shape
    lines = unit[3]
    own_rows = lines // SUBS
    dma, regular = pltpu.SemaphoreType.DMA, pltpu.SemaphoreType.REGULAR
    nets = 3 * SUBS + 1
    scratch = [
        pltpu.VMEM(unit, low),
        pltpu.VMEM(unit, low),
        pltpu.VMEM(unit, low),
        pltpu.VMEM((2 * SUBS, tokens, width), low),
        pltpu.VMEM((4, depth, lines, width), low),
        pltpu.VMEM((2, 2, depth, lines, width), low),
        pltpu.VMEM((2, depth, lines, width), low),
        pltpu.VMEM((2, depth - 1, lines, width), low),
        pltpu.VMEM((tokens, width), low),
        pltpu.VMEM((tokens, width), low),
        pltpu.VMEM((tokens, width), high),
        pltpu.VMEM((tokens, width), high),
        pltpu.VMEM((tokens, width), low),
        pltpu.VMEM(projected.shape, low),
        pltpu.VMEM(probs.shape, low),
        pltpu.VMEM((tokens, width), low),
        pltpu.VMEM((8, width), high),
        pltpu.VMEM((1, hidden), high),
        pltpu.VMEM((4, depth, 2, 16, 128), high),
        pltpu.VMEM((4, depth, 16, 128), high),
        pltpu.VMEM((1, 2, depth, 16, 128), high),
        pltpu.VMEM((1, depth, 16, 128), high),
        pltpu.VMEM((1, depth - 1, 16, 128), high),
        dma((40,)),
        dma,
        dma((nets, 4)), dma((nets, 4)), dma((nets, 2)), dma((nets, 2)), dma((nets,)), dma((nets,)),
        dma((nets, depth - 1)), dma((nets, depth - 1)),
        regular((4, SUBS)), regular((2, SUBS)), regular((SUBS,)), regular((SUBS, depth - 1)),
    ]
    shapes = [(tokens, width), (lines, width), (own_rows, hidden)] + [(own_rows, width)] * 4 + [(16, 128)]
    here = pl.BlockSpec(memory_space=pltpu.VMEM)
    away = pl.BlockSpec(memory_space=pl.ANY)
    return pl.pallas_call(
        functools.partial(backward_kernel, depth, block),
        out_shape=[jax.ShapeDtypeStruct(shape, high) for shape in shapes],
        in_specs=[here] * 2 + [away] * len(kept),
        out_specs=[away] + [here] * 7,
        scratch_shapes=scratch,
        compiler_params=pltpu.CompilerParams(
            collective_id=1, has_side_effects=True, vmem_limit_bytes=62 * 1024 * 1024
        ),
        name="backward",
    )(vectors, known, *kept)


def finish_kernel(block, *refs):
    count = 8
    table = refs[0]
    sources, targets = refs[1 : 1 + count], refs[1 + count : 1 + 2 * count]
    rows = refs[1 + 2 * count : 10 + 2 * count]
    held = refs[10 + 2 * count : 10 + 3 * count]
    in_sem, out_sem = refs[10 + 3 * count :]
    fetches = [pltpu.make_async_copy(source, target, in_sem.at[at]) for at, (source, target) in enumerate(zip(sources, held))]
    stores = [pltpu.make_async_copy(source, target, out_sem.at[at]) for at, (source, target) in enumerate(zip(held, targets))]
    for copy in fetches:
        copy.start()
    for index, row in enumerate(rows):
        row[...] = table[index, : row.shape[0]]
    for fetch, store in zip(fetches, stores):
        fetch.wait()
        store.start()
    for store in stores:
        store.wait()


def finish_all(block, table, arrays):
    shapes = [jax.ShapeDtypeStruct(array.shape, array.dtype) for array in arrays]
    shapes += [jax.ShapeDtypeStruct((block,), jnp.float32)] * 8 + [jax.ShapeDtypeStruct((128,), jnp.float32)]
    here = pl.BlockSpec(memory_space=pltpu.VMEM)
    away = pl.BlockSpec(memory_space=pltpu.HBM)
    dma = pltpu.SemaphoreType.DMA
    return pl.pallas_call(
        functools.partial(finish_kernel, block),
        out_shape=shapes,
        in_specs=[here] + [away] * len(arrays),
        out_specs=[away] * len(arrays) + [here] * 9,
        scratch_shapes=[pltpu.VMEM(array.shape, array.dtype) for array in arrays] + [dma((len(arrays),))] * 2,
        compiler_params=pltpu.CompilerParams(vmem_limit_bytes=60 * 1024 * 1024),
        name="finish",
    )(table, *arrays)


def normalize(hidden, gain, shift):
    center = hidden - jnp.mean(hidden, axis=-1, keepdims=True)
    spread = jnp.mean(center * center, axis=-1, keepdims=True)
    return center * lax.rsqrt(spread + epsilon) * gain + shift


def exact_gelu(value):
    return jax.nn.gelu(value, approximate=False)


def contract_rows(left, right):
    return lax.dot_general(
        left, right, (((0,), (0,)), ((), ())), preferred_element_type=jnp.float32
    )


def times_transposed(left, right):
    return lax.dot_general(
        left, right, (((1,), (1,)), ((), ())), preferred_element_type=jnp.float32
    )


def collect(merged, attn, inner, outer, vectors, widened):
    return (
        lax.all_gather(merged, ("dp", "fsdp"), axis=0, tiled=True),
        lax.all_gather(attn, ("dp", "fsdp"), axis=0, tiled=True),
        lax.all_gather(inner, ("dp", "fsdp"), axis=0, tiled=True),
        lax.all_gather(outer, ("dp", "fsdp"), axis=0, tiled=True),
        lax.all_gather(vectors, ("dp", "fsdp"), axis=0, tiled=True),
        lax.all_gather(widened, ("dp", "fsdp"), axis=0, tiled=True),
    )


def reduce_grads(merged, attn, inner, outer, vectors, widened):
    return (
        lax.psum_scatter(merged, ("dp", "fsdp"), scatter_dimension=0, tiled=True),
        lax.psum_scatter(attn, ("dp", "fsdp"), scatter_dimension=0, tiled=True),
        lax.psum_scatter(inner, ("dp", "fsdp"), scatter_dimension=0, tiled=True),
        lax.psum_scatter(outer, ("dp", "fsdp"), scatter_dimension=0, tiled=True),
        lax.psum_scatter(vectors, ("dp", "fsdp"), scatter_dimension=0, tiled=True),
        lax.psum_scatter(widened, ("dp", "fsdp"), scatter_dimension=0, tiled=True),
    )


def split_heads(projected, segments):
    total_rows, triple = projected.shape
    width = triple // 3
    return projected.reshape(segments, total_rows // segments, 3, HEADS, width // HEADS)


def attention_probs(queries, keysets, keep, scale):
    scores = (
        jnp.einsum("sqhd,skhd->shqk", queries, keysets, preferred_element_type=jnp.float32) * scale
    )
    scores = jnp.where(keep[:, None, None, :] > 0, scores, neg_fill)
    peaks = jnp.max(scores, axis=-1, keepdims=True)
    raised = jnp.exp(scores - peaks)
    return raised / jnp.sum(raised, axis=-1, keepdims=True)


def forward_pass(rows, keep, weights):
    merged, attn, inner, outer, vectors, widened = weights
    vector_full = vectors.astype(jnp.float32)
    width = rows.shape[1]
    scale = (width // HEADS) ** (-0.5)
    merged_bias = jnp.concatenate(
        (vector_full[:, 0], jnp.zeros((width,), jnp.float32), vector_full[:, 1])
    )
    projected = (jnp.dot(rows, merged, preferred_element_type=jnp.float32) + merged_bias).astype(
        jnp.bfloat16
    )
    split = split_heads(projected, keep.shape[0])
    probs = attention_probs(split[:, :, 0], split[:, :, 1], keep, scale).astype(jnp.bfloat16)
    context = jnp.einsum(
        "shqk,skhd->sqhd", probs, split[:, :, 2], preferred_element_type=jnp.float32
    )
    context = context.reshape(rows.shape[0], width).astype(jnp.bfloat16)
    attended = jnp.dot(context, attn, preferred_element_type=jnp.float32) + vector_full[:, 2]
    first_sum = rows.astype(jnp.float32) + attended
    first_norm = normalize(first_sum, vector_full[:, 3], vector_full[:, 4])
    first_low = first_norm.astype(jnp.bfloat16)
    inner_act = jnp.dot(first_low, inner, preferred_element_type=jnp.float32) + widened.astype(
        jnp.float32
    )
    activated = exact_gelu(inner_act).astype(jnp.bfloat16)
    outer_act = jnp.dot(activated, outer, preferred_element_type=jnp.float32) + vector_full[:, 5]
    second_sum = first_norm + outer_act
    encoded = normalize(second_sum, vector_full[:, 6], vector_full[:, 7]).astype(jnp.bfloat16)
    return (encoded, (projected, context, first_sum, first_low, inner_act, activated, second_sum))


def backward_pass(rows, keep, cotangent, weights, kept):
    merged, attn, inner, outer, vectors, widened = weights
    projected, context, first_sum, first_low, inner_act, activated, second_sum = kept
    vector_full = vectors.astype(jnp.float32)
    width = rows.shape[1]
    scale = (width // HEADS) ** (-0.5)
    second_out, second_pull = jax.vjp(normalize, second_sum, vector_full[:, 6], vector_full[:, 7])
    second_grad, second_gain_g, second_shift_g = second_pull(cotangent.astype(jnp.float32))
    outer_low = second_grad.astype(jnp.bfloat16)
    outer_bias_g = jnp.sum(outer_low.astype(jnp.float32), axis=0)
    outer_weight_g = contract_rows(activated, outer_low)
    act_grad = times_transposed(outer_low, outer)
    gelu_out, gelu_pull = jax.vjp(exact_gelu, inner_act)
    inner_low = gelu_pull(act_grad)[0].astype(jnp.bfloat16)
    inner_bias_g = jnp.sum(inner_low.astype(jnp.float32), axis=0)
    inner_weight_g = contract_rows(first_low, inner_low)
    first_total = second_grad + times_transposed(inner_low, inner)
    first_out, first_pull = jax.vjp(normalize, first_sum, vector_full[:, 3], vector_full[:, 4])
    first_grad, first_gain_g, first_shift_g = first_pull(first_total)
    attended_low = first_grad.astype(jnp.bfloat16)
    attn_bias_g = jnp.sum(attended_low.astype(jnp.float32), axis=0)
    attn_weight_g = contract_rows(context, attended_low)
    context_low = times_transposed(attended_low, attn).astype(jnp.bfloat16)
    split = split_heads(projected, keep.shape[0])
    queries = split[:, :, 0]
    keysets = split[:, :, 1]
    valuesets = split[:, :, 2]
    probs = attention_probs(queries, keysets, keep, scale)
    probs_low = probs.astype(jnp.bfloat16)
    context_heads = context_low.reshape(queries.shape)
    prob_grad = jnp.einsum(
        "sqhd,skhd->shqk", context_heads, valuesets, preferred_element_type=jnp.float32
    )
    value_grad = jnp.einsum(
        "shqk,sqhd->skhd", probs_low, context_heads, preferred_element_type=jnp.float32
    )
    score_low = (probs * (prob_grad - jnp.sum(probs * prob_grad, axis=-1, keepdims=True))).astype(
        jnp.bfloat16
    )
    query_grad = (
        jnp.einsum("shqk,skhd->sqhd", score_low, keysets, preferred_element_type=jnp.float32)
        * scale
    )
    key_grad = (
        jnp.einsum("shqk,sqhd->skhd", score_low, queries, preferred_element_type=jnp.float32)
        * scale
    )
    merged_low = jnp.stack((query_grad, key_grad, value_grad), axis=2).astype(jnp.bfloat16)
    merged_low = merged_low.reshape(rows.shape[0], 3 * width)
    merged_weight_g = contract_rows(rows, merged_low)
    merged_bias_g = jnp.sum(merged_low.astype(jnp.float32), axis=0)
    states_part = first_grad + times_transposed(merged_low, merged)
    vector_grads = jnp.stack(
        (
            merged_bias_g[:width],
            merged_bias_g[2 * width :],
            attn_bias_g,
            first_gain_g,
            first_shift_g,
            outer_bias_g,
            second_gain_g,
            second_shift_g,
        ),
        axis=1,
    )
    return (
        states_part,
        (
            merged_weight_g,
            attn_weight_g,
            inner_weight_g,
            outer_weight_g,
            vector_grads,
            inner_bias_g,
        ),
    )


def shards(depth, *arrays):
    (states, pad_mask, query_proj, key_proj, value_proj, attn_proj, query_bias, value_bias, attn_bias, first_gain,
     first_shift, inner_proj, inner_bias, outer_proj, outer_bias, second_gain, second_shift, out_grad) = arrays
    width = states.shape[1]
    short = (query_bias, value_bias, attn_bias, first_gain, first_shift, outer_bias, second_gain, second_shift)
    if depth:
        return kernel_shards(depth, short, states, pad_mask, query_proj, key_proj, value_proj, attn_proj, inner_proj,
                             inner_bias, outer_proj, out_grad)
    merged_shard = jnp.concatenate((query_proj, key_proj, value_proj), axis=1)
    fetched = collect(merged_shard, attn_proj, inner_proj, outer_proj, jnp.stack(short, axis=1), inner_bias)
    encoded, kept = forward_pass(states, pad_mask, fetched)
    states_part, totals = backward_pass(states, pad_mask, out_grad, fetched, kept)
    merged_sum, attn_sum, inner_sum, outer_sum, vector_sum, widened_sum = reduce_grads(*totals)
    return ordered(encoded, states_part, merged_sum, attn_sum, inner_sum, outer_sum, vector_sum.T, widened_sum)


def ordered(encoded, states_part, merged_sum, attn_sum, inner_sum, outer_sum, vectors, widened_sum):
    width = attn_sum.shape[1]
    return (encoded, states_part, merged_sum[:, :width], merged_sum[:, width : 2 * width], merged_sum[:, 2 * width :],
            attn_sum, vectors[0], vectors[1], vectors[2], vectors[3], vectors[4], inner_sum, widened_sum, outer_sum,
            vectors[5], vectors[6], vectors[7])


def kernel_shards(depth, short, states, pad_mask, query_proj, key_proj, value_proj, attn_proj, inner_proj, inner_bias,
                  outer_proj, out_grad):
    width = states.shape[1]
    block = short[0].shape[0]
    (merged, attn, inner, outer, encoded, projected, probs, context, first_sum, first_low, activated, slope, second_grad,
     outer_low, vectors, sums) = forward_all(
        depth, block, states, pad_mask, out_grad,
        (query_proj, key_proj, value_proj, attn_proj, inner_proj, outer_proj, *short, inner_bias))
    states_part, outer_sum, inner_sum, query_sum, key_sum, value_sum, attn_sum, table_sum = backward_all(
        depth, block, vectors, sums,
        (states, activated, slope, outer_low, second_grad, first_sum, first_low, context, projected, probs,
         merged.reshape(width, -1), attn.reshape(width, -1), inner, outer))
    (encoded, states_part, query_sum, key_sum, value_sum, attn_sum, inner_sum, outer_sum, *rows) = finish_all(
        block, table_sum, (encoded, states_part, query_sum, key_sum, value_sum, attn_sum, inner_sum, outer_sum))
    return (encoded, states_part, query_sum, key_sum, value_sum, attn_sum, *rows[:5], inner_sum, rows[8], outer_sum,
            *rows[5:8])


def solution(mesh):
    dps, others = mesh.shape["dp"], mesh.shape["fsdp"]
    matrix = P(("dp", "fsdp"), None)
    vector = P(("dp", "fsdp"))

    def whole(*arrays):
        rows = arrays[2].shape[0] // (dps * others)
        tiles = rows % 16 == 0 and arrays[12].shape[0] == 128 * dps * others
        depth = others // 2 if tiles and dps == 4 and others == 2 * dps else 0
        return jax.shard_map(
            functools.partial(shards, depth),
            mesh=mesh,
            in_specs=(matrix,) * 6 + (vector,) * 5 + (matrix, vector, matrix) + (vector,) * 3 + (matrix,),
            out_specs=(matrix,) * 6 + (vector,) * 5 + (matrix, vector, matrix) + (vector,) * 3,
            check_vma=False,
        )(*arrays)

    return whole
```

```python
import functools

import jax
import jax.numpy as jnp
from jax import lax
from jax.experimental import pallas as pl
from jax.experimental.pallas import tpu as pltpu
from jax.sharding import PartitionSpec as P

HEADS = 16
MESH = pl.DeviceIdType.MESH

epsilon = 1e-05
neg_fill = -1e30


class Place:
    def __init__(self, depth):
        dp = lax.axis_index("dp")
        fsdp = lax.axis_index("fsdp")
        self.depth = depth
        self.dp = dp
        self.z = fsdp // 2
        self.core = lax.rem(fsdp, 2)
        flip_x = dp + 1 - 2 * lax.rem(dp, 2)
        flip_y = lax.rem(dp + 2, 4)
        self.near = flip_x + self.core * (flip_y - flip_x)
        self.far = flip_y + self.core * (flip_x - flip_y)
        self.both = lax.rem(flip_x + 2, 4)
        self.fsdp = fsdp
        self.sibling = fsdp + 1 - 2 * self.core
        self.pair = self.z + 1 - 2 * lax.rem(self.z, 2)
        self.jump = self.up(2)
        self.cross = 3 - self.z

    def up(self, step):
        return lax.rem(self.z + step, self.depth)

    def down(self, step):
        return lax.rem(self.z + self.depth - step, self.depth)

    def along(self, z):
        return (self.dp, z * 2 + self.core)

    def greet(self):
        barrier = pltpu.get_barrier_semaphore()
        others = [self.along(self.up(step)) for step in range(1, self.depth)]
        others += [(self.near, self.fsdp), (self.far, self.fsdp), (self.dp, self.sibling)]
        for other in others:
            pl.semaphore_signal(barrier, inc=1, device_id=other, device_id_type=MESH)

    def greeted(self):
        pl.semaphore_wait(pltpu.get_barrier_semaphore(), self.depth + 2)


def remote(source, target, send, recv, device):
    return pltpu.make_async_remote_copy(
        src_ref=source, dst_ref=target, send_sem=send, recv_sem=recv, device_id=device, device_id_type=MESH
    )


class Gather:
    def __init__(self, place, full, own, sems, piece, lines=None):
        self.lines = pl.ds(0, full.shape[3]) if lines is None else lines
        self.place, self.full, self.own, self.piece = place, full, own.at[self.lines], piece
        self.su, self.ru, self.sd, self.rd, self.sb, self.rb, self.sa, self.ra, self.sc, self.rc, self.so = sems

    def copy_own(self):
        p = self.place
        return pltpu.make_async_copy(self.own, self.full.at[p.dp, p.z, p.core, self.lines], self.so.at[self.piece])

    def copy_up(self, z, first=False):
        p = self.place
        block = self.full.at[p.dp, z, p.core, self.lines]
        source = self.own if first else block
        return remote(source, block, self.su.at[self.piece, z], self.ru.at[self.piece, z], p.along(p.z + 1))

    def copy_down(self, z, first=False):
        p = self.place
        block = self.full.at[p.dp, z, p.core, self.lines]
        source = self.own if first else block
        return remote(source, block, self.sd.at[self.piece, z], self.rd.at[self.piece, z], p.along(p.z - 1))

    def copy_near(self, z, first=False, arriving=False):
        p = self.place
        block = self.full.at[p.near if arriving else p.dp, z, p.core, self.lines]
        source = self.own if first else block
        return remote(source, block, self.sb.at[self.piece, z], self.rb.at[self.piece, z], (p.near, p.fsdp))

    def copy_far(self, half, z, first=False, arriving=False):
        p = self.place
        row = (p.both if half else p.far) if arriving else (p.near if half else p.dp)
        block = self.full.at[row, z, p.core, self.lines]
        source = self.own if first else block
        at = half * p.depth + z
        return remote(source, block, self.sa.at[self.piece, at], self.ra.at[self.piece, at], (p.far, p.fsdp))

    def copy_core(self, part, arriving=False):
        p = self.place
        if arriving:
            row = (p.dp, p.far, p.near, p.both)[part]
            block = self.full.at[row, :, 1 - p.core, self.lines]
        else:
            row = (p.dp, p.near, p.far, p.both)[part]
            block = self.full.at[row, :, p.core, self.lines]
        return remote(block, block, self.sc.at[self.piece, part], self.rc.at[self.piece, part], (p.dp, p.sibling))

    def start(self):
        p = self.place
        pl.when(p.z < p.depth - 1)(lambda: self.copy_up(p.z, True).start())
        pl.when(p.z > 0)(lambda: self.copy_down(p.z, True).start())
        self.copy_own().start()

    def send(self, step):
        p = self.place

        def act(z, first=False):
            self.copy_near(z, first).start()
            self.copy_far(0, z, first).start()

        if step == 0:
            act(p.z, True)
        else:
            pl.when(p.z >= step)(lambda: act(p.z - step))
            pl.when(p.z + step < p.depth)(lambda: act(p.z + step))

    def hop(self, step):
        p = self.place

        @pl.when(p.z >= step)
        def _():
            z = p.z - step
            self.copy_up(z).wait_recv()
            pl.when(p.z < p.depth - 1)(lambda: self.copy_up(z).start())

        @pl.when(p.z + step < p.depth)
        def _():
            z = p.z + step
            self.copy_down(z).wait_recv()
            pl.when(p.z > 0)(lambda: self.copy_down(z).start())

    def last_hop(self):
        self.hop(self.place.depth - 1)
        self.copy_own().wait()
        self.copy_core(0).start()

    def spread(self, step):
        p = self.place

        def act(z):
            self.copy_near(z, arriving=True).wait_recv()
            self.copy_far(1, z).start()

        if step == 0:
            act(p.z)
        else:
            pl.when(p.z >= step)(lambda: act(p.z - step))
            pl.when(p.z + step < p.depth)(lambda: act(p.z + step))
        if step == p.depth - 1:
            self.copy_core(1).start()

    def arrive_far(self, half):
        p = self.place
        for z in range(p.depth):
            self.copy_far(half, z, arriving=True).wait_recv()
        self.copy_core(2 + half).start()

    def arrive_core(self, *parts):
        for part in parts:
            self.copy_core(part, arriving=True).wait_recv()

    def drain(self):
        p = self.place
        for z in range(p.depth):
            pl.when((p.z < p.depth - 1) & (z <= p.z))(lambda: self.copy_up(z).wait_send())
            pl.when((p.z > 0) & (z >= p.z))(lambda: self.copy_down(z).wait_send())
            self.copy_near(z).wait_send()
            self.copy_far(0, z).wait_send()
            self.copy_far(1, z).wait_send()
        for part in range(4):
            self.copy_core(part).wait_send()


class GatherLine:
    def __init__(self, place, full, own, sems, piece, lines):
        self.place, self.full, self.own, self.piece, self.lines = place, full, own.at[lines], piece, lines
        self.sj, self.rj, self.sp, self.rp, self.sb, self.rb, self.sa, self.ra, self.sc, self.rc, self.so = sems

    def block(self, row):
        return self.full.at[row, self.place.z, self.place.core, self.lines]

    def column(self, z, core):
        return self.full.at[:, z, core, self.lines]

    def copy_own(self):
        return pltpu.make_async_copy(self.own, self.block(self.place.dp), self.so.at[self.piece])

    def copy_near(self, arriving=False):
        p = self.place
        target = self.block(p.near if arriving else p.dp)
        return remote(self.own, target, self.sb.at[self.piece, 0], self.rb.at[self.piece, 0], (p.near, p.fsdp))

    def copy_far(self, half, arriving=False):
        p = self.place
        target = self.block((p.both if half else p.far) if arriving else (p.near if half else p.dp))
        source = target if half else self.own
        return remote(source, target, self.sa.at[self.piece, half], self.ra.at[self.piece, half], (p.far, p.fsdp))

    def copy_jump(self, arriving=False):
        p = self.place
        column = self.column(p.jump if arriving else p.z, p.core)
        return remote(column, column, self.sj.at[self.piece, 0], self.rj.at[self.piece, 0], p.along(p.jump))

    def copy_pair(self, part, arriving=False):
        p = self.place
        z = (p.cross if part else p.pair) if arriving else (p.jump if part else p.z)
        column = self.column(z, p.core)
        return remote(column, column, self.sp.at[self.piece, part], self.rp.at[self.piece, part], p.along(p.pair))

    def copy_core(self, part, arriving=False):
        p = self.place
        column = self.column((p.z, p.jump, p.pair, p.cross)[part], 1 - p.core if arriving else p.core)
        return remote(column, column, self.sc.at[self.piece, part], self.rc.at[self.piece, part], (p.dp, p.sibling))

    def start(self):
        self.copy_near().start()
        self.copy_far(0).start()
        self.copy_own().start()

    def spread(self):
        self.copy_near(arriving=True).wait_recv()
        self.copy_far(1).start()

    def join(self):
        self.copy_own().wait()
        for half in range(2):
            self.copy_far(half, arriving=True).wait_recv()
        self.copy_jump().start()
        self.copy_pair(0).start()
        self.copy_core(0).start()

    def relay(self):
        self.copy_jump(arriving=True).wait_recv()
        self.copy_pair(1).start()
        self.copy_core(1).start()

    def arrive(self):
        for part in range(2):
            self.copy_pair(part, arriving=True).wait_recv()
            self.copy_core(2 + part).start()

    def arrive_core(self):
        for part in range(4):
            self.copy_core(part, arriving=True).wait_recv()

    def drain(self):
        self.copy_near().wait_send()
        self.copy_jump().wait_send()
        for part in range(2):
            self.copy_far(part).wait_send()
            self.copy_pair(part).wait_send()
        for part in range(4):
            self.copy_core(part).wait_send()


def gather_sems(pieces, depth):
    dma = pltpu.SemaphoreType.DMA
    counts = (depth, depth, depth, depth, depth, depth, 2 * depth, 2 * depth, 4, 4)
    return [dma((pieces, count)) for count in counts] + [dma((pieces,))]


def matmul(left, right):
    return lax.dot_general(left, right, (((1,), (0,)), ((), ())), preferred_element_type=jnp.float32)


def matmul_nt(left, right):
    return lax.dot_general(left, right, (((1,), (1,)), ((), ())), preferred_element_type=jnp.float32)


def matmul_tn(left, right):
    return lax.dot_general(left, right, (((0,), (0,)), ((), ())), preferred_element_type=jnp.float32)


def flat(value):
    return value.reshape(-1, value.shape[-1])


def span(index, size):
    return pl.ds(pl.multiple_of(index * size, size), size)


def unpack_table(table, block, vectors, long_bias):
    dps, depth, cores = table.shape[:3]
    places = dps * depth * cores
    width = vectors.shape[1]
    lane = lax.broadcasted_iota(jnp.int32, (128, width), 1)
    source = lax.broadcasted_iota(jnp.int32, (128, width), 0)
    pick = jnp.where(source == lax.rem(lane, block), 1.0, 0.0).astype(jnp.bfloat16)
    owner = lax.broadcasted_iota(jnp.int32, (places, width), 1) // block
    mine = owner == lax.broadcasted_iota(jnp.int32, (places, width), 0)
    blocks = [table[:, :, :, vector, :].reshape(places, 128) for vector in range(8)]
    spread = matmul(jnp.concatenate(blocks, axis=0).astype(jnp.bfloat16), pick)
    for vector in range(8):
        own = jnp.where(mine, spread[vector * places : (vector + 1) * places], 0.0)
        vectors[vector : vector + 1, :] = jnp.sum(own, axis=0, keepdims=True)
    for index in range(places):
        dp, z, core = index // (depth * cores), index // cores % depth, index % cores
        long_bias[:, index * 128 : (index + 1) * 128] = table[dp, z, core, 8:9, :]


CHUNK = 256


def project(rows, weights, vectors, projected):
    chunks = rows.shape[1] // CHUNK
    for part, bias in ((0, 0), (1, None), (2, 1)):

        def one(index, _):
            at = span(part * chunks + index, CHUNK)
            total = matmul(rows[...], flat(weights[:, :, :, :, at]))
            if bias is not None:
                total = total + vectors[bias : bias + 1, span(index, CHUNK)]
            projected[:, at] = total.astype(jnp.bfloat16)
            return 0

        lax.fori_loop(0, chunks, one, 0)


def head_lanes(heads, rows, size):
    lane = lax.broadcasted_iota(jnp.int32, (rows, heads * size), 1) // size
    return [lane == head for head in range(heads)]


def stack_heads(value, lanes):
    return jnp.concatenate([jnp.where(lane, value, jnp.zeros_like(value)) for lane in lanes], axis=0)


def merge_heads(value, lanes):
    rows = value.shape[0] // len(lanes)
    result = value[:rows]
    for head in range(1, len(lanes)):
        result = jnp.where(lanes[head], value[head * rows : (head + 1) * rows], result)
    return result


QUAD = 4


def attend(projected, keep, probs, context, first, last):
    width = context.shape[1]
    size = width // HEADS
    length = keep.shape[1]
    scale = size ** (-0.5)
    lanes = head_lanes(QUAD, length, size)
    quads = HEADS // QUAD

    def one(index, _):
        segment = index // quads
        quad = lax.rem(index, quads)
        at = span(segment, length)
        queries = projected[at, span(quad, QUAD * size)]
        keysets = projected[at, span(quad + quads, QUAD * size)]
        valuesets = projected[at, span(quad + 2 * quads, QUAD * size)]
        scores = matmul_nt(stack_heads(queries, lanes), keysets) * scale
        mask = keep[pl.ds(segment, 1), :] > 0
        scores = jnp.where(mask, scores, neg_fill)
        raised = jnp.exp(scores - jnp.max(scores, axis=1, keepdims=True))
        low = (raised / jnp.sum(raised, axis=1, keepdims=True)).astype(jnp.bfloat16)
        probs[index] = low
        context[at, span(quad, QUAD * size)] = merge_heads(matmul(low, valuesets), lanes).astype(jnp.bfloat16)
        return 0

    lax.fori_loop(first, last, one, 0)


def center_scale(hidden):
    center = hidden - jnp.mean(hidden, axis=1, keepdims=True)
    spread = jnp.mean(center * center, axis=1, keepdims=True)
    rate = lax.rsqrt(spread + epsilon)
    return center * rate, rate


def first_block(rows, context, weights, vectors, first_sum, first_norm, first_low):
    def product(index, _):
        at = span(index, CHUNK)
        attended = matmul(context[...], flat(weights[:, :, :, :, at])) + vectors[2:3, at]
        first_sum[:, at] = rows[:, at].astype(jnp.float32) + attended
        return 0

    lax.fori_loop(0, rows.shape[1] // CHUNK, product, 0)

    def one(index, _):
        at = span(index, 64)
        normed, _ = center_scale(first_sum[at, :])
        result = normed * vectors[3:4, :] + vectors[4:5, :]
        first_norm[at, :] = result
        first_low[at, :] = result.astype(jnp.bfloat16)
        return 0

    lax.fori_loop(0, rows.shape[0] // 64, one, 0)


def inner_block(first_low, weights, long_bias, activated, slope, first, last):
    def one(index, _):
        at = span(index, CHUNK)
        value = matmul(first_low[...], flat(weights[:, :, :, :, at])) + long_bias[:, at]
        share = 0.5 * (1.0 + lax.erf(value * (0.5**0.5)))
        bell = jnp.exp(-0.5 * value * value) * ((0.5 / jnp.pi) ** 0.5)
        activated[:, at] = (value * share).astype(jnp.bfloat16)
        slope[:, at] = (share + value * bell).astype(jnp.bfloat16)
        return 0

    lax.fori_loop(first, last, one, 0)


def outer_part(activated, weights, row, total, fresh):
    size = weights.shape[1] * weights.shape[2] * weights.shape[3]

    def one(index, _):
        at = span(index, CHUNK)
        value = matmul(activated[:, span(row, size)], flat(weights[row, :, :, :, at]))
        total[:, at] = value if fresh else total[:, at] + value
        return 0

    lax.fori_loop(0, total.shape[1] // CHUNK, one, 0)


def norm_back(grad, normed, rate, gain):
    scaled = grad * gain
    mean = jnp.mean(scaled, axis=1, keepdims=True)
    along = jnp.mean(scaled * normed, axis=1, keepdims=True)
    return rate * (scaled - mean - normed * along)


def second_block(first_norm, total, cotangent, vectors, encoded, second_grad, outer_low, sums, first, last):

    def one(index, _):
        at = span(index, 64)
        normed, rate = center_scale(first_norm[at, :] + (total[at, :] + vectors[5:6, :]))
        gain = vectors[6:7, :]
        encoded[at, :] = (normed * gain + vectors[7:8, :]).astype(jnp.bfloat16)
        grad = cotangent[at, :].astype(jnp.float32)
        back = norm_back(grad, normed, rate, gain)
        low = back.astype(jnp.bfloat16)
        second_grad[at, :] = back
        outer_low[at, :] = low
        sums[5:6, :] += jnp.sum(low.astype(jnp.float32), axis=0, keepdims=True)
        sums[6:7, :] += jnp.sum(grad * normed, axis=0, keepdims=True)
        sums[7:8, :] += jnp.sum(grad, axis=0, keepdims=True)
        return 0

    lax.fori_loop(first, last, one, 0)


def forward_kernel(depth, block, *refs):
    (rows_in, keep, cotangent_in, query_own, key_own, value_own, attn_own, inner_own, outer_own) = refs[:9]
    short_vectors = refs[9:18]
    merged_out, attn_out, inner_out, outer_out = refs[18:22]
    (encoded_out, projected_out, probs_out, context_out, first_sum_out, first_low_out, activated_out, slope_out,
     second_grad_out, outer_low_out, vectors, sums) = refs[22:34]
    (table_own, merged_own, table, merged, attn, inner, outer, projected, probs, context, first_sum, first_norm, first_low,
     activated, slope, total, encoded, second_grad, outer_low, long_bias, save_sem, rows, cotangent, load_sem) = refs[34:58]
    sems = refs[58:]
    place = Place(depth)
    place.greet()
    loads = [
        pltpu.make_async_copy(rows_in, rows, load_sem.at[0]),
        pltpu.make_async_copy(cotangent_in, cotangent, load_sem.at[1]),
    ]
    table_own[...] = jnp.zeros_like(table_own)
    for index, vector in enumerate(short_vectors):
        table_own[index, : vector.shape[0]] = vector[...].astype(jnp.float32)
    width = rows.shape[1]
    for part, own in enumerate((query_own, key_own, value_own)):
        merged_own[:, part * width : (part + 1) * width] = own[...]
    net_table = Gather(place, table, table_own, sems, 0)
    net_merged = Gather(place, merged, merged_own, sems, 1)
    net_attn = Gather(place, attn, attn_own, sems, 2)
    net_inner = Gather(place, inner, inner_own, sems, 3)
    half = outer.shape[3] // 2
    net_outer = Gather(place, outer, outer_own, sems, 4, pl.ds(0, half))
    line = GatherLine(place, outer, outer_own, sems, 5, pl.ds(half, half))
    nets = (net_table, net_merged, net_attn, net_inner, net_outer, line)
    front = nets[:3]
    place.greeted()
    for copy in loads:
        copy.start()
    saves = []

    def save(source, target):
        copy = pltpu.make_async_copy(source, target, save_sem.at[len(saves)])
        copy.start()
        saves.append(copy)

    def hop(net, step):
        if step == depth - 1:
            net.last_hop()
        else:
            net.hop(step)

    def each(nets_of, *names, step):
        for name in names:
            for net in nets_of:
                hop(net, step) if name == "hop" else getattr(net, name)(step)

    for net in front:
        net.start()
    each(front, "send", step=0)
    line.start()
    each(front, "hop", "send", step=1)
    line.spread()
    net_inner.start()
    each(front, "spread", step=0)
    for step in range(2, depth):
        each(front, "hop", "send", step=step)
        each(front, "spread", step=step - 1)
    net_inner.send(0)
    net_outer.start()
    net_inner.hop(1)
    net_inner.send(1)
    each(front, "spread", step=depth - 1)
    net_inner.spread(0)
    net_outer.hop(1)
    for step in range(2, depth - 1):
        net_inner.hop(step)
        net_inner.send(step)
        net_inner.spread(step - 1)
    line.join()
    for net in front:
        net.arrive_far(0)
        net.arrive_far(1)
        net.arrive_core(0, 1, 2, 3)
    save(merged, merged_out)
    save(attn, attn_out)
    unpack_table(table, block, vectors, long_bias)
    loads[0].wait()
    project(rows, merged, vectors, projected)
    save(projected, projected_out)
    for step in range(2, depth - 1):
        net_outer.hop(step)
    net_inner.last_hop()
    net_inner.send(depth - 1)
    net_inner.spread(depth - 2)
    line.relay()
    count = probs.shape[0]
    attend(projected, keep, probs, context, 0, count // 2)
    net_outer.last_hop()
    net_inner.spread(depth - 1)
    attend(projected, keep, probs, context, count // 2, count)
    save(probs, probs_out)
    save(context, context_out)
    first_block(rows, context, attn, vectors, first_sum, first_norm, first_low)
    save(first_sum, first_sum_out)
    save(first_low, first_low_out)
    net_inner.arrive_far(0)
    for step in range(depth):
        net_outer.send(step)
    net_inner.arrive_far(1)
    net_inner.arrive_core(0, 1, 2, 3)
    save(inner, inner_out)
    quarter = inner.shape[4] // CHUNK // 4

    def inner_quarter(index):
        inner_block(first_low, inner, long_bias, activated, slope, index * quarter, (index + 1) * quarter)

    inner_quarter(0)
    net_outer.spread(0)
    inner_quarter(1)
    for step in range(1, depth - 1):
        net_outer.spread(step)
    inner_quarter(2)
    net_outer.spread(depth - 1)
    line.arrive()
    inner_quarter(3)
    save(activated, activated_out)
    save(slope, slope_out)
    sums[...] = jnp.zeros_like(sums)
    loads[1].wait()
    line.arrive_core()
    net_outer.arrive_core(0)
    outer_part(activated, outer, place.dp, total, True)
    net_outer.arrive_far(0)
    net_outer.arrive_core(1, 2)
    outer_part(activated, outer, place.near, total, False)
    outer_part(activated, outer, place.far, total, False)
    net_outer.arrive_far(1)
    net_outer.arrive_core(3)
    save(outer, outer_out)
    outer_part(activated, outer, place.both, total, False)
    for part in range(4):
        size = rows.shape[0] // 4
        second_block(
            first_norm, total, cotangent, vectors, encoded, second_grad, outer_low, sums, part * size // 64,
            (part + 1) * size // 64,
        )
        at = pl.ds(part * size, size)
        save(outer_low.at[at], outer_low_out.at[at])
        save(second_grad.at[at], second_grad_out.at[at])
        save(encoded.at[at], encoded_out.at[at])
    for net in nets:
        net.drain()
    for copy in saves:
        copy.wait()


def forward_all(depth, block, rows, keep, cotangent, owns):
    query_own, _, _, attn_own, inner_own, outer_own = owns[:6]
    tokens, width = rows.shape
    hidden = inner_own.shape[1]
    segments, length = keep.shape
    low, high = jnp.bfloat16, jnp.float32

    def fulls(own, columns):
        return (4, depth, 2, own.shape[0], columns)

    full_shapes = [fulls(query_own, 3 * width), fulls(attn_own, width), fulls(inner_own, hidden), fulls(outer_own, width)]
    kept = [
        ((tokens, width), low),
        ((tokens, 3 * width), low),
        ((segments * HEADS // QUAD, QUAD * length, length), low),
        ((tokens, width), low),
        ((tokens, width), high),
        ((tokens, width), low),
        ((tokens, hidden), low),
        ((tokens, hidden), low),
        ((tokens, width), high),
        ((tokens, width), low),
    ]
    small = [((8, width), high), ((8, width), high)]
    shapes = [jax.ShapeDtypeStruct(shape, low) for shape in full_shapes]
    shapes += [jax.ShapeDtypeStruct(*one) for one in kept + small]
    held = {name: pltpu.VMEM(*one) for name, one in zip(
        ("encoded", "projected", "probs", "context", "first_sum", "first_low", "activated", "slope", "second_grad", "outer_low"),
        kept)}
    scratch = [pltpu.VMEM((16, 128), high), pltpu.VMEM((query_own.shape[0], 3 * width), low)]
    scratch += [pltpu.VMEM((4, depth, 2, 16, 128), high)]
    scratch += [pltpu.VMEM(shape, low) for shape in full_shapes]
    scratch += [held[name] for name in ("projected", "probs", "context", "first_sum")]
    scratch += [pltpu.VMEM((tokens, width), high)]
    scratch += [held[name] for name in ("first_low", "activated", "slope")]
    scratch += [pltpu.VMEM((tokens, width), high)]
    scratch += [held[name] for name in ("encoded", "second_grad", "outer_low")]
    scratch += [pltpu.VMEM((1, hidden), high)]
    scratch += [pltpu.SemaphoreType.DMA((len(full_shapes) + len(kept) + 9,))]
    scratch += [pltpu.VMEM((tokens, width), low), pltpu.VMEM((tokens, width), low), pltpu.SemaphoreType.DMA((2,))]
    here = pl.BlockSpec(memory_space=pltpu.VMEM)
    away = pl.BlockSpec(memory_space=pl.ANY)
    return pl.pallas_call(
        functools.partial(forward_kernel, depth, block),
        out_shape=shapes,
        in_specs=[away, here, away] + [here] * len(owns),
        out_specs=[away] * (len(full_shapes) + len(kept)) + [here] * 2,
        scratch_shapes=scratch + gather_sems(6, depth),
        compiler_params=pltpu.CompilerParams(
            collective_id=0, has_side_effects=True, vmem_limit_bytes=60 * 1024 * 1024
        ),
        name="forward",
    )(rows, keep, cotangent, *owns)


SUBS = 4


class Slots:
    def __init__(self, core, far, near, along):
        self.core, self.far, self.near, self.along = core, far, near, along


class Scatter:
    def __init__(self, place, whole, slots, sems, credits, number, lot, first, count, after=False, before=False,
                 late_after=False, late_before=False):
        self.place, self.whole, self.slots = place, whole, slots
        self.sc, self.rc, self.sa, self.ra, self.sb, self.rb, self.sz, self.rz = sems
        self.core_free, self.far_free, self.near_free, self.z_free = credits
        self.number, self.lot, self.first, self.count = number, lot, first, count
        self.sub = first * SUBS // whole.shape[3]
        self.after, self.before, self.late_after, self.late_before = after, before, late_after, late_before
        self.tile = 8 if whole.dtype == jnp.float32 else 16

    def lines(self):
        return pl.ds(self.first, self.count)

    def mine(self, row):
        return self.whole.at[row, :, self.place.core, self.lines()]

    def sent_row(self, at):
        p = self.place
        return (p.both, p.near, p.far, p.dp)[at]

    def got_row(self, at):
        p = self.place
        return (p.both, p.far, p.near, p.dp)[at]

    def copy_core(self, at):
        p = self.place
        return remote(
            self.whole.at[self.sent_row(at), :, 1 - p.core, self.lines()], self.slots.core.at[at, :, self.lines()],
            self.sc.at[self.number, at], self.rc.at[self.number, at], (p.dp, p.sibling),
        )

    def copy_far(self, half):
        p = self.place
        return remote(
            self.mine(p.both if half else p.far), self.slots.far.at[self.lot, half, :, self.lines()],
            self.sa.at[self.number, half], self.ra.at[self.number, half], (p.far, p.fsdp),
        )

    def copy_near(self):
        p = self.place
        return remote(
            self.mine(p.near), self.slots.near.at[self.lot, :, self.lines()], self.sb.at[self.number],
            self.rb.at[self.number], (p.near, p.fsdp),
        )

    def copy_z(self, step):
        p = self.place
        return remote(
            self.whole.at[p.dp, p.up(step), p.core, self.lines()], self.slots.along.at[self.lot, step - 1, self.lines()],
            self.sz.at[self.number, step - 1], self.rz.at[self.number, step - 1], p.along(p.up(step)),
        )

    def add(self, row, slot):
        p = self.place
        tiles = self.count // self.tile

        def one(index, _):
            z = index // tiles
            at = pl.ds(pl.multiple_of(self.first + lax.rem(index, tiles) * self.tile, self.tile), self.tile)
            self.whole[row, z, p.core, at, :] = self.whole[row, z, p.core, at, :] + slot[z, at, :]
            return 0

        lax.fori_loop(0, p.depth * tiles, one, 0)

    def start_core(self, at):
        if self.after:
            pl.semaphore_wait(self.core_free.at[at, self.sub], 1)
        self.copy_core(at).start()

    def add_core(self, at):
        p = self.place
        self.copy_core(at).wait_recv()
        self.add(self.got_row(at), self.slots.core.at[at])
        if self.before:
            pl.semaphore_signal(self.core_free.at[at, self.sub], inc=1, device_id=(p.dp, p.sibling), device_id_type=MESH)

    def start_far(self, half):
        if self.late_after:
            pl.semaphore_wait(self.far_free.at[half, self.sub], 1)
        self.copy_far(half).start()

    def add_far(self, half):
        p = self.place
        self.copy_far(half).wait_recv()
        self.add(p.near if half else p.dp, self.slots.far.at[self.lot, half])
        if self.late_before:
            pl.semaphore_signal(self.far_free.at[half, self.sub], inc=1, device_id=(p.far, p.fsdp), device_id_type=MESH)
        if half:
            if self.late_after:
                pl.semaphore_wait(self.near_free.at[self.sub], 1)
            self.copy_near().start()

    def add_near(self):
        p = self.place
        self.copy_near().wait_recv()
        self.add(p.dp, self.slots.near.at[self.lot])
        if self.late_before:
            pl.semaphore_signal(self.near_free.at[self.sub], inc=1, device_id=(p.near, p.fsdp), device_id_type=MESH)
        for step in range(1, p.depth):
            if self.late_after:
                pl.semaphore_wait(self.z_free.at[self.sub, step - 1], 1)
            self.copy_z(step).start()

    def finish(self, out):
        p = self.place
        for step in range(1, p.depth):
            self.copy_z(step).wait_recv()

        def one(index, _):
            start = pl.multiple_of(index * self.tile, self.tile)
            at = pl.ds(pl.multiple_of(self.first + start, self.tile), self.tile)
            total = self.whole[p.dp, p.z, p.core, at, :].astype(jnp.float32)
            for step in range(p.depth - 1):
                total = total + self.slots.along[self.lot, step, at, :].astype(jnp.float32)
            out[pl.ds(start, self.tile), :] = total
            return 0

        lax.fori_loop(0, self.count // self.tile, one, 0)
        if self.late_before:
            for step in range(1, p.depth):
                pl.semaphore_signal(
                    self.z_free.at[self.sub, step - 1], inc=1, device_id=p.along(p.down(step)), device_id_type=MESH
                )

    def drain(self):
        for at in range(4):
            self.copy_core(at).wait_send()
        self.copy_far(1).wait_send()
        self.copy_far(0).wait_send()
        self.copy_near().wait_send()
        for step in range(1, self.place.depth):
            self.copy_z(step).wait_send()


class ScatterLine(Scatter):
    def column(self, z):
        return self.whole.at[:, z, self.place.core, self.lines()]

    def copy_pair(self, part):
        p = self.place
        return remote(
            self.column(p.cross if part else p.pair), self.slots.far.at[0, part, :, self.lines()],
            self.sa.at[self.number, part], self.ra.at[self.number, part], p.along(p.pair),
        )

    def copy_jump(self):
        p = self.place
        return remote(
            self.column(p.jump), self.slots.near.at[0, :, self.lines()], self.sb.at[self.number], self.rb.at[self.number],
            p.along(p.jump),
        )

    def copy_axis(self, part):
        p = self.place
        row = (p.both, p.far, p.near)[part]
        target = p.near if part == 2 else p.far
        return remote(
            self.whole.at[row, p.z, p.core, self.lines()], self.slots.along.at[0, part, self.lines()],
            self.sz.at[self.number, part], self.rz.at[self.number, part], (target, p.fsdp),
        )

    def add_column(self, z, slot):
        p = self.place
        tiles = self.count // self.tile

        def one(index, _):
            row = index // tiles
            at = pl.ds(pl.multiple_of(self.first + lax.rem(index, tiles) * self.tile, self.tile), self.tile)
            self.whole[row, z, p.core, at, :] = self.whole[row, z, p.core, at, :] + slot[row, at, :]
            return 0

        lax.fori_loop(0, self.whole.shape[0] * tiles, one, 0)

    def add_block(self, row, part):
        p = self.place

        def one(index, _):
            at = pl.ds(pl.multiple_of(self.first + index * self.tile, self.tile), self.tile)
            self.whole[row, p.z, p.core, at, :] = self.whole[row, p.z, p.core, at, :] + self.slots.along[0, part, at, :]
            return 0

        lax.fori_loop(0, self.count // self.tile, one, 0)

    def tell(self, semaphore, device):
        pl.semaphore_signal(semaphore, inc=1, device_id=device, device_id_type=MESH)

    def add_core(self, at):
        p = self.place
        self.copy_core(at).wait_recv()
        self.add(self.got_row(at), self.slots.core.at[at])
        for sub in range(SUBS // 2, SUBS):
            self.tell(self.core_free.at[at, sub], (p.dp, p.sibling))

    def start_pair(self):
        self.copy_pair(1).start()
        self.copy_pair(0).start()

    def add_pair(self, part):
        p = self.place
        self.copy_pair(part).wait_recv()
        self.add_column(p.jump if part else p.z, self.slots.far.at[0, part])
        if part:
            self.copy_jump().start()
        for sub in range(SUBS // 2, SUBS):
            self.tell(self.far_free.at[part, sub], (p.far, p.fsdp))

    def add_jump(self):
        p = self.place
        self.copy_jump().wait_recv()
        self.add_column(p.z, self.slots.near.at[0])
        for sub in range(SUBS // 2, SUBS):
            self.tell(self.near_free.at[sub], (p.near, p.fsdp))
        self.copy_axis(0).start()
        self.copy_axis(1).start()

    def add_far_axis(self):
        p = self.place
        for part in range(2):
            self.copy_axis(part).wait_recv()
            self.add_block(p.dp if part else p.near, part)
        self.copy_axis(2).start()

    def finish(self, out):
        p = self.place
        self.copy_axis(2).wait_recv()

        def one(index, _):
            start = pl.multiple_of(index * self.tile, self.tile)
            at = pl.ds(pl.multiple_of(self.first + start, self.tile), self.tile)
            total = self.whole[p.dp, p.z, p.core, at, :].astype(jnp.float32)
            out[pl.ds(start, self.tile), :] = total + self.slots.along[0, 2, at, :].astype(jnp.float32)
            return 0

        lax.fori_loop(0, self.count // self.tile, one, 0)
        for sub in range(SUBS // 2, SUBS):
            for step in range(1, p.depth):
                self.tell(self.z_free.at[sub, step - 1], p.along(p.down(step)))

    def drain(self):
        for at in range(4):
            self.copy_core(at).wait_send()
        for part in range(2):
            self.copy_pair(part).wait_send()
        self.copy_jump().wait_send()
        for part in range(3):
            self.copy_axis(part).wait_send()


def outer_gradient(acts, low, grads, row):
    depth, cores, count, _ = grads.shape[1:]
    size = cores * count

    def one(z, _):
        value = matmul_tn(acts[row, :, span(z, size)], low[...])
        grads[row, z] = value.astype(jnp.bfloat16).reshape(grads.shape[2:])
        return 0

    lax.fori_loop(0, depth, one, 0)


def input_gradient(inputs, low, grads, row, part):
    depth, cores, count, width = grads.shape[1:]
    size = inputs.shape[1] // grads.shape[0]
    lines = count // SUBS
    value = matmul_tn(inputs[:, span(row, size)], low)
    grads[row, :, :, part * lines : (part + 1) * lines, :] = value.astype(jnp.bfloat16).reshape(depth, cores, lines, width)


def hidden_back(low, weights, slopes, bias_sum, part):
    depth, cores, count, width = weights.shape[1:]
    size = cores * count

    def one(index, _):
        at = span(index, size)
        value = matmul_nt(low[...], flat(weights[part, index])) * slopes[SUBS + part, :, at].astype(jnp.float32)
        rounded = value.astype(jnp.bfloat16)
        slopes[SUBS + part, :, at] = rounded
        total = jnp.sum(rounded.astype(jnp.float32), axis=0, keepdims=True)
        bias_sum[:, pl.ds(pl.multiple_of(part * width + index * size, size), size)] = total
        return 0

    lax.fori_loop(0, depth, one, 0)


def first_total_rows(grad, inner_low, weights):
    lines = weights.shape[3] // SUBS
    size = grad.shape[1] // weights.shape[0]

    def one(index, _):
        at = span(index, size)
        total = grad[:, at]
        for part in range(SUBS):
            weight = flat(weights[index, :, :, part * lines : (part + 1) * lines, :])
            total = total + matmul_nt(inner_low[SUBS + part], weight)
        grad[:, at] = total
        return 0

    lax.fori_loop(0, weights.shape[0], one, 0)


def first_back(first_sum, grad, low, vectors, sums):
    for row in (2, 3, 4):
        sums[row : row + 1, :] = jnp.zeros((1, grad.shape[1]), jnp.float32)

    def one(index, _):
        at = span(index, 64)
        normed, rate = center_scale(first_sum[at, :])
        upper = grad[at, :]
        back = norm_back(upper, normed, rate, vectors[3:4, :])
        rounded = back.astype(jnp.bfloat16)
        grad[at, :] = back
        low[at, :] = rounded
        sums[2:3, :] += jnp.sum(rounded.astype(jnp.float32), axis=0, keepdims=True)
        sums[3:4, :] += jnp.sum(upper * normed, axis=0, keepdims=True)
        sums[4:5, :] += jnp.sum(upper, axis=0, keepdims=True)
        return 0

    lax.fori_loop(0, grad.shape[0] // 64, one, 0)


def context_back(low, weights, context):
    halves = weights.shape[1] // CHUNK

    def one(index, _):
        weight = weights[index // halves, span(lax.rem(index, halves), CHUNK), :]
        context[:, span(index, CHUNK)] = matmul_nt(low[...], weight).astype(jnp.bfloat16)
        return 0

    lax.fori_loop(0, context.shape[1] // CHUNK, one, 0)


def attend_back(projected, probs, context_low, sums, first, last):
    width = context_low.shape[1]
    size = width // HEADS
    length = probs.shape[2]
    scale = size ** (-0.5)
    lanes = head_lanes(QUAD, length, size)
    quads = HEADS // QUAD

    def one(index, _):
        segment = index // quads
        quad = lax.rem(index, quads)
        at = span(segment, length)
        columns = [span(quad + part * quads, QUAD * size) for part in range(3)]
        queries, keysets, valuesets = [projected[at, column] for column in columns]
        low = probs[index]
        wide = low.astype(jnp.float32)
        upper = stack_heads(context_low[at, columns[0]], lanes)
        prob_grad = matmul_nt(upper, valuesets)
        score_low = (wide * (prob_grad - jnp.sum(wide * prob_grad, axis=1, keepdims=True))).astype(jnp.bfloat16)
        value_low = matmul_tn(low, upper).astype(jnp.bfloat16)
        query_low = (merge_heads(matmul(score_low, keysets), lanes) * scale).astype(jnp.bfloat16)
        key_low = (matmul_tn(score_low, stack_heads(queries, lanes)) * scale).astype(jnp.bfloat16)
        projected[at, columns[0]] = query_low
        projected[at, columns[1]] = key_low
        projected[at, columns[2]] = value_low
        sums[0:1, columns[0]] += jnp.sum(query_low.astype(jnp.float32), axis=0, keepdims=True)
        sums[1:2, columns[0]] += jnp.sum(value_low.astype(jnp.float32), axis=0, keepdims=True)
        return 0

    lax.fori_loop(first, last, one, 0)


def states_back(grad, projected, weights):
    width = grad.shape[1]
    halves = weights.shape[1] // CHUNK

    def one(index, _):
        at = span(index, CHUNK)
        total = grad[:, at]
        for part in range(3):
            weight = weights[2 + 2 * part + index // halves, span(lax.rem(index, halves), CHUNK), :]
            total = total + matmul_nt(projected[:, part * width : (part + 1) * width], weight)
        grad[:, at] = total
        return 0

    lax.fori_loop(0, width // CHUNK, one, 0)


def pack_sums(sums, bias_sum, block, table):
    dps, depth, cores = table.shape[:3]
    places = dps * depth * cores
    width = sums.shape[1]
    lane = lax.broadcasted_iota(jnp.int32, (width, 128), 1)
    source = lax.broadcasted_iota(jnp.int32, (width, 128), 0)
    pick = jnp.where(lane == lax.rem(source, block), 1.0, 0.0).astype(jnp.bfloat16)
    owner = lax.broadcasted_iota(jnp.int32, (places, width), 1) // block
    mine = owner == lax.broadcasted_iota(jnp.int32, (places, width), 0)
    values = jnp.concatenate([jnp.where(mine, sums[vector : vector + 1, :], 0.0) for vector in range(8)], axis=0)
    upper = values.astype(jnp.bfloat16)
    lower = (values - upper.astype(jnp.float32)).astype(jnp.bfloat16)
    total = matmul(upper, pick) + matmul(lower, pick)
    table[...] = jnp.zeros_like(table)
    for vector in range(8):
        table[:, :, :, vector, :] = total[vector * places : (vector + 1) * places].reshape(dps, depth, cores, 128)
    for index in range(places):
        dp, z, core = index // (depth * cores), index // cores % depth, index % cores
        table[dp, z, core, 8:9, :] = bias_sum[:, index * 128 : (index + 1) * 128]


EARLY = 2
SCHEDULE = (
    ("outer",), ("hidden",), ("far", 0), ("inner",), ("far", 1), ("line", 0), ("near", 0), ("total",), ("line", 1),
    ("go", 4), ("norm",), ("attn",), ("go", 6), ("context",), ("far", 2), ("near", 1), ("heads", 0), ("go", 5),
    ("heads", 1), ("far", 3), ("near", 2), ("line", 2), ("merged",), ("go", 7), ("far", 4), ("near", 3), ("end", 0),
    ("far", 5), ("go", 8), ("near", 4), ("end", 1), ("line", 3), ("pack",), ("states",), ("far", 6), ("go", 9),
    ("go", 10), ("near", 5), ("line", 4), ("end", 2), ("far", 7), ("go", 11), ("near", 6), ("end", 3), ("far", 8),
    ("near", 7), ("end", 4), ("far", 9), ("far", 10), ("near", 8), ("end", 5), ("near", 9), ("far", 11), ("near", 10),
    ("end", 6), ("end", 7), ("near", 11), ("end", 8), ("end", 9), ("end", 10), ("end", 11),
)


def backward_kernel(depth, block, *refs):
    (vectors, known, rows_in, activated_in, slope_in, outer_low_in, second_grad_in, first_sum_in, first_low_in, context_in,
     projected_in, probs_in, merged_in, attn_in, inner_in, outer_in) = refs[:16]
    states_out, outer_out, inner_out, query_out, key_out, value_out, attn_out, table_out = refs[16:24]
    (first_buffer, second_buffer, outer_grads, wide, from_core, from_far, from_near, from_z, low, first_low, grad, first_sum,
     context, projected, probs, rows, sums, bias_sum, table, table_core, table_far, table_near, table_z) = refs[24:47]
    load_sem, save_sem = refs[47:49]
    sems = refs[49:57]
    credits = refs[57:61]
    place = Place(depth)
    place.greet()
    width = rows.shape[1]
    tokens = rows.shape[0]
    lines = outer_grads.shape[3] // SUBS
    loads = []

    def load(source, target):
        copy = pltpu.make_async_copy(source, target, load_sem.at[len(loads)])
        copy.start()
        loads.append(copy)
        return copy

    def load_columns(source, targets):
        return [load(source.at[:, part * width : (part + 1) * width], target) for part, target in enumerate(targets)]

    low_load = load(outer_low_in, low)
    act_loads = load_columns(activated_in, [wide.at[part] for part in range(SUBS)])
    outer_load = load(outer_in, first_buffer)
    slope_loads = load_columns(slope_in, [wide.at[SUBS + part] for part in range(SUBS)])
    first_low_load = load(first_low_in, first_low)
    grad_load = load(second_grad_in, grad)
    inner_loads = [
        load(inner_in.at[:, :, :, :, part * width : (part + 1) * width],
             second_buffer.at[:, :, :, part * lines : (part + 1) * lines, :])
        for part in range(SUBS)
    ]
    first_sum_load = load(first_sum_in, first_sum)
    context_load = load(context_in, context)
    projected_load = load(projected_in, projected)
    probs_load = load(probs_in, probs)
    rows_load = load(rows_in, rows)

    slots = Slots(from_core, from_far, from_near, from_z)
    table_slots = Slots(table_core, table_far, table_near, table_z)
    outers = [
        Scatter(place, outer_grads, slots, sems, credits, sub, 0, sub * lines, lines, before=True, late_before=True)
        for sub in range(SUBS // 2)
    ]
    line = ScatterLine(place, outer_grads, slots, sems, credits, SUBS - 1, 0, SUBS // 2 * lines, SUBS // 2 * lines)
    inner_grads = first_buffer
    inners = [
        Scatter(place, inner_grads, slots, sems, credits, SUBS + sub, 1, sub * lines, lines, after=True, before=True)
        for sub in range(SUBS)
    ]
    other_grads = second_buffer
    others = [
        Scatter(place, other_grads, slots, sems, credits, 2 * SUBS + sub, 0, sub * lines, lines, after=True, late_after=True)
        for sub in range(SUBS - 1)
    ]
    attn_net = others[0]
    mergeds = others[1:3]
    lowest = lines // 2
    mergeds += [
        Scatter(place, other_grads, slots, sems, credits, 3 * SUBS - 1, 0, 3 * lines, lowest, after=True, late_after=True),
        Scatter(place, other_grads, slots, sems, credits, 3 * SUBS + 1, 0, 3 * lines + lowest, lowest),
    ]
    small = Scatter(place, table, table_slots, sems, credits, 3 * SUBS, 0, 0, 16)
    row_order = (place.both, place.near, place.far, place.dp)
    sums[...] = known[...]
    sums[0:2, :] = jnp.zeros((2, width), jnp.float32)

    def pieces(nets, compute, early=(), first=False):
        def added(at):
            for net in nets:
                net.add_core(at)
            if at < 2:
                for net in early:
                    net.start_far(1 - at)

        for at in range(4):
            compute(row_order[at])
            if first and at == 0:
                place.greeted()
            for net in nets:
                net.start_core(at)
            if at:
                added(at - 1)
        added(3)

    order = outers + inners + [attn_net] + mergeds[:2] + [small] + mergeds[2:]
    outs = [outer_out.at[pl.ds(sub * lines, lines), :] for sub in range(SUBS // 2)]
    outs += [inner_out.at[:, pl.ds(sub * width, width)] for sub in range(SUBS)]
    outs += [attn_out, query_out, key_out, table_out, value_out.at[pl.ds(0, lowest), :], value_out.at[pl.ds(lowest, lowest), :]]
    def far(number):
        order[number].add_far(1)
        order[number].add_far(0)

    def go(number):
        order[number].start_far(1)
        order[number].start_far(0)

    def near(number):
        order[number].add_near()

    def end(number):
        order[number].finish(outs[number])

    def ready(copies):
        for copy in copies:
            copy.wait()

    def load_merged(part):
        return [
            load(merged_in.at[at * tokens : (at + 1) * tokens, part * width : (part + 1) * width], wide.at[2 + 2 * part + at])
            for at in range(2)
        ]

    late_loads = []

    def outer_step():
        ready([low_load] + act_loads)
        pieces(outers + [line], lambda row: outer_gradient(wide, low, outer_grads, row), outers, True)
        line.start_pair()
        late_loads.append(load(attn_in.at[:tokens], wide.at[0]))
        late_loads.append(load(attn_in.at[tokens:], wide.at[1]))
        late_loads.extend(load_merged(0))

    def hidden_step():
        ready([outer_load] + slope_loads)
        for part in range(SUBS):
            hidden_back(low, first_buffer, wide, bias_sum, part)

    def inner_step():
        def compute(row):
            for part in range(SUBS):
                input_gradient(first_low, wide[SUBS + part], inner_grads, row, part)

        ready([first_low_load])
        pieces(inners, compute, inners[:EARLY])

    def total_step():
        ready([grad_load] + inner_loads)
        first_total_rows(grad, wide, second_buffer)
        late_loads.extend(load_merged(1) + load_merged(2))

    def norm_step():
        ready([first_sum_load])
        first_back(first_sum, grad, low, vectors, sums)

    def attn_step():
        ready([context_load])
        pieces([attn_net], lambda row: input_gradient(context, low[...], other_grads, row, 0))

    def context_step():
        ready(late_loads[:2])
        context_back(low, wide, context)

    def heads_step(part):
        if part == 0:
            ready([projected_load, probs_load])
        count = probs.shape[0]
        attend_back(projected, probs, context, sums, part * count // 2, (part + 1) * count // 2)

    def merged_step():
        def compute(row):
            for part in range(3):
                input_gradient(rows, projected[:, part * width : (part + 1) * width], other_grads, row, 1 + part)

        ready([rows_load])
        pieces(mergeds, compute)

    def pack_step():
        pack_sums(sums, bias_sum, block, table)
        pieces([small], lambda row: None)

    save = pltpu.make_async_copy(grad, states_out, save_sem)

    def states_step():
        ready(late_loads[2:])
        states_back(grad, projected, wide)
        save.start()

    def line_step(part):
        (line.add_pair, line.add_jump, line.add_far_axis, line.finish)[max(part - 1, 0)](
            *(((1,), (0,), (), (), (outer_out.at[pl.ds(SUBS // 2 * lines, SUBS // 2 * lines), :],))[part])
        )

    steps = {
        "outer": outer_step, "hidden": hidden_step, "inner": inner_step, "total": total_step, "norm": norm_step,
        "attn": attn_step, "context": context_step, "heads": heads_step, "merged": merged_step, "pack": pack_step,
        "states": states_step, "line": line_step, "go": go, "far": far, "near": near, "end": end,
    }
    for entry in SCHEDULE:
        steps[entry[0]](*entry[1:])
    for net in order + [line]:
        net.drain()
    save.wait()


def backward_all(depth, block, vectors, known, kept):
    low, high = jnp.bfloat16, jnp.float32
    (rows, activated, _, _, _, first_sum, _, _, projected, probs, _, _, inner, outer) = kept
    tokens, width = rows.shape
    hidden = activated.shape[1]
    unit = outer.shape
    lines = unit[3]
    own_rows = lines // SUBS
    dma, regular = pltpu.SemaphoreType.DMA, pltpu.SemaphoreType.REGULAR
    nets = 3 * SUBS + 2
    scratch = [
        pltpu.VMEM(unit, low),
        pltpu.VMEM(unit, low),
        pltpu.VMEM(unit, low),
        pltpu.VMEM((2 * SUBS, tokens, width), low),
        pltpu.VMEM((4, depth, lines, width), low),
        pltpu.VMEM((2, 2, depth, lines, width), low),
        pltpu.VMEM((2, depth, lines, width), low),
        pltpu.VMEM((2, depth - 1, lines, width), low),
        pltpu.VMEM((tokens, width), low),
        pltpu.VMEM((tokens, width), low),
        pltpu.VMEM((tokens, width), high),
        pltpu.VMEM((tokens, width), high),
        pltpu.VMEM((tokens, width), low),
        pltpu.VMEM(projected.shape, low),
        pltpu.VMEM(probs.shape, low),
        pltpu.VMEM((tokens, width), low),
        pltpu.VMEM((8, width), high),
        pltpu.VMEM((1, hidden), high),
        pltpu.VMEM((4, depth, 2, 16, 128), high),
        pltpu.VMEM((4, depth, 16, 128), high),
        pltpu.VMEM((1, 2, depth, 16, 128), high),
        pltpu.VMEM((1, depth, 16, 128), high),
        pltpu.VMEM((1, depth - 1, 16, 128), high),
        dma((40,)),
        dma,
        dma((nets, 4)), dma((nets, 4)), dma((nets, 2)), dma((nets, 2)), dma((nets,)), dma((nets,)),
        dma((nets, depth - 1)), dma((nets, depth - 1)),
        regular((4, SUBS)), regular((2, SUBS)), regular((SUBS,)), regular((SUBS, depth - 1)),
    ]
    shapes = [(tokens, width), (lines, width), (own_rows, hidden)] + [(own_rows, width)] * 4 + [(16, 128)]
    here = pl.BlockSpec(memory_space=pltpu.VMEM)
    away = pl.BlockSpec(memory_space=pl.ANY)
    return pl.pallas_call(
        functools.partial(backward_kernel, depth, block),
        out_shape=[jax.ShapeDtypeStruct(shape, high) for shape in shapes],
        in_specs=[here] * 2 + [away] * len(kept),
        out_specs=[away] + [here] * 7,
        scratch_shapes=scratch,
        compiler_params=pltpu.CompilerParams(
            collective_id=1, has_side_effects=True, vmem_limit_bytes=62 * 1024 * 1024
        ),
        name="backward",
    )(vectors, known, *kept)


def finish_kernel(block, *refs):
    count = 8
    table = refs[0]
    sources, targets = refs[1 : 1 + count], refs[1 + count : 1 + 2 * count]
    rows = refs[1 + 2 * count : 10 + 2 * count]
    held = refs[10 + 2 * count : 10 + 3 * count]
    in_sem, out_sem = refs[10 + 3 * count :]
    fetches = [pltpu.make_async_copy(source, target, in_sem.at[at]) for at, (source, target) in enumerate(zip(sources, held))]
    stores = [pltpu.make_async_copy(source, target, out_sem.at[at]) for at, (source, target) in enumerate(zip(held, targets))]
    for copy in fetches:
        copy.start()
    for index, row in enumerate(rows):
        row[...] = table[index, : row.shape[0]]
    for fetch, store in zip(fetches, stores):
        fetch.wait()
        store.start()
    for store in stores:
        store.wait()


def finish_all(block, table, arrays):
    shapes = [jax.ShapeDtypeStruct(array.shape, array.dtype) for array in arrays]
    shapes += [jax.ShapeDtypeStruct((block,), jnp.float32)] * 8 + [jax.ShapeDtypeStruct((128,), jnp.float32)]
    here = pl.BlockSpec(memory_space=pltpu.VMEM)
    away = pl.BlockSpec(memory_space=pltpu.HBM)
    dma = pltpu.SemaphoreType.DMA
    return pl.pallas_call(
        functools.partial(finish_kernel, block),
        out_shape=shapes,
        in_specs=[here] + [away] * len(arrays),
        out_specs=[away] * len(arrays) + [here] * 9,
        scratch_shapes=[pltpu.VMEM(array.shape, array.dtype) for array in arrays] + [dma((len(arrays),))] * 2,
        compiler_params=pltpu.CompilerParams(vmem_limit_bytes=60 * 1024 * 1024),
        name="finish",
    )(table, *arrays)


def normalize(hidden, gain, shift):
    center = hidden - jnp.mean(hidden, axis=-1, keepdims=True)
    spread = jnp.mean(center * center, axis=-1, keepdims=True)
    return center * lax.rsqrt(spread + epsilon) * gain + shift


def exact_gelu(value):
    return jax.nn.gelu(value, approximate=False)


def contract_rows(left, right):
    return lax.dot_general(
        left, right, (((0,), (0,)), ((), ())), preferred_element_type=jnp.float32
    )


def times_transposed(left, right):
    return lax.dot_general(
        left, right, (((1,), (1,)), ((), ())), preferred_element_type=jnp.float32
    )


def collect(merged, attn, inner, outer, vectors, widened):
    return (
        lax.all_gather(merged, ("dp", "fsdp"), axis=0, tiled=True),
        lax.all_gather(attn, ("dp", "fsdp"), axis=0, tiled=True),
        lax.all_gather(inner, ("dp", "fsdp"), axis=0, tiled=True),
        lax.all_gather(outer, ("dp", "fsdp"), axis=0, tiled=True),
        lax.all_gather(vectors, ("dp", "fsdp"), axis=0, tiled=True),
        lax.all_gather(widened, ("dp", "fsdp"), axis=0, tiled=True),
    )


def reduce_grads(merged, attn, inner, outer, vectors, widened):
    return (
        lax.psum_scatter(merged, ("dp", "fsdp"), scatter_dimension=0, tiled=True),
        lax.psum_scatter(attn, ("dp", "fsdp"), scatter_dimension=0, tiled=True),
        lax.psum_scatter(inner, ("dp", "fsdp"), scatter_dimension=0, tiled=True),
        lax.psum_scatter(outer, ("dp", "fsdp"), scatter_dimension=0, tiled=True),
        lax.psum_scatter(vectors, ("dp", "fsdp"), scatter_dimension=0, tiled=True),
        lax.psum_scatter(widened, ("dp", "fsdp"), scatter_dimension=0, tiled=True),
    )


def split_heads(projected, segments):
    total_rows, triple = projected.shape
    width = triple // 3
    return projected.reshape(segments, total_rows // segments, 3, HEADS, width // HEADS)


def attention_probs(queries, keysets, keep, scale):
    scores = (
        jnp.einsum("sqhd,skhd->shqk", queries, keysets, preferred_element_type=jnp.float32) * scale
    )
    scores = jnp.where(keep[:, None, None, :] > 0, scores, neg_fill)
    peaks = jnp.max(scores, axis=-1, keepdims=True)
    raised = jnp.exp(scores - peaks)
    return raised / jnp.sum(raised, axis=-1, keepdims=True)


def forward_pass(rows, keep, weights):
    merged, attn, inner, outer, vectors, widened = weights
    vector_full = vectors.astype(jnp.float32)
    width = rows.shape[1]
    scale = (width // HEADS) ** (-0.5)
    merged_bias = jnp.concatenate(
        (vector_full[:, 0], jnp.zeros((width,), jnp.float32), vector_full[:, 1])
    )
    projected = (jnp.dot(rows, merged, preferred_element_type=jnp.float32) + merged_bias).astype(
        jnp.bfloat16
    )
    split = split_heads(projected, keep.shape[0])
    probs = attention_probs(split[:, :, 0], split[:, :, 1], keep, scale).astype(jnp.bfloat16)
    context = jnp.einsum(
        "shqk,skhd->sqhd", probs, split[:, :, 2], preferred_element_type=jnp.float32
    )
    context = context.reshape(rows.shape[0], width).astype(jnp.bfloat16)
    attended = jnp.dot(context, attn, preferred_element_type=jnp.float32) + vector_full[:, 2]
    first_sum = rows.astype(jnp.float32) + attended
    first_norm = normalize(first_sum, vector_full[:, 3], vector_full[:, 4])
    first_low = first_norm.astype(jnp.bfloat16)
    inner_act = jnp.dot(first_low, inner, preferred_element_type=jnp.float32) + widened.astype(
        jnp.float32
    )
    activated = exact_gelu(inner_act).astype(jnp.bfloat16)
    outer_act = jnp.dot(activated, outer, preferred_element_type=jnp.float32) + vector_full[:, 5]
    second_sum = first_norm + outer_act
    encoded = normalize(second_sum, vector_full[:, 6], vector_full[:, 7]).astype(jnp.bfloat16)
    return (encoded, (projected, context, first_sum, first_low, inner_act, activated, second_sum))


def backward_pass(rows, keep, cotangent, weights, kept):
    merged, attn, inner, outer, vectors, widened = weights
    projected, context, first_sum, first_low, inner_act, activated, second_sum = kept
    vector_full = vectors.astype(jnp.float32)
    width = rows.shape[1]
    scale = (width // HEADS) ** (-0.5)
    second_out, second_pull = jax.vjp(normalize, second_sum, vector_full[:, 6], vector_full[:, 7])
    second_grad, second_gain_g, second_shift_g = second_pull(cotangent.astype(jnp.float32))
    outer_low = second_grad.astype(jnp.bfloat16)
    outer_bias_g = jnp.sum(outer_low.astype(jnp.float32), axis=0)
    outer_weight_g = contract_rows(activated, outer_low)
    act_grad = times_transposed(outer_low, outer)
    gelu_out, gelu_pull = jax.vjp(exact_gelu, inner_act)
    inner_low = gelu_pull(act_grad)[0].astype(jnp.bfloat16)
    inner_bias_g = jnp.sum(inner_low.astype(jnp.float32), axis=0)
    inner_weight_g = contract_rows(first_low, inner_low)
    first_total = second_grad + times_transposed(inner_low, inner)
    first_out, first_pull = jax.vjp(normalize, first_sum, vector_full[:, 3], vector_full[:, 4])
    first_grad, first_gain_g, first_shift_g = first_pull(first_total)
    attended_low = first_grad.astype(jnp.bfloat16)
    attn_bias_g = jnp.sum(attended_low.astype(jnp.float32), axis=0)
    attn_weight_g = contract_rows(context, attended_low)
    context_low = times_transposed(attended_low, attn).astype(jnp.bfloat16)
    split = split_heads(projected, keep.shape[0])
    queries = split[:, :, 0]
    keysets = split[:, :, 1]
    valuesets = split[:, :, 2]
    probs = attention_probs(queries, keysets, keep, scale)
    probs_low = probs.astype(jnp.bfloat16)
    context_heads = context_low.reshape(queries.shape)
    prob_grad = jnp.einsum(
        "sqhd,skhd->shqk", context_heads, valuesets, preferred_element_type=jnp.float32
    )
    value_grad = jnp.einsum(
        "shqk,sqhd->skhd", probs_low, context_heads, preferred_element_type=jnp.float32
    )
    score_low = (probs * (prob_grad - jnp.sum(probs * prob_grad, axis=-1, keepdims=True))).astype(
        jnp.bfloat16
    )
    query_grad = (
        jnp.einsum("shqk,skhd->sqhd", score_low, keysets, preferred_element_type=jnp.float32)
        * scale
    )
    key_grad = (
        jnp.einsum("shqk,sqhd->skhd", score_low, queries, preferred_element_type=jnp.float32)
        * scale
    )
    merged_low = jnp.stack((query_grad, key_grad, value_grad), axis=2).astype(jnp.bfloat16)
    merged_low = merged_low.reshape(rows.shape[0], 3 * width)
    merged_weight_g = contract_rows(rows, merged_low)
    merged_bias_g = jnp.sum(merged_low.astype(jnp.float32), axis=0)
    states_part = first_grad + times_transposed(merged_low, merged)
    vector_grads = jnp.stack(
        (
            merged_bias_g[:width],
            merged_bias_g[2 * width :],
            attn_bias_g,
            first_gain_g,
            first_shift_g,
            outer_bias_g,
            second_gain_g,
            second_shift_g,
        ),
        axis=1,
    )
    return (
        states_part,
        (
            merged_weight_g,
            attn_weight_g,
            inner_weight_g,
            outer_weight_g,
            vector_grads,
            inner_bias_g,
        ),
    )


def shards(depth, *arrays):
    (states, pad_mask, query_proj, key_proj, value_proj, attn_proj, query_bias, value_bias, attn_bias, first_gain,
     first_shift, inner_proj, inner_bias, outer_proj, outer_bias, second_gain, second_shift, out_grad) = arrays
    width = states.shape[1]
    short = (query_bias, value_bias, attn_bias, first_gain, first_shift, outer_bias, second_gain, second_shift)
    if depth:
        return kernel_shards(depth, short, states, pad_mask, query_proj, key_proj, value_proj, attn_proj, inner_proj,
                             inner_bias, outer_proj, out_grad)
    merged_shard = jnp.concatenate((query_proj, key_proj, value_proj), axis=1)
    fetched = collect(merged_shard, attn_proj, inner_proj, outer_proj, jnp.stack(short, axis=1), inner_bias)
    encoded, kept = forward_pass(states, pad_mask, fetched)
    states_part, totals = backward_pass(states, pad_mask, out_grad, fetched, kept)
    merged_sum, attn_sum, inner_sum, outer_sum, vector_sum, widened_sum = reduce_grads(*totals)
    return ordered(encoded, states_part, merged_sum, attn_sum, inner_sum, outer_sum, vector_sum.T, widened_sum)


def ordered(encoded, states_part, merged_sum, attn_sum, inner_sum, outer_sum, vectors, widened_sum):
    width = attn_sum.shape[1]
    return (encoded, states_part, merged_sum[:, :width], merged_sum[:, width : 2 * width], merged_sum[:, 2 * width :],
            attn_sum, vectors[0], vectors[1], vectors[2], vectors[3], vectors[4], inner_sum, widened_sum, outer_sum,
            vectors[5], vectors[6], vectors[7])


def kernel_shards(depth, short, states, pad_mask, query_proj, key_proj, value_proj, attn_proj, inner_proj, inner_bias,
                  outer_proj, out_grad):
    width = states.shape[1]
    block = short[0].shape[0]
    (merged, attn, inner, outer, encoded, projected, probs, context, first_sum, first_low, activated, slope, second_grad,
     outer_low, vectors, sums) = forward_all(
        depth, block, states, pad_mask, out_grad,
        (query_proj, key_proj, value_proj, attn_proj, inner_proj, outer_proj, *short, inner_bias))
    states_part, outer_sum, inner_sum, query_sum, key_sum, value_sum, attn_sum, table_sum = backward_all(
        depth, block, vectors, sums,
        (states, activated, slope, outer_low, second_grad, first_sum, first_low, context, projected, probs,
         merged.reshape(width, -1), attn.reshape(width, -1), inner, outer))
    (encoded, states_part, query_sum, key_sum, value_sum, attn_sum, inner_sum, outer_sum, *rows) = finish_all(
        block, table_sum, (encoded, states_part, query_sum, key_sum, value_sum, attn_sum, inner_sum, outer_sum))
    return (encoded, states_part, query_sum, key_sum, value_sum, attn_sum, *rows[:5], inner_sum, rows[8], outer_sum,
            *rows[5:8])


def solution(mesh):
    dps, others = mesh.shape["dp"], mesh.shape["fsdp"]
    matrix = P(("dp", "fsdp"), None)
    vector = P(("dp", "fsdp"))

    def whole(*arrays):
        rows = arrays[2].shape[0] // (dps * others)
        tiles = rows % 16 == 0 and arrays[12].shape[0] == 128 * dps * others
        depth = others // 2 if tiles and dps == 4 and others == 2 * dps else 0
        return jax.shard_map(
            functools.partial(shards, depth),
            mesh=mesh,
            in_specs=(matrix,) * 6 + (vector,) * 5 + (matrix, vector, matrix) + (vector,) * 3 + (matrix,),
            out_specs=(matrix,) * 6 + (vector,) * 5 + (matrix, vector, matrix) + (vector,) * 3,
            check_vma=False,
        )(*arrays)

    return whole
```

```python
import functools

import jax
import jax.numpy as jnp
from jax import lax
from jax.experimental import pallas as pl
from jax.experimental.pallas import tpu as pltpu
from jax.sharding import PartitionSpec as P

HEADS = 16
MESH = pl.DeviceIdType.MESH

epsilon = 1e-05
neg_fill = -1e30


class Place:
    def __init__(self, depth):
        dp = lax.axis_index("dp")
        fsdp = lax.axis_index("fsdp")
        self.depth = depth
        self.dp = dp
        self.z = fsdp // 2
        self.core = lax.rem(fsdp, 2)
        flip_x = dp + 1 - 2 * lax.rem(dp, 2)
        flip_y = lax.rem(dp + 2, 4)
        self.near = flip_x + self.core * (flip_y - flip_x)
        self.far = flip_y + self.core * (flip_x - flip_y)
        self.both = lax.rem(flip_x + 2, 4)
        self.fsdp = fsdp
        self.sibling = fsdp + 1 - 2 * self.core
        self.pair = self.z + 1 - 2 * lax.rem(self.z, 2)
        self.jump = self.up(2)
        self.cross = 3 - self.z

    def up(self, step):
        return lax.rem(self.z + step, self.depth)

    def down(self, step):
        return lax.rem(self.z + self.depth - step, self.depth)

    def along(self, z):
        return (self.dp, z * 2 + self.core)

    def greet(self):
        barrier = pltpu.get_barrier_semaphore()
        others = [self.along(self.up(step)) for step in range(1, self.depth)]
        others += [(self.near, self.fsdp), (self.far, self.fsdp), (self.dp, self.sibling)]
        for other in others:
            pl.semaphore_signal(barrier, inc=1, device_id=other, device_id_type=MESH)

    def greeted(self):
        pl.semaphore_wait(pltpu.get_barrier_semaphore(), self.depth + 2)


def remote(source, target, send, recv, device):
    return pltpu.make_async_remote_copy(
        src_ref=source, dst_ref=target, send_sem=send, recv_sem=recv, device_id=device, device_id_type=MESH
    )


class Gather:
    def __init__(self, place, full, own, sems, piece, lines=None):
        self.lines = pl.ds(0, full.shape[3]) if lines is None else lines
        self.place, self.full, self.own, self.piece = place, full, own.at[self.lines], piece
        self.su, self.ru, self.sd, self.rd, self.sb, self.rb, self.sa, self.ra, self.sc, self.rc, self.so = sems

    def copy_own(self):
        p = self.place
        return pltpu.make_async_copy(self.own, self.full.at[p.dp, p.z, p.core, self.lines], self.so.at[self.piece])

    def copy_up(self, z, first=False):
        p = self.place
        block = self.full.at[p.dp, z, p.core, self.lines]
        source = self.own if first else block
        return remote(source, block, self.su.at[self.piece, z], self.ru.at[self.piece, z], p.along(p.z + 1))

    def copy_down(self, z, first=False):
        p = self.place
        block = self.full.at[p.dp, z, p.core, self.lines]
        source = self.own if first else block
        return remote(source, block, self.sd.at[self.piece, z], self.rd.at[self.piece, z], p.along(p.z - 1))

    def copy_near(self, z, first=False, arriving=False):
        p = self.place
        block = self.full.at[p.near if arriving else p.dp, z, p.core, self.lines]
        source = self.own if first else block
        return remote(source, block, self.sb.at[self.piece, z], self.rb.at[self.piece, z], (p.near, p.fsdp))

    def copy_far(self, half, z, first=False, arriving=False):
        p = self.place
        row = (p.both if half else p.far) if arriving else (p.near if half else p.dp)
        block = self.full.at[row, z, p.core, self.lines]
        source = self.own if first else block
        at = half * p.depth + z
        return remote(source, block, self.sa.at[self.piece, at], self.ra.at[self.piece, at], (p.far, p.fsdp))

    def copy_core(self, part, arriving=False):
        p = self.place
        if arriving:
            row = (p.dp, p.far, p.near, p.both)[part]
            block = self.full.at[row, :, 1 - p.core, self.lines]
        else:
            row = (p.dp, p.near, p.far, p.both)[part]
            block = self.full.at[row, :, p.core, self.lines]
        return remote(block, block, self.sc.at[self.piece, part], self.rc.at[self.piece, part], (p.dp, p.sibling))

    def start(self):
        p = self.place
        pl.when(p.z < p.depth - 1)(lambda: self.copy_up(p.z, True).start())
        pl.when(p.z > 0)(lambda: self.copy_down(p.z, True).start())
        self.copy_own().start()

    def send(self, step):
        p = self.place

        def act(z, first=False):
            self.copy_near(z, first).start()
            self.copy_far(0, z, first).start()

        if step == 0:
            act(p.z, True)
        else:
            pl.when(p.z >= step)(lambda: act(p.z - step))
            pl.when(p.z + step < p.depth)(lambda: act(p.z + step))

    def hop(self, step):
        p = self.place

        @pl.when(p.z >= step)
        def _():
            z = p.z - step
            self.copy_up(z).wait_recv()
            pl.when(p.z < p.depth - 1)(lambda: self.copy_up(z).start())

        @pl.when(p.z + step < p.depth)
        def _():
            z = p.z + step
            self.copy_down(z).wait_recv()
            pl.when(p.z > 0)(lambda: self.copy_down(z).start())

    def last_hop(self):
        self.hop(self.place.depth - 1)
        self.copy_own().wait()
        self.copy_core(0).start()

    def spread(self, step):
        p = self.place

        def act(z):
            self.copy_near(z, arriving=True).wait_recv()
            self.copy_far(1, z).start()

        if step == 0:
            act(p.z)
        else:
            pl.when(p.z >= step)(lambda: act(p.z - step))
            pl.when(p.z + step < p.depth)(lambda: act(p.z + step))
        if step == p.depth - 1:
            self.copy_core(1).start()

    def arrive_far(self, half):
        p = self.place
        for z in range(p.depth):
            self.copy_far(half, z, arriving=True).wait_recv()
        self.copy_core(2 + half).start()

    def arrive_core(self, *parts):
        for part in parts:
            self.copy_core(part, arriving=True).wait_recv()

    def drain(self):
        p = self.place
        for z in range(p.depth):
            pl.when((p.z < p.depth - 1) & (z <= p.z))(lambda: self.copy_up(z).wait_send())
            pl.when((p.z > 0) & (z >= p.z))(lambda: self.copy_down(z).wait_send())
            self.copy_near(z).wait_send()
            self.copy_far(0, z).wait_send()
            self.copy_far(1, z).wait_send()
        for part in range(4):
            self.copy_core(part).wait_send()


class GatherLine:
    def __init__(self, place, full, own, sems, piece, lines):
        self.place, self.full, self.own, self.piece, self.lines = place, full, own.at[lines], piece, lines
        self.sj, self.rj, self.sp, self.rp, self.sb, self.rb, self.sa, self.ra, self.sc, self.rc, self.so = sems

    def block(self, row):
        return self.full.at[row, self.place.z, self.place.core, self.lines]

    def column(self, z, core):
        return self.full.at[:, z, core, self.lines]

    def copy_own(self):
        return pltpu.make_async_copy(self.own, self.block(self.place.dp), self.so.at[self.piece])

    def copy_near(self, arriving=False):
        p = self.place
        target = self.block(p.near if arriving else p.dp)
        return remote(self.own, target, self.sb.at[self.piece, 0], self.rb.at[self.piece, 0], (p.near, p.fsdp))

    def copy_far(self, half, arriving=False):
        p = self.place
        target = self.block((p.both if half else p.far) if arriving else (p.near if half else p.dp))
        source = target if half else self.own
        return remote(source, target, self.sa.at[self.piece, half], self.ra.at[self.piece, half], (p.far, p.fsdp))

    def copy_jump(self, arriving=False):
        p = self.place
        column = self.column(p.jump if arriving else p.z, p.core)
        return remote(column, column, self.sj.at[self.piece, 0], self.rj.at[self.piece, 0], p.along(p.jump))

    def copy_pair(self, part, arriving=False):
        p = self.place
        z = (p.cross if part else p.pair) if arriving else (p.jump if part else p.z)
        column = self.column(z, p.core)
        return remote(column, column, self.sp.at[self.piece, part], self.rp.at[self.piece, part], p.along(p.pair))

    def copy_core(self, part, arriving=False):
        p = self.place
        column = self.column((p.z, p.jump, p.pair, p.cross)[part], 1 - p.core if arriving else p.core)
        return remote(column, column, self.sc.at[self.piece, part], self.rc.at[self.piece, part], (p.dp, p.sibling))

    def start(self):
        self.copy_near().start()
        self.copy_far(0).start()
        self.copy_own().start()

    def spread(self):
        self.copy_near(arriving=True).wait_recv()
        self.copy_far(1).start()

    def join(self):
        self.copy_own().wait()
        for half in range(2):
            self.copy_far(half, arriving=True).wait_recv()
        self.copy_jump().start()
        self.copy_pair(0).start()
        self.copy_core(0).start()

    def relay(self):
        self.copy_jump(arriving=True).wait_recv()
        self.copy_pair(1).start()
        self.copy_core(1).start()

    def arrive(self):
        for part in range(2):
            self.copy_pair(part, arriving=True).wait_recv()
            self.copy_core(2 + part).start()

    def arrive_core(self):
        for part in range(4):
            self.copy_core(part, arriving=True).wait_recv()

    def drain(self):
        self.copy_near().wait_send()
        self.copy_jump().wait_send()
        for part in range(2):
            self.copy_far(part).wait_send()
            self.copy_pair(part).wait_send()
        for part in range(4):
            self.copy_core(part).wait_send()


def gather_sems(pieces, depth):
    dma = pltpu.SemaphoreType.DMA
    counts = (depth, depth, depth, depth, depth, depth, 2 * depth, 2 * depth, 4, 4)
    return [dma((pieces, count)) for count in counts] + [dma((pieces,))]


def matmul(left, right):
    return lax.dot_general(left, right, (((1,), (0,)), ((), ())), preferred_element_type=jnp.float32)


def matmul_nt(left, right):
    return lax.dot_general(left, right, (((1,), (1,)), ((), ())), preferred_element_type=jnp.float32)


def matmul_tn(left, right):
    return lax.dot_general(left, right, (((0,), (0,)), ((), ())), preferred_element_type=jnp.float32)


def flat(value):
    return value.reshape(-1, value.shape[-1])


def span(index, size):
    return pl.ds(pl.multiple_of(index * size, size), size)


def unpack_table(table, block, vectors, long_bias):
    dps, depth, cores = table.shape[:3]
    places = dps * depth * cores
    width = vectors.shape[1]
    lane = lax.broadcasted_iota(jnp.int32, (128, width), 1)
    source = lax.broadcasted_iota(jnp.int32, (128, width), 0)
    pick = jnp.where(source == lax.rem(lane, block), 1.0, 0.0).astype(jnp.bfloat16)
    owner = lax.broadcasted_iota(jnp.int32, (places, width), 1) // block
    mine = owner == lax.broadcasted_iota(jnp.int32, (places, width), 0)
    blocks = [table[:, :, :, vector, :].reshape(places, 128) for vector in range(8)]
    spread = matmul(jnp.concatenate(blocks, axis=0).astype(jnp.bfloat16), pick)
    for vector in range(8):
        own = jnp.where(mine, spread[vector * places : (vector + 1) * places], 0.0)
        vectors[vector : vector + 1, :] = jnp.sum(own, axis=0, keepdims=True)
    for index in range(places):
        dp, z, core = index // (depth * cores), index // cores % depth, index % cores
        long_bias[:, index * 128 : (index + 1) * 128] = table[dp, z, core, 8:9, :]


CHUNK = 256


def project(rows, weights, vectors, projected):
    chunks = rows.shape[1] // CHUNK
    for part, bias in ((0, 0), (1, None), (2, 1)):

        def one(index, _):
            at = span(part * chunks + index, CHUNK)
            total = matmul(rows[...], flat(weights[:, :, :, :, at]))
            if bias is not None:
                total = total + vectors[bias : bias + 1, span(index, CHUNK)]
            projected[:, at] = total.astype(jnp.bfloat16)
            return 0

        lax.fori_loop(0, chunks, one, 0)


def head_lanes(heads, rows, size):
    lane = lax.broadcasted_iota(jnp.int32, (rows, heads * size), 1) // size
    return [lane == head for head in range(heads)]


def stack_heads(value, lanes):
    return jnp.concatenate([jnp.where(lane, value, jnp.zeros_like(value)) for lane in lanes], axis=0)


def merge_heads(value, lanes):
    rows = value.shape[0] // len(lanes)
    result = value[:rows]
    for head in range(1, len(lanes)):
        result = jnp.where(lanes[head], value[head * rows : (head + 1) * rows], result)
    return result


QUAD = 4


def attend(projected, keep, probs, context, first, last):
    width = context.shape[1]
    size = width // HEADS
    length = keep.shape[1]
    scale = size ** (-0.5)
    lanes = head_lanes(QUAD, length, size)
    quads = HEADS // QUAD

    def one(index, _):
        segment = index // quads
        quad = lax.rem(index, quads)
        at = span(segment, length)
        queries = projected[at, span(quad, QUAD * size)]
        keysets = projected[at, span(quad + quads, QUAD * size)]
        valuesets = projected[at, span(quad + 2 * quads, QUAD * size)]
        scores = matmul_nt(stack_heads(queries, lanes), keysets) * scale
        mask = keep[pl.ds(segment, 1), :] > 0
        scores = jnp.where(mask, scores, neg_fill)
        raised = jnp.exp(scores - jnp.max(scores, axis=1, keepdims=True))
        low = (raised / jnp.sum(raised, axis=1, keepdims=True)).astype(jnp.bfloat16)
        probs[index] = low
        context[at, span(quad, QUAD * size)] = merge_heads(matmul(low, valuesets), lanes).astype(jnp.bfloat16)
        return 0

    lax.fori_loop(first, last, one, 0)


def center_scale(hidden):
    center = hidden - jnp.mean(hidden, axis=1, keepdims=True)
    spread = jnp.mean(center * center, axis=1, keepdims=True)
    rate = lax.rsqrt(spread + epsilon)
    return center * rate, rate


def first_block(rows, context, weights, vectors, first_sum, first_norm, first_low):
    def product(index, _):
        at = span(index, CHUNK)
        attended = matmul(context[...], flat(weights[:, :, :, :, at])) + vectors[2:3, at]
        first_sum[:, at] = rows[:, at].astype(jnp.float32) + attended
        return 0

    lax.fori_loop(0, rows.shape[1] // CHUNK, product, 0)

    def one(index, _):
        at = span(index, 64)
        normed, _ = center_scale(first_sum[at, :])
        result = normed * vectors[3:4, :] + vectors[4:5, :]
        first_norm[at, :] = result
        first_low[at, :] = result.astype(jnp.bfloat16)
        return 0

    lax.fori_loop(0, rows.shape[0] // 64, one, 0)


def inner_block(first_low, weights, long_bias, activated, slope, first, last):
    def one(index, _):
        at = span(index, CHUNK)
        value = matmul(first_low[...], flat(weights[:, :, :, :, at])) + long_bias[:, at]
        share = 0.5 * (1.0 + lax.erf(value * (0.5**0.5)))
        bell = jnp.exp(-0.5 * value * value) * ((0.5 / jnp.pi) ** 0.5)
        activated[:, at] = (value * share).astype(jnp.bfloat16)
        slope[:, at] = (share + value * bell).astype(jnp.bfloat16)
        return 0

    lax.fori_loop(first, last, one, 0)


def outer_part(activated, weights, row, total, fresh):
    size = weights.shape[1] * weights.shape[2] * weights.shape[3]

    def one(index, _):
        at = span(index, CHUNK)
        value = matmul(activated[:, span(row, size)], flat(weights[row, :, :, :, at]))
        total[:, at] = value if fresh else total[:, at] + value
        return 0

    lax.fori_loop(0, total.shape[1] // CHUNK, one, 0)


def norm_back(grad, normed, rate, gain):
    scaled = grad * gain
    mean = jnp.mean(scaled, axis=1, keepdims=True)
    along = jnp.mean(scaled * normed, axis=1, keepdims=True)
    return rate * (scaled - mean - normed * along)


def second_block(first_norm, total, cotangent, vectors, encoded, second_grad, outer_low, sums, first, last):

    def one(index, _):
        at = span(index, 64)
        normed, rate = center_scale(first_norm[at, :] + (total[at, :] + vectors[5:6, :]))
        gain = vectors[6:7, :]
        encoded[at, :] = (normed * gain + vectors[7:8, :]).astype(jnp.bfloat16)
        grad = cotangent[at, :].astype(jnp.float32)
        back = norm_back(grad, normed, rate, gain)
        low = back.astype(jnp.bfloat16)
        second_grad[at, :] = back
        outer_low[at, :] = low
        sums[5:6, :] += jnp.sum(low.astype(jnp.float32), axis=0, keepdims=True)
        sums[6:7, :] += jnp.sum(grad * normed, axis=0, keepdims=True)
        sums[7:8, :] += jnp.sum(grad, axis=0, keepdims=True)
        return 0

    lax.fori_loop(first, last, one, 0)


def forward_kernel(depth, block, *refs):
    (rows_in, keep, cotangent_in, query_own, key_own, value_own, attn_own, inner_own, outer_own) = refs[:9]
    short_vectors = refs[9:18]
    merged_out, attn_out, inner_out, outer_out = refs[18:22]
    (encoded_out, projected_out, probs_out, context_out, first_sum_out, first_low_out, activated_out, slope_out,
     second_grad_out, outer_low_out, vectors, sums) = refs[22:34]
    (table_own, merged_own, table, merged, attn, inner, outer, projected, probs, context, first_sum, first_norm, first_low,
     activated, slope, total, encoded, second_grad, outer_low, long_bias, save_sem, rows, cotangent, load_sem) = refs[34:58]
    sems = refs[58:]
    place = Place(depth)
    place.greet()
    loads = [
        pltpu.make_async_copy(rows_in, rows, load_sem.at[0]),
        pltpu.make_async_copy(cotangent_in, cotangent, load_sem.at[1]),
    ]
    table_own[...] = jnp.zeros_like(table_own)
    for index, vector in enumerate(short_vectors):
        table_own[index, : vector.shape[0]] = vector[...].astype(jnp.float32)
    width = rows.shape[1]
    for part, own in enumerate((query_own, key_own, value_own)):
        merged_own[:, part * width : (part + 1) * width] = own[...]
    net_table = Gather(place, table, table_own, sems, 0)
    net_merged = Gather(place, merged, merged_own, sems, 1)
    net_attn = Gather(place, attn, attn_own, sems, 2)
    net_inner = Gather(place, inner, inner_own, sems, 3)
    half = outer.shape[3] // 2
    net_outer = Gather(place, outer, outer_own, sems, 4, pl.ds(0, half))
    line = GatherLine(place, outer, outer_own, sems, 5, pl.ds(half, half))
    nets = (net_table, net_merged, net_attn, net_inner, net_outer, line)
    front = nets[:3]
    place.greeted()
    for copy in loads:
        copy.start()
    saves = []

    def save(source, target):
        copy = pltpu.make_async_copy(source, target, save_sem.at[len(saves)])
        copy.start()
        saves.append(copy)

    def hop(net, step):
        if step == depth - 1:
            net.last_hop()
        else:
            net.hop(step)

    def each(nets_of, *names, step):
        for name in names:
            for net in nets_of:
                hop(net, step) if name == "hop" else getattr(net, name)(step)

    for net in front:
        net.start()
    each(front, "send", step=0)
    line.start()
    each(front, "hop", "send", step=1)
    line.spread()
    net_inner.start()
    each(front, "spread", step=0)
    for step in range(2, depth):
        each(front, "hop", "send", step=step)
        each(front, "spread", step=step - 1)
    net_inner.send(0)
    net_outer.start()
    net_inner.hop(1)
    net_inner.send(1)
    each(front, "spread", step=depth - 1)
    net_inner.spread(0)
    net_outer.hop(1)
    for step in range(2, depth - 1):
        net_inner.hop(step)
        net_inner.send(step)
        net_inner.spread(step - 1)
    line.join()
    for net in front:
        net.arrive_far(0)
        net.arrive_far(1)
        net.arrive_core(0, 1, 2, 3)
    save(merged, merged_out)
    save(attn, attn_out)
    unpack_table(table, block, vectors, long_bias)
    loads[0].wait()
    project(rows, merged, vectors, projected)
    save(projected, projected_out)
    for step in range(2, depth - 1):
        net_outer.hop(step)
    net_inner.last_hop()
    net_inner.send(depth - 1)
    net_inner.spread(depth - 2)
    count = probs.shape[0]
    attend(projected, keep, probs, context, 0, count // 2)
    net_outer.last_hop()
    line.relay()
    net_inner.spread(depth - 1)
    attend(projected, keep, probs, context, count // 2, count)
    save(probs, probs_out)
    save(context, context_out)
    first_block(rows, context, attn, vectors, first_sum, first_norm, first_low)
    save(first_sum, first_sum_out)
    save(first_low, first_low_out)
    net_inner.arrive_far(0)
    for step in range(depth):
        net_outer.send(step)
    net_inner.arrive_far(1)
    net_inner.arrive_core(0, 1, 2, 3)
    save(inner, inner_out)
    quarter = inner.shape[4] // CHUNK // 4

    def inner_quarter(index):
        inner_block(first_low, inner, long_bias, activated, slope, index * quarter, (index + 1) * quarter)

    inner_quarter(0)
    net_outer.spread(0)
    inner_quarter(1)
    for step in range(1, depth - 1):
        net_outer.spread(step)
    inner_quarter(2)
    net_outer.spread(depth - 1)
    line.arrive()
    inner_quarter(3)
    save(activated, activated_out)
    save(slope, slope_out)
    sums[...] = jnp.zeros_like(sums)
    loads[1].wait()
    line.arrive_core()
    net_outer.arrive_core(0)
    outer_part(activated, outer, place.dp, total, True)
    net_outer.arrive_far(0)
    net_outer.arrive_core(1, 2)
    outer_part(activated, outer, place.near, total, False)
    outer_part(activated, outer, place.far, total, False)
    net_outer.arrive_far(1)
    net_outer.arrive_core(3)
    save(outer, outer_out)
    outer_part(activated, outer, place.both, total, False)
    for part in range(4):
        size = rows.shape[0] // 4
        second_block(
            first_norm, total, cotangent, vectors, encoded, second_grad, outer_low, sums, part * size // 64,
            (part + 1) * size // 64,
        )
        at = pl.ds(part * size, size)
        save(outer_low.at[at], outer_low_out.at[at])
        save(second_grad.at[at], second_grad_out.at[at])
        save(encoded.at[at], encoded_out.at[at])
    for net in nets:
        net.drain()
    for copy in saves:
        copy.wait()


def forward_all(depth, block, rows, keep, cotangent, owns):
    query_own, _, _, attn_own, inner_own, outer_own = owns[:6]
    tokens, width = rows.shape
    hidden = inner_own.shape[1]
    segments, length = keep.shape
    low, high = jnp.bfloat16, jnp.float32

    def fulls(own, columns):
        return (4, depth, 2, own.shape[0], columns)

    full_shapes = [fulls(query_own, 3 * width), fulls(attn_own, width), fulls(inner_own, hidden), fulls(outer_own, width)]
    kept = [
        ((tokens, width), low),
        ((tokens, 3 * width), low),
        ((segments * HEADS // QUAD, QUAD * length, length), low),
        ((tokens, width), low),
        ((tokens, width), high),
        ((tokens, width), low),
        ((tokens, hidden), low),
        ((tokens, hidden), low),
        ((tokens, width), high),
        ((tokens, width), low),
    ]
    small = [((8, width), high), ((8, width), high)]
    shapes = [jax.ShapeDtypeStruct(shape, low) for shape in full_shapes]
    shapes += [jax.ShapeDtypeStruct(*one) for one in kept + small]
    held = {name: pltpu.VMEM(*one) for name, one in zip(
        ("encoded", "projected", "probs", "context", "first_sum", "first_low", "activated", "slope", "second_grad", "outer_low"),
        kept)}
    scratch = [pltpu.VMEM((16, 128), high), pltpu.VMEM((query_own.shape[0], 3 * width), low)]
    scratch += [pltpu.VMEM((4, depth, 2, 16, 128), high)]
    scratch += [pltpu.VMEM(shape, low) for shape in full_shapes]
    scratch += [held[name] for name in ("projected", "probs", "context", "first_sum")]
    scratch += [pltpu.VMEM((tokens, width), high)]
    scratch += [held[name] for name in ("first_low", "activated", "slope")]
    scratch += [pltpu.VMEM((tokens, width), high)]
    scratch += [held[name] for name in ("encoded", "second_grad", "outer_low")]
    scratch += [pltpu.VMEM((1, hidden), high)]
    scratch += [pltpu.SemaphoreType.DMA((len(full_shapes) + len(kept) + 9,))]
    scratch += [pltpu.VMEM((tokens, width), low), pltpu.VMEM((tokens, width), low), pltpu.SemaphoreType.DMA((2,))]
    here = pl.BlockSpec(memory_space=pltpu.VMEM)
    away = pl.BlockSpec(memory_space=pl.ANY)
    return pl.pallas_call(
        functools.partial(forward_kernel, depth, block),
        out_shape=shapes,
        in_specs=[away, here, away] + [here] * len(owns),
        out_specs=[away] * (len(full_shapes) + len(kept)) + [here] * 2,
        scratch_shapes=scratch + gather_sems(6, depth),
        compiler_params=pltpu.CompilerParams(
            collective_id=0, has_side_effects=True, vmem_limit_bytes=60 * 1024 * 1024
        ),
        name="forward",
    )(rows, keep, cotangent, *owns)


SUBS = 4


class Slots:
    def __init__(self, core, far, near, along):
        self.core, self.far, self.near, self.along = core, far, near, along


class Scatter:
    def __init__(self, place, whole, slots, sems, credits, number, lot, first, count, after=False, before=False,
                 late_after=False, late_before=False):
        self.place, self.whole, self.slots = place, whole, slots
        self.sc, self.rc, self.sa, self.ra, self.sb, self.rb, self.sz, self.rz = sems
        self.core_free, self.far_free, self.near_free, self.z_free = credits
        self.number, self.lot, self.first, self.count = number, lot, first, count
        self.sub = first * SUBS // whole.shape[3]
        self.after, self.before, self.late_after, self.late_before = after, before, late_after, late_before
        self.tile = 8 if whole.dtype == jnp.float32 else 16

    def lines(self):
        return pl.ds(self.first, self.count)

    def mine(self, row):
        return self.whole.at[row, :, self.place.core, self.lines()]

    def sent_row(self, at):
        p = self.place
        return (p.both, p.near, p.far, p.dp)[at]

    def got_row(self, at):
        p = self.place
        return (p.both, p.far, p.near, p.dp)[at]

    def copy_core(self, at):
        p = self.place
        return remote(
            self.whole.at[self.sent_row(at), :, 1 - p.core, self.lines()], self.slots.core.at[at, :, self.lines()],
            self.sc.at[self.number, at], self.rc.at[self.number, at], (p.dp, p.sibling),
        )

    def copy_far(self, half):
        p = self.place
        return remote(
            self.mine(p.both if half else p.far), self.slots.far.at[self.lot, half, :, self.lines()],
            self.sa.at[self.number, half], self.ra.at[self.number, half], (p.far, p.fsdp),
        )

    def copy_near(self):
        p = self.place
        return remote(
            self.mine(p.near), self.slots.near.at[self.lot, :, self.lines()], self.sb.at[self.number],
            self.rb.at[self.number], (p.near, p.fsdp),
        )

    def copy_z(self, step):
        p = self.place
        return remote(
            self.whole.at[p.dp, p.up(step), p.core, self.lines()], self.slots.along.at[self.lot, step - 1, self.lines()],
            self.sz.at[self.number, step - 1], self.rz.at[self.number, step - 1], p.along(p.up(step)),
        )

    def add(self, row, slot):
        p = self.place
        tiles = self.count // self.tile

        def one(index, _):
            z = index // tiles
            at = pl.ds(pl.multiple_of(self.first + lax.rem(index, tiles) * self.tile, self.tile), self.tile)
            self.whole[row, z, p.core, at, :] = self.whole[row, z, p.core, at, :] + slot[z, at, :]
            return 0

        lax.fori_loop(0, p.depth * tiles, one, 0)

    def start_core(self, at):
        if self.after:
            pl.semaphore_wait(self.core_free.at[at, self.sub], 1)
        self.copy_core(at).start()

    def add_core(self, at):
        p = self.place
        self.copy_core(at).wait_recv()
        self.add(self.got_row(at), self.slots.core.at[at])
        if self.before:
            pl.semaphore_signal(self.core_free.at[at, self.sub], inc=1, device_id=(p.dp, p.sibling), device_id_type=MESH)

    def start_far(self, half):
        if self.late_after:
            pl.semaphore_wait(self.far_free.at[half, self.sub], 1)
        self.copy_far(half).start()

    def add_far(self, half):
        p = self.place
        self.copy_far(half).wait_recv()
        self.add(p.near if half else p.dp, self.slots.far.at[self.lot, half])
        if self.late_before:
            pl.semaphore_signal(self.far_free.at[half, self.sub], inc=1, device_id=(p.far, p.fsdp), device_id_type=MESH)
        if half:
            if self.late_after:
                pl.semaphore_wait(self.near_free.at[self.sub], 1)
            self.copy_near().start()

    def add_near(self):
        p = self.place
        self.copy_near().wait_recv()
        self.add(p.dp, self.slots.near.at[self.lot])
        if self.late_before:
            pl.semaphore_signal(self.near_free.at[self.sub], inc=1, device_id=(p.near, p.fsdp), device_id_type=MESH)
        for step in range(1, p.depth):
            if self.late_after:
                pl.semaphore_wait(self.z_free.at[self.sub, step - 1], 1)
            self.copy_z(step).start()

    def finish(self, out):
        p = self.place
        for step in range(1, p.depth):
            self.copy_z(step).wait_recv()

        def one(index, _):
            start = pl.multiple_of(index * self.tile, self.tile)
            at = pl.ds(pl.multiple_of(self.first + start, self.tile), self.tile)
            total = self.whole[p.dp, p.z, p.core, at, :].astype(jnp.float32)
            for step in range(p.depth - 1):
                total = total + self.slots.along[self.lot, step, at, :].astype(jnp.float32)
            out[pl.ds(start, self.tile), :] = total
            return 0

        lax.fori_loop(0, self.count // self.tile, one, 0)
        if self.late_before:
            for step in range(1, p.depth):
                pl.semaphore_signal(
                    self.z_free.at[self.sub, step - 1], inc=1, device_id=p.along(p.down(step)), device_id_type=MESH
                )

    def drain(self):
        for at in range(4):
            self.copy_core(at).wait_send()
        self.copy_far(1).wait_send()
        self.copy_far(0).wait_send()
        self.copy_near().wait_send()
        for step in range(1, self.place.depth):
            self.copy_z(step).wait_send()


class ScatterLine(Scatter):
    def column(self, z):
        return self.whole.at[:, z, self.place.core, self.lines()]

    def copy_pair(self, part):
        p = self.place
        return remote(
            self.column(p.cross if part else p.pair), self.slots.far.at[0, part, :, self.lines()],
            self.sa.at[self.number, part], self.ra.at[self.number, part], p.along(p.pair),
        )

    def copy_jump(self):
        p = self.place
        return remote(
            self.column(p.jump), self.slots.near.at[0, :, self.lines()], self.sb.at[self.number], self.rb.at[self.number],
            p.along(p.jump),
        )

    def copy_axis(self, part):
        p = self.place
        row = (p.both, p.far, p.near)[part]
        target = p.near if part == 2 else p.far
        return remote(
            self.whole.at[row, p.z, p.core, self.lines()], self.slots.along.at[0, part, self.lines()],
            self.sz.at[self.number, part], self.rz.at[self.number, part], (target, p.fsdp),
        )

    def add_column(self, z, slot):
        p = self.place
        tiles = self.count // self.tile

        def one(index, _):
            row = index // tiles
            at = pl.ds(pl.multiple_of(self.first + lax.rem(index, tiles) * self.tile, self.tile), self.tile)
            self.whole[row, z, p.core, at, :] = self.whole[row, z, p.core, at, :] + slot[row, at, :]
            return 0

        lax.fori_loop(0, self.whole.shape[0] * tiles, one, 0)

    def add_block(self, row, part):
        p = self.place

        def one(index, _):
            at = pl.ds(pl.multiple_of(self.first + index * self.tile, self.tile), self.tile)
            self.whole[row, p.z, p.core, at, :] = self.whole[row, p.z, p.core, at, :] + self.slots.along[0, part, at, :]
            return 0

        lax.fori_loop(0, self.count // self.tile, one, 0)

    def tell(self, semaphore, device):
        pl.semaphore_signal(semaphore, inc=1, device_id=device, device_id_type=MESH)

    def add_core(self, at):
        p = self.place
        self.copy_core(at).wait_recv()
        self.add(self.got_row(at), self.slots.core.at[at])
        for sub in range(SUBS // 2, SUBS):
            self.tell(self.core_free.at[at, sub], (p.dp, p.sibling))

    def start_pair(self):
        self.copy_pair(1).start()
        self.copy_pair(0).start()

    def add_pair(self, part):
        p = self.place
        self.copy_pair(part).wait_recv()
        self.add_column(p.jump if part else p.z, self.slots.far.at[0, part])
        if part:
            self.copy_jump().start()
        for sub in range(SUBS // 2, SUBS):
            self.tell(self.far_free.at[part, sub], (p.far, p.fsdp))

    def add_jump(self):
        p = self.place
        self.copy_jump().wait_recv()
        self.add_column(p.z, self.slots.near.at[0])
        for sub in range(SUBS // 2, SUBS):
            self.tell(self.near_free.at[sub], (p.near, p.fsdp))
        self.copy_axis(0).start()
        self.copy_axis(1).start()

    def add_far_axis(self):
        p = self.place
        for part in range(2):
            self.copy_axis(part).wait_recv()
            self.add_block(p.dp if part else p.near, part)
        self.copy_axis(2).start()

    def finish(self, out):
        p = self.place
        self.copy_axis(2).wait_recv()

        def one(index, _):
            start = pl.multiple_of(index * self.tile, self.tile)
            at = pl.ds(pl.multiple_of(self.first + start, self.tile), self.tile)
            total = self.whole[p.dp, p.z, p.core, at, :].astype(jnp.float32)
            out[pl.ds(start, self.tile), :] = total + self.slots.along[0, 2, at, :].astype(jnp.float32)
            return 0

        lax.fori_loop(0, self.count // self.tile, one, 0)
        for sub in range(SUBS // 2, SUBS):
            for step in range(1, p.depth):
                self.tell(self.z_free.at[sub, step - 1], p.along(p.down(step)))

    def drain(self):
        for at in range(4):
            self.copy_core(at).wait_send()
        for part in range(2):
            self.copy_pair(part).wait_send()
        self.copy_jump().wait_send()
        for part in range(3):
            self.copy_axis(part).wait_send()


def outer_gradient(acts, low, grads, row):
    depth, cores, count, _ = grads.shape[1:]
    size = cores * count

    def one(z, _):
        value = matmul_tn(acts[row, :, span(z, size)], low[...])
        grads[row, z] = value.astype(jnp.bfloat16).reshape(grads.shape[2:])
        return 0

    lax.fori_loop(0, depth, one, 0)


def input_gradient(inputs, low, grads, row, part):
    depth, cores, count, width = grads.shape[1:]
    size = inputs.shape[1] // grads.shape[0]
    lines = count // SUBS
    value = matmul_tn(inputs[:, span(row, size)], low)
    grads[row, :, :, part * lines : (part + 1) * lines, :] = value.astype(jnp.bfloat16).reshape(depth, cores, lines, width)


def hidden_back(low, weights, slopes, bias_sum, part):
    depth, cores, count, width = weights.shape[1:]
    size = cores * count

    def one(index, _):
        at = span(index, size)
        value = matmul_nt(low[...], flat(weights[part, index])) * slopes[SUBS + part, :, at].astype(jnp.float32)
        rounded = value.astype(jnp.bfloat16)
        slopes[SUBS + part, :, at] = rounded
        total = jnp.sum(rounded.astype(jnp.float32), axis=0, keepdims=True)
        bias_sum[:, pl.ds(pl.multiple_of(part * width + index * size, size), size)] = total
        return 0

    lax.fori_loop(0, depth, one, 0)


def first_total_rows(grad, inner_low, weights):
    lines = weights.shape[3] // SUBS
    size = grad.shape[1] // weights.shape[0]

    def one(index, _):
        at = span(index, size)
        total = grad[:, at]
        for part in range(SUBS):
            weight = flat(weights[index, :, :, part * lines : (part + 1) * lines, :])
            total = total + matmul_nt(inner_low[SUBS + part], weight)
        grad[:, at] = total
        return 0

    lax.fori_loop(0, weights.shape[0], one, 0)


def first_back(first_sum, grad, low, vectors, sums):
    for row in (2, 3, 4):
        sums[row : row + 1, :] = jnp.zeros((1, grad.shape[1]), jnp.float32)

    def one(index, _):
        at = span(index, 64)
        normed, rate = center_scale(first_sum[at, :])
        upper = grad[at, :]
        back = norm_back(upper, normed, rate, vectors[3:4, :])
        rounded = back.astype(jnp.bfloat16)
        grad[at, :] = back
        low[at, :] = rounded
        sums[2:3, :] += jnp.sum(rounded.astype(jnp.float32), axis=0, keepdims=True)
        sums[3:4, :] += jnp.sum(upper * normed, axis=0, keepdims=True)
        sums[4:5, :] += jnp.sum(upper, axis=0, keepdims=True)
        return 0

    lax.fori_loop(0, grad.shape[0] // 64, one, 0)


def context_back(low, weights, context):
    halves = weights.shape[1] // CHUNK

    def one(index, _):
        weight = weights[index // halves, span(lax.rem(index, halves), CHUNK), :]
        context[:, span(index, CHUNK)] = matmul_nt(low[...], weight).astype(jnp.bfloat16)
        return 0

    lax.fori_loop(0, context.shape[1] // CHUNK, one, 0)


def attend_back(projected, probs, context_low, sums, first, last):
    width = context_low.shape[1]
    size = width // HEADS
    length = probs.shape[2]
    scale = size ** (-0.5)
    lanes = head_lanes(QUAD, length, size)
    quads = HEADS // QUAD

    def one(index, _):
        segment = index // quads
        quad = lax.rem(index, quads)
        at = span(segment, length)
        columns = [span(quad + part * quads, QUAD * size) for part in range(3)]
        queries, keysets, valuesets = [projected[at, column] for column in columns]
        low = probs[index]
        wide = low.astype(jnp.float32)
        upper = stack_heads(context_low[at, columns[0]], lanes)
        prob_grad = matmul_nt(upper, valuesets)
        score_low = (wide * (prob_grad - jnp.sum(wide * prob_grad, axis=1, keepdims=True))).astype(jnp.bfloat16)
        value_low = matmul_tn(low, upper).astype(jnp.bfloat16)
        query_low = (merge_heads(matmul(score_low, keysets), lanes) * scale).astype(jnp.bfloat16)
        key_low = (matmul_tn(score_low, stack_heads(queries, lanes)) * scale).astype(jnp.bfloat16)
        projected[at, columns[0]] = query_low
        projected[at, columns[1]] = key_low
        projected[at, columns[2]] = value_low
        sums[0:1, columns[0]] += jnp.sum(query_low.astype(jnp.float32), axis=0, keepdims=True)
        sums[1:2, columns[0]] += jnp.sum(value_low.astype(jnp.float32), axis=0, keepdims=True)
        return 0

    lax.fori_loop(first, last, one, 0)


def states_back(grad, projected, weights):
    width = grad.shape[1]
    halves = weights.shape[1] // CHUNK

    def one(index, _):
        at = span(index, CHUNK)
        total = grad[:, at]
        for part in range(3):
            weight = weights[2 + 2 * part + index // halves, span(lax.rem(index, halves), CHUNK), :]
            total = total + matmul_nt(projected[:, part * width : (part + 1) * width], weight)
        grad[:, at] = total
        return 0

    lax.fori_loop(0, width // CHUNK, one, 0)


def pack_sums(sums, bias_sum, block, table):
    dps, depth, cores = table.shape[:3]
    places = dps * depth * cores
    width = sums.shape[1]
    lane = lax.broadcasted_iota(jnp.int32, (width, 128), 1)
    source = lax.broadcasted_iota(jnp.int32, (width, 128), 0)
    pick = jnp.where(lane == lax.rem(source, block), 1.0, 0.0).astype(jnp.bfloat16)
    owner = lax.broadcasted_iota(jnp.int32, (places, width), 1) // block
    mine = owner == lax.broadcasted_iota(jnp.int32, (places, width), 0)
    values = jnp.concatenate([jnp.where(mine, sums[vector : vector + 1, :], 0.0) for vector in range(8)], axis=0)
    upper = values.astype(jnp.bfloat16)
    lower = (values - upper.astype(jnp.float32)).astype(jnp.bfloat16)
    total = matmul(upper, pick) + matmul(lower, pick)
    table[...] = jnp.zeros_like(table)
    for vector in range(8):
        table[:, :, :, vector, :] = total[vector * places : (vector + 1) * places].reshape(dps, depth, cores, 128)
    for index in range(places):
        dp, z, core = index // (depth * cores), index // cores % depth, index % cores
        table[dp, z, core, 8:9, :] = bias_sum[:, index * 128 : (index + 1) * 128]


EARLY = 3
SCHEDULE = (
    ("outer",), ("hidden",), ("far", 0), ("inner",), ("line", 0), ("far", 1), ("near", 0), ("total",), ("line", 1),
    ("norm",), ("attn",), ("context",), ("far", 2), ("go", 5), ("go", 6), ("near", 1), ("heads", 0), ("heads", 1),
    ("far", 3), ("near", 2), ("line", 2), ("merged",), ("go", 7), ("far", 4), ("near", 3), ("end", 0), ("far", 5),
    ("go", 8), ("near", 4), ("end", 1), ("line", 3), ("pack",), ("states",), ("far", 6), ("go", 9), ("go", 10),
    ("near", 5), ("line", 4), ("end", 2), ("far", 7), ("go", 11), ("near", 6), ("end", 3), ("far", 8), ("near", 7),
    ("end", 4), ("far", 9), ("far", 10), ("near", 8), ("end", 5), ("near", 9), ("far", 11), ("near", 10), ("end", 6),
    ("end", 7), ("near", 11), ("end", 8), ("end", 9), ("end", 10), ("end", 11),
)


def backward_kernel(depth, block, *refs):
    (vectors, known, rows_in, activated_in, slope_in, outer_low_in, second_grad_in, first_sum_in, first_low_in, context_in,
     projected_in, probs_in, merged_in, attn_in, inner_in, outer_in) = refs[:16]
    states_out, outer_out, inner_out, query_out, key_out, value_out, attn_out, table_out = refs[16:24]
    (first_buffer, second_buffer, outer_grads, wide, from_core, from_far, from_near, from_z, low, first_low, grad, first_sum,
     context, projected, probs, rows, sums, bias_sum, table, table_core, table_far, table_near, table_z) = refs[24:47]
    load_sem, save_sem = refs[47:49]
    sems = refs[49:57]
    credits = refs[57:61]
    place = Place(depth)
    place.greet()
    width = rows.shape[1]
    tokens = rows.shape[0]
    lines = outer_grads.shape[3] // SUBS
    loads = []

    def load(source, target):
        copy = pltpu.make_async_copy(source, target, load_sem.at[len(loads)])
        copy.start()
        loads.append(copy)
        return copy

    def load_columns(source, targets):
        return [load(source.at[:, part * width : (part + 1) * width], target) for part, target in enumerate(targets)]

    low_load = load(outer_low_in, low)
    act_loads = load_columns(activated_in, [wide.at[part] for part in range(SUBS)])
    outer_load = load(outer_in, first_buffer)
    slope_loads = load_columns(slope_in, [wide.at[SUBS + part] for part in range(SUBS)])
    first_low_load = load(first_low_in, first_low)
    grad_load = load(second_grad_in, grad)
    inner_loads = [
        load(inner_in.at[:, :, :, :, part * width : (part + 1) * width],
             second_buffer.at[:, :, :, part * lines : (part + 1) * lines, :])
        for part in range(SUBS)
    ]
    first_sum_load = load(first_sum_in, first_sum)
    context_load = load(context_in, context)
    projected_load = load(projected_in, projected)
    probs_load = load(probs_in, probs)
    rows_load = load(rows_in, rows)

    slots = Slots(from_core, from_far, from_near, from_z)
    table_slots = Slots(table_core, table_far, table_near, table_z)
    outers = [
        Scatter(place, outer_grads, slots, sems, credits, sub, 0, sub * lines, lines, before=True, late_before=True)
        for sub in range(SUBS // 2)
    ]
    line = ScatterLine(place, outer_grads, slots, sems, credits, SUBS - 1, 0, SUBS // 2 * lines, SUBS // 2 * lines)
    inner_grads = first_buffer
    inners = [
        Scatter(place, inner_grads, slots, sems, credits, SUBS + sub, 1, sub * lines, lines, after=True, before=True)
        for sub in range(SUBS)
    ]
    other_grads = second_buffer
    others = [
        Scatter(place, other_grads, slots, sems, credits, 2 * SUBS + sub, 0, sub * lines, lines, after=True, late_after=True)
        for sub in range(SUBS - 1)
    ]
    attn_net = others[0]
    mergeds = others[1:3]
    lowest = lines // 2
    mergeds += [
        Scatter(place, other_grads, slots, sems, credits, 3 * SUBS - 1, 0, 3 * lines, lowest, after=True, late_after=True),
        Scatter(place, other_grads, slots, sems, credits, 3 * SUBS + 1, 0, 3 * lines + lowest, lowest),
    ]
    small = Scatter(place, table, table_slots, sems, credits, 3 * SUBS, 0, 0, 16)
    row_order = (place.both, place.near, place.far, place.dp)
    sums[...] = known[...]
    sums[0:2, :] = jnp.zeros((2, width), jnp.float32)

    def pieces(nets, compute, early=(), first=False):
        def added(at):
            for net in nets:
                net.add_core(at)
            if at < 2:
                for net in early:
                    net.start_far(1 - at)

        for at in range(4):
            compute(row_order[at])
            if first and at == 0:
                place.greeted()
            for net in nets:
                net.start_core(at)
            if at:
                added(at - 1)
        added(3)

    order = outers + inners + [attn_net] + mergeds[:2] + [small] + mergeds[2:]
    outs = [outer_out.at[pl.ds(sub * lines, lines), :] for sub in range(SUBS // 2)]
    outs += [inner_out.at[:, pl.ds(sub * width, width)] for sub in range(SUBS)]
    outs += [attn_out, query_out, key_out, table_out, value_out.at[pl.ds(0, lowest), :], value_out.at[pl.ds(lowest, lowest), :]]
    def far(number):
        order[number].add_far(1)
        order[number].add_far(0)

    def go(number):
        order[number].start_far(1)
        order[number].start_far(0)

    def near(number):
        order[number].add_near()

    def end(number):
        order[number].finish(outs[number])

    def ready(copies):
        for copy in copies:
            copy.wait()

    def load_merged(part):
        return [
            load(merged_in.at[at * tokens : (at + 1) * tokens, part * width : (part + 1) * width], wide.at[2 + 2 * part + at])
            for at in range(2)
        ]

    late_loads = []

    def outer_step():
        ready([low_load] + act_loads)
        pieces(outers + [line], lambda row: outer_gradient(wide, low, outer_grads, row), outers, True)
        line.start_pair()
        late_loads.append(load(attn_in.at[:tokens], wide.at[0]))
        late_loads.append(load(attn_in.at[tokens:], wide.at[1]))
        late_loads.extend(load_merged(0))

    def hidden_step():
        ready([outer_load] + slope_loads)
        for part in range(SUBS):
            hidden_back(low, first_buffer, wide, bias_sum, part)

    def inner_step():
        def compute(row):
            for part in range(SUBS):
                input_gradient(first_low, wide[SUBS + part], inner_grads, row, part)

        ready([first_low_load])
        pieces(inners, compute, inners[:EARLY])

    def total_step():
        ready([grad_load] + inner_loads)
        first_total_rows(grad, wide, second_buffer)
        late_loads.extend(load_merged(1) + load_merged(2))

    def norm_step():
        ready([first_sum_load])
        first_back(first_sum, grad, low, vectors, sums)

    def attn_step():
        ready([context_load])
        pieces([attn_net], lambda row: input_gradient(context, low[...], other_grads, row, 0))

    def context_step():
        ready(late_loads[:2])
        context_back(low, wide, context)

    def heads_step(part):
        if part == 0:
            ready([projected_load, probs_load])
        count = probs.shape[0]
        attend_back(projected, probs, context, sums, part * count // 2, (part + 1) * count // 2)

    def merged_step():
        def compute(row):
            for part in range(3):
                input_gradient(rows, projected[:, part * width : (part + 1) * width], other_grads, row, 1 + part)

        ready([rows_load])
        pieces(mergeds, compute)

    def pack_step():
        pack_sums(sums, bias_sum, block, table)
        pieces([small], lambda row: None)

    save = pltpu.make_async_copy(grad, states_out, save_sem)

    def states_step():
        ready(late_loads[2:])
        states_back(grad, projected, wide)
        save.start()

    def line_step(part):
        (line.add_pair, line.add_jump, line.add_far_axis, line.finish)[max(part - 1, 0)](
            *(((1,), (0,), (), (), (outer_out.at[pl.ds(SUBS // 2 * lines, SUBS // 2 * lines), :],))[part])
        )

    steps = {
        "outer": outer_step, "hidden": hidden_step, "inner": inner_step, "total": total_step, "norm": norm_step,
        "attn": attn_step, "context": context_step, "heads": heads_step, "merged": merged_step, "pack": pack_step,
        "states": states_step, "line": line_step, "go": go, "far": far, "near": near, "end": end,
    }
    for entry in SCHEDULE:
        steps[entry[0]](*entry[1:])
    for net in order + [line]:
        net.drain()
    save.wait()


def backward_all(depth, block, vectors, known, kept):
    low, high = jnp.bfloat16, jnp.float32
    (rows, activated, _, _, _, first_sum, _, _, projected, probs, _, _, inner, outer) = kept
    tokens, width = rows.shape
    hidden = activated.shape[1]
    unit = outer.shape
    lines = unit[3]
    own_rows = lines // SUBS
    dma, regular = pltpu.SemaphoreType.DMA, pltpu.SemaphoreType.REGULAR
    nets = 3 * SUBS + 2
    scratch = [
        pltpu.VMEM(unit, low),
        pltpu.VMEM(unit, low),
        pltpu.VMEM(unit, low),
        pltpu.VMEM((2 * SUBS, tokens, width), low),
        pltpu.VMEM((4, depth, lines, width), low),
        pltpu.VMEM((2, 2, depth, lines, width), low),
        pltpu.VMEM((2, depth, lines, width), low),
        pltpu.VMEM((2, depth - 1, lines, width), low),
        pltpu.VMEM((tokens, width), low),
        pltpu.VMEM((tokens, width), low),
        pltpu.VMEM((tokens, width), high),
        pltpu.VMEM((tokens, width), high),
        pltpu.VMEM((tokens, width), low),
        pltpu.VMEM(projected.shape, low),
        pltpu.VMEM(probs.shape, low),
        pltpu.VMEM((tokens, width), low),
        pltpu.VMEM((8, width), high),
        pltpu.VMEM((1, hidden), high),
        pltpu.VMEM((4, depth, 2, 16, 128), high),
        pltpu.VMEM((4, depth, 16, 128), high),
        pltpu.VMEM((1, 2, depth, 16, 128), high),
        pltpu.VMEM((1, depth, 16, 128), high),
        pltpu.VMEM((1, depth - 1, 16, 128), high),
        dma((40,)),
        dma,
        dma((nets, 4)), dma((nets, 4)), dma((nets, 2)), dma((nets, 2)), dma((nets,)), dma((nets,)),
        dma((nets, depth - 1)), dma((nets, depth - 1)),
        regular((4, SUBS)), regular((2, SUBS)), regular((SUBS,)), regular((SUBS, depth - 1)),
    ]
    shapes = [(tokens, width), (lines, width), (own_rows, hidden)] + [(own_rows, width)] * 4 + [(16, 128)]
    here = pl.BlockSpec(memory_space=pltpu.VMEM)
    away = pl.BlockSpec(memory_space=pl.ANY)
    return pl.pallas_call(
        functools.partial(backward_kernel, depth, block),
        out_shape=[jax.ShapeDtypeStruct(shape, high) for shape in shapes],
        in_specs=[here] * 2 + [away] * len(kept),
        out_specs=[away] + [here] * 7,
        scratch_shapes=scratch,
        compiler_params=pltpu.CompilerParams(
            collective_id=1, has_side_effects=True, vmem_limit_bytes=62 * 1024 * 1024
        ),
        name="backward",
    )(vectors, known, *kept)


def finish_kernel(block, *refs):
    count = 8
    table = refs[0]
    sources, targets = refs[1 : 1 + count], refs[1 + count : 1 + 2 * count]
    rows = refs[1 + 2 * count : 10 + 2 * count]
    held = refs[10 + 2 * count : 10 + 3 * count]
    in_sem, out_sem = refs[10 + 3 * count :]
    fetches = [pltpu.make_async_copy(source, target, in_sem.at[at]) for at, (source, target) in enumerate(zip(sources, held))]
    stores = [pltpu.make_async_copy(source, target, out_sem.at[at]) for at, (source, target) in enumerate(zip(held, targets))]
    for copy in fetches:
        copy.start()
    for index, row in enumerate(rows):
        row[...] = table[index, : row.shape[0]]
    for fetch, store in zip(fetches, stores):
        fetch.wait()
        store.start()
    for store in stores:
        store.wait()


def finish_all(block, table, arrays):
    shapes = [jax.ShapeDtypeStruct(array.shape, array.dtype) for array in arrays]
    shapes += [jax.ShapeDtypeStruct((block,), jnp.float32)] * 8 + [jax.ShapeDtypeStruct((128,), jnp.float32)]
    here = pl.BlockSpec(memory_space=pltpu.VMEM)
    away = pl.BlockSpec(memory_space=pltpu.HBM)
    dma = pltpu.SemaphoreType.DMA
    return pl.pallas_call(
        functools.partial(finish_kernel, block),
        out_shape=shapes,
        in_specs=[here] + [away] * len(arrays),
        out_specs=[away] * len(arrays) + [here] * 9,
        scratch_shapes=[pltpu.VMEM(array.shape, array.dtype) for array in arrays] + [dma((len(arrays),))] * 2,
        compiler_params=pltpu.CompilerParams(vmem_limit_bytes=60 * 1024 * 1024),
        name="finish",
    )(table, *arrays)


def normalize(hidden, gain, shift):
    center = hidden - jnp.mean(hidden, axis=-1, keepdims=True)
    spread = jnp.mean(center * center, axis=-1, keepdims=True)
    return center * lax.rsqrt(spread + epsilon) * gain + shift


def exact_gelu(value):
    return jax.nn.gelu(value, approximate=False)


def contract_rows(left, right):
    return lax.dot_general(
        left, right, (((0,), (0,)), ((), ())), preferred_element_type=jnp.float32
    )


def times_transposed(left, right):
    return lax.dot_general(
        left, right, (((1,), (1,)), ((), ())), preferred_element_type=jnp.float32
    )


def collect(merged, attn, inner, outer, vectors, widened):
    return (
        lax.all_gather(merged, ("dp", "fsdp"), axis=0, tiled=True),
        lax.all_gather(attn, ("dp", "fsdp"), axis=0, tiled=True),
        lax.all_gather(inner, ("dp", "fsdp"), axis=0, tiled=True),
        lax.all_gather(outer, ("dp", "fsdp"), axis=0, tiled=True),
        lax.all_gather(vectors, ("dp", "fsdp"), axis=0, tiled=True),
        lax.all_gather(widened, ("dp", "fsdp"), axis=0, tiled=True),
    )


def reduce_grads(merged, attn, inner, outer, vectors, widened):
    return (
        lax.psum_scatter(merged, ("dp", "fsdp"), scatter_dimension=0, tiled=True),
        lax.psum_scatter(attn, ("dp", "fsdp"), scatter_dimension=0, tiled=True),
        lax.psum_scatter(inner, ("dp", "fsdp"), scatter_dimension=0, tiled=True),
        lax.psum_scatter(outer, ("dp", "fsdp"), scatter_dimension=0, tiled=True),
        lax.psum_scatter(vectors, ("dp", "fsdp"), scatter_dimension=0, tiled=True),
        lax.psum_scatter(widened, ("dp", "fsdp"), scatter_dimension=0, tiled=True),
    )


def split_heads(projected, segments):
    total_rows, triple = projected.shape
    width = triple // 3
    return projected.reshape(segments, total_rows // segments, 3, HEADS, width // HEADS)


def attention_probs(queries, keysets, keep, scale):
    scores = (
        jnp.einsum("sqhd,skhd->shqk", queries, keysets, preferred_element_type=jnp.float32) * scale
    )
    scores = jnp.where(keep[:, None, None, :] > 0, scores, neg_fill)
    peaks = jnp.max(scores, axis=-1, keepdims=True)
    raised = jnp.exp(scores - peaks)
    return raised / jnp.sum(raised, axis=-1, keepdims=True)


def forward_pass(rows, keep, weights):
    merged, attn, inner, outer, vectors, widened = weights
    vector_full = vectors.astype(jnp.float32)
    width = rows.shape[1]
    scale = (width // HEADS) ** (-0.5)
    merged_bias = jnp.concatenate(
        (vector_full[:, 0], jnp.zeros((width,), jnp.float32), vector_full[:, 1])
    )
    projected = (jnp.dot(rows, merged, preferred_element_type=jnp.float32) + merged_bias).astype(
        jnp.bfloat16
    )
    split = split_heads(projected, keep.shape[0])
    probs = attention_probs(split[:, :, 0], split[:, :, 1], keep, scale).astype(jnp.bfloat16)
    context = jnp.einsum(
        "shqk,skhd->sqhd", probs, split[:, :, 2], preferred_element_type=jnp.float32
    )
    context = context.reshape(rows.shape[0], width).astype(jnp.bfloat16)
    attended = jnp.dot(context, attn, preferred_element_type=jnp.float32) + vector_full[:, 2]
    first_sum = rows.astype(jnp.float32) + attended
    first_norm = normalize(first_sum, vector_full[:, 3], vector_full[:, 4])
    first_low = first_norm.astype(jnp.bfloat16)
    inner_act = jnp.dot(first_low, inner, preferred_element_type=jnp.float32) + widened.astype(
        jnp.float32
    )
    activated = exact_gelu(inner_act).astype(jnp.bfloat16)
    outer_act = jnp.dot(activated, outer, preferred_element_type=jnp.float32) + vector_full[:, 5]
    second_sum = first_norm + outer_act
    encoded = normalize(second_sum, vector_full[:, 6], vector_full[:, 7]).astype(jnp.bfloat16)
    return (encoded, (projected, context, first_sum, first_low, inner_act, activated, second_sum))


def backward_pass(rows, keep, cotangent, weights, kept):
    merged, attn, inner, outer, vectors, widened = weights
    projected, context, first_sum, first_low, inner_act, activated, second_sum = kept
    vector_full = vectors.astype(jnp.float32)
    width = rows.shape[1]
    scale = (width // HEADS) ** (-0.5)
    second_out, second_pull = jax.vjp(normalize, second_sum, vector_full[:, 6], vector_full[:, 7])
    second_grad, second_gain_g, second_shift_g = second_pull(cotangent.astype(jnp.float32))
    outer_low = second_grad.astype(jnp.bfloat16)
    outer_bias_g = jnp.sum(outer_low.astype(jnp.float32), axis=0)
    outer_weight_g = contract_rows(activated, outer_low)
    act_grad = times_transposed(outer_low, outer)
    gelu_out, gelu_pull = jax.vjp(exact_gelu, inner_act)
    inner_low = gelu_pull(act_grad)[0].astype(jnp.bfloat16)
    inner_bias_g = jnp.sum(inner_low.astype(jnp.float32), axis=0)
    inner_weight_g = contract_rows(first_low, inner_low)
    first_total = second_grad + times_transposed(inner_low, inner)
    first_out, first_pull = jax.vjp(normalize, first_sum, vector_full[:, 3], vector_full[:, 4])
    first_grad, first_gain_g, first_shift_g = first_pull(first_total)
    attended_low = first_grad.astype(jnp.bfloat16)
    attn_bias_g = jnp.sum(attended_low.astype(jnp.float32), axis=0)
    attn_weight_g = contract_rows(context, attended_low)
    context_low = times_transposed(attended_low, attn).astype(jnp.bfloat16)
    split = split_heads(projected, keep.shape[0])
    queries = split[:, :, 0]
    keysets = split[:, :, 1]
    valuesets = split[:, :, 2]
    probs = attention_probs(queries, keysets, keep, scale)
    probs_low = probs.astype(jnp.bfloat16)
    context_heads = context_low.reshape(queries.shape)
    prob_grad = jnp.einsum(
        "sqhd,skhd->shqk", context_heads, valuesets, preferred_element_type=jnp.float32
    )
    value_grad = jnp.einsum(
        "shqk,sqhd->skhd", probs_low, context_heads, preferred_element_type=jnp.float32
    )
    score_low = (probs * (prob_grad - jnp.sum(probs * prob_grad, axis=-1, keepdims=True))).astype(
        jnp.bfloat16
    )
    query_grad = (
        jnp.einsum("shqk,skhd->sqhd", score_low, keysets, preferred_element_type=jnp.float32)
        * scale
    )
    key_grad = (
        jnp.einsum("shqk,sqhd->skhd", score_low, queries, preferred_element_type=jnp.float32)
        * scale
    )
    merged_low = jnp.stack((query_grad, key_grad, value_grad), axis=2).astype(jnp.bfloat16)
    merged_low = merged_low.reshape(rows.shape[0], 3 * width)
    merged_weight_g = contract_rows(rows, merged_low)
    merged_bias_g = jnp.sum(merged_low.astype(jnp.float32), axis=0)
    states_part = first_grad + times_transposed(merged_low, merged)
    vector_grads = jnp.stack(
        (
            merged_bias_g[:width],
            merged_bias_g[2 * width :],
            attn_bias_g,
            first_gain_g,
            first_shift_g,
            outer_bias_g,
            second_gain_g,
            second_shift_g,
        ),
        axis=1,
    )
    return (
        states_part,
        (
            merged_weight_g,
            attn_weight_g,
            inner_weight_g,
            outer_weight_g,
            vector_grads,
            inner_bias_g,
        ),
    )


def shards(depth, *arrays):
    (states, pad_mask, query_proj, key_proj, value_proj, attn_proj, query_bias, value_bias, attn_bias, first_gain,
     first_shift, inner_proj, inner_bias, outer_proj, outer_bias, second_gain, second_shift, out_grad) = arrays
    width = states.shape[1]
    short = (query_bias, value_bias, attn_bias, first_gain, first_shift, outer_bias, second_gain, second_shift)
    if depth:
        return kernel_shards(depth, short, states, pad_mask, query_proj, key_proj, value_proj, attn_proj, inner_proj,
                             inner_bias, outer_proj, out_grad)
    merged_shard = jnp.concatenate((query_proj, key_proj, value_proj), axis=1)
    fetched = collect(merged_shard, attn_proj, inner_proj, outer_proj, jnp.stack(short, axis=1), inner_bias)
    encoded, kept = forward_pass(states, pad_mask, fetched)
    states_part, totals = backward_pass(states, pad_mask, out_grad, fetched, kept)
    merged_sum, attn_sum, inner_sum, outer_sum, vector_sum, widened_sum = reduce_grads(*totals)
    return ordered(encoded, states_part, merged_sum, attn_sum, inner_sum, outer_sum, vector_sum.T, widened_sum)


def ordered(encoded, states_part, merged_sum, attn_sum, inner_sum, outer_sum, vectors, widened_sum):
    width = attn_sum.shape[1]
    return (encoded, states_part, merged_sum[:, :width], merged_sum[:, width : 2 * width], merged_sum[:, 2 * width :],
            attn_sum, vectors[0], vectors[1], vectors[2], vectors[3], vectors[4], inner_sum, widened_sum, outer_sum,
            vectors[5], vectors[6], vectors[7])


def kernel_shards(depth, short, states, pad_mask, query_proj, key_proj, value_proj, attn_proj, inner_proj, inner_bias,
                  outer_proj, out_grad):
    width = states.shape[1]
    block = short[0].shape[0]
    (merged, attn, inner, outer, encoded, projected, probs, context, first_sum, first_low, activated, slope, second_grad,
     outer_low, vectors, sums) = forward_all(
        depth, block, states, pad_mask, out_grad,
        (query_proj, key_proj, value_proj, attn_proj, inner_proj, outer_proj, *short, inner_bias))
    states_part, outer_sum, inner_sum, query_sum, key_sum, value_sum, attn_sum, table_sum = backward_all(
        depth, block, vectors, sums,
        (states, activated, slope, outer_low, second_grad, first_sum, first_low, context, projected, probs,
         merged.reshape(width, -1), attn.reshape(width, -1), inner, outer))
    (encoded, states_part, query_sum, key_sum, value_sum, attn_sum, inner_sum, outer_sum, *rows) = finish_all(
        block, table_sum, (encoded, states_part, query_sum, key_sum, value_sum, attn_sum, inner_sum, outer_sum))
    return (encoded, states_part, query_sum, key_sum, value_sum, attn_sum, *rows[:5], inner_sum, rows[8], outer_sum,
            *rows[5:8])


def solution(mesh):
    dps, others = mesh.shape["dp"], mesh.shape["fsdp"]
    matrix = P(("dp", "fsdp"), None)
    vector = P(("dp", "fsdp"))

    def whole(*arrays):
        rows = arrays[2].shape[0] // (dps * others)
        tiles = rows % 16 == 0 and arrays[12].shape[0] == 128 * dps * others
        depth = others // 2 if tiles and dps == 4 and others == 2 * dps else 0
        return jax.shard_map(
            functools.partial(shards, depth),
            mesh=mesh,
            in_specs=(matrix,) * 6 + (vector,) * 5 + (matrix, vector, matrix) + (vector,) * 3 + (matrix,),
            out_specs=(matrix,) * 6 + (vector,) * 5 + (matrix, vector, matrix) + (vector,) * 3,
            check_vma=False,
        )(*arrays)

    return whole
```

```python
import functools

import jax
import jax.numpy as jnp
from jax import lax
from jax.experimental import pallas as pl
from jax.experimental.pallas import tpu as pltpu
from jax.sharding import PartitionSpec as P

HEADS = 16
MESH = pl.DeviceIdType.MESH

epsilon = 1e-05
neg_fill = -1e30


class Place:
    def __init__(self, depth):
        dp = lax.axis_index("dp")
        fsdp = lax.axis_index("fsdp")
        self.depth = depth
        self.dp = dp
        self.z = fsdp // 2
        self.core = lax.rem(fsdp, 2)
        flip_x = dp + 1 - 2 * lax.rem(dp, 2)
        flip_y = lax.rem(dp + 2, 4)
        self.near = flip_x + self.core * (flip_y - flip_x)
        self.far = flip_y + self.core * (flip_x - flip_y)
        self.both = lax.rem(flip_x + 2, 4)
        self.fsdp = fsdp
        self.sibling = fsdp + 1 - 2 * self.core
        self.pair = self.z + 1 - 2 * lax.rem(self.z, 2)
        self.jump = self.up(2)
        self.cross = 3 - self.z

    def up(self, step):
        return lax.rem(self.z + step, self.depth)

    def down(self, step):
        return lax.rem(self.z + self.depth - step, self.depth)

    def along(self, z):
        return (self.dp, z * 2 + self.core)

    def greet(self):
        barrier = pltpu.get_barrier_semaphore()
        others = [self.along(self.up(step)) for step in range(1, self.depth)]
        others += [(self.near, self.fsdp), (self.far, self.fsdp), (self.dp, self.sibling)]
        for other in others:
            pl.semaphore_signal(barrier, inc=1, device_id=other, device_id_type=MESH)

    def greeted(self):
        pl.semaphore_wait(pltpu.get_barrier_semaphore(), self.depth + 2)


def remote(source, target, send, recv, device):
    return pltpu.make_async_remote_copy(
        src_ref=source, dst_ref=target, send_sem=send, recv_sem=recv, device_id=device, device_id_type=MESH
    )


class Gather:
    def __init__(self, place, full, own, sems, piece, lines=None):
        self.lines = pl.ds(0, full.shape[3]) if lines is None else lines
        self.place, self.full, self.own, self.piece = place, full, own.at[self.lines], piece
        self.su, self.ru, self.sd, self.rd, self.sb, self.rb, self.sa, self.ra, self.sc, self.rc, self.so = sems

    def copy_own(self):
        p = self.place
        return pltpu.make_async_copy(self.own, self.full.at[p.dp, p.z, p.core, self.lines], self.so.at[self.piece])

    def copy_up(self, z, first=False):
        p = self.place
        block = self.full.at[p.dp, z, p.core, self.lines]
        source = self.own if first else block
        return remote(source, block, self.su.at[self.piece, z], self.ru.at[self.piece, z], p.along(p.z + 1))

    def copy_down(self, z, first=False):
        p = self.place
        block = self.full.at[p.dp, z, p.core, self.lines]
        source = self.own if first else block
        return remote(source, block, self.sd.at[self.piece, z], self.rd.at[self.piece, z], p.along(p.z - 1))

    def copy_near(self, z, first=False, arriving=False):
        p = self.place
        block = self.full.at[p.near if arriving else p.dp, z, p.core, self.lines]
        source = self.own if first else block
        return remote(source, block, self.sb.at[self.piece, z], self.rb.at[self.piece, z], (p.near, p.fsdp))

    def copy_far(self, half, z, first=False, arriving=False):
        p = self.place
        row = (p.both if half else p.far) if arriving else (p.near if half else p.dp)
        block = self.full.at[row, z, p.core, self.lines]
        source = self.own if first else block
        at = half * p.depth + z
        return remote(source, block, self.sa.at[self.piece, at], self.ra.at[self.piece, at], (p.far, p.fsdp))

    def copy_core(self, part, arriving=False):
        p = self.place
        if arriving:
            row = (p.dp, p.far, p.near, p.both)[part]
            block = self.full.at[row, :, 1 - p.core, self.lines]
        else:
            row = (p.dp, p.near, p.far, p.both)[part]
            block = self.full.at[row, :, p.core, self.lines]
        return remote(block, block, self.sc.at[self.piece, part], self.rc.at[self.piece, part], (p.dp, p.sibling))

    def start(self):
        p = self.place
        pl.when(p.z < p.depth - 1)(lambda: self.copy_up(p.z, True).start())
        pl.when(p.z > 0)(lambda: self.copy_down(p.z, True).start())
        self.copy_own().start()

    def send(self, step):
        p = self.place

        def act(z, first=False):
            self.copy_near(z, first).start()
            self.copy_far(0, z, first).start()

        if step == 0:
            act(p.z, True)
        else:
            pl.when(p.z >= step)(lambda: act(p.z - step))
            pl.when(p.z + step < p.depth)(lambda: act(p.z + step))

    def hop(self, step):
        p = self.place

        @pl.when(p.z >= step)
        def _():
            z = p.z - step
            self.copy_up(z).wait_recv()
            pl.when(p.z < p.depth - 1)(lambda: self.copy_up(z).start())

        @pl.when(p.z + step < p.depth)
        def _():
            z = p.z + step
            self.copy_down(z).wait_recv()
            pl.when(p.z > 0)(lambda: self.copy_down(z).start())

    def last_hop(self):
        self.hop(self.place.depth - 1)
        self.copy_own().wait()
        self.copy_core(0).start()

    def spread(self, step):
        p = self.place

        def act(z):
            self.copy_near(z, arriving=True).wait_recv()
            self.copy_far(1, z).start()

        if step == 0:
            act(p.z)
        else:
            pl.when(p.z >= step)(lambda: act(p.z - step))
            pl.when(p.z + step < p.depth)(lambda: act(p.z + step))
        if step == p.depth - 1:
            self.copy_core(1).start()

    def arrive_far(self, half):
        p = self.place
        for z in range(p.depth):
            self.copy_far(half, z, arriving=True).wait_recv()
        self.copy_core(2 + half).start()

    def arrive_core(self, *parts):
        for part in parts:
            self.copy_core(part, arriving=True).wait_recv()

    def drain(self):
        p = self.place
        for z in range(p.depth):
            pl.when((p.z < p.depth - 1) & (z <= p.z))(lambda: self.copy_up(z).wait_send())
            pl.when((p.z > 0) & (z >= p.z))(lambda: self.copy_down(z).wait_send())
            self.copy_near(z).wait_send()
            self.copy_far(0, z).wait_send()
            self.copy_far(1, z).wait_send()
        for part in range(4):
            self.copy_core(part).wait_send()


class GatherLine:
    def __init__(self, place, full, own, sems, piece, lines):
        self.place, self.full, self.own, self.piece, self.lines = place, full, own.at[lines], piece, lines
        self.sj, self.rj, self.sp, self.rp, self.sb, self.rb, self.sa, self.ra, self.sc, self.rc, self.so = sems

    def block(self, row):
        return self.full.at[row, self.place.z, self.place.core, self.lines]

    def column(self, z, core):
        return self.full.at[:, z, core, self.lines]

    def copy_own(self):
        return pltpu.make_async_copy(self.own, self.block(self.place.dp), self.so.at[self.piece])

    def copy_near(self, arriving=False):
        p = self.place
        target = self.block(p.near if arriving else p.dp)
        return remote(self.own, target, self.sb.at[self.piece, 0], self.rb.at[self.piece, 0], (p.near, p.fsdp))

    def copy_far(self, half, arriving=False):
        p = self.place
        target = self.block((p.both if half else p.far) if arriving else (p.near if half else p.dp))
        source = target if half else self.own
        return remote(source, target, self.sa.at[self.piece, half], self.ra.at[self.piece, half], (p.far, p.fsdp))

    def copy_jump(self, arriving=False):
        p = self.place
        column = self.column(p.jump if arriving else p.z, p.core)
        return remote(column, column, self.sj.at[self.piece, 0], self.rj.at[self.piece, 0], p.along(p.jump))

    def copy_pair(self, part, arriving=False):
        p = self.place
        z = (p.cross if part else p.pair) if arriving else (p.jump if part else p.z)
        column = self.column(z, p.core)
        return remote(column, column, self.sp.at[self.piece, part], self.rp.at[self.piece, part], p.along(p.pair))

    def copy_core(self, part, arriving=False):
        p = self.place
        column = self.column((p.z, p.jump, p.pair, p.cross)[part], 1 - p.core if arriving else p.core)
        return remote(column, column, self.sc.at[self.piece, part], self.rc.at[self.piece, part], (p.dp, p.sibling))

    def start(self):
        self.copy_near().start()
        self.copy_far(0).start()
        self.copy_own().start()

    def spread(self):
        self.copy_near(arriving=True).wait_recv()
        self.copy_far(1).start()

    def join(self):
        self.copy_own().wait()
        for half in range(2):
            self.copy_far(half, arriving=True).wait_recv()
        self.copy_jump().start()
        self.copy_pair(0).start()
        self.copy_core(0).start()

    def relay(self):
        self.copy_jump(arriving=True).wait_recv()
        self.copy_pair(1).start()
        self.copy_core(1).start()

    def arrive(self):
        for part in range(2):
            self.copy_pair(part, arriving=True).wait_recv()
            self.copy_core(2 + part).start()

    def arrive_core(self):
        for part in range(4):
            self.copy_core(part, arriving=True).wait_recv()

    def drain(self):
        self.copy_near().wait_send()
        self.copy_jump().wait_send()
        for part in range(2):
            self.copy_far(part).wait_send()
            self.copy_pair(part).wait_send()
        for part in range(4):
            self.copy_core(part).wait_send()


def gather_sems(pieces, depth):
    dma = pltpu.SemaphoreType.DMA
    counts = (depth, depth, depth, depth, depth, depth, 2 * depth, 2 * depth, 4, 4)
    return [dma((pieces, count)) for count in counts] + [dma((pieces,))]


def matmul(left, right):
    return lax.dot_general(left, right, (((1,), (0,)), ((), ())), preferred_element_type=jnp.float32)


def matmul_nt(left, right):
    return lax.dot_general(left, right, (((1,), (1,)), ((), ())), preferred_element_type=jnp.float32)


def matmul_tn(left, right):
    return lax.dot_general(left, right, (((0,), (0,)), ((), ())), preferred_element_type=jnp.float32)


def flat(value):
    return value.reshape(-1, value.shape[-1])


def span(index, size):
    return pl.ds(pl.multiple_of(index * size, size), size)


def unpack_table(table, block, vectors, long_bias):
    dps, depth, cores = table.shape[:3]
    places = dps * depth * cores
    width = vectors.shape[1]
    lane = lax.broadcasted_iota(jnp.int32, (128, width), 1)
    source = lax.broadcasted_iota(jnp.int32, (128, width), 0)
    pick = jnp.where(source == lax.rem(lane, block), 1.0, 0.0).astype(jnp.bfloat16)
    owner = lax.broadcasted_iota(jnp.int32, (places, width), 1) // block
    mine = owner == lax.broadcasted_iota(jnp.int32, (places, width), 0)
    blocks = [table[:, :, :, vector, :].reshape(places, 128) for vector in range(8)]
    spread = matmul(jnp.concatenate(blocks, axis=0).astype(jnp.bfloat16), pick)
    for vector in range(8):
        own = jnp.where(mine, spread[vector * places : (vector + 1) * places], 0.0)
        vectors[vector : vector + 1, :] = jnp.sum(own, axis=0, keepdims=True)
    for index in range(places):
        dp, z, core = index // (depth * cores), index // cores % depth, index % cores
        long_bias[:, index * 128 : (index + 1) * 128] = table[dp, z, core, 8:9, :]


CHUNK = 256


def project(rows, weights, vectors, projected):
    chunks = rows.shape[1] // CHUNK
    for part, bias in ((0, 0), (1, None), (2, 1)):

        def one(index, _):
            at = span(part * chunks + index, CHUNK)
            total = matmul(rows[...], flat(weights[:, :, :, :, at]))
            if bias is not None:
                total = total + vectors[bias : bias + 1, span(index, CHUNK)]
            projected[:, at] = total.astype(jnp.bfloat16)
            return 0

        lax.fori_loop(0, chunks, one, 0)


def head_lanes(heads, rows, size):
    lane = lax.broadcasted_iota(jnp.int32, (rows, heads * size), 1) // size
    return [lane == head for head in range(heads)]


def stack_heads(value, lanes):
    return jnp.concatenate([jnp.where(lane, value, jnp.zeros_like(value)) for lane in lanes], axis=0)


def merge_heads(value, lanes):
    rows = value.shape[0] // len(lanes)
    result = value[:rows]
    for head in range(1, len(lanes)):
        result = jnp.where(lanes[head], value[head * rows : (head + 1) * rows], result)
    return result


QUAD = 4


def attend(projected, keep, probs, context, first, last):
    width = context.shape[1]
    size = width // HEADS
    length = keep.shape[1]
    scale = size ** (-0.5)
    lanes = head_lanes(QUAD, length, size)
    quads = HEADS // QUAD

    def one(index, _):
        segment = index // quads
        quad = lax.rem(index, quads)
        at = span(segment, length)
        queries = projected[at, span(quad, QUAD * size)]
        keysets = projected[at, span(quad + quads, QUAD * size)]
        valuesets = projected[at, span(quad + 2 * quads, QUAD * size)]
        scores = matmul_nt(stack_heads(queries, lanes), keysets) * scale
        mask = keep[pl.ds(segment, 1), :] > 0
        scores = jnp.where(mask, scores, neg_fill)
        raised = jnp.exp(scores - jnp.max(scores, axis=1, keepdims=True))
        low = (raised / jnp.sum(raised, axis=1, keepdims=True)).astype(jnp.bfloat16)
        probs[index] = low
        context[at, span(quad, QUAD * size)] = merge_heads(matmul(low, valuesets), lanes).astype(jnp.bfloat16)
        return 0

    lax.fori_loop(first, last, one, 0)


def center_scale(hidden):
    center = hidden - jnp.mean(hidden, axis=1, keepdims=True)
    spread = jnp.mean(center * center, axis=1, keepdims=True)
    rate = lax.rsqrt(spread + epsilon)
    return center * rate, rate


def first_block(rows, context, weights, vectors, first_sum, first_norm, first_low):
    def product(index, _):
        at = span(index, CHUNK)
        attended = matmul(context[...], flat(weights[:, :, :, :, at])) + vectors[2:3, at]
        first_sum[:, at] = rows[:, at].astype(jnp.float32) + attended
        return 0

    lax.fori_loop(0, rows.shape[1] // CHUNK, product, 0)

    def one(index, _):
        at = span(index, 64)
        normed, _ = center_scale(first_sum[at, :])
        result = normed * vectors[3:4, :] + vectors[4:5, :]
        first_norm[at, :] = result
        first_low[at, :] = result.astype(jnp.bfloat16)
        return 0

    lax.fori_loop(0, rows.shape[0] // 64, one, 0)


def inner_block(first_low, weights, long_bias, activated, slope, first, last):
    def one(index, _):
        at = span(index, CHUNK)
        value = matmul(first_low[...], flat(weights[:, :, :, :, at])) + long_bias[:, at]
        share = 0.5 * (1.0 + lax.erf(value * (0.5**0.5)))
        bell = jnp.exp(-0.5 * value * value) * ((0.5 / jnp.pi) ** 0.5)
        activated[:, at] = (value * share).astype(jnp.bfloat16)
        slope[:, at] = (share + value * bell).astype(jnp.bfloat16)
        return 0

    lax.fori_loop(first, last, one, 0)


def outer_part(activated, weights, row, total, fresh):
    size = weights.shape[1] * weights.shape[2] * weights.shape[3]

    def one(index, _):
        at = span(index, CHUNK)
        value = matmul(activated[:, span(row, size)], flat(weights[row, :, :, :, at]))
        total[:, at] = value if fresh else total[:, at] + value
        return 0

    lax.fori_loop(0, total.shape[1] // CHUNK, one, 0)


def norm_back(grad, normed, rate, gain):
    scaled = grad * gain
    mean = jnp.mean(scaled, axis=1, keepdims=True)
    along = jnp.mean(scaled * normed, axis=1, keepdims=True)
    return rate * (scaled - mean - normed * along)


def second_block(first_norm, total, cotangent, vectors, encoded, second_grad, outer_low, sums, first, last):

    def one(index, _):
        at = span(index, 64)
        normed, rate = center_scale(first_norm[at, :] + (total[at, :] + vectors[5:6, :]))
        gain = vectors[6:7, :]
        encoded[at, :] = (normed * gain + vectors[7:8, :]).astype(jnp.bfloat16)
        grad = cotangent[at, :].astype(jnp.float32)
        back = norm_back(grad, normed, rate, gain)
        low = back.astype(jnp.bfloat16)
        second_grad[at, :] = back
        outer_low[at, :] = low
        sums[5:6, :] += jnp.sum(low.astype(jnp.float32), axis=0, keepdims=True)
        sums[6:7, :] += jnp.sum(grad * normed, axis=0, keepdims=True)
        sums[7:8, :] += jnp.sum(grad, axis=0, keepdims=True)
        return 0

    lax.fori_loop(first, last, one, 0)


def forward_kernel(depth, block, *refs):
    (rows_in, keep, cotangent_in, query_own, key_own, value_own, attn_own, inner_own, outer_own) = refs[:9]
    short_vectors = refs[9:18]
    merged_out, attn_out, inner_out, outer_out = refs[18:22]
    (encoded_out, projected_out, probs_out, context_out, first_sum_out, first_low_out, activated_out, slope_out,
     second_grad_out, outer_low_out, vectors, sums) = refs[22:34]
    (table_own, merged_own, table, merged, attn, inner, outer, projected, probs, context, first_sum, first_norm, first_low,
     activated, slope, total, encoded, second_grad, outer_low, long_bias, save_sem, rows, cotangent, load_sem) = refs[34:58]
    sems = refs[58:]
    place = Place(depth)
    place.greet()
    loads = [
        pltpu.make_async_copy(rows_in, rows, load_sem.at[0]),
        pltpu.make_async_copy(cotangent_in, cotangent, load_sem.at[1]),
    ]
    table_own[...] = jnp.zeros_like(table_own)
    for index, vector in enumerate(short_vectors):
        table_own[index, : vector.shape[0]] = vector[...].astype(jnp.float32)
    width = rows.shape[1]
    for part, own in enumerate((query_own, key_own, value_own)):
        merged_own[:, part * width : (part + 1) * width] = own[...]
    net_table = Gather(place, table, table_own, sems, 0)
    net_merged = Gather(place, merged, merged_own, sems, 1)
    net_attn = Gather(place, attn, attn_own, sems, 2)
    net_inner = Gather(place, inner, inner_own, sems, 3)
    half = outer.shape[3] // 2
    net_outer = Gather(place, outer, outer_own, sems, 4, pl.ds(0, half))
    line = GatherLine(place, outer, outer_own, sems, 5, pl.ds(half, half))
    nets = (net_table, net_merged, net_attn, net_inner, net_outer, line)
    front = nets[:3]
    place.greeted()
    for copy in loads:
        copy.start()
    saves = []

    def save(source, target):
        copy = pltpu.make_async_copy(source, target, save_sem.at[len(saves)])
        copy.start()
        saves.append(copy)

    def hop(net, step):
        if step == depth - 1:
            net.last_hop()
        else:
            net.hop(step)

    def each(nets_of, *names, step):
        for name in names:
            for net in nets_of:
                hop(net, step) if name == "hop" else getattr(net, name)(step)

    for net in front:
        net.start()
    each(front, "send", step=0)
    line.start()
    each(front, "hop", "send", step=1)
    line.spread()
    net_inner.start()
    each(front, "spread", step=0)
    for step in range(2, depth):
        each(front, "hop", "send", step=step)
        each(front, "spread", step=step - 1)
    net_inner.send(0)
    net_outer.start()
    net_inner.hop(1)
    net_inner.send(1)
    each(front, "spread", step=depth - 1)
    net_inner.spread(0)
    net_outer.hop(1)
    for step in range(2, depth - 1):
        net_inner.hop(step)
        net_inner.send(step)
        net_inner.spread(step - 1)
    line.join()
    for net in front:
        net.arrive_far(0)
        net.arrive_far(1)
        net.arrive_core(0, 1, 2, 3)
    save(merged, merged_out)
    save(attn, attn_out)
    unpack_table(table, block, vectors, long_bias)
    loads[0].wait()
    project(rows, merged, vectors, projected)
    save(projected, projected_out)
    for step in range(2, depth - 1):
        net_outer.hop(step)
    net_inner.last_hop()
    net_inner.send(depth - 1)
    net_inner.spread(depth - 2)
    line.relay()
    count = probs.shape[0]
    attend(projected, keep, probs, context, 0, count // 2)
    net_outer.last_hop()
    net_inner.spread(depth - 1)
    attend(projected, keep, probs, context, count // 2, count)
    save(probs, probs_out)
    save(context, context_out)
    first_block(rows, context, attn, vectors, first_sum, first_norm, first_low)
    save(first_sum, first_sum_out)
    save(first_low, first_low_out)
    net_inner.arrive_far(0)
    for step in range(depth):
        net_outer.send(step)
    net_inner.arrive_far(1)
    net_inner.arrive_core(0, 1, 2, 3)
    save(inner, inner_out)
    quarter = inner.shape[4] // CHUNK // 4

    def inner_quarter(index):
        inner_block(first_low, inner, long_bias, activated, slope, index * quarter, (index + 1) * quarter)

    inner_quarter(0)
    net_outer.spread(0)
    inner_quarter(1)
    for step in range(1, depth - 1):
        net_outer.spread(step)
    inner_quarter(2)
    net_outer.spread(depth - 1)
    line.arrive()
    inner_quarter(3)
    save(activated, activated_out)
    save(slope, slope_out)
    sums[...] = jnp.zeros_like(sums)
    loads[1].wait()
    line.arrive_core()
    net_outer.arrive_core(0)
    save(outer.at[place.dp], outer_out.at[place.dp])
    outer_part(activated, outer, place.dp, total, True)
    net_outer.arrive_far(0)
    net_outer.arrive_core(1, 2)
    for row in (place.near, place.far):
        save(outer.at[row], outer_out.at[row])
    outer_part(activated, outer, place.near, total, False)
    outer_part(activated, outer, place.far, total, False)
    net_outer.arrive_far(1)
    net_outer.arrive_core(3)
    save(outer.at[place.both], outer_out.at[place.both])
    outer_part(activated, outer, place.both, total, False)
    for part in range(4):
        size = rows.shape[0] // 4
        second_block(
            first_norm, total, cotangent, vectors, encoded, second_grad, outer_low, sums, part * size // 64,
            (part + 1) * size // 64,
        )
        at = pl.ds(part * size, size)
        save(outer_low.at[at], outer_low_out.at[at])
        save(second_grad.at[at], second_grad_out.at[at])
        save(encoded.at[at], encoded_out.at[at])
    for net in nets:
        net.drain()
    for copy in saves:
        copy.wait()


def forward_all(depth, block, rows, keep, cotangent, owns):
    query_own, _, _, attn_own, inner_own, outer_own = owns[:6]
    tokens, width = rows.shape
    hidden = inner_own.shape[1]
    segments, length = keep.shape
    low, high = jnp.bfloat16, jnp.float32

    def fulls(own, columns):
        return (4, depth, 2, own.shape[0], columns)

    full_shapes = [fulls(query_own, 3 * width), fulls(attn_own, width), fulls(inner_own, hidden), fulls(outer_own, width)]
    kept = [
        ((tokens, width), low),
        ((tokens, 3 * width), low),
        ((segments * HEADS // QUAD, QUAD * length, length), low),
        ((tokens, width), low),
        ((tokens, width), high),
        ((tokens, width), low),
        ((tokens, hidden), low),
        ((tokens, hidden), low),
        ((tokens, width), high),
        ((tokens, width), low),
    ]
    small = [((8, width), high), ((8, width), high)]
    shapes = [jax.ShapeDtypeStruct(shape, low) for shape in full_shapes]
    shapes += [jax.ShapeDtypeStruct(*one) for one in kept + small]
    held = {name: pltpu.VMEM(*one) for name, one in zip(
        ("encoded", "projected", "probs", "context", "first_sum", "first_low", "activated", "slope", "second_grad", "outer_low"),
        kept)}
    scratch = [pltpu.VMEM((16, 128), high), pltpu.VMEM((query_own.shape[0], 3 * width), low)]
    scratch += [pltpu.VMEM((4, depth, 2, 16, 128), high)]
    scratch += [pltpu.VMEM(shape, low) for shape in full_shapes]
    scratch += [held[name] for name in ("projected", "probs", "context", "first_sum")]
    scratch += [pltpu.VMEM((tokens, width), high)]
    scratch += [held[name] for name in ("first_low", "activated", "slope")]
    scratch += [pltpu.VMEM((tokens, width), high)]
    scratch += [held[name] for name in ("encoded", "second_grad", "outer_low")]
    scratch += [pltpu.VMEM((1, hidden), high)]
    scratch += [pltpu.SemaphoreType.DMA((len(full_shapes) + len(kept) + 12,))]
    scratch += [pltpu.VMEM((tokens, width), low), pltpu.VMEM((tokens, width), low), pltpu.SemaphoreType.DMA((2,))]
    here = pl.BlockSpec(memory_space=pltpu.VMEM)
    away = pl.BlockSpec(memory_space=pl.ANY)
    return pl.pallas_call(
        functools.partial(forward_kernel, depth, block),
        out_shape=shapes,
        in_specs=[away, here, away] + [here] * len(owns),
        out_specs=[away] * (len(full_shapes) + len(kept)) + [here] * 2,
        scratch_shapes=scratch + gather_sems(6, depth),
        compiler_params=pltpu.CompilerParams(
            collective_id=0, has_side_effects=True, vmem_limit_bytes=60 * 1024 * 1024
        ),
        name="forward",
    )(rows, keep, cotangent, *owns)


SUBS = 4


class Slots:
    def __init__(self, core, far, near, along):
        self.core, self.far, self.near, self.along = core, far, near, along


class Scatter:
    def __init__(self, place, whole, slots, sems, credits, number, lot, first, count, after=False, before=False,
                 late_after=False, late_before=False):
        self.place, self.whole, self.slots = place, whole, slots
        self.sc, self.rc, self.sa, self.ra, self.sb, self.rb, self.sz, self.rz = sems
        self.core_free, self.far_free, self.near_free, self.z_free = credits
        self.number, self.lot, self.first, self.count = number, lot, first, count
        self.sub = first * SUBS // whole.shape[3]
        self.after, self.before, self.late_after, self.late_before = after, before, late_after, late_before
        self.tile = 8 if whole.dtype == jnp.float32 else 16

    def lines(self):
        return pl.ds(self.first, self.count)

    def mine(self, row):
        return self.whole.at[row, :, self.place.core, self.lines()]

    def sent_row(self, at):
        p = self.place
        return (p.both, p.near, p.far, p.dp)[at]

    def got_row(self, at):
        p = self.place
        return (p.both, p.far, p.near, p.dp)[at]

    def copy_core(self, at):
        p = self.place
        return remote(
            self.whole.at[self.sent_row(at), :, 1 - p.core, self.lines()], self.slots.core.at[at, :, self.lines()],
            self.sc.at[self.number, at], self.rc.at[self.number, at], (p.dp, p.sibling),
        )

    def copy_far(self, half):
        p = self.place
        return remote(
            self.mine(p.both if half else p.far), self.slots.far.at[self.lot, half, :, self.lines()],
            self.sa.at[self.number, half], self.ra.at[self.number, half], (p.far, p.fsdp),
        )

    def copy_near(self):
        p = self.place
        return remote(
            self.mine(p.near), self.slots.near.at[self.lot, :, self.lines()], self.sb.at[self.number],
            self.rb.at[self.number], (p.near, p.fsdp),
        )

    def copy_z(self, step):
        p = self.place
        return remote(
            self.whole.at[p.dp, p.up(step), p.core, self.lines()], self.slots.along.at[self.lot, step - 1, self.lines()],
            self.sz.at[self.number, step - 1], self.rz.at[self.number, step - 1], p.along(p.up(step)),
        )

    def add(self, row, slot):
        p = self.place
        tiles = self.count // self.tile

        def one(index, _):
            z = index // tiles
            at = pl.ds(pl.multiple_of(self.first + lax.rem(index, tiles) * self.tile, self.tile), self.tile)
            self.whole[row, z, p.core, at, :] = self.whole[row, z, p.core, at, :] + slot[z, at, :]
            return 0

        lax.fori_loop(0, p.depth * tiles, one, 0)

    def start_core(self, at):
        if self.after:
            pl.semaphore_wait(self.core_free.at[at, self.sub], 1)
        self.copy_core(at).start()

    def add_core(self, at):
        p = self.place
        self.copy_core(at).wait_recv()
        self.add(self.got_row(at), self.slots.core.at[at])
        if self.before:
            pl.semaphore_signal(self.core_free.at[at, self.sub], inc=1, device_id=(p.dp, p.sibling), device_id_type=MESH)

    def start_far(self, half):
        if self.late_after:
            pl.semaphore_wait(self.far_free.at[half, self.sub], 1)
        self.copy_far(half).start()

    def add_far(self, half):
        p = self.place
        self.copy_far(half).wait_recv()
        self.add(p.near if half else p.dp, self.slots.far.at[self.lot, half])
        if self.late_before:
            pl.semaphore_signal(self.far_free.at[half, self.sub], inc=1, device_id=(p.far, p.fsdp), device_id_type=MESH)
        if half:
            if self.late_after:
                pl.semaphore_wait(self.near_free.at[self.sub], 1)
            self.copy_near().start()

    def add_near(self):
        p = self.place
        self.copy_near().wait_recv()
        self.add(p.dp, self.slots.near.at[self.lot])
        if self.late_before:
            pl.semaphore_signal(self.near_free.at[self.sub], inc=1, device_id=(p.near, p.fsdp), device_id_type=MESH)
        for step in range(1, p.depth):
            if self.late_after:
                pl.semaphore_wait(self.z_free.at[self.sub, step - 1], 1)
            self.copy_z(step).start()

    def finish(self, out):
        p = self.place
        for step in range(1, p.depth):
            self.copy_z(step).wait_recv()

        def one(index, _):
            start = pl.multiple_of(index * self.tile, self.tile)
            at = pl.ds(pl.multiple_of(self.first + start, self.tile), self.tile)
            total = self.whole[p.dp, p.z, p.core, at, :].astype(jnp.float32)
            for step in range(p.depth - 1):
                total = total + self.slots.along[self.lot, step, at, :].astype(jnp.float32)
            out[pl.ds(start, self.tile), :] = total
            return 0

        lax.fori_loop(0, self.count // self.tile, one, 0)
        if self.late_before:
            for step in range(1, p.depth):
                pl.semaphore_signal(
                    self.z_free.at[self.sub, step - 1], inc=1, device_id=p.along(p.down(step)), device_id_type=MESH
                )

    def drain(self):
        for at in range(4):
            self.copy_core(at).wait_send()
        self.copy_far(1).wait_send()
        self.copy_far(0).wait_send()
        self.copy_near().wait_send()
        for step in range(1, self.place.depth):
            self.copy_z(step).wait_send()


class ScatterLine(Scatter):
    def column(self, z):
        return self.whole.at[:, z, self.place.core, self.lines()]

    def copy_pair(self, part):
        p = self.place
        return remote(
            self.column(p.cross if part else p.pair), self.slots.far.at[0, part, :, self.lines()],
            self.sa.at[self.number, part], self.ra.at[self.number, part], p.along(p.pair),
        )

    def copy_jump(self):
        p = self.place
        return remote(
            self.column(p.jump), self.slots.near.at[0, :, self.lines()], self.sb.at[self.number], self.rb.at[self.number],
            p.along(p.jump),
        )

    def copy_axis(self, part):
        p = self.place
        row = (p.both, p.far, p.near)[part]
        target = p.near if part == 2 else p.far
        return remote(
            self.whole.at[row, p.z, p.core, self.lines()], self.slots.along.at[0, part, self.lines()],
            self.sz.at[self.number, part], self.rz.at[self.number, part], (target, p.fsdp),
        )

    def add_column(self, z, slot):
        p = self.place
        tiles = self.count // self.tile

        def one(index, _):
            row = index // tiles
            at = pl.ds(pl.multiple_of(self.first + lax.rem(index, tiles) * self.tile, self.tile), self.tile)
            self.whole[row, z, p.core, at, :] = self.whole[row, z, p.core, at, :] + slot[row, at, :]
            return 0

        lax.fori_loop(0, self.whole.shape[0] * tiles, one, 0)

    def add_block(self, row, part):
        p = self.place

        def one(index, _):
            at = pl.ds(pl.multiple_of(self.first + index * self.tile, self.tile), self.tile)
            self.whole[row, p.z, p.core, at, :] = self.whole[row, p.z, p.core, at, :] + self.slots.along[0, part, at, :]
            return 0

        lax.fori_loop(0, self.count // self.tile, one, 0)

    def tell(self, semaphore, device):
        pl.semaphore_signal(semaphore, inc=1, device_id=device, device_id_type=MESH)

    def add_core(self, at):
        p = self.place
        self.copy_core(at).wait_recv()
        self.add(self.got_row(at), self.slots.core.at[at])
        for sub in range(SUBS // 2, SUBS):
            self.tell(self.core_free.at[at, sub], (p.dp, p.sibling))

    def start_pair(self):
        self.copy_pair(1).start()
        self.copy_pair(0).start()

    def add_pair(self, part):
        p = self.place
        self.copy_pair(part).wait_recv()
        self.add_column(p.jump if part else p.z, self.slots.far.at[0, part])
        if part:
            self.copy_jump().start()
        for sub in range(SUBS // 2, SUBS):
            self.tell(self.far_free.at[part, sub], (p.far, p.fsdp))

    def add_jump(self):
        p = self.place
        self.copy_jump().wait_recv()
        self.add_column(p.z, self.slots.near.at[0])
        for sub in range(SUBS // 2, SUBS):
            self.tell(self.near_free.at[sub], (p.near, p.fsdp))
        self.copy_axis(0).start()
        self.copy_axis(1).start()

    def add_far_axis(self):
        p = self.place
        for part in range(2):
            self.copy_axis(part).wait_recv()
            self.add_block(p.dp if part else p.near, part)
        self.copy_axis(2).start()

    def finish(self, out):
        p = self.place
        self.copy_axis(2).wait_recv()

        def one(index, _):
            start = pl.multiple_of(index * self.tile, self.tile)
            at = pl.ds(pl.multiple_of(self.first + start, self.tile), self.tile)
            total = self.whole[p.dp, p.z, p.core, at, :].astype(jnp.float32)
            out[pl.ds(start, self.tile), :] = total + self.slots.along[0, 2, at, :].astype(jnp.float32)
            return 0

        lax.fori_loop(0, self.count // self.tile, one, 0)
        for sub in range(SUBS // 2, SUBS):
            for step in range(1, p.depth):
                self.tell(self.z_free.at[sub, step - 1], p.along(p.down(step)))

    def drain(self):
        for at in range(4):
            self.copy_core(at).wait_send()
        for part in range(2):
            self.copy_pair(part).wait_send()
        self.copy_jump().wait_send()
        for part in range(3):
            self.copy_axis(part).wait_send()


def outer_gradient(acts, low, grads, row):
    depth, cores, count, _ = grads.shape[1:]
    size = cores * count

    def one(z, _):
        value = matmul_tn(acts[row, :, span(z, size)], low[...])
        grads[row, z] = value.astype(jnp.bfloat16).reshape(grads.shape[2:])
        return 0

    lax.fori_loop(0, depth, one, 0)


def input_gradient(inputs, low, grads, row, part):
    depth, cores, count, width = grads.shape[1:]
    size = inputs.shape[1] // grads.shape[0]
    lines = count // SUBS
    value = matmul_tn(inputs[:, span(row, size)], low)
    grads[row, :, :, part * lines : (part + 1) * lines, :] = value.astype(jnp.bfloat16).reshape(depth, cores, lines, width)


def hidden_back(low, weights, slopes, bias_sum, part):
    depth, cores, count, width = weights.shape[1:]
    size = cores * count

    def one(index, _):
        at = span(index, size)
        value = matmul_nt(low[...], flat(weights[part, index])) * slopes[SUBS + part, :, at].astype(jnp.float32)
        rounded = value.astype(jnp.bfloat16)
        slopes[SUBS + part, :, at] = rounded
        total = jnp.sum(rounded.astype(jnp.float32), axis=0, keepdims=True)
        bias_sum[:, pl.ds(pl.multiple_of(part * width + index * size, size), size)] = total
        return 0

    lax.fori_loop(0, depth, one, 0)


def first_total_rows(grad, inner_low, weights):
    lines = weights.shape[3] // SUBS
    size = grad.shape[1] // weights.shape[0]

    def one(index, _):
        at = span(index, size)
        total = grad[:, at]
        for part in range(SUBS):
            weight = flat(weights[index, :, :, part * lines : (part + 1) * lines, :])
            total = total + matmul_nt(inner_low[SUBS + part], weight)
        grad[:, at] = total
        return 0

    lax.fori_loop(0, weights.shape[0], one, 0)


def first_back(first_sum, grad, low, vectors, sums):
    for row in (2, 3, 4):
        sums[row : row + 1, :] = jnp.zeros((1, grad.shape[1]), jnp.float32)

    def one(index, _):
        at = span(index, 64)
        normed, rate = center_scale(first_sum[at, :])
        upper = grad[at, :]
        back = norm_back(upper, normed, rate, vectors[3:4, :])
        rounded = back.astype(jnp.bfloat16)
        grad[at, :] = back
        low[at, :] = rounded
        sums[2:3, :] += jnp.sum(rounded.astype(jnp.float32), axis=0, keepdims=True)
        sums[3:4, :] += jnp.sum(upper * normed, axis=0, keepdims=True)
        sums[4:5, :] += jnp.sum(upper, axis=0, keepdims=True)
        return 0

    lax.fori_loop(0, grad.shape[0] // 64, one, 0)


def context_back(low, weights, context):
    halves = weights.shape[1] // CHUNK

    def one(index, _):
        weight = weights[index // halves, span(lax.rem(index, halves), CHUNK), :]
        context[:, span(index, CHUNK)] = matmul_nt(low[...], weight).astype(jnp.bfloat16)
        return 0

    lax.fori_loop(0, context.shape[1] // CHUNK, one, 0)


def attend_back(projected, probs, context_low, sums, first, last):
    width = context_low.shape[1]
    size = width // HEADS
    length = probs.shape[2]
    scale = size ** (-0.5)
    lanes = head_lanes(QUAD, length, size)
    quads = HEADS // QUAD

    def one(index, _):
        segment = index // quads
        quad = lax.rem(index, quads)
        at = span(segment, length)
        columns = [span(quad + part * quads, QUAD * size) for part in range(3)]
        queries, keysets, valuesets = [projected[at, column] for column in columns]
        low = probs[index]
        wide = low.astype(jnp.float32)
        upper = stack_heads(context_low[at, columns[0]], lanes)
        prob_grad = matmul_nt(upper, valuesets)
        score_low = (wide * (prob_grad - jnp.sum(wide * prob_grad, axis=1, keepdims=True))).astype(jnp.bfloat16)
        value_low = matmul_tn(low, upper).astype(jnp.bfloat16)
        query_low = (merge_heads(matmul(score_low, keysets), lanes) * scale).astype(jnp.bfloat16)
        key_low = (matmul_tn(score_low, stack_heads(queries, lanes)) * scale).astype(jnp.bfloat16)
        projected[at, columns[0]] = query_low
        projected[at, columns[1]] = key_low
        projected[at, columns[2]] = value_low
        sums[0:1, columns[0]] += jnp.sum(query_low.astype(jnp.float32), axis=0, keepdims=True)
        sums[1:2, columns[0]] += jnp.sum(value_low.astype(jnp.float32), axis=0, keepdims=True)
        return 0

    lax.fori_loop(first, last, one, 0)


def states_back(grad, projected, weights):
    width = grad.shape[1]
    halves = weights.shape[1] // CHUNK

    def one(index, _):
        at = span(index, CHUNK)
        total = grad[:, at]
        for part in range(3):
            weight = weights[2 + 2 * part + index // halves, span(lax.rem(index, halves), CHUNK), :]
            total = total + matmul_nt(projected[:, part * width : (part + 1) * width], weight)
        grad[:, at] = total
        return 0

    lax.fori_loop(0, width // CHUNK, one, 0)


def pack_sums(sums, bias_sum, block, table):
    dps, depth, cores = table.shape[:3]
    places = dps * depth * cores
    width = sums.shape[1]
    lane = lax.broadcasted_iota(jnp.int32, (width, 128), 1)
    source = lax.broadcasted_iota(jnp.int32, (width, 128), 0)
    pick = jnp.where(lane == lax.rem(source, block), 1.0, 0.0).astype(jnp.bfloat16)
    owner = lax.broadcasted_iota(jnp.int32, (places, width), 1) // block
    mine = owner == lax.broadcasted_iota(jnp.int32, (places, width), 0)
    values = jnp.concatenate([jnp.where(mine, sums[vector : vector + 1, :], 0.0) for vector in range(8)], axis=0)
    upper = values.astype(jnp.bfloat16)
    lower = (values - upper.astype(jnp.float32)).astype(jnp.bfloat16)
    total = matmul(upper, pick) + matmul(lower, pick)
    table[...] = jnp.zeros_like(table)
    for vector in range(8):
        table[:, :, :, vector, :] = total[vector * places : (vector + 1) * places].reshape(dps, depth, cores, 128)
    for index in range(places):
        dp, z, core = index // (depth * cores), index // cores % depth, index % cores
        table[dp, z, core, 8:9, :] = bias_sum[:, index * 128 : (index + 1) * 128]


EARLY = 2
SCHEDULE = (
    ("outer",), ("hidden",), ("far", 0), ("inner",), ("far", 1), ("line", 0), ("near", 0), ("total",), ("line", 1),
    ("go", 4), ("norm",), ("attn",), ("go", 6), ("context",), ("far", 2), ("near", 1), ("heads", 0), ("go", 5),
    ("heads", 1), ("far", 3), ("near", 2), ("line", 2), ("merged",), ("go", 7), ("far", 4), ("near", 3), ("end", 0),
    ("far", 5), ("go", 8), ("near", 4), ("end", 1), ("line", 3), ("pack",), ("states",), ("far", 6), ("go", 9),
    ("go", 10), ("near", 5), ("line", 4), ("end", 2), ("far", 7), ("go", 11), ("near", 6), ("end", 3), ("far", 8),
    ("near", 7), ("end", 4), ("far", 9), ("far", 10), ("near", 8), ("end", 5), ("near", 9), ("far", 11), ("near", 10),
    ("end", 6), ("end", 7), ("near", 11), ("end", 8), ("end", 9), ("end", 10), ("end", 11),
)


def backward_kernel(depth, block, *refs):
    (vectors, known, rows_in, activated_in, slope_in, outer_low_in, second_grad_in, first_sum_in, first_low_in, context_in,
     projected_in, probs_in, merged_in, attn_in, inner_in, outer_in) = refs[:16]
    states_out, outer_out, inner_out, query_out, key_out, value_out, attn_out, table_out = refs[16:24]
    (first_buffer, second_buffer, outer_grads, wide, from_core, from_far, from_near, from_z, low, first_low, grad, first_sum,
     context, projected, probs, rows, sums, bias_sum, table, table_core, table_far, table_near, table_z) = refs[24:47]
    load_sem, save_sem = refs[47:49]
    sems = refs[49:57]
    credits = refs[57:61]
    place = Place(depth)
    place.greet()
    width = rows.shape[1]
    tokens = rows.shape[0]
    lines = outer_grads.shape[3] // SUBS
    loads = []

    def load(source, target):
        copy = pltpu.make_async_copy(source, target, load_sem.at[len(loads)])
        copy.start()
        loads.append(copy)
        return copy

    def load_columns(source, targets):
        return [load(source.at[:, part * width : (part + 1) * width], target) for part, target in enumerate(targets)]

    low_load = load(outer_low_in, low)
    act_loads = load_columns(activated_in, [wide.at[part] for part in range(SUBS)])
    outer_load = load(outer_in, first_buffer)
    slope_loads = load_columns(slope_in, [wide.at[SUBS + part] for part in range(SUBS)])
    first_low_load = load(first_low_in, first_low)
    grad_load = load(second_grad_in, grad)
    inner_loads = [
        load(inner_in.at[:, :, :, :, part * width : (part + 1) * width],
             second_buffer.at[:, :, :, part * lines : (part + 1) * lines, :])
        for part in range(SUBS)
    ]
    first_sum_load = load(first_sum_in, first_sum)
    context_load = load(context_in, context)
    projected_load = load(projected_in, projected)
    probs_load = load(probs_in, probs)
    rows_load = load(rows_in, rows)

    slots = Slots(from_core, from_far, from_near, from_z)
    table_slots = Slots(table_core, table_far, table_near, table_z)
    outers = [
        Scatter(place, outer_grads, slots, sems, credits, sub, 0, sub * lines, lines, before=True, late_before=True)
        for sub in range(SUBS // 2)
    ]
    line = ScatterLine(place, outer_grads, slots, sems, credits, SUBS - 1, 0, SUBS // 2 * lines, SUBS // 2 * lines)
    inner_grads = first_buffer
    inners = [
        Scatter(place, inner_grads, slots, sems, credits, SUBS + sub, 1, sub * lines, lines, after=True, before=True)
        for sub in range(SUBS)
    ]
    other_grads = second_buffer
    others = [
        Scatter(place, other_grads, slots, sems, credits, 2 * SUBS + sub, 0, sub * lines, lines, after=True, late_after=True)
        for sub in range(SUBS - 1)
    ]
    attn_net = others[0]
    mergeds = others[1:3]
    lowest = lines // 2
    mergeds += [
        Scatter(place, other_grads, slots, sems, credits, 3 * SUBS - 1, 0, 3 * lines, lowest, after=True, late_after=True),
        Scatter(place, other_grads, slots, sems, credits, 3 * SUBS + 1, 0, 3 * lines + lowest, lowest),
    ]
    small = Scatter(place, table, table_slots, sems, credits, 3 * SUBS, 0, 0, 16)
    row_order = (place.both, place.near, place.far, place.dp)
    sums[...] = known[...]
    sums[0:2, :] = jnp.zeros((2, width), jnp.float32)

    def pieces(nets, compute, early=(), first=False):
        def added(at):
            for net in nets:
                net.add_core(at)
            if at < 2:
                for net in early:
                    net.start_far(1 - at)

        for at in range(4):
            compute(row_order[at])
            if first and at == 0:
                place.greeted()
            for net in nets:
                net.start_core(at)
            if at:
                added(at - 1)
        added(3)

    order = outers + inners + [attn_net] + mergeds[:2] + [small] + mergeds[2:]
    outs = [outer_out.at[pl.ds(sub * lines, lines), :] for sub in range(SUBS // 2)]
    outs += [inner_out.at[:, pl.ds(sub * width, width)] for sub in range(SUBS)]
    outs += [attn_out, query_out, key_out, table_out, value_out.at[pl.ds(0, lowest), :], value_out.at[pl.ds(lowest, lowest), :]]
    def far(number):
        order[number].add_far(1)
        order[number].add_far(0)

    def go(number):
        order[number].start_far(1)
        order[number].start_far(0)

    def near(number):
        order[number].add_near()

    def end(number):
        order[number].finish(outs[number])

    def ready(copies):
        for copy in copies:
            copy.wait()

    def load_merged(part):
        return [
            load(merged_in.at[at * tokens : (at + 1) * tokens, part * width : (part + 1) * width], wide.at[2 + 2 * part + at])
            for at in range(2)
        ]

    late_loads = []

    def outer_step():
        ready([low_load] + act_loads)
        pieces(outers + [line], lambda row: outer_gradient(wide, low, outer_grads, row), outers, True)
        line.start_pair()
        late_loads.append(load(attn_in.at[:tokens], wide.at[0]))
        late_loads.append(load(attn_in.at[tokens:], wide.at[1]))
        late_loads.extend(load_merged(0))

    def hidden_step():
        ready([outer_load] + slope_loads)
        for part in range(SUBS):
            hidden_back(low, first_buffer, wide, bias_sum, part)

    def inner_step():
        def compute(row):
            for part in range(SUBS):
                input_gradient(first_low, wide[SUBS + part], inner_grads, row, part)

        ready([first_low_load])
        pieces(inners, compute, inners[:EARLY])

    def total_step():
        ready([grad_load] + inner_loads)
        first_total_rows(grad, wide, second_buffer)
        late_loads.extend(load_merged(1) + load_merged(2))

    def norm_step():
        ready([first_sum_load])
        first_back(first_sum, grad, low, vectors, sums)

    def attn_step():
        ready([context_load])
        pieces([attn_net], lambda row: input_gradient(context, low[...], other_grads, row, 0))

    def context_step():
        ready(late_loads[:2])
        context_back(low, wide, context)

    def heads_step(part):
        if part == 0:
            ready([projected_load, probs_load])
        count = probs.shape[0]
        attend_back(projected, probs, context, sums, part * count // 2, (part + 1) * count // 2)

    def merged_step():
        def compute(row):
            for part in range(3):
                input_gradient(rows, projected[:, part * width : (part + 1) * width], other_grads, row, 1 + part)

        ready([rows_load])
        pieces(mergeds, compute)

    def pack_step():
        pack_sums(sums, bias_sum, block, table)
        pieces([small], lambda row: None)

    save = pltpu.make_async_copy(grad, states_out, save_sem)

    def states_step():
        ready(late_loads[2:])
        states_back(grad, projected, wide)
        save.start()

    def line_step(part):
        (line.add_pair, line.add_jump, line.add_far_axis, line.finish)[max(part - 1, 0)](
            *(((1,), (0,), (), (), (outer_out.at[pl.ds(SUBS // 2 * lines, SUBS // 2 * lines), :],))[part])
        )

    steps = {
        "outer": outer_step, "hidden": hidden_step, "inner": inner_step, "total": total_step, "norm": norm_step,
        "attn": attn_step, "context": context_step, "heads": heads_step, "merged": merged_step, "pack": pack_step,
        "states": states_step, "line": line_step, "go": go, "far": far, "near": near, "end": end,
    }
    for entry in SCHEDULE:
        steps[entry[0]](*entry[1:])
    for net in order + [line]:
        net.drain()
    save.wait()


def backward_all(depth, block, vectors, known, kept):
    low, high = jnp.bfloat16, jnp.float32
    (rows, activated, _, _, _, first_sum, _, _, projected, probs, _, _, inner, outer) = kept
    tokens, width = rows.shape
    hidden = activated.shape[1]
    unit = outer.shape
    lines = unit[3]
    own_rows = lines // SUBS
    dma, regular = pltpu.SemaphoreType.DMA, pltpu.SemaphoreType.REGULAR
    nets = 3 * SUBS + 2
    scratch = [
        pltpu.VMEM(unit, low),
        pltpu.VMEM(unit, low),
        pltpu.VMEM(unit, low),
        pltpu.VMEM((2 * SUBS, tokens, width), low),
        pltpu.VMEM((4, depth, lines, width), low),
        pltpu.VMEM((2, 2, depth, lines, width), low),
        pltpu.VMEM((2, depth, lines, width), low),
        pltpu.VMEM((2, depth - 1, lines, width), low),
        pltpu.VMEM((tokens, width), low),
        pltpu.VMEM((tokens, width), low),
        pltpu.VMEM((tokens, width), high),
        pltpu.VMEM((tokens, width), high),
        pltpu.VMEM((tokens, width), low),
        pltpu.VMEM(projected.shape, low),
        pltpu.VMEM(probs.shape, low),
        pltpu.VMEM((tokens, width), low),
        pltpu.VMEM((8, width), high),
        pltpu.VMEM((1, hidden), high),
        pltpu.VMEM((4, depth, 2, 16, 128), high),
        pltpu.VMEM((4, depth, 16, 128), high),
        pltpu.VMEM((1, 2, depth, 16, 128), high),
        pltpu.VMEM((1, depth, 16, 128), high),
        pltpu.VMEM((1, depth - 1, 16, 128), high),
        dma((40,)),
        dma,
        dma((nets, 4)), dma((nets, 4)), dma((nets, 2)), dma((nets, 2)), dma((nets,)), dma((nets,)),
        dma((nets, depth - 1)), dma((nets, depth - 1)),
        regular((4, SUBS)), regular((2, SUBS)), regular((SUBS,)), regular((SUBS, depth - 1)),
    ]
    shapes = [(tokens, width), (lines, width), (own_rows, hidden)] + [(own_rows, width)] * 4 + [(16, 128)]
    here = pl.BlockSpec(memory_space=pltpu.VMEM)
    away = pl.BlockSpec(memory_space=pl.ANY)
    return pl.pallas_call(
        functools.partial(backward_kernel, depth, block),
        out_shape=[jax.ShapeDtypeStruct(shape, high) for shape in shapes],
        in_specs=[here] * 2 + [away] * len(kept),
        out_specs=[away] + [here] * 7,
        scratch_shapes=scratch,
        compiler_params=pltpu.CompilerParams(
            collective_id=1, has_side_effects=True, vmem_limit_bytes=62 * 1024 * 1024
        ),
        name="backward",
    )(vectors, known, *kept)


def finish_kernel(block, *refs):
    count = 8
    table = refs[0]
    sources, targets = refs[1 : 1 + count], refs[1 + count : 1 + 2 * count]
    rows = refs[1 + 2 * count : 10 + 2 * count]
    held = refs[10 + 2 * count : 10 + 3 * count]
    in_sem, out_sem = refs[10 + 3 * count :]
    fetches = [pltpu.make_async_copy(source, target, in_sem.at[at]) for at, (source, target) in enumerate(zip(sources, held))]
    stores = [pltpu.make_async_copy(source, target, out_sem.at[at]) for at, (source, target) in enumerate(zip(held, targets))]
    for copy in fetches:
        copy.start()
    for index, row in enumerate(rows):
        row[...] = table[index, : row.shape[0]]
    for fetch, store in zip(fetches, stores):
        fetch.wait()
        store.start()
    for store in stores:
        store.wait()


def finish_all(block, table, arrays):
    shapes = [jax.ShapeDtypeStruct(array.shape, array.dtype) for array in arrays]
    shapes += [jax.ShapeDtypeStruct((block,), jnp.float32)] * 8 + [jax.ShapeDtypeStruct((128,), jnp.float32)]
    here = pl.BlockSpec(memory_space=pltpu.VMEM)
    away = pl.BlockSpec(memory_space=pltpu.HBM)
    dma = pltpu.SemaphoreType.DMA
    return pl.pallas_call(
        functools.partial(finish_kernel, block),
        out_shape=shapes,
        in_specs=[here] + [away] * len(arrays),
        out_specs=[away] * len(arrays) + [here] * 9,
        scratch_shapes=[pltpu.VMEM(array.shape, array.dtype) for array in arrays] + [dma((len(arrays),))] * 2,
        compiler_params=pltpu.CompilerParams(vmem_limit_bytes=60 * 1024 * 1024),
        name="finish",
    )(table, *arrays)


def normalize(hidden, gain, shift):
    center = hidden - jnp.mean(hidden, axis=-1, keepdims=True)
    spread = jnp.mean(center * center, axis=-1, keepdims=True)
    return center * lax.rsqrt(spread + epsilon) * gain + shift


def exact_gelu(value):
    return jax.nn.gelu(value, approximate=False)


def contract_rows(left, right):
    return lax.dot_general(
        left, right, (((0,), (0,)), ((), ())), preferred_element_type=jnp.float32
    )


def times_transposed(left, right):
    return lax.dot_general(
        left, right, (((1,), (1,)), ((), ())), preferred_element_type=jnp.float32
    )


def collect(merged, attn, inner, outer, vectors, widened):
    return (
        lax.all_gather(merged, ("dp", "fsdp"), axis=0, tiled=True),
        lax.all_gather(attn, ("dp", "fsdp"), axis=0, tiled=True),
        lax.all_gather(inner, ("dp", "fsdp"), axis=0, tiled=True),
        lax.all_gather(outer, ("dp", "fsdp"), axis=0, tiled=True),
        lax.all_gather(vectors, ("dp", "fsdp"), axis=0, tiled=True),
        lax.all_gather(widened, ("dp", "fsdp"), axis=0, tiled=True),
    )


def reduce_grads(merged, attn, inner, outer, vectors, widened):
    return (
        lax.psum_scatter(merged, ("dp", "fsdp"), scatter_dimension=0, tiled=True),
        lax.psum_scatter(attn, ("dp", "fsdp"), scatter_dimension=0, tiled=True),
        lax.psum_scatter(inner, ("dp", "fsdp"), scatter_dimension=0, tiled=True),
        lax.psum_scatter(outer, ("dp", "fsdp"), scatter_dimension=0, tiled=True),
        lax.psum_scatter(vectors, ("dp", "fsdp"), scatter_dimension=0, tiled=True),
        lax.psum_scatter(widened, ("dp", "fsdp"), scatter_dimension=0, tiled=True),
    )


def split_heads(projected, segments):
    total_rows, triple = projected.shape
    width = triple // 3
    return projected.reshape(segments, total_rows // segments, 3, HEADS, width // HEADS)


def attention_probs(queries, keysets, keep, scale):
    scores = (
        jnp.einsum("sqhd,skhd->shqk", queries, keysets, preferred_element_type=jnp.float32) * scale
    )
    scores = jnp.where(keep[:, None, None, :] > 0, scores, neg_fill)
    peaks = jnp.max(scores, axis=-1, keepdims=True)
    raised = jnp.exp(scores - peaks)
    return raised / jnp.sum(raised, axis=-1, keepdims=True)


def forward_pass(rows, keep, weights):
    merged, attn, inner, outer, vectors, widened = weights
    vector_full = vectors.astype(jnp.float32)
    width = rows.shape[1]
    scale = (width // HEADS) ** (-0.5)
    merged_bias = jnp.concatenate(
        (vector_full[:, 0], jnp.zeros((width,), jnp.float32), vector_full[:, 1])
    )
    projected = (jnp.dot(rows, merged, preferred_element_type=jnp.float32) + merged_bias).astype(
        jnp.bfloat16
    )
    split = split_heads(projected, keep.shape[0])
    probs = attention_probs(split[:, :, 0], split[:, :, 1], keep, scale).astype(jnp.bfloat16)
    context = jnp.einsum(
        "shqk,skhd->sqhd", probs, split[:, :, 2], preferred_element_type=jnp.float32
    )
    context = context.reshape(rows.shape[0], width).astype(jnp.bfloat16)
    attended = jnp.dot(context, attn, preferred_element_type=jnp.float32) + vector_full[:, 2]
    first_sum = rows.astype(jnp.float32) + attended
    first_norm = normalize(first_sum, vector_full[:, 3], vector_full[:, 4])
    first_low = first_norm.astype(jnp.bfloat16)
    inner_act = jnp.dot(first_low, inner, preferred_element_type=jnp.float32) + widened.astype(
        jnp.float32
    )
    activated = exact_gelu(inner_act).astype(jnp.bfloat16)
    outer_act = jnp.dot(activated, outer, preferred_element_type=jnp.float32) + vector_full[:, 5]
    second_sum = first_norm + outer_act
    encoded = normalize(second_sum, vector_full[:, 6], vector_full[:, 7]).astype(jnp.bfloat16)
    return (encoded, (projected, context, first_sum, first_low, inner_act, activated, second_sum))


def backward_pass(rows, keep, cotangent, weights, kept):
    merged, attn, inner, outer, vectors, widened = weights
    projected, context, first_sum, first_low, inner_act, activated, second_sum = kept
    vector_full = vectors.astype(jnp.float32)
    width = rows.shape[1]
    scale = (width // HEADS) ** (-0.5)
    second_out, second_pull = jax.vjp(normalize, second_sum, vector_full[:, 6], vector_full[:, 7])
    second_grad, second_gain_g, second_shift_g = second_pull(cotangent.astype(jnp.float32))
    outer_low = second_grad.astype(jnp.bfloat16)
    outer_bias_g = jnp.sum(outer_low.astype(jnp.float32), axis=0)
    outer_weight_g = contract_rows(activated, outer_low)
    act_grad = times_transposed(outer_low, outer)
    gelu_out, gelu_pull = jax.vjp(exact_gelu, inner_act)
    inner_low = gelu_pull(act_grad)[0].astype(jnp.bfloat16)
    inner_bias_g = jnp.sum(inner_low.astype(jnp.float32), axis=0)
    inner_weight_g = contract_rows(first_low, inner_low)
    first_total = second_grad + times_transposed(inner_low, inner)
    first_out, first_pull = jax.vjp(normalize, first_sum, vector_full[:, 3], vector_full[:, 4])
    first_grad, first_gain_g, first_shift_g = first_pull(first_total)
    attended_low = first_grad.astype(jnp.bfloat16)
    attn_bias_g = jnp.sum(attended_low.astype(jnp.float32), axis=0)
    attn_weight_g = contract_rows(context, attended_low)
    context_low = times_transposed(attended_low, attn).astype(jnp.bfloat16)
    split = split_heads(projected, keep.shape[0])
    queries = split[:, :, 0]
    keysets = split[:, :, 1]
    valuesets = split[:, :, 2]
    probs = attention_probs(queries, keysets, keep, scale)
    probs_low = probs.astype(jnp.bfloat16)
    context_heads = context_low.reshape(queries.shape)
    prob_grad = jnp.einsum(
        "sqhd,skhd->shqk", context_heads, valuesets, preferred_element_type=jnp.float32
    )
    value_grad = jnp.einsum(
        "shqk,sqhd->skhd", probs_low, context_heads, preferred_element_type=jnp.float32
    )
    score_low = (probs * (prob_grad - jnp.sum(probs * prob_grad, axis=-1, keepdims=True))).astype(
        jnp.bfloat16
    )
    query_grad = (
        jnp.einsum("shqk,skhd->sqhd", score_low, keysets, preferred_element_type=jnp.float32)
        * scale
    )
    key_grad = (
        jnp.einsum("shqk,sqhd->skhd", score_low, queries, preferred_element_type=jnp.float32)
        * scale
    )
    merged_low = jnp.stack((query_grad, key_grad, value_grad), axis=2).astype(jnp.bfloat16)
    merged_low = merged_low.reshape(rows.shape[0], 3 * width)
    merged_weight_g = contract_rows(rows, merged_low)
    merged_bias_g = jnp.sum(merged_low.astype(jnp.float32), axis=0)
    states_part = first_grad + times_transposed(merged_low, merged)
    vector_grads = jnp.stack(
        (
            merged_bias_g[:width],
            merged_bias_g[2 * width :],
            attn_bias_g,
            first_gain_g,
            first_shift_g,
            outer_bias_g,
            second_gain_g,
            second_shift_g,
        ),
        axis=1,
    )
    return (
        states_part,
        (
            merged_weight_g,
            attn_weight_g,
            inner_weight_g,
            outer_weight_g,
            vector_grads,
            inner_bias_g,
        ),
    )


def shards(depth, *arrays):
    (states, pad_mask, query_proj, key_proj, value_proj, attn_proj, query_bias, value_bias, attn_bias, first_gain,
     first_shift, inner_proj, inner_bias, outer_proj, outer_bias, second_gain, second_shift, out_grad) = arrays
    width = states.shape[1]
    short = (query_bias, value_bias, attn_bias, first_gain, first_shift, outer_bias, second_gain, second_shift)
    if depth:
        return kernel_shards(depth, short, states, pad_mask, query_proj, key_proj, value_proj, attn_proj, inner_proj,
                             inner_bias, outer_proj, out_grad)
    merged_shard = jnp.concatenate((query_proj, key_proj, value_proj), axis=1)
    fetched = collect(merged_shard, attn_proj, inner_proj, outer_proj, jnp.stack(short, axis=1), inner_bias)
    encoded, kept = forward_pass(states, pad_mask, fetched)
    states_part, totals = backward_pass(states, pad_mask, out_grad, fetched, kept)
    merged_sum, attn_sum, inner_sum, outer_sum, vector_sum, widened_sum = reduce_grads(*totals)
    return ordered(encoded, states_part, merged_sum, attn_sum, inner_sum, outer_sum, vector_sum.T, widened_sum)


def ordered(encoded, states_part, merged_sum, attn_sum, inner_sum, outer_sum, vectors, widened_sum):
    width = attn_sum.shape[1]
    return (encoded, states_part, merged_sum[:, :width], merged_sum[:, width : 2 * width], merged_sum[:, 2 * width :],
            attn_sum, vectors[0], vectors[1], vectors[2], vectors[3], vectors[4], inner_sum, widened_sum, outer_sum,
            vectors[5], vectors[6], vectors[7])


def kernel_shards(depth, short, states, pad_mask, query_proj, key_proj, value_proj, attn_proj, inner_proj, inner_bias,
                  outer_proj, out_grad):
    width = states.shape[1]
    block = short[0].shape[0]
    (merged, attn, inner, outer, encoded, projected, probs, context, first_sum, first_low, activated, slope, second_grad,
     outer_low, vectors, sums) = forward_all(
        depth, block, states, pad_mask, out_grad,
        (query_proj, key_proj, value_proj, attn_proj, inner_proj, outer_proj, *short, inner_bias))
    states_part, outer_sum, inner_sum, query_sum, key_sum, value_sum, attn_sum, table_sum = backward_all(
        depth, block, vectors, sums,
        (states, activated, slope, outer_low, second_grad, first_sum, first_low, context, projected, probs,
         merged.reshape(width, -1), attn.reshape(width, -1), inner, outer))
    (encoded, states_part, query_sum, key_sum, value_sum, attn_sum, inner_sum, outer_sum, *rows) = finish_all(
        block, table_sum, (encoded, states_part, query_sum, key_sum, value_sum, attn_sum, inner_sum, outer_sum))
    return (encoded, states_part, query_sum, key_sum, value_sum, attn_sum, *rows[:5], inner_sum, rows[8], outer_sum,
            *rows[5:8])


def solution(mesh):
    dps, others = mesh.shape["dp"], mesh.shape["fsdp"]
    matrix = P(("dp", "fsdp"), None)
    vector = P(("dp", "fsdp"))

    def whole(*arrays):
        rows = arrays[2].shape[0] // (dps * others)
        tiles = rows % 16 == 0 and arrays[12].shape[0] == 128 * dps * others
        depth = others // 2 if tiles and dps == 4 and others == 2 * dps else 0
        return jax.shard_map(
            functools.partial(shards, depth),
            mesh=mesh,
            in_specs=(matrix,) * 6 + (vector,) * 5 + (matrix, vector, matrix) + (vector,) * 3 + (matrix,),
            out_specs=(matrix,) * 6 + (vector,) * 5 + (matrix, vector, matrix) + (vector,) * 3,
            check_vma=False,
        )(*arrays)

    return whole
```
